32 devices in a mesh: batch: 16 (over z, x, core), src: 2 (over y).
Axes of the slice: x: 2, y: 2, z: 4, core: 2. Of those that a mesh axis runs over, the one named last changes fastest.
Arguments:
- dec_input: bfloat16 [16384, 512], P(('batch', 'src')), may hold values from -6 to 6
- enc_output: bfloat16 [65536, 512], P(('batch', 'src')), may hold values from -6 to 6
- segment_ids: int32 [32, 512], P(('batch', 'src')), may hold values from 0 to 7, never falling along the last dimension, each value on 1 to 128 neighbouring positions
- padding: int32 [32, 512], P(('batch', 'src')), may hold values 0 or 1
- pair_ids: int32 [32, 8], P(('batch', 'src')), may hold values from 0 to 7
- src_lengths: int32 [16, 16], P('batch'), may hold values from 1 to 2304, 4096 in all within a row
- delete_labels: int32 [32, 512], P(('batch', 'src')), may hold values 0 or 1
- insert_counts: int32 [32, 512], P(('batch', 'src')), may hold values from 0 to 255
- masked_positions: int32 [32, 16], P(('batch', 'src')), may hold values from 0 to 511, as said below
- masked_targets: int32 [32, 16], P(('batch', 'src')), may hold values from 0 to 32767
- norm_gain: bfloat16 [4, 512], P(None, ('batch', 'src')), may hold values from 0.5 to 1.5
- norm_bias: bfloat16 [4, 512], P(None, ('batch', 'src')), may hold values from -1 to 1
- pair_table: bfloat16 [8, 512], P(None, ('batch', 'src')), may hold values from -3 to 3
- self_qkv: bfloat16 [512, 1536], P(('batch', 'src')), may hold values from -0.25 to 0.25
- self_out: bfloat16 [512, 512], P(('batch', 'src')), may hold values from -1 to 1
- cross_q: bfloat16 [512, 512], P(('batch', 'src')), may hold values from -0.25 to 0.25
- cross_kv: bfloat16 [512, 1024], P(('batch', 'src')), may hold values from -0.25 to 0.25
- cross_out: bfloat16 [512, 512], P(('batch', 'src')), may hold values from -1 to 1
- ffn_in: bfloat16 [512, 2048], P(('batch', 'src')), may hold values from -0.25 to 0.25
- ffn_out: bfloat16 [2048, 512], P(('batch', 'src')), may hold values from -0.125 to 0.125
- w_delete: bfloat16 [512, 2], P(('batch', 'src')), may hold values from -0.75 to 0.75
- w_insert: bfloat16 [1024, 256], P(('batch', 'src')), may hold values from -0.375 to 0.375
- w_vocab: bfloat16 [32768, 512], P(('batch', 'src')), may hold values from -0.5 to 0.5
Outputs:
- block_out: bfloat16 [16384, 512], P(('batch', 'src'))
- grad_input: bfloat16 [16384, 512], P(('batch', 'src'))
- grad_enc: bfloat16 [65536, 512], P(('batch', 'src'))
- grad_norm_gain: float32 [4, 512], P(None, ('batch', 'src'))
- grad_norm_bias: float32 [4, 512], P(None, ('batch', 'src'))
- grad_pair_table: float32 [8, 512], P(None, ('batch', 'src'))
- grad_self_qkv: float32 [512, 1536], P(('batch', 'src'))
- grad_self_out: float32 [512, 512], P(('batch', 'src'))
- grad_cross_q: float32 [512, 512], P(('batch', 'src'))
- grad_cross_kv: float32 [512, 1024], P(('batch', 'src'))
- grad_cross_out: float32 [512, 512], P(('batch', 'src'))
- grad_ffn_in: float32 [512, 2048], P(('batch', 'src'))
- grad_ffn_out: float32 [2048, 512], P(('batch', 'src'))
- grad_delete: float32 [512, 2], P(('batch', 'src'))
- grad_insert: float32 [1024, 256], P(('batch', 'src'))
- grad_vocab: float32 [32768, 512], P(('batch', 'src'))
- mean_loss: float32 [], replicated
- token_losses: float32 [32, 16], P(('batch', 'src'))
The draws below stay inside these ranges and needn't reach their ends.
Inputs may be any that keep to these rules, and one draw needn't show every extreme that they name: `masked_positions`: within each row the 16 positions are distinct. `src_lengths`: each row sums to 4096. `segment_ids`: never falling along a row; every number is used in every row.
All inputs are finite; a program needn't handle non-finite values. No bound on the sum of `padding` or of `delete_labels` on one device may be relied on, other than what follows from the above.
Results may differ from the reference program's by a relative error of at most 0.02.
Values may be sent and summed in bfloat16 or wider, within the bound.
A program may use at most 320 MiB of HBM per device.

```python
import math
import jax
import jax.numpy as jnp
import numpy as np
from jax import lax

D = 512
HD = 64
FF = 2048
V = 32768
PLH = 256
PAIRS = 8
SEGS = 8
TOK_DEV = 512
SRC_DEV = 2048
MASKED = 16
ROWS = 32
TOKENS = 16384
SOURCE = 65536
N_BATCH = 16
N_SRC = 2


def draw_masked_positions(key, part):
    key = jax.random.fold_in(key, 11)
    row_keys = jax.random.split(key, ROWS)
    chosen = jax.vmap(lambda row_key: jax.random.permutation(row_key, TOK_DEV)[:MASKED])(row_keys)
    return jnp.sort(chosen, axis=1).astype(jnp.int32)


def plant(array, stream_key, low, high):
    extent = array.shape
    place = [jax.random.randint(jax.random.fold_in(stream_key, axis), (), 0, extent[axis]) for axis in range(len(extent))]
    array = array.at[tuple(place)].set(low)
    longest = extent.index(max(extent))
    place[longest] = (place[longest] + 1) % extent[longest]
    return array.at[tuple(place)].set(high)


def level_of(key, extent, cuts, low, top_value):
    def one(position, shards_of):
        draws = jax.random.uniform(jax.random.fold_in(jax.random.fold_in(key, 6), position), (shards_of,), jnp.float32, low / len(cuts), top_value / len(cuts))
        return jnp.repeat(jnp.exp(draws), extent[position] // shards_of).reshape((-1,) + (1,) * (len(extent) - position - 1))

    factor_of = one(*cuts[0])
    for cut in cuts[1:]:
        factor_of = factor_of * one(*cut)
    return factor_of


def rank_bounds(number_of, lean):
    weights = [(1 << 20) // math.isqrt(grade ** lean) + 1 for grade in range(1, number_of + 1)]
    scale = 1 + sum(weights) // (1 << 30)
    return np.cumsum(np.array([max(1, weight // scale) for weight in weights]))


def ranked(rng, extent, amount, slope):
    table = rank_bounds(amount, slope)
    lot = jax.random.randint(jax.random.fold_in(rng, 1), extent, 0, int(table[amount - 1]))
    rank = jnp.searchsorted(jnp.asarray(table, jnp.int32), lot, side="right")
    return jax.random.permutation(jax.random.fold_in(rng, 2), amount)[rank].astype(jnp.int32)


def length_profile(amount, total, bound, skew):
    loads = [(1 << 20) // math.isqrt(grade ** skew) + 1 for grade in range(2, amount + 1)]
    spare, counts = total - bound - (amount - 1), [1] * (amount - 1)
    while spare > 0:
        free = [i for i in range(amount - 1) if counts[i] < bound]
        whole, budget = sum([loads[i] for i in free]), spare
        for i in free:
            addition = min(bound - counts[i], max(1, budget * loads[i] // whole), spare)
            counts[i] = counts[i] + addition
            spare = spare - addition
    return np.array([bound] + counts)


def ragged(key, number_of, total, limit, lean):
    if number_of == 2:
        one = jax.random.randint(key, (), max(1, total - limit), min(limit, total - 1) + 1)
        return jnp.stack([one, total - one])
    lengths = jnp.asarray(length_profile(number_of, total, limit, lean), jnp.int32)
    twos = (number_of - 1) // 2
    source_of, taker = lengths[1:1 + 2 * twos:2], lengths[2:2 + 2 * twos:2]
    room = jnp.minimum(source_of - 1, limit - taker)
    passed = jax.random.randint(jax.random.fold_in(key, 1), (twos,), 0, 1 << 20) % (room + 1)
    lengths = lengths.at[1:1 + 2 * twos:2].set(source_of - passed).at[2:2 + 2 * twos:2].set(taker + passed)
    return lengths[jax.random.permutation(jax.random.fold_in(key, 2), number_of)]


def gaussian(rng, extent, width, reach, cuts=(), kind=jnp.bfloat16):
    result = width * jax.random.normal(rng, extent, jnp.float32)
    if cuts:
        result = result * level_of(rng, extent, cuts, -0.22, 0.18)
    return jnp.clip(result, -reach, reach).astype(kind)


def setup_inputs(seed: int = 0) -> dict:
    splits = jax.random.split(jax.random.key(seed), 24)
    dec_input = gaussian(splits[0], (TOKENS, D), 1.0, 6.0, ((0, 32),))
    enc_output = gaussian(splits[1], (SOURCE, D), 1.0, 6.0, ((0, 32),))
    segment_ids = jax.vmap(lambda own: jnp.searchsorted(jnp.cumsum(ragged(own, SEGS, TOK_DEV, max(TOK_DEV // 4, 8), 2)), jnp.arange(TOK_DEV), side="right"))(jax.random.split(splits[2], ROWS)).reshape((ROWS, TOK_DEV)).astype(jnp.int32)
    padding = plant((jax.random.randint(splits[3], (ROWS, TOK_DEV), 0, 8) < 1).astype(jnp.int32), jax.random.fold_in(splits[3], 1), 0, 1)
    pair_ids = plant(jax.random.randint(splits[4], (ROWS, SEGS), 0, PAIRS), jax.random.fold_in(splits[4], 1), 0, PAIRS - 1).astype(jnp.int32)
    src_lengths = jax.vmap(lambda own: ragged(own, N_SRC * SEGS, N_SRC * SRC_DEV, SRC_DEV + SRC_DEV // 8, 2))(jax.random.split(splits[5], N_BATCH)).reshape((N_BATCH, N_SRC * SEGS)).astype(jnp.int32)
    delete_labels = plant((jax.random.randint(splits[6], (ROWS, TOK_DEV), 0, 3) < 1).astype(jnp.int32), jax.random.fold_in(splits[6], 1), 0, 1)
    insert_counts = plant(ranked(splits[7], (ROWS, TOK_DEV), PLH, 2), jax.random.fold_in(splits[7], 3), 0, PLH - 1).astype(jnp.int32)
    masked_positions = draw_masked_positions(jax.random.fold_in(splits[23], 71), 0)
    masked_targets = plant(ranked(splits[9], (ROWS, MASKED), V, 2), jax.random.fold_in(splits[9], 3), 0, V - 1).astype(jnp.int32)
    norm_gain = jnp.clip(1.0 + 0.1 * jax.random.normal(splits[10], (4, D), jnp.float32), 0.5, 1.5).astype(jnp.bfloat16)
    norm_bias = gaussian(splits[11], (4, D), 0.2, 1.0, ((1, 32),))
    pair_table = gaussian(splits[12], (PAIRS, D), 0.5, 3.0, ((1, 32),))
    self_qkv = gaussian(splits[13], (D, 3 * D), D ** -0.5, 0.25, ((0, 32),))
    self_out = gaussian(splits[14], (D, D), (D // 16) ** -0.5, 1.0, ((0, 32),))
    cross_q = gaussian(splits[15], (D, D), D ** -0.5, 0.25, ((0, 32),))
    cross_kv = gaussian(splits[16], (D, 2 * D), D ** -0.5, 0.25, ((0, 32),))
    cross_out = gaussian(splits[17], (D, D), (D // 16) ** -0.5, 1.0, ((0, 32),))
    ffn_in = gaussian(splits[18], (D, FF), D ** -0.5, 0.25, ((0, 32),))
    ffn_out = gaussian(splits[19], (FF, D), FF ** -0.5, 0.125, ((0, 32),))
    w_delete = gaussian(splits[20], (D, 2), (D // 8) ** -0.5, 0.75, ((0, 32),))
    w_insert = gaussian(splits[21], (2 * D, PLH), (D // 2) ** -0.5, 0.375, ((0, 32),))
    w_vocab = gaussian(splits[22], (V, D), (D // 4) ** -0.5, 0.5, ((0, 32),))
    return {"dec_input": dec_input, "enc_output": enc_output, "segment_ids": segment_ids, "padding": padding, "pair_ids": pair_ids, "src_lengths": src_lengths, "delete_labels": delete_labels, "insert_counts": insert_counts, "masked_positions": masked_positions, "masked_targets": masked_targets, "norm_gain": norm_gain, "norm_bias": norm_bias, "pair_table": pair_table, "self_qkv": self_qkv, "self_out": self_out, "cross_q": cross_q, "cross_kv": cross_kv, "cross_out": cross_out, "ffn_in": ffn_in, "ffn_out": ffn_out, "w_delete": w_delete, "w_insert": w_insert, "w_vocab": w_vocab}


@jax.custom_vjp
def low(v):
    return lax.optimization_barrier(v.astype(jnp.bfloat16)).astype(jnp.float32)

@jax.custom_vjp
def low_back(v):
    return v

def low_keep(v):
    return (low(v), None)

def low_pass(kept, grad):
    return (grad,)

def back_keep(v):
    return (v, None)

def back_low(kept, grad):
    return (low(grad),)
low.defvjp(low_keep, low_pass)
low_back.defvjp(back_keep, back_low)
epsilon = 1e-05
score_scale = 0.125
masked_fill = -1e+30
highest = lax.Precision.HIGHEST

def matmul(left, right):
    return jnp.dot(left, right, precision=highest)

def layer_norm(activation, scale_row, shift_row):
    centred = activation - lax.optimization_barrier(jnp.mean(activation, axis=-1, keepdims=True))
    spread = lax.optimization_barrier(jnp.mean(centred * centred, axis=-1, keepdims=True))
    return centred * lax.rsqrt(spread + epsilon) * scale_row + shift_row

def attention(queries, key_rows, values, allowed):
    count_q = queries.shape[0]
    split_q = queries.reshape(count_q, -1, HD)
    split_k = key_rows.reshape(key_rows.shape[0], -1, HD)
    split_v = values.reshape(values.shape[0], -1, HD)
    scores = low_back(jnp.einsum('qhd,khd->hqk', split_q, split_k, precision=highest) * score_scale)
    scores = jnp.where(allowed[None], scores, masked_fill)
    probabilities = low(jax.nn.softmax(scores, axis=-1))
    mixture = jnp.einsum('hqk,khd->qhd', probabilities, split_v, precision=highest)
    return mixture.reshape(count_q, -1)

def cross_entropy(logits, labels):
    chosen = jnp.take_along_axis(logits, labels[:, None], axis=1)[:, 0]
    return jax.nn.logsumexp(logits, axis=1) - chosen

def pair_step(params, inputs):
    norm_gain, norm_bias, pair_table, self_qkv, self_out, cross_q, cross_kv, cross_out, ffn_in, ffn_out, w_delete, w_insert, w_vocab = params
    dec_rows, enc_row, seg_rows, pad_rows, pair_rows, src_lengths, delete_rows, insert_rows, position_rows, target_rows = inputs
    model_width = dec_rows.shape[-1]
    tok_count = dec_rows.shape[1]
    src_total = enc_row.shape[0]
    seg_ends = jnp.cumsum(src_lengths)
    src_segment = lax.optimization_barrier(jnp.sum((jnp.arange(src_total, dtype=jnp.int32)[:, None] >= seg_ends[None, :]).astype(jnp.int32), axis=1))
    kv_proj = low_back(low(matmul(enc_row, cross_kv)))
    cross_keys = kv_proj[:, :model_width]
    cross_values = kv_proj[:, model_width:]
    diagonal = jnp.eye(tok_count, dtype=bool)
    total_loss = jnp.zeros((), jnp.float32)
    outputs = []
    token_parts = []
    for row_pos in range(N_SRC):
        segment = seg_rows[row_pos]
        not_padding = 1 - pad_rows[row_pos]
        keep_float = not_padding.astype(jnp.float32)
        token_pair = pair_rows[row_pos][segment]
        pair_onehot = (token_pair[:, None] == jnp.arange(PAIRS, dtype=jnp.int32)[None, :]).astype(jnp.float32)
        start_state = dec_rows[row_pos] + matmul(pair_onehot, pair_table)
        normed_one = low(layer_norm(start_state, norm_gain[0], norm_bias[0]))
        qkv_proj = low_back(low(matmul(normed_one, self_qkv)))
        self_allowed = (segment[:, None] == segment[None, :]) & ((not_padding[None, :] == 1) | diagonal)
        self_attn = low_back(low(attention(qkv_proj[:, :model_width], qkv_proj[:, model_width:2 * model_width], qkv_proj[:, 2 * model_width:], self_allowed)))
        after_self = start_state + low_back(matmul(self_attn, self_out))
        normed_two = low(layer_norm(after_self, norm_gain[1], norm_bias[1]))
        cross_query = low_back(low(matmul(normed_two, cross_q)))
        cross_allowed = (row_pos * SEGS + segment)[:, None] == src_segment[None, :]
        cross_attn = low_back(low(attention(cross_query, cross_keys, cross_values, cross_allowed)))
        after_cross = after_self + low_back(matmul(cross_attn, cross_out))
        normed_three = low(layer_norm(after_cross, norm_gain[2], norm_bias[2]))
        pre_act = low_back(matmul(normed_three, ffn_in))
        activation = low(jax.nn.gelu(pre_act, approximate=True))
        block_state = after_cross + low_back(matmul(activation, ffn_out))
        head_in = low(layer_norm(block_state, norm_gain[3], norm_bias[3]))
        delete_logits = low_back(matmul(head_in, w_delete))
        delete_loss = jnp.sum(keep_float * cross_entropy(delete_logits, delete_rows[row_pos]))
        next_in = jnp.concatenate([head_in[1:], jnp.zeros((1, model_width), jnp.float32)], axis=0)
        insert_logits = low_back(matmul(jnp.concatenate([head_in, next_in], axis=1), w_insert))
        next_segment = jnp.concatenate([segment[1:], -jnp.ones((1,), jnp.int32)])
        next_keep = jnp.concatenate([not_padding[1:], jnp.zeros((1,), jnp.int32)])
        insert_valid = ((segment == next_segment) & (not_padding == 1) & (next_keep == 1)).astype(jnp.float32)
        insert_loss = jnp.sum(insert_valid * cross_entropy(insert_logits, insert_rows[row_pos]))
        picked = head_in[position_rows[row_pos]]
        vocab_logits = low_back(jnp.dot(picked, w_vocab.T, precision=highest))
        picked_keep = keep_float[position_rows[row_pos]]
        token_rows = picked_keep * cross_entropy(vocab_logits, target_rows[row_pos])
        token_loss = jnp.sum(token_rows)
        total_loss = total_loss + delete_loss + insert_loss + token_loss
        outputs.append(block_state)
        token_parts.append(token_rows)
    return (total_loss, (jnp.stack(outputs), jnp.stack(token_parts)))

def reference(dec_input, enc_output, segment_ids, padding, pair_ids, src_lengths, delete_labels, insert_counts, masked_positions, masked_targets, norm_gain, norm_bias, pair_table, self_qkv, self_out, cross_q, cross_kv, cross_out, ffn_in, ffn_out, w_delete, w_insert, w_vocab):
    params = tuple((weight.astype(jnp.float32) for weight in (norm_gain, norm_bias, pair_table, self_qkv, self_out, cross_q, cross_kv, cross_out, ffn_in, ffn_out, w_delete, w_insert, w_vocab)))
    dec_rows = dec_input.astype(jnp.float32).reshape(N_BATCH, N_SRC, TOK_DEV, D)
    enc_rows = enc_output.astype(jnp.float32).reshape(N_BATCH, N_SRC * SRC_DEV, D)
    int_pieces = (segment_ids.reshape(N_BATCH, N_SRC, TOK_DEV), padding.reshape(N_BATCH, N_SRC, TOK_DEV), pair_ids.reshape(N_BATCH, N_SRC, SEGS), src_lengths, delete_labels.reshape(N_BATCH, N_SRC, TOK_DEV), insert_counts.reshape(N_BATCH, N_SRC, TOK_DEV), masked_positions.reshape(N_BATCH, N_SRC, MASKED), masked_targets.reshape(N_BATCH, N_SRC, MASKED))
    step_fn = jax.checkpoint(pair_step)

    def forward(weights, dec_all, enc_all):

        def scan_body(carry, pieces):
            loss_part, extras = step_fn(weights, pieces)
            return (carry + loss_part, extras)
        loss_sum, extras_all = lax.scan(scan_body, jnp.zeros((), jnp.float32), (dec_all, enc_all) + int_pieces)
        return (loss_sum, extras_all)
    loss_sum, pull_back, extras_all = jax.vjp(forward, params, dec_rows, enc_rows, has_aux=True)
    blocks, token_all = extras_all
    grad_params, grad_dec, grad_src = pull_back(jnp.ones((), jnp.float32))
    grad_scale = TOKENS ** (-0.5)
    return (blocks.reshape(TOKENS, D).astype(jnp.bfloat16), grad_dec.reshape(TOKENS, D).astype(jnp.bfloat16), grad_src.reshape(SOURCE, D).astype(jnp.bfloat16), grad_params[0] * grad_scale, grad_params[1] * grad_scale, grad_params[2] * grad_scale, grad_params[3] * grad_scale, grad_params[4] * grad_scale, grad_params[5] * grad_scale, grad_params[6] * grad_scale, grad_params[7] * grad_scale, grad_params[8] * grad_scale, grad_params[9] * grad_scale, grad_params[10] * grad_scale, grad_params[11] * grad_scale, grad_params[12] * grad_scale, loss_sum / TOKENS, token_all.reshape(ROWS, MASKED))
```

```python
from functools import partial

import jax
import jax.numpy as jnp
from jax import lax
from jax.experimental import pallas as pl
from jax.experimental.pallas import tpu as pltpu
from jax.sharding import PartitionSpec as P

HD = 64
PAIRS = 8
SEGS = 8


epsilon = 1e-05
score_scale = 0.125
masked_fill = -1e30
BLOCK = 512
PIECES = 18


MESH = pl.DeviceIdType.MESH
ANY = pl.BlockSpec(memory_space=pl.ANY)
BOTH = ("batch", "src")
LOW = jnp.bfloat16
WIDE = jnp.float32


def greet(peers):
    barrier = pltpu.get_barrier_semaphore()
    for peer in peers:
        pl.semaphore_signal(barrier, inc=1, device_id=peer, device_id_type=MESH)
    pl.semaphore_wait(barrier, len(peers))


def remote(src, dst, send, recv, peer):
    return pltpu.make_async_remote_copy(
        src_ref=src,
        dst_ref=dst,
        send_sem=send,
        recv_sem=recv,
        device_id=peer,
        device_id_type=MESH,
    )


class Place:
    def __init__(self, depth):
        b = lax.axis_index("batch")
        self.depth = depth
        self.y = lax.axis_index("src")
        self.c = lax.rem(b, 2)
        self.x = lax.rem(b // 2, 2)
        self.z = b // 4

    def at(self, z=None, x=None, c=None, y=None):
        z = self.z if z is None else z
        x = self.x if x is None else x
        c = self.c if c is None else c
        y = self.y if y is None else y
        return ((z * 2 + x) * 2 + c, y)

    def along(self, k):
        return self.at(z=lax.rem(self.z + k, self.depth))

    def peers(self):
        return [self.along(k) for k in range(1, self.depth)] + [
            self.at(x=1 - self.x),
            self.at(y=1 - self.y),
            self.at(c=1 - self.c),
        ]


def gather_kernel(depth, bounds, x_ref, g_ref, own_sem, send, recv):
    me = Place(depth)
    z, x, c, y = me.z, me.x, me.c, me.y
    greet(me.peers())
    own = pltpu.make_async_copy(x_ref, g_ref.at[z, x, c, y], own_sem)
    own.start()
    count = len(bounds) - 1
    started = [[None] * 4 for _ in range(count)]

    def launch(k, stage):
        low, high = bounds[k], bounds[k + 1]
        middle = (low + high) // 2
        if stage == 0:
            rows = pl.ds(low, high - low)
            copies = [
                remote(
                    x_ref.at[rows],
                    g_ref.at[z, x, c, y, rows],
                    send.at[k, j],
                    recv.at[k, j],
                    me.along(j + 1),
                )
                for j in range(depth - 1)
            ]
        elif stage == 3:
            block = g_ref.at[:, :, c, :, pl.ds(low, high - low)]
            slot = depth + 3
            copies = [remote(block, block, send.at[k, slot], recv.at[k, slot], me.at(c=1 - c))]
        else:
            one, two = pl.ds(low, middle - low), pl.ds(middle, high - middle)
            if stage == 1:
                blocks = (g_ref.at[:, x, c, y, one], g_ref.at[:, x, c, y, two])
                peers = (me.at(x=1 - x), me.at(y=1 - y))
            else:
                blocks = (g_ref.at[:, :, c, y, one], g_ref.at[:, x, c, :, two])
                peers = (me.at(y=1 - y), me.at(x=1 - x))
            slot = depth - 1 + 2 * (stage - 1)
            copies = [
                remote(block, block, send.at[k, slot + i], recv.at[k, slot + i], peer)
                for i, (block, peer) in enumerate(zip(blocks, peers))
            ]
        for copy in copies:
            copy.start()
        started[k][stage] = copies

    for step in range(count + 4):
        for stage in range(4, -1, -1):
            k = step - stage
            if not 0 <= k < count:
                continue
            if stage == 1 and k == 0:
                own.wait()
            if stage > 0:
                for copy in started[k][stage - 1]:
                    copy.wait_recv()
            if stage < 4:
                launch(k, stage)
    for stages in started:
        for copies in stages:
            for copy in copies:
                copy.wait_send()


def gather_packed(packed, depth, bounds):
    count = len(bounds) - 1
    rows, cols = packed.shape
    out = pl.pallas_call(
        partial(gather_kernel, depth, bounds),
        name="gather_packed",
        out_shape=jax.ShapeDtypeStruct((depth, 2, 2, 2, rows, cols), packed.dtype),
        in_specs=[ANY],
        out_specs=ANY,
        scratch_shapes=[
            pltpu.SemaphoreType.DMA(()),
            pltpu.SemaphoreType.DMA((count, depth + 4)),
            pltpu.SemaphoreType.DMA((count, depth + 4)),
        ],
        compiler_params=pltpu.CompilerParams(collective_id=0, has_side_effects=True),
    )(packed)
    return out.reshape(depth * 8, rows, cols)


def reduce_kernel(depth, bounds, s_ref, o_ref, mine, got_c, got_1, got_2, got_z, load, send, recv):
    me = Place(depth)
    z, x, c, y = me.z, me.x, me.c, me.y
    greet(me.peers())
    count = len(bounds) - 1
    pieces = [pl.ds(lo, hi - lo) for lo, hi in zip(bounds[:-1], bounds[1:])]
    loads = []
    for k, rows in enumerate(pieces):
        copy = pltpu.make_async_copy(s_ref.at[:, :, c, :, rows], mine.at[:, :, :, rows], load.at[k])
        copy.start()
        loads.append(copy)
    started = [[None] * 4 for _ in pieces]

    def halves(k):
        low, high = bounds[k], bounds[k + 1]
        middle = (low + high) // 2
        return pl.ds(low, middle - low), pl.ds(middle, high - middle)

    def launch(k, stage):
        rows = pieces[k]
        one, two = halves(k)
        if stage == 0:
            blocks = [s_ref.at[:, :, 1 - c, :, rows]]
            places = [got_c.at[:, :, :, rows]]
            peers = [me.at(c=1 - c)]
        elif stage == 1:
            blocks = [mine.at[:, :, 1 - y, one], mine.at[:, 1 - x, :, two]]
            places = [got_1.at[:, :, one], got_1.at[:, :, two]]
            peers = [me.at(y=1 - y), me.at(x=1 - x)]
        elif stage == 2:
            blocks = [mine.at[:, 1 - x, y, one], mine.at[:, x, 1 - y, two]]
            places = [got_2.at[:, one], got_2.at[:, two]]
            peers = [me.at(x=1 - x), me.at(y=1 - y)]
        else:
            hops = range(1, depth)
            blocks = [mine.at[lax.rem(z + j, depth), x, y, rows] for j in hops]
            places = [got_z.at[j - 1, rows] for j in hops]
            peers = [me.along(j) for j in hops]
        slot = (0, 1, 3, 5)[stage]
        copies = [
            remote(block, where, send.at[k, slot + i], recv.at[k, slot + i], peer)
            for i, (block, where, peer) in enumerate(zip(blocks, places, peers))
        ]
        for copy in copies:
            copy.start()
        started[k][stage] = copies

    def add(where, other):
        mine[where] = (mine[where].astype(WIDE) + other.astype(WIDE)).astype(LOW)

    def absorb(k, stage):
        rows = pieces[k]
        one, two = halves(k)
        for copy in started[k][stage]:
            copy.wait_recv()
        if stage == 0:
            loads[k].wait()

            @pl.loop(0, depth)
            def _(zz):
                for xx in range(2):
                    for yy in range(2):
                        add((zz, xx, yy, rows), got_c[zz, xx, yy, rows])

        elif stage == 1:

            @pl.loop(0, depth)
            def _(zz):
                for q in range(2):
                    add((zz, q, y, one), got_1[zz, q, one])
                    add((zz, x, q, two), got_1[zz, q, two])

        elif stage == 2:

            @pl.loop(0, depth)
            def _(zz):
                add((zz, x, y, rows), got_2[zz, rows])

        else:
            total = mine[z, x, y, rows].astype(WIDE)
            for j in range(1, depth):
                total = total + got_z[j - 1, rows].astype(WIDE)
            o_ref[rows] = total

    for step in range(count + 4):
        for stage in range(4, -1, -1):
            k = step - stage
            if not 0 <= k < count:
                continue
            if stage > 0:
                absorb(k, stage - 1)
            if stage < 4:
                launch(k, stage)
    for stages in started:
        for copies in stages:
            for copy in copies:
                copy.wait_send()


def reduce_packed(parts, depth, bounds):
    count = len(bounds) - 1
    rows, cols = parts.shape[1:]
    return pl.pallas_call(
        partial(reduce_kernel, depth, bounds),
        name="reduce_packed",
        out_shape=jax.ShapeDtypeStruct((rows, cols), WIDE),
        in_specs=[ANY],
        out_specs=pl.BlockSpec(memory_space=pltpu.VMEM),
        scratch_shapes=[
            pltpu.VMEM((depth, 2, 2, rows, cols), LOW),
            pltpu.VMEM((depth, 2, 2, rows, cols), LOW),
            pltpu.VMEM((depth, 2, rows, cols), LOW),
            pltpu.VMEM((depth, rows, cols), LOW),
            pltpu.VMEM((depth - 1, rows, cols), LOW),
            pltpu.SemaphoreType.DMA((count,)),
            pltpu.SemaphoreType.DMA((count, depth + 4)),
            pltpu.SemaphoreType.DMA((count, depth + 4)),
        ],
        compiler_params=pltpu.CompilerParams(
            collective_id=1, has_side_effects=True, vmem_limit_bytes=48 << 20
        ),
    )(parts.reshape((depth, 2, 2, 2, rows, cols)))


def swap_kernel(count, *refs):
    ins, outs, (send, recv) = refs[:count], refs[count : 2 * count], refs[2 * count :]
    peer = (lax.axis_index("batch"), 1 - lax.axis_index("src"))
    greet([peer])
    copies = [
        remote(ins[k], outs[k], send.at[k], recv.at[k], peer) for k in range(count)
    ]
    for copy in copies:
        copy.start()
    for copy in copies:
        copy.wait()


def swap(arrays, cid):
    count = len(arrays)
    return pl.pallas_call(
        partial(swap_kernel, count),
        name=f"swap_{cid}",
        out_shape=[jax.ShapeDtypeStruct(a.shape, a.dtype) for a in arrays],
        in_specs=[ANY] * count,
        out_specs=[ANY] * count,
        scratch_shapes=[
            pltpu.SemaphoreType.DMA((count,)),
            pltpu.SemaphoreType.DMA((count,)),
        ],
        compiler_params=pltpu.CompilerParams(collective_id=cid, has_side_effects=True),
    )(*arrays)


def spread_kernel(count, devices, split, *refs):
    ins, outs, (own_sem, send, recv) = refs[:count], refs[count : 2 * count], refs[2 * count :]
    pos = lax.axis_index(BOTH)
    barrier = pltpu.get_barrier_semaphore()

    def peer_of(k):
        other = lax.rem(pos + k, devices)
        return other, (other // 2, lax.rem(other, 2))

    def meet(k, carry):
        pl.semaphore_signal(barrier, inc=1, device_id=peer_of(k)[1], device_id_type=MESH)
        return carry

    lax.fori_loop(1, devices, meet, 0)
    pl.semaphore_wait(barrier, devices - 1)
    locals_ = []
    for a in range(count):
        src = ins[a].at[pos] if split else ins[a]
        locals_.append(pltpu.make_async_copy(src, outs[a].at[pos], own_sem.at[a]))
        locals_[-1].start()

    def copy_to(a, k):
        other, peer = peer_of(k)
        src = ins[a].at[other] if split else ins[a]
        return remote(src, outs[a].at[pos], send.at[a, k], recv.at[a, k], peer)

    def begin(k, carry):
        for a in range(count):
            copy_to(a, k).start()
        return carry

    def finish(k, carry):
        for a in range(count):
            copy_to(a, k).wait()
        return carry

    lax.fori_loop(1, devices, begin, 0)
    for copy in locals_:
        copy.wait()
    lax.fori_loop(1, devices, finish, 0)


def spread(arrays, devices, cid, split):
    count = len(arrays)
    lead = () if split else (devices,)
    return pl.pallas_call(
        partial(spread_kernel, count, devices, split),
        name=f"spread_{cid}",
        out_shape=[jax.ShapeDtypeStruct(lead + a.shape, a.dtype) for a in arrays],
        in_specs=[ANY] * count,
        out_specs=[ANY] * count,
        scratch_shapes=[
            pltpu.SemaphoreType.DMA((count,)),
            pltpu.SemaphoreType.DMA((count, devices)),
            pltpu.SemaphoreType.DMA((count, devices)),
        ],
        compiler_params=pltpu.CompilerParams(collective_id=cid, has_side_effects=True),
    )(*arrays)


def piece_bounds(rows, count):
    step = rows // 32
    return tuple(32 * (-(-step * k // count)) for k in range(count)) + (rows,)


def blocks_of(a, rows):
    return a.reshape(rows, -1, BLOCK).swapaxes(0, 1).reshape(-1, BLOCK)


def pack_weights(
    gain, bias, table, qkv, self_out, cross_q, cross_kv, cross_out, ffn_in, ffn_out, delete, insert
):
    rows = qkv.shape[0]
    small = jnp.concatenate([gain, bias, table, delete.T], axis=0).T
    small = jnp.pad(small, ((0, 0), (0, BLOCK - small.shape[1])))
    pair = jnp.concatenate([insert[:rows], insert[rows:]], axis=1)
    return jnp.concatenate(
        [
            blocks_of(qkv, rows),
            self_out,
            cross_q,
            blocks_of(cross_kv, rows),
            cross_out,
            blocks_of(ffn_in, rows),
            ffn_out,
            pair,
            small,
        ],
        axis=0,
    )


def unpack_weights(whole):
    devices = whole.shape[0]
    rows = whole.shape[1] // PIECES

    def blocks(first, count):
        part = whole[:, first * rows : (first + count) * rows]
        part = part.reshape(devices, count, rows, BLOCK).swapaxes(1, 2)
        return part.reshape(devices * rows, count * BLOCK)

    ffn_out = whole[:, 12 * rows : 16 * rows].reshape(devices * rows * 4, BLOCK)
    insert = whole[:, 16 * rows : 17 * rows].reshape(devices, rows, 2, BLOCK // 2)
    insert = insert.swapaxes(1, 2).reshape(devices * rows * 2, BLOCK // 2)
    small = whole[:, 17 * rows :].reshape(devices * rows, BLOCK)
    return (
        small[:, 0:4].T,
        small[:, 4:8].T,
        small[:, 8:16].T,
        blocks(0, 3),
        blocks(3, 1),
        blocks(4, 1),
        blocks(5, 2),
        blocks(7, 1),
        blocks(8, 4),
        ffn_out,
        small[:, 16:18],
        insert,
    )


def pack_grads(
    devices, gain, bias, table, qkv, self_out, cross_q, cross_kv, cross_out, ffn_in, ffn_out, delete, insert
):
    rows = BLOCK // devices

    def blocks(a):
        a = a.astype(LOW).reshape(devices, rows, -1, BLOCK).swapaxes(1, 2)
        return a.reshape(devices, -1, BLOCK)

    small = jnp.concatenate([gain, bias, table, delete.T], axis=0).T.astype(LOW)
    small = jnp.pad(small, ((0, 0), (0, BLOCK - small.shape[1])))
    pair = insert.astype(LOW).reshape(devices, 2, rows, BLOCK // 2).swapaxes(1, 2)
    return jnp.concatenate(
        [
            blocks(qkv),
            blocks(self_out),
            blocks(cross_q),
            blocks(cross_kv),
            blocks(cross_out),
            blocks(ffn_in),
            ffn_out.astype(LOW).reshape(devices, rows * 4, BLOCK),
            pair.reshape(devices, rows, BLOCK),
            small.reshape(devices, rows, BLOCK),
        ],
        axis=1,
    )


def unpack_grads(own):
    rows = own.shape[0] // PIECES

    def blocks(first, count):
        part = own[first * rows : (first + count) * rows].reshape(count, rows, BLOCK)
        return part.swapaxes(0, 1).reshape(rows, count * BLOCK)

    pair = own[16 * rows : 17 * rows]
    small = own[17 * rows :]
    return (
        small[:, 0:4].T,
        small[:, 4:8].T,
        small[:, 8:16].T,
        blocks(0, 3),
        blocks(3, 1),
        blocks(4, 1),
        blocks(5, 2),
        blocks(7, 1),
        blocks(8, 4),
        own[12 * rows : 16 * rows],
        small[:, 16:18],
        jnp.concatenate([pair[:, : BLOCK // 2], pair[:, BLOCK // 2 :]], axis=0),
    )


def gather_weights(packed, devices):
    rows = packed.shape[0]
    if rows % (16 * PIECES):
        return lax.all_gather(packed, BOTH)
    return gather_packed(packed, devices // 8, piece_bounds(rows, 5))


def reduce_grads(parts):
    devices, rows = parts.shape[:2]
    if rows % (16 * PIECES):
        return lax.psum_scatter(
            parts.astype(WIDE).reshape(devices * rows, -1), BOTH, scatter_dimension=0, tiled=True
        )
    return reduce_packed(parts, devices // 8, piece_bounds(rows, 5))


def layer_norm(activation, scale_row, shift_row):
    centred = activation - jnp.mean(activation, axis=-1, keepdims=True)
    spread = jnp.mean(centred * centred, axis=-1, keepdims=True)
    return centred * lax.rsqrt(spread + epsilon) * scale_row + shift_row


def norm_backward(activation, scale_row, shift_row, upstream):
    pull_norm = jax.vjp(layer_norm, activation, scale_row, shift_row)[1]
    return pull_norm(upstream)


def matmul(left, right):
    return jnp.dot(left, right, preferred_element_type=jnp.float32)


def matmul_tn(left, right):
    return lax.dot_general(
        left, right, (((0,), (0,)), ((), ())), preferred_element_type=jnp.float32
    )


def matmul_nt(left, right):
    return lax.dot_general(
        left, right, (((1,), (1,)), ((), ())), preferred_element_type=jnp.float32
    )


def entropy_rows(logits, labels):
    row_top = jnp.max(logits, axis=1, keepdims=True)
    log_total = row_top[:, 0] + jnp.log(jnp.sum(jnp.exp(logits - row_top), axis=1))
    hits = labels[:, None] == lax.broadcasted_iota(jnp.int32, logits.shape, 1)
    return log_total - jnp.sum(jnp.where(hits, logits, 0.0), axis=1)


def entropy_grad(logits, labels, weight_rows):
    row_top = jnp.max(logits, axis=1, keepdims=True)
    exps_row = jnp.exp(logits - row_top)
    probabilities = exps_row / jnp.sum(exps_row, axis=1, keepdims=True)
    hits = (labels[:, None] == lax.broadcasted_iota(jnp.int32, logits.shape, 1)).astype(jnp.float32)
    return (weight_rows[:, None] * (probabilities - hits)).astype(jnp.bfloat16)


def head_columns(head_pos):
    return slice(head_pos * HD, (head_pos + 1) * HD)


def masked_scores(queries, key_rows, allowed):
    scores = matmul_nt(queries, key_rows) * score_scale
    return jnp.where(allowed, scores, masked_fill)


def attention_probs(queries, key_rows, allowed, row_top, row_total):
    scores = masked_scores(queries, key_rows, allowed)
    return jnp.where(allowed, jnp.exp(scores - row_top), 0.0) / row_total


def attention_stats(queries, key_rows, allowed):
    maxima, totals = ([], [])
    block_max = []
    block_total = []
    for head_pos in range(queries.shape[1] // HD):
        columns = head_columns(head_pos)
        scores = masked_scores(queries[:, columns], key_rows[:, columns], allowed)
        row_top = jnp.max(scores, axis=1, keepdims=True)
        block_max.append(row_top)
        block_total.append(
            jnp.sum(jnp.where(allowed, jnp.exp(scores - row_top), 0.0), axis=1, keepdims=True)
        )
    maxima.append(jnp.concatenate(block_max, 1))
    totals.append(jnp.concatenate(block_total, 1))
    return (maxima[0], totals[0])


def attention_output(queries, key_rows, values, allowed, row_top, row_total):
    pieces = []
    for head_pos in range(queries.shape[1] // HD):
        columns = head_columns(head_pos)
        probabilities = attention_probs(
            queries[:, columns],
            key_rows[:, columns],
            allowed,
            row_top[:, head_pos : head_pos + 1],
            row_total[:, head_pos : head_pos + 1],
        )
        pieces.append(matmul(probabilities.astype(jnp.bfloat16), values[:, columns]))
    return jnp.concatenate(pieces, 1)


def attention_delta(queries, key_rows, values, allowed, row_top, row_total, grad_rows, block):
    head_parts = []
    for head_pos in range(queries.shape[1] // HD):
        columns = head_columns(head_pos)
        probs_full = attention_probs(
            queries[0:block, columns],
            key_rows[:, columns],
            allowed,
            row_top[0:block, head_pos : head_pos + 1],
            row_total[0:block, head_pos : head_pos + 1],
        )
        grad_prob = matmul_nt(grad_rows[0:block, columns], values[:, columns])
        head_parts.append(jnp.sum(probs_full * grad_prob, axis=1, keepdims=True))
    parts = [jnp.concatenate(head_parts, 1)]
    return jnp.concatenate(parts, 0)


def attention_backward(
    queries, key_rows, values, allowed, row_top, row_total, delta, grad_rows, block
):
    heads_count = queries.shape[1] // HD
    grad_k = [jnp.zeros((key_rows.shape[0], HD), jnp.float32) for head_pos in range(heads_count)]
    grad_v = [jnp.zeros((key_rows.shape[0], HD), jnp.float32) for head_pos in range(heads_count)]
    rows_grad = grad_rows[0:block]
    q_pieces = []
    for head_pos in range(heads_count):
        columns = head_columns(head_pos)
        probs_full = attention_probs(
            queries[:, columns],
            key_rows[:, columns],
            allowed,
            row_top[0:block, head_pos : head_pos + 1],
            row_total[0:block, head_pos : head_pos + 1],
        )
        grad_prob = matmul_nt(rows_grad[:, columns], values[:, columns])
        grad_score = (probs_full * (grad_prob - delta[0:block, head_pos : head_pos + 1])).astype(
            jnp.bfloat16
        )
        q_pieces.append(matmul(grad_score, key_rows[:, columns]) * score_scale)
        grad_k[head_pos] = (
            grad_k[head_pos] + matmul_tn(grad_score, queries[:, columns]) * score_scale
        )
        grad_v[head_pos] = grad_v[head_pos] + matmul_tn(
            probs_full.astype(jnp.bfloat16), rows_grad[:, columns]
        )
    query_blocks = [jnp.concatenate(q_pieces, 1)]
    return (
        jnp.concatenate(query_blocks, 0),
        jnp.concatenate(grad_k, 1),
        jnp.concatenate(grad_v, 1),
    )


def merge_stats(first_part, second_part):
    top_both = jnp.maximum(first_part[0], second_part[0])
    return (
        top_both,
        first_part[1] * jnp.exp(first_part[0] - top_both)
        + second_part[1] * jnp.exp(second_part[0] - top_both),
    )


def body(
    dec_input,
    enc_output,
    segment_ids,
    padding,
    pair_ids,
    src_lengths,
    delete_labels,
    insert_counts,
    masked_positions,
    masked_targets,
    norm_gain,
    norm_bias,
    pair_table,
    self_qkv,
    self_out,
    cross_q,
    cross_kv,
    cross_out,
    ffn_in,
    ffn_out,
    w_delete,
    w_insert,
    w_vocab,
):
    tok_count = dec_input.shape[0]
    model_width = dec_input.shape[1]
    src_count = enc_output.shape[0]
    masked_count = masked_positions.shape[1]
    src_pos = lax.axis_index("src")
    device_pos = lax.axis_index(("batch", "src"))
    everyone = lax.axis_size(("batch", "src"))
    grad_scale = (tok_count * everyone) ** (-0.5)
    segment = segment_ids[0]
    not_padding = 1 - padding[0]
    keep_float = not_padding.astype(jnp.float32)
    positions = masked_positions[0]
    (
        full_gain,
        full_bias,
        full_table,
        full_qkv,
        full_self_out,
        full_cross_q,
        full_cross_kv,
        full_cross_out,
        full_ffn_in,
        full_ffn_out,
        full_delete,
        full_insert,
    ) = unpack_weights(
        gather_weights(
            pack_weights(
                norm_gain,
                norm_bias,
                pair_table,
                self_qkv,
                self_out,
                cross_q,
                cross_kv,
                cross_out,
                ffn_in,
                ffn_out,
                w_delete,
                w_insert,
            ),
            everyone,
        )
    )
    gains_float = full_gain.astype(jnp.float32)
    biases_float = full_bias.astype(jnp.float32)
    seg_onehot = segment[:, None] == lax.broadcasted_iota(jnp.int32, (tok_count, SEGS), 1)
    token_pair = jnp.sum(jnp.where(seg_onehot, pair_ids[0][None, :], 0), axis=1)
    pair_onehot = (
        token_pair[:, None] == lax.broadcasted_iota(jnp.int32, (tok_count, PAIRS), 1)
    ).astype(jnp.bfloat16)
    start_state = dec_input.astype(jnp.float32) + matmul(pair_onehot, full_table)
    normed_one = layer_norm(start_state, gains_float[0], biases_float[0]).astype(jnp.bfloat16)
    qkv_proj = matmul(normed_one, full_qkv).astype(jnp.bfloat16)
    self_query = qkv_proj[:, :model_width]
    self_keys = qkv_proj[:, model_width : 2 * model_width]
    self_values = qkv_proj[:, 2 * model_width :]
    row_iota = lax.broadcasted_iota(jnp.int32, (tok_count, tok_count), 0)
    col_iota = lax.broadcasted_iota(jnp.int32, (tok_count, tok_count), 1)
    self_allowed = (segment[:, None] == segment[None, :]) & (
        (not_padding[None, :] == 1) | (row_iota == col_iota)
    )
    self_top, self_total = attention_stats(self_query, self_keys, self_allowed)
    self_low = attention_output(
        self_query, self_keys, self_values, self_allowed, self_top, self_total
    ).astype(jnp.bfloat16)
    after_self = start_state + matmul(self_low, full_self_out)
    normed_two = layer_norm(after_self, gains_float[1], biases_float[1]).astype(jnp.bfloat16)
    cross_query = matmul(normed_two, full_cross_q).astype(jnp.bfloat16)
    kv_proj = matmul(enc_output, full_cross_kv).astype(jnp.bfloat16)
    cross_keys = kv_proj[:, :model_width]
    cross_values = kv_proj[:, model_width:]
    own_segment = src_pos * SEGS + segment
    other_query, other_segment = swap(
        [cross_query, jnp.broadcast_to(own_segment[None, :], (8, tok_count))], 2
    )
    in_order = lambda own, other: jnp.where(
        src_pos == 0, jnp.concatenate([own, other]), jnp.concatenate([other, own])
    )
    query_all = in_order(cross_query, other_query)
    segment_all = in_order(own_segment, other_segment[0])
    seg_ends = jnp.cumsum(src_lengths[0])
    src_index = src_pos * src_count + lax.broadcasted_iota(jnp.int32, (src_count, 1), 0)
    src_segment = jnp.sum((src_index >= seg_ends[None, :]).astype(jnp.int32), axis=1)
    cross_allowed = segment_all[:, None] == src_segment[None, :]
    block_rows = min(query_all.shape[0], 1024)
    part_top, part_total = attention_stats(query_all, cross_keys, cross_allowed)
    other_stats = swap(
        [jnp.concatenate([part_top, part_total], axis=1).T], 3
    )[0].T
    heads = part_top.shape[1]
    cross_top, cross_total = merge_stats(
        (part_top, part_total), (other_stats[:, :heads], other_stats[:, heads:])
    )
    part_out = attention_output(
        query_all, cross_keys, cross_values, cross_allowed, cross_top, cross_total
    )
    own_part = lax.dynamic_slice_in_dim(part_out, src_pos * tok_count, tok_count)
    sent_part = lax.dynamic_slice_in_dim(part_out, (1 - src_pos) * tok_count, tok_count)
    cross_low = (own_part + swap([sent_part.astype(LOW)], 4)[0].astype(WIDE)).astype(LOW)
    after_cross = after_self + matmul(cross_low, full_cross_out)
    normed_three = layer_norm(after_cross, gains_float[2], biases_float[2]).astype(jnp.bfloat16)
    pre_act = matmul(normed_three, full_ffn_in)
    gelu_tanh = partial(jax.nn.gelu, approximate=True)
    act_low = gelu_tanh(pre_act).astype(jnp.bfloat16)
    block_state = after_cross + matmul(act_low, full_ffn_out)
    head_in = layer_norm(block_state, gains_float[3], biases_float[3]).astype(jnp.bfloat16)
    delete_logits = matmul(head_in, full_delete)
    next_in = jnp.concatenate([head_in[1:], jnp.zeros((1, model_width), jnp.bfloat16)], axis=0)
    pair_in = jnp.concatenate([head_in, next_in], axis=1)
    insert_logits = matmul(pair_in, full_insert)
    next_segment = jnp.concatenate([segment[1:], -jnp.ones((1,), jnp.int32)])
    next_keep = jnp.concatenate([not_padding[1:], jnp.zeros((1,), jnp.int32)])
    insert_valid = ((segment == next_segment) & (not_padding == 1) & (next_keep == 1)).astype(
        jnp.float32
    )
    picked = jnp.take(head_in, positions, axis=0)
    picked_keep = jnp.take(not_padding, positions)
    target_or_none = jnp.where(picked_keep == 1, masked_targets[0], -1)
    target_tile = jnp.broadcast_to(
        jnp.pad(target_or_none, (0, 128 - masked_count))[None, :], (8, 128)
    )
    rows_all, targets_all = spread([picked, target_tile], everyone, 5, False)
    rows_all = rows_all.reshape(-1, model_width)
    targets_all = targets_all[:, 0, :masked_count].reshape(-1)
    vocab_local = w_vocab.shape[0]
    vocab_logits = matmul_nt(rows_all, w_vocab)
    vocab_ids = device_pos * vocab_local + lax.broadcasted_iota(jnp.int32, (1, vocab_local), 1)
    vocab_hits = targets_all[:, None] == vocab_ids
    local_top = jnp.max(vocab_logits, axis=1)
    local_total = jnp.sum(jnp.exp(vocab_logits - local_top[:, None]), axis=1)
    local_chosen = jnp.sum(jnp.where(vocab_hits, vocab_logits, 0.0), axis=1)
    local_stats = jnp.stack([local_top + jnp.log(local_total), local_chosen]).reshape(-1, 128)
    stats_all = spread([local_stats], everyone, 6, False)[0]
    stats_all = stats_all.reshape(everyone, 2, -1)
    vocab_top = jax.nn.logsumexp(stats_all[:, 0], axis=0)
    vocab_chosen = jnp.sum(stats_all[:, 1], axis=0)
    token_weight = (targets_all >= 0).astype(jnp.float32)
    token_losses = token_weight * (vocab_top - vocab_chosen)
    own_token = lax.dynamic_slice_in_dim(token_losses, device_pos * masked_count, masked_count)
    local_loss = (
        jnp.sum(keep_float * entropy_rows(delete_logits, delete_labels[0]))
        + jnp.sum(insert_valid * entropy_rows(insert_logits, insert_counts[0]))
        + jnp.sum(own_token)
    )
    mean_loss = lax.psum(local_loss, ("batch", "src")) / (tok_count * everyone)
    vocab_probs = jnp.exp(vocab_logits - vocab_top[:, None])
    grad_vocab_logits = (
        token_weight[:, None] * (vocab_probs - vocab_hits.astype(jnp.float32))
    ).astype(jnp.bfloat16)
    grad_vocab = matmul_tn(grad_vocab_logits, rows_all) * grad_scale
    grad_rows = matmul(grad_vocab_logits, w_vocab).astype(LOW)
    grad_rows = spread([grad_rows.reshape(everyone, masked_count, model_width)], everyone, 7, True)
    grad_picked = jnp.sum(grad_rows[0].astype(WIDE), axis=0)
    grad_delete_logits = entropy_grad(delete_logits, delete_labels[0], keep_float)
    grad_delete_w = matmul_tn(head_in, grad_delete_logits)
    grad_insert_logits = entropy_grad(insert_logits, insert_counts[0], insert_valid)
    grad_insert_w = matmul_tn(pair_in, grad_insert_logits)
    grad_pair = matmul_nt(grad_insert_logits, full_insert)
    grad_head = (
        matmul_nt(grad_delete_logits, full_delete)
        + grad_pair[:, :model_width]
        + jnp.concatenate(
            [jnp.zeros((1, model_width), jnp.float32), grad_pair[:-1, model_width:]], axis=0
        )
    )
    grad_head = grad_head.at[positions].add(grad_picked)
    grad_block, grad_gain_four, grad_bias_four = norm_backward(
        block_state, gains_float[3], biases_float[3], grad_head
    )
    grad_ffn_branch = grad_block.astype(jnp.bfloat16)
    grad_ffn_out_w = matmul_tn(act_low, grad_ffn_branch)
    grad_act = matmul_nt(grad_ffn_branch, full_ffn_out)
    pull_act = jax.vjp(gelu_tanh, pre_act)[1]
    grad_pre = pull_act(grad_act)[0].astype(jnp.bfloat16)
    grad_ffn_in_w = matmul_tn(normed_three, grad_pre)
    grad_norm_three, grad_gain_three, grad_bias_three = norm_backward(
        after_cross, gains_float[2], biases_float[2], matmul_nt(grad_pre, full_ffn_in)
    )
    grad_cross_state = grad_block + grad_norm_three
    grad_cross_branch = grad_cross_state.astype(jnp.bfloat16)
    grad_cross_out_w = matmul_tn(cross_low, grad_cross_branch)
    grad_cross_attn = matmul_nt(grad_cross_branch, full_cross_out).astype(jnp.bfloat16)
    grad_attn_all = in_order(grad_cross_attn, swap([grad_cross_attn], 8)[0])
    delta_part = attention_delta(
        query_all,
        cross_keys,
        cross_values,
        cross_allowed,
        cross_top,
        cross_total,
        grad_attn_all,
        block_rows,
    )
    delta_full = delta_part + swap([delta_part.T], 9)[0].T
    grad_query_all, grad_cross_keys, grad_cross_values = attention_backward(
        query_all,
        cross_keys,
        cross_values,
        cross_allowed,
        cross_top,
        cross_total,
        delta_full,
        grad_attn_all,
        block_rows,
    )
    own_part = lax.dynamic_slice_in_dim(grad_query_all, src_pos * tok_count, tok_count)
    sent_part = lax.dynamic_slice_in_dim(grad_query_all, (1 - src_pos) * tok_count, tok_count)
    grad_query = (own_part + swap([sent_part.astype(LOW)], 10)[0].astype(WIDE)).astype(LOW)
    grad_cross_q_w = matmul_tn(normed_two, grad_query)
    grad_kv = jnp.concatenate([grad_cross_keys, grad_cross_values], axis=1).astype(jnp.bfloat16)
    grad_cross_kv_w = matmul_tn(enc_output, grad_kv)
    grad_enc = matmul_nt(grad_kv, full_cross_kv).astype(jnp.bfloat16)
    grad_norm_two, grad_gain_two, grad_bias_two = norm_backward(
        after_self, gains_float[1], biases_float[1], matmul_nt(grad_query, full_cross_q)
    )
    grad_self_state = grad_cross_state + grad_norm_two
    grad_self_branch = grad_self_state.astype(jnp.bfloat16)
    grad_self_out_w = matmul_tn(self_low, grad_self_branch)
    grad_self_attn = matmul_nt(grad_self_branch, full_self_out).astype(jnp.bfloat16)
    self_delta = attention_delta(
        self_query,
        self_keys,
        self_values,
        self_allowed,
        self_top,
        self_total,
        grad_self_attn,
        tok_count,
    )
    grad_self_q, grad_self_k, grad_self_v = attention_backward(
        self_query,
        self_keys,
        self_values,
        self_allowed,
        self_top,
        self_total,
        self_delta,
        grad_self_attn,
        tok_count,
    )
    grad_qkv = jnp.concatenate([grad_self_q, grad_self_k, grad_self_v], axis=1).astype(jnp.bfloat16)
    grad_qkv_w = matmul_tn(normed_one, grad_qkv)
    grad_norm_one, grad_gain_one, grad_bias_one = norm_backward(
        start_state, gains_float[0], biases_float[0], matmul_nt(grad_qkv, full_qkv)
    )
    grad_start = grad_self_state + grad_norm_one
    grad_input = grad_start.astype(jnp.bfloat16)
    grad_table = lax.dot_general(
        pair_onehot.astype(jnp.float32),
        grad_start,
        (((0,), (0,)), ((), ())),
        precision=lax.Precision.HIGHEST,
        preferred_element_type=jnp.float32,
    )
    summed = unpack_grads(
        reduce_grads(
            pack_grads(
                everyone,
                jnp.stack([grad_gain_one, grad_gain_two, grad_gain_three, grad_gain_four]),
                jnp.stack([grad_bias_one, grad_bias_two, grad_bias_three, grad_bias_four]),
                grad_table,
                grad_qkv_w,
                grad_self_out_w,
                grad_cross_q_w,
                grad_cross_kv_w,
                grad_cross_out_w,
                grad_ffn_in_w,
                grad_ffn_out_w,
                grad_delete_w,
                grad_insert_w,
            )
        )
    )
    return (
        block_state.astype(jnp.bfloat16),
        grad_input,
        grad_enc,
        summed[0] * grad_scale,
        summed[1] * grad_scale,
        summed[2] * grad_scale,
        summed[3] * grad_scale,
        summed[4] * grad_scale,
        summed[5] * grad_scale,
        summed[6] * grad_scale,
        summed[7] * grad_scale,
        summed[8] * grad_scale,
        summed[9] * grad_scale,
        summed[10] * grad_scale,
        summed[11] * grad_scale,
        grad_vocab,
        mean_loss,
        own_token[None, :],
    )


def solution(mesh):
    return jax.shard_map(
        body,
        mesh=mesh,
        in_specs=(
            P(("batch", "src"), None),
            P(("batch", "src"), None),
            P(("batch", "src"), None),
            P(("batch", "src"), None),
            P(("batch", "src"), None),
            P("batch", None),
            P(("batch", "src"), None),
            P(("batch", "src"), None),
            P(("batch", "src"), None),
            P(("batch", "src"), None),
            P(None, ("batch", "src")),
            P(None, ("batch", "src")),
            P(None, ("batch", "src")),
            P(("batch", "src"), None),
            P(("batch", "src"), None),
            P(("batch", "src"), None),
            P(("batch", "src"), None),
            P(("batch", "src"), None),
            P(("batch", "src"), None),
            P(("batch", "src"), None),
            P(("batch", "src"), None),
            P(("batch", "src"), None),
            P(("batch", "src"), None),
        ),
        out_specs=(
            P(("batch", "src"), None),
            P(("batch", "src"), None),
            P(("batch", "src"), None),
            P(None, ("batch", "src")),
            P(None, ("batch", "src")),
            P(None, ("batch", "src")),
            P(("batch", "src"), None),
            P(("batch", "src"), None),
            P(("batch", "src"), None),
            P(("batch", "src"), None),
            P(("batch", "src"), None),
            P(("batch", "src"), None),
            P(("batch", "src"), None),
            P(("batch", "src"), None),
            P(("batch", "src"), None),
            P(("batch", "src"), None),
            P(),
            P(("batch", "src"), None),
        ),
        check_vma=False,
    )
```

```python
from functools import partial

import jax
import jax.numpy as jnp
from jax import lax
from jax.experimental import pallas as pl
from jax.experimental.pallas import tpu as pltpu
from jax.sharding import PartitionSpec as P

HD = 64
PAIRS = 8
SEGS = 8
BLOCK = 512
EPSILON = 1e-05
SCALE = 0.125
FILL = -1e30
GELU = 0.7978845608
CUBIC = 0.044715

MESH = pl.DeviceIdType.MESH
ANY = pl.BlockSpec(memory_space=pl.ANY)
VMEM = pl.BlockSpec(memory_space=pltpu.VMEM)
SMEM = pl.BlockSpec(memory_space=pltpu.SMEM)
BOTH = ("batch", "src")
LOW = jnp.bfloat16
WIDE = jnp.float32
LIMIT = 60 << 20


def shape_of(shape, kind):
    return jax.ShapeDtypeStruct(shape, kind)


def dot(left, right):
    return jnp.dot(left, right, preferred_element_type=WIDE)


def dot_tn(left, right):
    return lax.dot_general(left, right, (((0,), (0,)), ((), ())), preferred_element_type=WIDE)


def dot_nt(left, right):
    return lax.dot_general(left, right, (((1,), (1,)), ((), ())), preferred_element_type=WIDE)


def normalised(v):
    centred = v - jnp.mean(v, axis=-1, keepdims=True)
    r = lax.rsqrt(jnp.mean(centred * centred, axis=-1, keepdims=True) + EPSILON)
    return centred * r, r


def norm_back(v, gain, upstream):
    hat, r = normalised(v)
    scaled = upstream * gain
    first = jnp.mean(scaled, axis=-1, keepdims=True)
    second = jnp.mean(scaled * hat, axis=-1, keepdims=True)
    grad_gain = jnp.sum(upstream * hat, axis=0, keepdims=True)
    grad_bias = jnp.sum(upstream, axis=0, keepdims=True)
    return r * (scaled - first - hat * second), grad_gain, grad_bias


def lanes(shape):
    return lax.broadcasted_iota(jnp.int32, shape, len(shape) - 1)


def rows_of(shape):
    return lax.broadcasted_iota(jnp.int32, shape, len(shape) - 2)


def both_heads(x):
    low = lanes(x.shape) < HD
    zero = jnp.zeros_like(x)
    return jnp.concatenate([jnp.where(low, x, zero), jnp.where(low, zero, x)], axis=0)


def join_heads(x):
    half = x.shape[0] // 2
    return jnp.where(lanes((half, x.shape[1])) < HD, x[:half], x[half:])


def twice(x):
    return jnp.concatenate([x, x], axis=0)


def transposed_rows(rows):
    count, width = rows.shape
    return jnp.concatenate([rows, jnp.zeros((128 - count, width), WIDE)], axis=0).T


def greet(peers):
    barrier = pltpu.get_barrier_semaphore()
    for peer in peers:
        pl.semaphore_signal(barrier, inc=1, device_id=peer, device_id_type=MESH)
    pl.semaphore_wait(barrier, len(peers))


def remote(src, dst, send, recv, peer):
    return pltpu.make_async_remote_copy(
        src_ref=src,
        dst_ref=dst,
        send_sem=send,
        recv_sem=recv,
        device_id=peer,
        device_id_type=MESH,
    )


class Place:
    def __init__(self, depth):
        b = lax.axis_index("batch")
        self.depth = depth
        self.y = lax.axis_index("src")
        self.c = lax.rem(b, 2)
        self.x = lax.rem(b // 2, 2)
        self.z = b // 4

    def at(self, z=None, x=None, c=None, y=None):
        z = self.z if z is None else z
        x = self.x if x is None else x
        c = self.c if c is None else c
        y = self.y if y is None else y
        return ((z * 2 + x) * 2 + c, y)

    def along(self, k):
        return self.at(z=lax.rem(self.z + k, self.depth))

    def others(self):
        return [self.along(k) for k in range(1, self.depth)]

    def across_x(self):
        return self.at(x=1 - self.x)

    def across_y(self):
        return self.at(y=1 - self.y)

    def across_both(self):
        return self.at(x=1 - self.x, y=1 - self.y)

    def across_core(self):
        return self.at(c=1 - self.c)


def gather_steps(me, chunks, send, recv):
    z, x, c, y = me.z, me.x, me.c, me.y
    depth = me.depth
    count = len(chunks)
    started = [[None] * 4 for _ in chunks]
    used = [0] * count

    def launch(k, stage):
        copies = []

        def push(block, peer):
            slot = used[k]
            used[k] += 1
            copy = remote(block, block, send.at[k, slot], recv.at[k, slot], peer)
            copy.start()
            copies.append(copy)

        one, two = chunks[k]
        every = slice(None)
        if stage == 0:
            for view in one + two:
                for j in range(1, depth):
                    push(view(z, x, c, y), me.along(j))
        elif stage == 1:
            for view in one:
                push(view(every, x, c, y), me.across_x())
            for view in two:
                push(view(every, x, c, y), me.across_y())
        elif stage == 2:
            for view in one:
                push(view(every, every, c, y), me.across_y())
            for view in two:
                push(view(every, x, c, every), me.across_x())
        else:
            for view in one + two:
                push(view(every, every, c, every), me.across_core())
        started[k][stage] = copies

    for step in range(count + 4):
        for stage in range(4, -1, -1):
            k = step - stage
            if not 0 <= k < count:
                continue
            if stage > 0:
                for copy in started[k][stage - 1]:
                    copy.wait_recv()
            if stage < 4:
                launch(k, stage)
        yield step - 4
    for stages in started:
        for copies in stages:
            for copy in copies:
                copy.wait_send()


def self_window(block, tok_count):
    low = jnp.clip(block * 128 - 128, 0, tok_count - 384)
    return pl.multiple_of(low, 128)


def self_mask(row_seg, row_keep, col_seg, block, low):
    at = pl.ds(low, 384)
    keys = row_seg[0:1, at]
    keep = row_keep[0:1, at]
    queries = col_seg[pl.ds(pl.multiple_of(block * 128, 128), 128), 0:1]
    shape = (128, 384)
    own = (rows_of(shape) + block * 128) == (lanes(shape) + low)
    return (queries == keys) & ((keep > 0.5) | own)


def self_forward(qkv, out, lse_ref, row_seg, row_keep, col_seg):
    tok_count, width = out.shape
    blocks = tok_count // 128
    lse_ref[...] = jnp.zeros_like(lse_ref)

    def one(t, carry):
        pair, block = t // blocks, lax.rem(t, blocks)
        at = pl.ds(pl.multiple_of(block * 128, 128), 128)
        low = self_window(block, tok_count)
        keys = pl.ds(low, 384)
        base = pl.multiple_of(pair * 128, 128)
        q = both_heads(qkv[at, pl.ds(base, 128)])
        k = qkv[keys, pl.ds(pl.multiple_of(base + width, 128), 128)]
        v = qkv[keys, pl.ds(pl.multiple_of(base + 2 * width, 128), 128)]
        allowed = self_mask(row_seg, row_keep, col_seg, block, low)
        scores = jnp.where(twice(allowed), dot_nt(q, k) * SCALE, FILL)
        top = jnp.max(scores, axis=1, keepdims=True)
        exps = jnp.exp(scores - top)
        total = jnp.sum(exps, axis=1, keepdims=True)
        probs = (exps * (1.0 / total)).astype(LOW)
        out[at, pl.ds(base, 128)] = join_heads(dot(probs, v)).astype(LOW)
        lse = top + jnp.log(total)
        lane = lanes((128, 128))
        lse_ref[at, :] = jnp.where(
            lane == 2 * pair, lse[:128], jnp.where(lane == 2 * pair + 1, lse[128:], lse_ref[at, :])
        )
        return carry

    lax.fori_loop(0, blocks * (width // 128), one, 0)


def first_kernel(depth, gathers, *refs):
    (seg, pad, pair, dec, enc, small, raw_qkv, raw_so, raw_cq, raw_kv, raw_co, raw_fi, raw_fo, raw_in) = refs[:14]
    refs = refs[14:]
    if gathers:
        (ga, gf, gi, gs) = refs[:4]
        refs = refs[4:]
    else:
        ga, gf, gi, gs = None, None, None, None
        (ga_in, gs_in) = refs[:2]
        refs = refs[2:]
    (start_out, one_out, qkv_out, low_out, lse_out, after_out, two_out, query_out, other_out, kv_out) = refs[:10]
    (w_qkv, w_so, w_cq, w_kv, w_s, row_seg, row_keep, col_seg, own_sem, load_sem, send, recv) = refs[10:]
    tok_count, width = dec.shape
    src_count = enc.shape[0]
    me = Place(depth)
    z, x, c, y = me.z, me.x, me.c, me.y

    if gathers:
        owns = []

        def own(src, dst):
            copy = pltpu.make_async_copy(src, dst, own_sem.at[len(owns)])
            copy.start()
            owns.append(copy)

        own(small, gs.at[z, x, c, y])
        first = 0
        for raw, count in ((raw_qkv, 3), (raw_so, 1), (raw_cq, 1), (raw_kv, 2), (raw_co, 1), (raw_fi, 4)):
            for k in range(count):
                own(raw.at[:, pl.ds(k * BLOCK, BLOCK)], ga.at[first + k, z, x, c, y])
            first += count
        own(raw_fo, gf.at[z, x, c, y])
        own(raw_in, gi.at[z, x, c, y])
        greet(me.others() + [me.across_x(), me.across_y(), me.across_core()])
        for copy in owns:
            copy.wait()

        def piece(lo, hi):
            return lambda *at: ga.at[(slice(lo, hi),) + at]

        def part(ref, lo, hi):
            return lambda *at: ref.at[at + (pl.ds(lo, hi - lo),)]

        half_f, half_i = raw_fo.shape[0] // 2, raw_in.shape[0] // 2
        chunks = [
            ([part(gs, 0, 16), piece(0, 2)], [piece(2, 4)]),
            ([piece(4, 6)], [piece(6, 8)]),
            ([piece(8, 10)], [piece(10, 12)]),
            (
                [part(gf, 0, half_f), part(gi, 0, half_i)],
                [part(gf, half_f, 2 * half_f), part(gi, half_i, 2 * half_i)],
            ),
        ]
        steps = gather_steps(me, chunks, send, recv)
    else:
        greet([me.across_y()])
        steps = iter(())

    def advance():
        return next(steps, None)

    def have(chunk):
        if gathers:
            while True:
                done = advance()
                if done is None or done >= chunk:
                    return

    loads = []

    def load(src, dst):
        copy = pltpu.make_async_copy(src, dst, load_sem.at[len(loads)])
        copy.start()
        loads.append(copy)
        return copy

    def fetch(lo, hi, dst):
        if gathers:
            return load(ga.at[lo:hi], dst)
        return load(ga_in.at[lo:hi], dst)

    segments = seg[...].astype(WIDE)
    row_seg[...] = segments
    row_keep[...] = 1.0 - pad[...].astype(WIDE)
    pair_row = jnp.zeros((1, tok_count), WIDE)
    for k in range(SEGS):
        pair_row = jnp.where(segments == k, pair[0, k].astype(WIDE), pair_row)
    columns = transposed_rows(jnp.concatenate([segments, pair_row, jnp.zeros((6, tok_count), WIDE)], axis=0))
    col_seg[...] = columns

    def flat(ref):
        value = ref[...]
        return value.reshape((-1, value.shape[-1]))

    have(0)
    copies = [load(gs if gathers else gs_in, w_s), fetch(0, 3, w_qkv), fetch(3, 4, w_so)]
    for copy in copies:
        copy.wait()
    table = flat(w_s).astype(WIDE).T
    onehot = (lanes((tok_count, 128)) == (columns[:, 1:2].astype(jnp.int32) + 8)).astype(LOW)
    start = dec[...].astype(WIDE) + dot(onehot, table.astype(LOW))
    start_out[...] = start
    one = (normalised(start)[0] * table[0:1] + table[4:5]).astype(LOW)
    one_out[...] = one
    for k in range(3):
        weight = w_qkv[k].reshape((-1, BLOCK))
        qkv_out[:, pl.ds(k * BLOCK, BLOCK)] = dot(one, weight).astype(LOW)
    advance()
    self_forward(qkv_out, low_out, lse_out, row_seg, row_keep, col_seg)
    have(1)
    copies = [fetch(4, 5, w_cq), fetch(5, 7, w_kv)]
    after = start_out[...] + dot(low_out[...], flat(w_so))
    after_out[...] = after
    two = (normalised(after)[0] * table[1:2] + table[5:6]).astype(LOW)
    two_out[...] = two
    for copy in copies:
        copy.wait()
    query_out[...] = dot(two, flat(w_cq)).astype(LOW)
    swap = remote(query_out, other_out, send.at[len(chunks) if gathers else 0, 0], recv.at[len(chunks) if gathers else 0, 0], me.across_y())
    swap.start()
    advance()
    w_key, w_val = w_kv[0].reshape((-1, BLOCK)), w_kv[1].reshape((-1, BLOCK))
    parts = 4
    for k in range(parts):
        span = src_count // parts
        at = pl.ds(k * span, span)
        kv_out[at, 0:width] = dot(enc[at, :], w_key).astype(LOW)
        kv_out[at, width : 2 * width] = dot(enc[at, :], w_val).astype(LOW)
        advance()
    for _ in steps:
        pass
    swap.wait()


def first_part(depth, gathers, seg, pad, pair, dec, enc, small, raw, whole):
    tok_count, width = dec.shape
    src_count = enc.shape[0]
    sharded = (depth, 2, 2, 2)
    rows = BLOCK // (depth * 8)
    lead = sharded + (rows,) if gathers else (BLOCK,)
    outs = []
    if gathers:
        outs = [
            (shape_of((12,) + sharded + (rows, BLOCK), LOW), ANY),
            (shape_of(sharded + raw[6].shape, LOW), ANY),
            (shape_of(sharded + raw[7].shape, LOW), ANY),
            (shape_of(sharded + small.shape, LOW), ANY),
        ]
    local = [
        (shape_of((tok_count, width), WIDE), VMEM),
        (shape_of((tok_count, width), LOW), VMEM),
        (shape_of((tok_count, 3 * width), LOW), VMEM),
        (shape_of((tok_count, width), LOW), VMEM),
        (shape_of((tok_count, 128), WIDE), VMEM),
        (shape_of((tok_count, width), WIDE), VMEM),
        (shape_of((tok_count, width), LOW), VMEM),
        (shape_of((tok_count, width), LOW), VMEM),
        (shape_of((tok_count, width), LOW), ANY),
        (shape_of((src_count, 2 * width), LOW), VMEM),
    ]
    outs += local
    extra = [] if gathers else [whole[0], whole[3]]
    res = pl.pallas_call(
        partial(first_kernel, depth, gathers),
        name="first_part",
        out_shape=[o for o, _ in outs],
        in_specs=[VMEM, VMEM, SMEM, VMEM, VMEM] + [ANY] * (9 + len(extra)),
        out_specs=[s for _, s in outs],
        scratch_shapes=[
            pltpu.VMEM((3,) + lead + (BLOCK,), LOW),
            pltpu.VMEM((1,) + lead + (BLOCK,), LOW),
            pltpu.VMEM((1,) + lead + (BLOCK,), LOW),
            pltpu.VMEM((2,) + lead + (BLOCK,), LOW),
            pltpu.VMEM((lead if gathers else (BLOCK,)) + (128,), LOW),
            pltpu.VMEM((1, tok_count), WIDE),
            pltpu.VMEM((1, tok_count), WIDE),
            pltpu.VMEM((tok_count, 128), WIDE),
            pltpu.SemaphoreType.DMA((16,)),
            pltpu.SemaphoreType.DMA((8,)),
            pltpu.SemaphoreType.DMA((5, 4 * (depth + 2))),
            pltpu.SemaphoreType.DMA((5, 4 * (depth + 2))),
        ],
        compiler_params=pltpu.CompilerParams(
            collective_id=0, has_side_effects=True, vmem_limit_bytes=LIMIT
        ),
    )(seg, pad, pair, dec, enc, small, *raw, *extra)
    if gathers:
        ga, gf, gi, gs = res[:4]
        whole = (
            ga.reshape((12, BLOCK, BLOCK)),
            gf.reshape((-1, BLOCK)),
            gi.reshape((-1, raw[7].shape[1])),
            gs.reshape((-1, 128)),
        )
        res = res[4:]
    return whole, res


def block_ranges(seg_s, ends_s, off, src_count, side, block, tile):
    at = pl.multiple_of(block * 128, 128)
    low_seg = seg_s[side, at]
    high_seg = seg_s[side, at + 127]
    low = jnp.clip(ends_s[low_seg] - off, 0, src_count)
    high = jnp.clip(ends_s[high_seg + 1] - off, 0, src_count)
    return low // tile, jnp.where(high > low, (high + tile - 1) // tile, low // tile)


def bounds_columns(ends_s, seg_col, off):
    low = jnp.zeros_like(seg_col)
    high = jnp.zeros_like(seg_col)
    for s in range(2 * SEGS):
        low = jnp.where(seg_col == s, ends_s[s] - off, low)
        high = jnp.where(seg_col == s, ends_s[s + 1] - off, high)
    return low, high


TILE = 256


def cross_forward_kernel(seg_s, ends_s, seg_cols, q_own, q_other, kv, o_own, o_other, lse_own, lse_other, top_ref, total_ref, acc_ref):
    tok_count, width = q_own.shape
    src_count = kv.shape[0]
    pairs = width // 128
    off = lax.axis_index("src") * src_count
    for side, (q, o, lse_ref) in enumerate(((q_own, o_own, lse_own), (q_other, o_other, lse_other))):

        @pl.loop(0, tok_count // 128)
        def _(block):
            at = pl.ds(pl.multiple_of(block * 128, 128), 128)
            first, last = block_ranges(seg_s, ends_s, off, src_count, side, block, TILE)
            low, high = bounds_columns(ends_s, seg_cols[at, side : side + 1], off)
            top_ref[...] = jnp.full_like(top_ref, FILL)
            total_ref[...] = jnp.zeros_like(total_ref)
            acc_ref[...] = jnp.zeros_like(acc_ref)

            def one(t, carry):
                base = pl.multiple_of(t * TILE, TILE)
                keys = pl.ds(base, TILE)
                index = lanes((128, TILE)) + base
                allowed = twice((index >= low) & (index < high))
                for p in range(pairs):
                    cols = pl.ds(p * 128, 128)
                    k = kv[keys, cols]
                    v = kv[keys, pl.ds(width + p * 128, 128)]
                    scores = dot_nt(both_heads(q[at, cols]), k) * SCALE
                    scores = jnp.where(allowed, scores, FILL)
                    old = top_ref[p]
                    top = jnp.maximum(old, jnp.max(scores, axis=1, keepdims=True))
                    exps = jnp.where(allowed, jnp.exp(scores - top[:, 0:1]), 0.0)
                    fade = jnp.exp(old - top)
                    top_ref[p] = top
                    total_ref[p] = total_ref[p] * fade + jnp.sum(exps, axis=1, keepdims=True)
                    acc_ref[p] = acc_ref[p] * fade + dot(exps.astype(LOW), v)
                return carry

            lax.fori_loop(first, last, one, 0)
            lane = lanes((128, 128))
            stats = jnp.zeros((128, 128), WIDE)
            for p in range(pairs):
                total = total_ref[p]
                safe = jnp.where(total > 0.0, total, 1.0)
                o[at, pl.ds(p * 128, 128)] = join_heads(acc_ref[p] / safe).astype(LOW)
                lse = jnp.where(total > 0.0, top_ref[p] + jnp.log(safe), FILL)
                stats = jnp.where(lane == 2 * p, lse[:128], jnp.where(lane == 2 * p + 1, lse[128:], stats))
            lse_ref[:, at] = stats.T[0:8]


def cross_forward(seg_s, ends_s, seg_cols, q_own, q_other, kv):
    tok_count, width = q_own.shape
    heads = width // HD
    out = shape_of((tok_count, width), LOW)
    lse = shape_of((heads, tok_count), WIDE)
    return pl.pallas_call(
        cross_forward_kernel,
        name="cross_forward",
        out_shape=[out, out, lse, lse],
        in_specs=[SMEM, SMEM, VMEM, VMEM, VMEM, VMEM],
        out_specs=[VMEM] * 4,
        scratch_shapes=[pltpu.VMEM((width // 128, 256, 128), WIDE)] * 3,
        compiler_params=pltpu.CompilerParams(vmem_limit_bytes=LIMIT),
    )(seg_s, ends_s, seg_cols, q_own, q_other, kv)


def cross_backward_kernel(
    seg_s, ends_s, seg_cols, q_own, q_other, g_own, g_other, st_own, st_other, kv, dq_own, dq_other, dkv, acc, col_ref, dq_acc
):
    tok_count, width = q_own.shape
    src_count = kv.shape[0]
    pairs = width // 128
    off = lax.axis_index("src") * src_count
    acc[...] = jnp.zeros_like(acc)
    sides = ((q_own, g_own, st_own, dq_own), (q_other, g_other, st_other, dq_other))
    for side, (q, g, st, dq) in enumerate(sides):

        @pl.loop(0, tok_count // 128)
        def _(block):
            at = pl.ds(pl.multiple_of(block * 128, 128), 128)
            first, last = block_ranges(seg_s, ends_s, off, src_count, side, block, TILE)
            low, high = bounds_columns(ends_s, seg_cols[at, side : side + 1], off)
            dq_acc[...] = jnp.zeros_like(dq_acc)
            col_ref[...] = jnp.concatenate([st[:, at], jnp.zeros((112, 128), WIDE)], axis=0).T

            def one(t, carry):
                base = pl.multiple_of(t * TILE, TILE)
                keys = pl.ds(base, TILE)
                index = lanes((128, TILE)) + base
                allowed = twice((index >= low) & (index < high))
                for p in range(pairs):
                    cols = pl.ds(p * 128, 128)
                    vals = pl.ds(width + p * 128, 128)
                    k = kv[keys, cols]
                    v = kv[keys, vals]
                    qs = both_heads(q[at, cols])
                    gs = both_heads(g[at, cols])
                    lse = jnp.concatenate([col_ref[:, 2 * p : 2 * p + 1], col_ref[:, 2 * p + 1 : 2 * p + 2]], axis=0)
                    delta = jnp.concatenate(
                        [col_ref[:, 8 + 2 * p : 9 + 2 * p], col_ref[:, 9 + 2 * p : 10 + 2 * p]], axis=0
                    )
                    scores = dot_nt(qs, k) * SCALE
                    probs = jnp.exp(jnp.where(allowed, scores - lse, FILL))
                    gscores = (probs * (dot_nt(gs, v) - delta)).astype(LOW)
                    dq_acc[:, cols] = dq_acc[:, cols] + join_heads(dot(gscores, k))
                    acc[keys, cols] = acc[keys, cols] + dot_tn(gscores, qs)
                    acc[keys, vals] = acc[keys, vals] + dot_tn(probs.astype(LOW), gs)
                return carry

            lax.fori_loop(first, last, one, 0)
            dq[at, :] = (dq_acc[...] * SCALE).astype(dq.dtype)

    @pl.loop(0, src_count // 256)
    def _(t):
        at = pl.ds(pl.multiple_of(t * 256, 256), 256)
        dkv[at, 0:width] = (acc[at, 0:width] * SCALE).astype(LOW)
        dkv[at, width : 2 * width] = acc[at, width : 2 * width].astype(LOW)


def cross_backward(seg_s, ends_s, seg_cols, q_own, q_other, g_own, g_other, st_own, st_other, kv):
    tok_count, width = q_own.shape
    src_count = kv.shape[0]
    return pl.pallas_call(
        cross_backward_kernel,
        name="cross_backward",
        out_shape=[
            shape_of((tok_count, width), WIDE),
            shape_of((tok_count, width), LOW),
            shape_of((src_count, 2 * width), LOW),
        ],
        in_specs=[SMEM, SMEM] + [VMEM] * 8,
        out_specs=[VMEM] * 3,
        scratch_shapes=[
            pltpu.VMEM((src_count, 2 * width), WIDE),
            pltpu.VMEM((128, 128), WIDE),
            pltpu.VMEM((128, width), WIDE),
        ],
        compiler_params=pltpu.CompilerParams(vmem_limit_bytes=LIMIT),
    )(seg_s, ends_s, seg_cols, q_own, q_other, g_own, g_other, st_own, st_other, kv)


def merge_all(parts):
    top = parts[0][0:1]
    for part in parts[1:]:
        top = jnp.maximum(top, part[0:1])
    total = sum(jnp.exp(part[0:1] - top) for part in parts)
    rest = sum(part for part in parts)
    return jnp.where(rows_of(rest.shape) == 0, top + jnp.log(total), rest)


def middle_kernel(depth, natural, *refs):
    (
        seg, pad, labels, counts, positions, targets, w_vocab, after_self, o_own, o_other, lse_own, lse_other,
        ga, gf, gi, gs,
    ) = refs[:16]
    refs = refs[16:]
    (
        block_out, state_out, g_own, g_other, st_own, st_other, gw_a, gw_f, gw_i, small_rows, small_cols,
        grad_vocab, token_out, loss_out,
    ) = refs[:14]
    (
        w_co, w_fi, w_fo, w_in, w_s, got_o, got_lse, cross_o, cross_low, ac, bs, n3, act, slope, gpre, head,
        lt, gt, pb, rb, got_rc, got_rq, got_rz, st_c, st_q, st_z, gh, load_sem, send, recv,
    ) = refs[14:]
    tok_count, width = after_self.shape
    hidden = act.shape[1]
    masked = positions.shape[0]
    vocab_local = w_vocab.shape[0]
    everyone = depth * 8
    me = Place(depth)
    z, x, c, y = me.z, me.x, me.c, me.y
    greet(me.others() + [me.across_x(), me.across_y(), me.across_both(), me.across_core()])
    used = [0]

    def push(src, dst, peer):
        k = used[0]
        used[0] += 1
        copy = remote(src, dst, send.at[k], recv.at[k], peer)
        copy.start()
        return copy

    pending = []

    def arrive(copies):
        for copy in copies:
            copy.wait_recv()
        pending.extend(copies)

    swap = [push(o_other, got_o, me.across_y()), push(lse_other, got_lse, me.across_y())]
    sources = ((ga.at[7:8], w_co), (ga.at[8:12], w_fi), (gf, w_fo), (gi, w_in), (gs, w_s))
    loads = []
    for k, (src, dst) in enumerate(sources):
        copy = pltpu.make_async_copy(src, dst, load_sem.at[k])
        copy.start()
        loads.append(copy)

    segments = seg[...].astype(WIDE)
    keep = 1.0 - pad[...].astype(WIDE)
    lane_row = lanes((1, tok_count))
    inside = lane_row < tok_count - 1

    def following(row):
        return pltpu.roll(jnp.concatenate([row, jnp.zeros((7, tok_count), WIDE)], axis=0), tok_count - 1, 1)[0:1]

    follows = inside & (following(segments) == segments) & (keep > 0.5) & (following(keep) > 0.5)
    valid = jnp.where(follows, 1.0, 0.0)
    rows = [keep, valid, labels[...].astype(WIDE), counts[...].astype(WIDE)]
    columns = transposed_rows(jnp.concatenate(rows + [jnp.zeros((4, tok_count), WIDE)], axis=0))
    col_keep, col_valid = columns[:, 0:1], columns[:, 1:2]
    col_label, col_count = columns[:, 2:3], columns[:, 3:4].astype(jnp.int32)

    for copy in loads:
        copy.wait()
    table = w_s[...].reshape((-1, 128)).astype(WIDE).T

    arrive(swap)
    top = jnp.maximum(lse_own[...], got_lse[...])
    lse = top + jnp.log(jnp.exp(lse_own[...] - top) + jnp.exp(got_lse[...] - top))
    shares = jnp.concatenate([jnp.exp(lse_own[...] - lse), jnp.exp(got_lse[...] - lse)], axis=0)
    shares = transposed_rows(shares)
    low_half = lanes((tok_count, 128)) < HD
    for p in range(width // 128):
        at = slice(p * 128, (p + 1) * 128)
        share_own = jnp.where(low_half, shares[:, 2 * p : 2 * p + 1], shares[:, 2 * p + 1 : 2 * p + 2])
        share_got = jnp.where(low_half, shares[:, 8 + 2 * p : 9 + 2 * p], shares[:, 9 + 2 * p : 10 + 2 * p])
        mixed = o_own[:, at].astype(WIDE) * share_own + got_o[:, at].astype(WIDE) * share_got
        cross_o[:, at] = mixed
        cross_low[:, at] = mixed.astype(LOW)
    weight_co = w_co[...].reshape((-1, BLOCK))
    after_cross = after_self[...] + dot(cross_low[...], weight_co)
    ac[...] = after_cross
    n3[...] = (normalised(after_cross)[0] * table[2:3] + table[6:7]).astype(LOW)
    bs[...] = after_cross
    blocks = hidden // BLOCK
    flat_fo = w_fo[...].reshape((-1, BLOCK))
    for j in range(blocks):
        at = slice(j * BLOCK, (j + 1) * BLOCK)
        pre = dot(n3[...], w_fi[j].reshape((-1, BLOCK)))
        square = pre * pre
        bent = jnp.tanh(GELU * pre * (1.0 + CUBIC * square))
        half = 0.5 * (1.0 + bent)
        act[:, at] = (pre * half).astype(LOW)
        slope[:, at] = half + 0.5 * pre * (1.0 - bent * bent) * (GELU * (1.0 + 3.0 * CUBIC * square))
        bs[...] = bs[...] + dot(act[:, at], flat_fo[at])
    state = bs[...]
    block_out[...] = state.astype(LOW)
    head_in = (normalised(state)[0] * table[3:4] + table[7:8]).astype(LOW)
    head[...] = head_in

    chosen_rows = positions[...] == lanes((masked, tok_count))
    picker = chosen_rows.astype(LOW)
    picked = dot(picker, head_in).astype(LOW)
    kept = jnp.sum(jnp.where(chosen_rows, keep, 0.0), axis=1, keepdims=True)
    code = jnp.where(kept > 0.5, targets[...] + 1, 0)
    lane = lanes((masked, 128))
    digits = jnp.where(lane == 0, code >> 8, jnp.where(lane == 1, code & 255, 0)).astype(WIDE).astype(LOW)
    pb[z, x, c, y, :, 0:width] = picked
    pb[z, x, c, y, :, width : width + 128] = digits
    mine = pb.at[z, x, c, y]
    flight = [push(mine, mine, peer) for peer in me.others()]

    flat_in = w_in[...].reshape((2 * width, -1))
    classes = flat_in.shape[1]
    w_one, w_two = flat_in[:width], flat_in[width:]
    token_row = rows_of((tok_count, classes))
    ahead = pltpu.roll(dot(head_in, w_two), tok_count - 1, 0)
    logits = dot(head_in, w_one) + jnp.where(token_row == tok_count - 1, 0.0, ahead)
    top = jnp.max(logits, axis=1, keepdims=True)
    exps = jnp.exp(logits - top)
    total = jnp.sum(exps, axis=1, keepdims=True)
    hits = lanes((tok_count, classes)) == col_count
    entropy = top + jnp.log(total) - jnp.sum(jnp.where(hits, logits, 0.0), axis=1, keepdims=True)
    loss_col = col_valid * entropy
    grads = col_valid * (exps * (1.0 / total) - jnp.where(hits, 1.0, 0.0))
    g_insert = grads.astype(LOW)
    before = pltpu.roll(g_insert.astype(WIDE), 1, 0)
    g_before = jnp.where(token_row == 0, 0.0, before).astype(LOW)

    arrive(flight)
    column = pb.at[:, x, c, y]
    flight = [push(column, column, peer) for peer in (me.across_x(), me.across_y(), me.across_both())]

    flat_s = w_s[...].reshape((-1, 128))
    two = dot(head_in, flat_s)
    l_zero, l_one = two[:, 16:17], two[:, 17:18]
    top = jnp.maximum(l_zero, l_one)
    e_zero, e_one = jnp.exp(l_zero - top), jnp.exp(l_one - top)
    total = e_zero + e_one
    is_one = col_label > 0.5
    loss_col = loss_col + col_keep * (top + jnp.log(total) - jnp.where(is_one, l_one, l_zero))
    d_zero = col_keep * (e_zero / total - jnp.where(is_one, 0.0, 1.0))
    d_one = col_keep * (e_one / total - jnp.where(is_one, 1.0, 0.0))
    lane = lanes((tok_count, 128))
    g_delete = jnp.where(lane == 16, d_zero, jnp.where(lane == 17, d_one, 0.0)).astype(LOW)
    gh[...] = dot_nt(g_delete, flat_s) + dot_nt(g_insert, w_one) + dot_nt(g_before, w_two)
    arrive(flight)
    plane = pb.at[:, :, c, :]
    flight = [push(plane, plane, me.across_core())]
    small_cols[...] = dot_tn(head_in, g_delete)
    gw_i[0:width] = dot_tn(head_in, g_insert).astype(LOW)
    gw_i[width : 2 * width] = dot_tn(head_in, g_before).astype(LOW)
    arrive(flight)

    gathered = pb[...].reshape((-1, width + 128))
    rows_all = gathered[:, 0:width]
    numbers = gathered[:, width : width + 128].astype(WIDE).T
    code = numbers[0:1] * 256.0 + numbers[1:2]
    weight = jnp.where(code > 0.5, 1.0, 0.0)
    count = rows_all.shape[0]
    pos = lax.axis_index(BOTH)
    place = rows_of((vocab_local, count)) + pos * vocab_local
    hits = place == (code.astype(jnp.int32) - 1)
    lt[...] = dot_nt(w_vocab[...], rows_all)
    logits = lt[...]
    top = jnp.max(logits, axis=0, keepdims=True)
    total = jnp.sum(jnp.exp(logits - top), axis=0, keepdims=True)
    chosen = jnp.sum(jnp.where(hits, logits, 0.0), axis=0, keepdims=True)
    loss_here = jnp.sum(loss_col, axis=0, keepdims=True)
    stat = jnp.concatenate(
        [top + jnp.log(total), chosen, jnp.broadcast_to(loss_here, (1, count)), jnp.zeros((5, count), WIDE)], axis=0
    )
    st_c[0] = stat
    flight = [push(st_c.at[0], st_c.at[1], me.across_core())]
    arrive(flight)
    st_q[x, y] = merge_all([st_c[0], st_c[1]])
    spot = st_q.at[x, y]
    flight = [push(spot, spot, peer) for peer in (me.across_x(), me.across_y(), me.across_both())]
    arrive(flight)
    st_z[z] = merge_all([st_q[0, 0], st_q[0, 1], st_q[1, 0], st_q[1, 1]])
    flight = [push(st_z.at[z], st_z.at[z], peer) for peer in me.others()]
    arrive(flight)
    stat = merge_all([st_z[k] for k in range(depth)])
    tokens = weight * (stat[0:1] - stat[1:2])
    token_out[...] = jnp.broadcast_to(tokens, (8, count))
    loss = (stat[2:3, 0:128] + jnp.sum(tokens, axis=1, keepdims=True)) * (1.0 / (tok_count * everyone))
    loss_out[...] = jnp.broadcast_to(loss, (8, 128))
    gt[...] = (weight * (jnp.exp(lt[...] - stat[0:1]) - jnp.where(hits, 1.0, 0.0))).astype(LOW)

    rb[...] = dot_tn(gt[...], w_vocab[...]).astype(LOW).reshape(rb.shape)
    flight = [push(rb.at[:, :, 1 - c], got_rc, me.across_core())]
    scale = (tok_count * everyone) ** (-0.5)
    grad_vocab[...] = dot(gt[...], rows_all) * scale
    arrive(flight)
    got_rc[...] = (rb[:, :, c].astype(WIDE) + got_rc[...].astype(WIDE)).astype(LOW)
    flight = [
        push(got_rc.at[:, 1 - x, y], got_rq.at[0], me.across_x()),
        push(got_rc.at[:, x, 1 - y], got_rq.at[1], me.across_y()),
        push(got_rc.at[:, 1 - x, 1 - y], got_rq.at[2], me.across_both()),
    ]
    arrive(flight)
    line = got_rc[:, x, y].astype(WIDE)
    for k in range(3):
        line = line + got_rq[k].astype(WIDE)
    got_rq[3] = line.astype(LOW)
    flight = [
        push(got_rq.at[3, lax.rem(z + k, depth)], got_rz.at[k - 1], me.along(k)) for k in range(1, depth)
    ]
    arrive(flight)
    grad_picked = got_rq[3, z].astype(WIDE)
    for k in range(1, depth):
        grad_picked = grad_picked + got_rz[k - 1].astype(WIDE)
    coarse = grad_picked.astype(LOW)
    fine = (grad_picked - coarse.astype(WIDE)).astype(LOW)
    grad_head = gh[...] + dot_tn(picker, coarse) + dot_tn(picker, fine)

    grad_block, gain_3, bias_3 = norm_back(bs[...], table[3:4], grad_head)
    bs[...] = grad_block
    g_ffn = grad_block.astype(LOW)
    gh[...] = jnp.zeros_like(gh)
    for j in range(blocks):
        at = slice(j * BLOCK, (j + 1) * BLOCK)
        gpre[:, at] = (dot_nt(g_ffn, flat_fo[at]) * slope[:, at]).astype(LOW)
        gh[...] = gh[...] + dot_nt(gpre[:, at], w_fi[j].reshape((-1, BLOCK)))
    back, gain_2, bias_2 = norm_back(ac[...], table[2:3], gh[...])
    grad_state = grad_block + back
    state_out[...] = grad_state
    g_cross = grad_state.astype(LOW)
    g_attn = dot_nt(g_cross, weight_co).astype(LOW)
    g_own[...] = g_attn
    deltas = jnp.zeros((tok_count, 128), WIDE)
    for p in range(width // 128):
        at = slice(p * 128, (p + 1) * 128)
        product = g_attn[:, at].astype(WIDE) * cross_o[:, at]
        first = jnp.sum(jnp.where(low_half, product, 0.0), axis=1, keepdims=True)
        second = jnp.sum(jnp.where(low_half, 0.0, product), axis=1, keepdims=True)
        deltas = jnp.where(lane == 2 * p, first, jnp.where(lane == 2 * p + 1, second, deltas))
    st_own[...] = jnp.concatenate([lse, deltas.T[0:8]], axis=0)
    swap = [push(g_own, g_other, me.across_y()), push(st_own, st_other, me.across_y())]

    for j in range(blocks):
        at = slice(j * BLOCK, (j + 1) * BLOCK)
        gw_f[at] = dot_tn(act[:, at], g_ffn).astype(LOW)
        gw_a[1 + j] = dot_tn(n3[...], gpre[:, at]).astype(LOW)
    gw_a[0] = dot_tn(cross_low[...], g_cross).astype(LOW)
    small_rows[...] = jnp.concatenate([gain_2, gain_3, bias_2, bias_3, jnp.zeros((4, width), WIDE)], axis=0)
    arrive(swap)
    for copy in pending:
        copy.wait_send()


def middle_part(depth, seg, pad, labels, counts, positions, targets, w_vocab, after_self, attended, whole):
    tok_count, width = after_self.shape
    ga, gf, gi, gs = whole
    hidden = gf.shape[0]
    vocab_local = w_vocab.shape[0]
    everyone = depth * 8
    masked = positions.shape[0]
    count = masked * everyone
    sharded = (depth, 2, 2, 2)
    outs = [
        (shape_of((tok_count, width), LOW), VMEM),
        (shape_of((tok_count, width), WIDE), VMEM),
        (shape_of((tok_count, width), LOW), VMEM),
        (shape_of((tok_count, width), LOW), ANY),
        (shape_of((16, tok_count), WIDE), VMEM),
        (shape_of((16, tok_count), WIDE), ANY),
        (shape_of((5, BLOCK, BLOCK), LOW), VMEM),
        (shape_of((hidden, width), LOW), VMEM),
        (shape_of(gi.shape, LOW), VMEM),
        (shape_of((8, width), WIDE), VMEM),
        (shape_of((width, 128), WIDE), VMEM),
        (shape_of((vocab_local, width), WIDE), VMEM),
        (shape_of((8, count), WIDE), VMEM),
        (shape_of((8, 128), WIDE), VMEM),
    ]
    copies = 2 + 2 + 2 * (depth - 1) + 3 + 1 + 1 + 3 + 1 + 3 + (depth - 1)
    return pl.pallas_call(
        partial(middle_kernel, depth, None),
        name="middle_part",
        out_shape=[o for o, _ in outs],
        in_specs=[VMEM] * 12 + [ANY] * 4,
        out_specs=[s for _, s in outs],
        scratch_shapes=[
            pltpu.VMEM((1, BLOCK, BLOCK), LOW),
            pltpu.VMEM((4, BLOCK, BLOCK), LOW),
            pltpu.VMEM(gf.shape, LOW),
            pltpu.VMEM(gi.shape, LOW),
            pltpu.VMEM(gs.shape, LOW),
            pltpu.VMEM((tok_count, width), LOW),
            pltpu.VMEM((8, tok_count), WIDE),
            pltpu.VMEM((tok_count, width), WIDE),
            pltpu.VMEM((tok_count, width), LOW),
            pltpu.VMEM((tok_count, width), WIDE),
            pltpu.VMEM((tok_count, width), WIDE),
            pltpu.VMEM((tok_count, width), LOW),
            pltpu.VMEM((tok_count, hidden), LOW),
            pltpu.VMEM((tok_count, hidden), WIDE),
            pltpu.VMEM((tok_count, hidden), LOW),
            pltpu.VMEM((tok_count, width), LOW),
            pltpu.VMEM((vocab_local, count), WIDE),
            pltpu.VMEM((vocab_local, count), LOW),
            pltpu.VMEM(sharded + (masked, width + 128), LOW),
            pltpu.VMEM(sharded + (masked, width), LOW),
            pltpu.VMEM((depth, 2, 2, masked, width), LOW),
            pltpu.VMEM((4, depth, masked, width), LOW),
            pltpu.VMEM((max(depth - 1, 1), masked, width), LOW),
            pltpu.VMEM((2, 8, count), WIDE),
            pltpu.VMEM((2, 2, 8, count), WIDE),
            pltpu.VMEM((depth, 8, count), WIDE),
            pltpu.VMEM((tok_count, width), WIDE),
            pltpu.SemaphoreType.DMA((5,)),
            pltpu.SemaphoreType.DMA((copies + depth,)),
            pltpu.SemaphoreType.DMA((copies + depth,)),
        ],
        compiler_params=pltpu.CompilerParams(
            collective_id=1, has_side_effects=True, vmem_limit_bytes=LIMIT
        ),
    )(seg, pad, labels, counts, positions, targets, w_vocab, after_self, *attended, *whole)


def self_backward(qkv, out, lse_ref, g_ref, dqkv, dk, dv, row_seg, row_keep, col_seg):
    tok_count, width = out.shape
    blocks = tok_count // 128

    def pair_step(pair, carry):
        base = pl.multiple_of(pair * 128, 128)
        cols = pl.ds(base, 128)
        kcols = pl.ds(pl.multiple_of(base + width, 128), 128)
        vcols = pl.ds(pl.multiple_of(base + 2 * width, 128), 128)
        dk[...] = jnp.zeros_like(dk)
        dv[...] = jnp.zeros_like(dv)

        def one(block, inner):
            at = pl.ds(pl.multiple_of(block * 128, 128), 128)
            low = self_window(block, tok_count)
            keys = pl.ds(low, 384)
            q = both_heads(qkv[at, cols])
            k = qkv[keys, kcols]
            v = qkv[keys, vcols]
            g = both_heads(g_ref[at, cols])
            delta = jnp.sum(g.astype(WIDE) * twice(out[at, cols].astype(WIDE)), axis=1, keepdims=True)
            lane = lanes((128, 128))
            stats = lse_ref[at, :]
            lse_low = jnp.sum(jnp.where(lane == 2 * pair, stats, 0.0), axis=1, keepdims=True)
            lse_high = jnp.sum(jnp.where(lane == 2 * pair + 1, stats, 0.0), axis=1, keepdims=True)
            lse = jnp.concatenate([lse_low, lse_high], axis=0)
            allowed = self_mask(row_seg, row_keep, col_seg, block, low)
            scores = dot_nt(q, k) * SCALE
            probs = jnp.exp(jnp.where(twice(allowed), scores - lse, FILL))
            gscores = (probs * (dot_nt(g, v) - delta)).astype(LOW)
            dqkv[at, cols] = (join_heads(dot(gscores, k)) * SCALE).astype(LOW)
            dk[keys, :] = dk[keys, :] + dot_tn(gscores, q)
            dv[keys, :] = dv[keys, :] + dot_tn(probs.astype(LOW), g)
            return inner

        lax.fori_loop(0, blocks, one, 0)
        dqkv[:, kcols] = (dk[...] * SCALE).astype(LOW)
        dqkv[:, vcols] = dv[...].astype(LOW)
        return carry

    lax.fori_loop(0, width // 128, pair_step, 0)


class Part:
    def __init__(self, src, pieces, span, bufs, put):
        self.src, self.pieces, self.bufs, self.put = src, pieces, bufs, put
        self.first, self.at = pieces[0], pl.ds(span[0], span[1] - span[0])


def reduce_steps(me, chunks, send, recv):
    z, x, c, y = me.z, me.x, me.c, me.y
    depth = me.depth
    count = len(chunks)
    started = [[None] * 4 for _ in chunks]
    used = [0] * count
    every = slice(None)

    def launch(k, stage):
        copies = []

        def push(src, dst, peer):
            slot = used[k]
            used[k] += 1
            copy = remote(src, dst, send.at[k, slot], recv.at[k, slot], peer)
            copy.start()
            copies.append(copy)

        for which, parts in enumerate(chunks[k]):
            for part in parts:
                got_c, got_1, got_2, got_z = part.bufs
                lo, hi = part.pieces
                n = slice(lo, hi)
                s = slice(lo - part.shift, hi - part.shift)
                if stage == 0:
                    push(part.src.at[s, :, :, 1 - c, :, part.at], got_c.at[n, :, :, :, part.at], me.across_core())
                elif stage == 1:
                    if which == 0:
                        push(got_c.at[n, :, :, 1 - y, part.at], got_1.at[n, :, :, part.at], me.across_y())
                    else:
                        push(got_c.at[n, :, 1 - x, :, part.at], got_1.at[n, :, :, part.at], me.across_x())
                elif stage == 2:
                    if which == 0:
                        push(got_c.at[n, :, 1 - x, y, part.at], got_2.at[n, :, part.at], me.across_x())
                    else:
                        push(got_c.at[n, :, x, 1 - y, part.at], got_2.at[n, :, part.at], me.across_y())
                else:
                    for j in range(1, depth):
                        push(
                            got_c.at[n, lax.rem(z + j, depth), x, y, part.at],
                            got_z.at[n, j - 1, part.at],
                            me.along(j),
                        )
        started[k][stage] = copies

    def absorb(k, stage):
        for copy in started[k][stage]:
            copy.wait_recv()
        for which, parts in enumerate(chunks[k]):
            for part in parts:
                got_c, got_1, got_2, got_z = part.bufs

                def each(i, carry, part=part, which=which, got_c=got_c, got_1=got_1, got_2=got_2):
                    piece, zz = part.pieces[0] + i // depth, lax.rem(i, depth)
                    at = part.at
                    if stage == 0:
                        for xx in range(2):
                            for yy in range(2):
                                got_c[piece, zz, xx, yy, at] = (
                                    part.src[piece - part.shift, zz, xx, c, yy, at].astype(WIDE)
                                    + got_c[piece, zz, xx, yy, at].astype(WIDE)
                                ).astype(LOW)
                    elif stage == 1:
                        for q in range(2):
                            where = (piece, zz, q, y, at) if which == 0 else (piece, zz, x, q, at)
                            got_c[where] = (
                                got_c[where].astype(WIDE) + got_1[piece, zz, q, at].astype(WIDE)
                            ).astype(LOW)
                    else:
                        where = (piece, zz, x, y, at)
                        got_c[where] = (got_c[where].astype(WIDE) + got_2[piece, zz, at].astype(WIDE)).astype(LOW)
                    return carry

                lo, hi = part.pieces
                if stage < 3:
                    lax.fori_loop(0, (hi - lo) * depth, each, 0)
                else:
                    for piece in range(lo, hi):
                        total = got_c[piece, z, x, y, part.at].astype(WIDE)
                        for j in range(1, depth):
                            total = total + got_z[piece, j - 1, part.at].astype(WIDE)
                        part.put(piece, total)

    for step in range(count + 4):
        for stage in range(4, -1, -1):
            k = step - stage
            if not 0 <= k < count:
                continue
            if stage > 0:
                absorb(k, stage - 1)
            if stage < 4:
                launch(k, stage)
        yield step
    for stages in started:
        for copies in stages:
            for copy in copies:
                copy.wait_send()


def last_kernel(depth, reduces, *refs):
    (
        pair, seg, pad, dq_own, dq_other, dkv, enc, start, one, qkv, low, lse, after, two, gstate,
        gw_a, gw_f, gw_i, small_rows, small_cols, ga, gs,
    ) = refs[:22]
    refs = refs[22:]
    grad_input, grad_enc = refs[:2]
    refs = refs[2:]
    outs = refs[:9] if reduces else refs[:2]
    refs = refs[9:] if reduces else refs[2:]
    (w_qkv, w_so, w_cq, w_kv, w_s, got_dq, g_attn, dqkv, dk, dv, row_seg, row_keep, col_seg, load_sem, sw_send, sw_recv) = refs[:16]
    refs = refs[16:]
    tok_count, width = dq_own.shape
    src_count = enc.shape[0]
    everyone = depth * 8
    me = Place(depth)
    scale = (tok_count * everyone) ** (-0.5)
    if reduces:
        greet(me.others() + [me.across_x(), me.across_y(), me.across_core()])
    else:
        greet([me.across_y()])
    swap = remote(dq_other, got_dq, sw_send.at[0], sw_recv.at[0], me.across_y())
    swap.start()
    loads = []
    sources = ((ga.at[0:3], w_qkv), (ga.at[3:4], w_so), (ga.at[4:5], w_cq), (ga.at[5:7], w_kv), (gs, w_s))
    for k, (src, dst) in enumerate(sources):
        copy = pltpu.make_async_copy(src, dst, load_sem.at[k])
        copy.start()
        loads.append(copy)

    if reduces:
        (late, late_s, c_a, c_f, c_i, c_s, a_1, f_1, i_1, s_1, a_2, f_2, i_2, s_2, a_z, f_z, i_z, s_z, send, recv) = refs
        (o_qkv, o_so, o_cq, o_kv, o_co, o_fi, o_fo, o_in, o_s) = outs
        homes = [(o_qkv, 0), (o_qkv, 1), (o_qkv, 2), (o_so, 0), (o_cq, 0), (o_kv, 0), (o_kv, 1), (o_co, 0)]
        homes += [(o_fi, k) for k in range(4)]

        def put_a(piece, total):
            ref, k = homes[piece]
            ref[:, k * BLOCK : (k + 1) * BLOCK] = total * scale

        bufs_a, bufs_f, bufs_i, bufs_s = (c_a, a_1, a_2, a_z), (c_f, f_1, f_2, f_z), (c_i, i_1, i_2, i_z), (c_s, s_1, s_2, s_z)
        rows = BLOCK // everyone

        def a_part(lo, hi):
            part = Part(late if lo < 7 else gw_a, (lo, hi), (0, rows), bufs_a, put_a)
            part.shift = 0 if lo < 7 else 7
            return part

        def other(src, bufs, span, out):
            def put(piece, total):
                out[pl.ds(span[0], span[1] - span[0])] = total * scale

            part = Part(src, (0, 1), span, bufs, put)
            part.shift = 0
            return part

        half_f, size_i = o_fo.shape[0] // 2, o_in.shape[0]
        chunks = [
            ([a_part(8, 10)], [a_part(10, 12)]),
            ([other(gw_f, bufs_f, (0, half_f), o_fo)], [other(gw_f, bufs_f, (half_f, 2 * half_f), o_fo)]),
            ([a_part(7, 8)], [other(gw_i, bufs_i, (0, size_i), o_in)]),
            ([a_part(5, 6)], [a_part(6, 7)]),
            ([a_part(3, 4)], [a_part(4, 5)]),
            ([a_part(0, 2)], [a_part(2, 3), other(late_s, bufs_s, (0, rows), o_s)]),
        ]
        steps = reduce_steps(me, chunks, send, recv)

        def keep(piece, value):
            late[piece] = value.astype(LOW).reshape(late.shape[1:])

        def keep_small(value):
            late_s[...] = value.astype(LOW).reshape(late_s.shape)
    else:
        steps = iter(())
        o_late, o_small = outs

        def keep(piece, value):
            o_late[piece] = value.astype(LOW)

        def keep_small(value):
            o_small[...] = value

    def advance():
        return next(steps, None)

    advance()
    segments = seg[...].astype(WIDE)
    row_seg[...] = segments
    row_keep[...] = 1.0 - pad[...].astype(WIDE)
    pair_row = jnp.zeros((1, tok_count), WIDE)
    for k in range(SEGS):
        pair_row = jnp.where(segments == k, pair[0, k].astype(WIDE), pair_row)
    columns = transposed_rows(jnp.concatenate([segments, pair_row, jnp.zeros((6, tok_count), WIDE)], axis=0))
    col_seg[...] = columns
    onehot = (lanes((tok_count, 128)) == (columns[:, 1:2].astype(jnp.int32) + 8)).astype(LOW)
    for copy in loads:
        copy.wait()

    def flat(value):
        return value.reshape((-1, value.shape[-1]))

    table = flat(w_s[...]).astype(WIDE).T
    w_key, w_val = flat(w_kv[0]), flat(w_kv[1])
    advance()
    parts = 4
    span = src_count // parts
    for k in range(parts):
        at = pl.ds(k * span, span)
        grads = dot_nt(dkv[at, 0:width], w_key) + dot_nt(dkv[at, width : 2 * width], w_val)
        grad_enc[at, :] = grads.astype(LOW)
    advance()
    keep(5, dot_tn(enc[...], dkv[:, 0:width]))
    keep(6, dot_tn(enc[...], dkv[:, width : 2 * width]))
    advance()
    swap.wait()
    g_query = (dq_own[...] + got_dq[...].astype(WIDE)).astype(LOW)
    keep(4, dot_tn(two[...], g_query))
    back, gain_1, bias_1 = norm_back(after[...], table[1:2], dot_nt(g_query, flat(w_cq[...])))
    grad_state = gstate[...] + back
    g_self = grad_state.astype(LOW)
    keep(3, dot_tn(low[...], g_self))
    g_attn[...] = dot_nt(g_self, flat(w_so[...])).astype(LOW)
    advance()
    self_backward(qkv, low, lse, g_attn, dqkv, dk, dv, row_seg, row_keep, col_seg)
    for k in range(3):
        keep(k, dot_tn(one[...], dqkv[:, k * width : (k + 1) * width]))
    upstream = dot_nt(dqkv[:, 0:width], flat(w_qkv[0]))
    upstream = upstream + dot_nt(dqkv[:, width : 2 * width], flat(w_qkv[1]))
    upstream = upstream + dot_nt(dqkv[:, 2 * width : 3 * width], flat(w_qkv[2]))
    back, gain_0, bias_0 = norm_back(start[...], table[0:1], upstream)
    grad_start = grad_state + back
    grad_input[...] = grad_start.astype(LOW)
    coarse = grad_start.astype(LOW)
    fine = (grad_start - coarse.astype(WIDE)).astype(LOW)
    g_table = (dot_tn(onehot, coarse) + dot_tn(onehot, fine))[8:16]
    mid = small_rows[...]
    stacked = jnp.concatenate(
        [gain_0, gain_1, mid[0:2], bias_0, bias_1, mid[2:4], g_table], axis=0
    )
    keep_small(transposed_rows(stacked) + small_cols[...])
    for _ in steps:
        pass


def last_part(depth, reduces, pair, seg, pad, dq_own, dq_other, dkv, enc, kept, gstate, grads, whole):
    tok_count, width = dq_own.shape
    src_count = enc.shape[0]
    ga, gf, gi, gs = whole
    gw_a, gw_f, gw_i, small_rows, small_cols = grads
    everyone = depth * 8
    rows = BLOCK // everyone
    sharded = (depth, 2, 2, 2)
    outs = [shape_of((tok_count, width), LOW), shape_of((src_count, width), LOW)]
    scratch = [
        pltpu.VMEM((3, BLOCK, BLOCK), LOW),
        pltpu.VMEM((1, BLOCK, BLOCK), LOW),
        pltpu.VMEM((1, BLOCK, BLOCK), LOW),
        pltpu.VMEM((2, BLOCK, BLOCK), LOW),
        pltpu.VMEM(gs.shape, LOW),
        pltpu.VMEM((tok_count, width), LOW),
        pltpu.VMEM((tok_count, width), LOW),
        pltpu.VMEM((tok_count, 3 * width), LOW),
        pltpu.VMEM((tok_count, 128), WIDE),
        pltpu.VMEM((tok_count, 128), WIDE),
        pltpu.VMEM((1, tok_count), WIDE),
        pltpu.VMEM((1, tok_count), WIDE),
        pltpu.VMEM((tok_count, 128), WIDE),
        pltpu.SemaphoreType.DMA((5,)),
        pltpu.SemaphoreType.DMA((1,)),
        pltpu.SemaphoreType.DMA((1,)),
    ]
    if reduces:
        shapes = [(12, rows, BLOCK), (1, gf.shape[0] // everyone, width), (1, gi.shape[0] // everyone, gi.shape[1]), (1, rows, 128)]
        outs += [
            shape_of((rows, 3 * BLOCK), WIDE),
            shape_of((rows, BLOCK), WIDE),
            shape_of((rows, BLOCK), WIDE),
            shape_of((rows, 2 * BLOCK), WIDE),
            shape_of((rows, BLOCK), WIDE),
            shape_of((rows, 4 * BLOCK), WIDE),
            shape_of(shapes[1][1:], WIDE),
            shape_of(shapes[2][1:], WIDE),
            shape_of((rows, 128), WIDE),
        ]
        gw_a = gw_a.reshape((5,) + sharded + shapes[0][1:])
        gw_f = gw_f.reshape((1,) + sharded + shapes[1][1:])
        gw_i = gw_i.reshape((1,) + sharded + shapes[2][1:])
        scratch += [
            pltpu.VMEM((7,) + sharded + shapes[0][1:], LOW),
            pltpu.VMEM((1,) + sharded + shapes[3][1:], LOW),
        ]
        for lead in ((depth, 2, 2), (depth, 2), (depth,), (depth - 1,)):
            scratch += [pltpu.VMEM((n,) + lead + (r, w), LOW) for n, r, w in shapes]
        slots = 2 * (5 + (depth - 1) * 2)
        scratch += [pltpu.SemaphoreType.DMA((6, slots)), pltpu.SemaphoreType.DMA((6, slots))]
    else:
        outs += [shape_of((7, BLOCK, BLOCK), LOW), shape_of((BLOCK, 128), WIDE)]
    return pl.pallas_call(
        partial(last_kernel, depth, reduces),
        name="last_part",
        out_shape=outs,
        in_specs=[SMEM] + [VMEM] * 19 + [ANY] * 2,
        out_specs=[VMEM] * len(outs),
        scratch_shapes=scratch,
        compiler_params=pltpu.CompilerParams(
            collective_id=2, has_side_effects=True, vmem_limit_bytes=LIMIT
        ),
    )(pair, seg, pad, dq_own, dq_other, dkv, enc, *kept, gstate, gw_a, gw_f, gw_i, small_rows, small_cols, ga, gs)


def gather_by_ops(raw, small):
    qkv, self_out, cross_q, cross_kv, cross_out, ffn_in, ffn_out, insert = raw
    wide = jnp.concatenate([qkv, self_out, cross_q, cross_kv, cross_out, ffn_in], axis=1)
    ga = lax.all_gather(wide, BOTH, axis=0, tiled=True).reshape(BLOCK, 12, BLOCK).swapaxes(0, 1)
    return (
        ga,
        lax.all_gather(ffn_out, BOTH, axis=0, tiled=True),
        lax.all_gather(insert, BOTH, axis=0, tiled=True),
        lax.all_gather(small, BOTH, axis=0, tiled=True),
    )


def reduce_by_ops(late, small, grads, scale):
    gw_a, gw_f, gw_i = grads
    wide = jnp.concatenate([late, gw_a]).swapaxes(0, 1).reshape(BLOCK, 12 * BLOCK)

    def sums(a):
        return lax.psum_scatter(a.astype(WIDE), BOTH, scatter_dimension=0, tiled=True) * scale

    own = sums(wide)
    edges = (0, 3, 4, 5, 7, 8, 12)
    pieces = [own[:, lo * BLOCK : hi * BLOCK] for lo, hi in zip(edges[:-1], edges[1:])]
    return pieces + [sums(gw_f), sums(gw_i), sums(small)]


def body(
    dec_input, enc_output, segment_ids, padding, pair_ids, src_lengths, delete_labels, insert_counts,
    masked_positions, masked_targets, norm_gain, norm_bias, pair_table, self_qkv, self_out, cross_q, cross_kv,
    cross_out, ffn_in, ffn_out, w_delete, w_insert, w_vocab,
):
    everyone = lax.axis_size(BOTH)
    depth = everyone // 8
    tok_count, width = dec_input.shape
    masked = masked_positions.shape[1]
    rows = self_qkv.shape[0]
    aligned = rows % 16 == 0
    src_pos = lax.axis_index("src")
    small = jnp.concatenate([norm_gain, norm_bias, pair_table, w_delete.T], axis=0).T
    small = jnp.pad(small, ((0, 0), (0, 128 - small.shape[1])))
    raw = (self_qkv, self_out, cross_q, cross_kv, cross_out, ffn_in, ffn_out, w_insert)
    whole = None if aligned else gather_by_ops(raw, small)
    whole, firsts = first_part(
        depth, aligned, segment_ids, padding, pair_ids, dec_input, enc_output, small, raw, whole
    )
    start, one, qkv, low, lse, after, two, query, other_query, kv = firsts

    partners = lax.all_gather(segment_ids[0], "src")
    other_seg = lax.dynamic_index_in_dim(partners, 1 - src_pos, 0, keepdims=False)
    seg_s = jnp.stack([src_pos * SEGS + segment_ids[0], (1 - src_pos) * SEGS + other_seg])
    seg_cols = jnp.pad(seg_s.T, ((0, 0), (0, 126)))
    ends_s = jnp.concatenate([jnp.zeros((1,), jnp.int32), jnp.cumsum(src_lengths[0])])
    attended = cross_forward(seg_s, ends_s, seg_cols, query, other_query, kv)

    mids = middle_part(
        depth, segment_ids, padding, delete_labels, insert_counts, masked_positions.reshape(-1, 1),
        masked_targets.reshape(-1, 1), w_vocab, after, attended, whole,
    )
    block_out, gstate, g_own, g_other, st_own, st_other = mids[:6]
    grads, (grad_vocab, tokens, loss) = mids[6:11], mids[11:]
    dq_own, dq_other, dkv = cross_backward(
        seg_s, ends_s, seg_cols, query, other_query, g_own, g_other, st_own, st_other, kv
    )
    res = last_part(
        depth, aligned, pair_ids, segment_ids, padding, dq_own, dq_other, dkv, enc_output,
        (start, one, qkv, low, lse, after, two), gstate, grads, whole,
    )
    grad_input, grad_enc = res[:2]
    if aligned:
        sums = res[2:]
    else:
        scale = (tok_count * everyone) ** (-0.5)
        sums = reduce_by_ops(res[2], res[3], grads[:3], scale)
    small_sum = sums[8].T
    pos = lax.axis_index(BOTH)
    own_tokens = lax.dynamic_slice_in_dim(tokens[0:1], pos * masked, masked, axis=1)
    return (
        block_out, grad_input, grad_enc, small_sum[0:4], small_sum[4:8], small_sum[8:16], *sums[:8][:6],
        sums[6], small_sum[16:18].T, sums[7], grad_vocab, loss[0, 0], own_tokens,
    )


def solution(mesh):
    shared = P(BOTH, None)
    across = P(None, BOTH)
    return jax.shard_map(
        body,
        mesh=mesh,
        in_specs=(shared,) * 5 + (P("batch", None),) + (shared,) * 4 + (across,) * 3 + (shared,) * 10,
        out_specs=(shared,) * 3 + (across,) * 3 + (shared,) * 10 + (P(), shared),
        check_vma=False,
    )
```

```python
from functools import partial

import jax
import jax.numpy as jnp
from jax import lax
from jax.experimental import pallas as pl
from jax.experimental.pallas import tpu as pltpu
from jax.sharding import PartitionSpec as P

HD = 64
PAIRS = 8
SEGS = 8
BLOCK = 512
EPSILON = 1e-05
SCALE = 0.125
FILL = -1e30
GELU = 0.7978845608
CUBIC = 0.044715

MESH = pl.DeviceIdType.MESH
ANY = pl.BlockSpec(memory_space=pl.ANY)
VMEM = pl.BlockSpec(memory_space=pltpu.VMEM)
SMEM = pl.BlockSpec(memory_space=pltpu.SMEM)
BOTH = ("batch", "src")
LOW = jnp.bfloat16
WIDE = jnp.float32
LIMIT = 60 << 20


def shape_of(shape, kind):
    return jax.ShapeDtypeStruct(shape, kind)


def dot(left, right):
    return jnp.dot(left, right, preferred_element_type=WIDE)


def dot_tn(left, right):
    return lax.dot_general(left, right, (((0,), (0,)), ((), ())), preferred_element_type=WIDE)


def dot_nt(left, right):
    return lax.dot_general(left, right, (((1,), (1,)), ((), ())), preferred_element_type=WIDE)


def normalised(v):
    centred = v - jnp.mean(v, axis=-1, keepdims=True)
    r = lax.rsqrt(jnp.mean(centred * centred, axis=-1, keepdims=True) + EPSILON)
    return centred * r, r


def norm_back(v, gain, upstream):
    hat, r = normalised(v)
    scaled = upstream * gain
    first = jnp.mean(scaled, axis=-1, keepdims=True)
    second = jnp.mean(scaled * hat, axis=-1, keepdims=True)
    grad_gain = jnp.sum(upstream * hat, axis=0, keepdims=True)
    grad_bias = jnp.sum(upstream, axis=0, keepdims=True)
    return r * (scaled - first - hat * second), grad_gain, grad_bias


def lanes(shape):
    return lax.broadcasted_iota(jnp.int32, shape, len(shape) - 1)


def rows_of(shape):
    return lax.broadcasted_iota(jnp.int32, shape, len(shape) - 2)


def both_heads(x):
    low = lanes(x.shape) < HD
    zero = jnp.zeros_like(x)
    return jnp.concatenate([jnp.where(low, x, zero), jnp.where(low, zero, x)], axis=0)


def join_heads(x):
    half = x.shape[0] // 2
    return jnp.where(lanes((half, x.shape[1])) < HD, x[:half], x[half:])


def twice(x):
    return jnp.concatenate([x, x], axis=0)


def transposed_rows(rows):
    count, width = rows.shape
    return jnp.concatenate([rows, jnp.zeros((128 - count, width), WIDE)], axis=0).T


def greet(peers):
    barrier = pltpu.get_barrier_semaphore()
    for peer in peers:
        pl.semaphore_signal(barrier, inc=1, device_id=peer, device_id_type=MESH)
    pl.semaphore_wait(barrier, len(peers))


def remote(src, dst, send, recv, peer):
    return pltpu.make_async_remote_copy(
        src_ref=src,
        dst_ref=dst,
        send_sem=send,
        recv_sem=recv,
        device_id=peer,
        device_id_type=MESH,
    )


class Place:
    def __init__(self, depth):
        b = lax.axis_index("batch")
        self.depth = depth
        self.y = lax.axis_index("src")
        self.c = lax.rem(b, 2)
        self.x = lax.rem(b // 2, 2)
        self.z = b // 4

    def at(self, z=None, x=None, c=None, y=None):
        z = self.z if z is None else z
        x = self.x if x is None else x
        c = self.c if c is None else c
        y = self.y if y is None else y
        return ((z * 2 + x) * 2 + c, y)

    def along(self, k):
        return self.at(z=lax.rem(self.z + k, self.depth))

    def others(self):
        return [self.along(k) for k in range(1, self.depth)]

    def across_x(self):
        return self.at(x=1 - self.x)

    def across_y(self):
        return self.at(y=1 - self.y)

    def across_both(self):
        return self.at(x=1 - self.x, y=1 - self.y)

    def across_core(self):
        return self.at(c=1 - self.c)


def gather_steps(me, chunks, send, recv):
    z, x, c, y = me.z, me.x, me.c, me.y
    count = len(chunks)
    started = [[None] * 3 for _ in chunks]
    used = [0] * count
    every = slice(None)

    def launch(k, stage):
        copies = []

        def push(block, peer):
            slot = used[k]
            used[k] += 1
            copy = remote(block, block, send.at[k, slot], recv.at[k, slot], peer)
            copy.start()
            copies.append(copy)

        for view in chunks[k]:
            if stage == 0:
                for peer in me.others():
                    push(view(z, x, c, y), peer)
            elif stage == 1:
                for peer in (me.across_x(), me.across_y(), me.across_both()):
                    push(view(every, x, c, y), peer)
            else:
                push(view(every, every, c, every), me.across_core())
        started[k][stage] = copies

    for step in range(count + 3):
        for stage in range(3, -1, -1):
            k = step - stage
            if not 0 <= k < count:
                continue
            if stage > 0:
                for copy in started[k][stage - 1]:
                    copy.wait_recv()
            if stage < 3:
                launch(k, stage)
        yield step - 3
    for stages in started:
        for copies in stages:
            for copy in copies:
                copy.wait_send()


def self_window(block, tok_count):
    low = jnp.clip(block * 128 - 128, 0, tok_count - 384)
    return pl.multiple_of(low, 128)


def self_mask(row_seg, row_keep, col_seg, block, low):
    at = pl.ds(low, 384)
    keys = row_seg[0:1, at]
    keep = row_keep[0:1, at]
    queries = col_seg[pl.ds(pl.multiple_of(block * 128, 128), 128), 0:1]
    shape = (128, 384)
    own = (rows_of(shape) + block * 128) == (lanes(shape) + low)
    return (queries == keys) & ((keep > 0.5) | own)


def self_forward(blocks, qkv, out, lse_ref, row_seg, row_keep, col_seg):
    tok_count, width = out.shape
    first, last = blocks
    pairs = width // 128

    def one(t, carry):
        block, pair = first + t // pairs, lax.rem(t, pairs)
        at = pl.ds(pl.multiple_of(block * 128, 128), 128)
        low = self_window(block, tok_count)
        keys = pl.ds(low, 384)
        base = pl.multiple_of(pair * 128, 128)
        q = both_heads(qkv[at, pl.ds(base, 128)] * SCALE)
        k = qkv[keys, pl.ds(pl.multiple_of(base + width, 128), 128)]
        v = qkv[keys, pl.ds(pl.multiple_of(base + 2 * width, 128), 128)]
        allowed = self_mask(row_seg, row_keep, col_seg, block, low)
        scores = jnp.where(twice(allowed), dot_nt(q, k), FILL)
        top = jnp.max(scores, axis=1, keepdims=True)
        exps = jnp.exp(scores - top)
        total = jnp.sum(exps, axis=1, keepdims=True)
        probs = (exps * (1.0 / total)).astype(LOW)
        out[at, pl.ds(base, 128)] = join_heads(dot(probs, v)).astype(LOW)
        lse = top + jnp.log(total)
        lane = lanes((128, 128))
        lse_ref[at, :] = jnp.where(
            lane == 2 * pair, lse[:128], jnp.where(lane == 2 * pair + 1, lse[128:], lse_ref[at, :])
        )
        return carry

    lax.fori_loop(0, (last - first) * pairs, one, 0)


def small_matrix(gain, bias, pair_rows, delete):
    def spot(count, first):
        shape = (count, 128)
        return (rows_of(shape) + first == lanes(shape)).astype(LOW)

    total = dot_tn(gain, spot(4, 0)) + dot_tn(bias, spot(4, 4)) + dot_tn(pair_rows, spot(PAIRS, 8))
    return (total + dot_tn(delete, spot(2, 8 + PAIRS))).astype(LOW)


def token_numbers(seg, pad, pair, row_seg, row_keep, col_seg):
    tok_count = seg.shape[1]
    segments = seg[...].astype(WIDE)
    row_seg[...] = segments
    row_keep[...] = 1.0 - pad[...].astype(WIDE)
    pair_row = jnp.zeros((1, tok_count), WIDE)
    for k in range(SEGS):
        pair_row = jnp.where(segments == k, pair[0, k].astype(WIDE), pair_row)
    columns = transposed_rows(jnp.concatenate([segments, pair_row, jnp.zeros((6, tok_count), WIDE)], axis=0))
    col_seg[...] = columns
    return (lanes((tok_count, 128)) == (columns[:, 1:2].astype(jnp.int32) + 8)).astype(LOW)


def cutter(ref):
    every = (slice(None),) * (len(ref.shape) - 2)

    def cut(lo, hi):
        value = ref[every + (slice(lo, hi),)]
        return value.reshape((-1, value.shape[-1]))

    return cut


QKV, SO, CQ, KV, EARLY = 0, 48, 64, 80, 112


def first_kernel(depth, gathers, *refs):
    (seg, pad, pair, dec, enc) = refs[:5]
    refs = refs[5:]
    if gathers:
        (gain, bias, pair_rows, delete, raw_qkv, raw_so, raw_cq, raw_kv, raw_co, raw_fi, raw_fo, raw_in) = refs[:12]
        (ga_out, gs_out, gz) = refs[12:15]
        refs = refs[15:]
    else:
        ga_in, gs_in = refs[:2]
        refs = refs[2:]
    (start_out, one_out, qkv_out, low_out, lse_out, after_out, two_out, query_out, other_out, kv_out, seg_out) = refs[:11]
    (ga, gs, row_seg, row_keep, col_seg, own_sem, send, recv, sw_send, sw_recv) = refs[11:]
    tok_count, width = dec.shape
    src_count = enc.shape[0]
    me = Place(depth)
    z, x, c, y = me.z, me.x, me.c, me.y
    owns = []

    def own(src, dst):
        copy = pltpu.make_async_copy(src, dst, own_sem.at[len(owns)])
        copy.start()
        owns.append(copy)

    if gathers:
        for raw, count, first in ((raw_qkv, 3, QKV), (raw_so, 1, SO), (raw_cq, 1, CQ), (raw_kv, 2, KV)):
            for k in range(count):
                own(raw.at[:, pl.ds(k * BLOCK, BLOCK)], ga.at[z, x, c, y, pl.ds(first + 16 * k, 16)])
        soon = len(owns)
        own(raw_co, gz.at[z, pl.ds(0, 16)])
        for k in range(4):
            own(raw_fi.at[:, pl.ds(k * BLOCK, BLOCK)], gz.at[z, pl.ds(16 + 16 * k, 16)])
        own(raw_fo, gz.at[z, pl.ds(80, 64)])
        for k in range(2):
            half = BLOCK // 2
            own(raw_in.at[pl.ds(16 * k, 16)], gz.at[z, pl.ds(144, 16), pl.ds(half * k, half)])
        gs[z, x, c, y] = small_matrix(gain[...], bias[...], pair_rows[...], delete[...])
        greet(me.others() + [me.across_x(), me.across_y(), me.across_both(), me.across_core()])
        for copy in owns[:soon]:
            copy.wait()

        def rows(lo, hi):
            return lambda *at: ga.at[at + (pl.ds(lo, hi - lo),)]

        chunks = [[lambda *at: gs.at[at], rows(QKV, SO)], [rows(SO, EARLY)]]
        steps = gather_steps(me, chunks, send, recv)
    else:
        own(ga_in, ga)
        own(gs_in, gs)
        greet([me.across_y()])
        for copy in owns:
            copy.wait()
        steps = iter(())

    def advance():
        return next(steps, None)

    def have(chunk):
        while gathers:
            done = advance()
            if done is None or done >= chunk:
                return

    advance()
    onehot = token_numbers(seg, pad, pair, row_seg, row_keep, col_seg)
    lse_out[...] = jnp.zeros_like(lse_out)
    meet = remote(seg, seg_out, sw_send.at[0], sw_recv.at[0], me.across_y())
    meet.start()
    cut = cutter(ga)
    have(0)
    line = []
    if gathers:
        for copy in owns[soon:]:
            copy.wait()
        for k in range(1, depth):
            line.append(remote(gz.at[z], gz.at[z], sw_send.at[3 + k], sw_recv.at[3 + k], me.along(k)))
            line[-1].start()
    table = cutter(gs)(0, gs.shape[-2]).astype(WIDE).T
    start = dec[...].astype(WIDE) + dot(onehot, table.astype(LOW))
    start_out[...] = start
    one = (normalised(start)[0] * table[0:1] + table[4:5]).astype(LOW)
    one_out[...] = one
    for k in range(3):
        qkv_out[:, pl.ds(k * BLOCK, BLOCK)] = dot(one, cut(QKV + 16 * k, QKV + 16 * (k + 1))).astype(LOW)
    advance()
    halves = 2
    span = tok_count // halves
    swaps = []
    for k in range(halves):
        at = pl.ds(k * span, span)
        self_forward((k * span // 128, (k + 1) * span // 128), qkv_out, low_out, lse_out, row_seg, row_keep, col_seg)
        if k == 0:
            have(1)
        after = start_out[at, :] + dot(low_out[at, :], cut(SO, CQ))
        after_out[at, :] = after
        two = (normalised(after)[0] * table[1:2] + table[5:6]).astype(LOW)
        two_out[at, :] = two
        query_out[at, :] = dot(two, cut(CQ, KV)).astype(LOW)
        swap = remote(query_out.at[at], other_out.at[at], sw_send.at[1 + k], sw_recv.at[1 + k], me.across_y())
        swap.start()
        swaps.append(swap)
    if gathers:
        own(ga, ga_out)
        own(gs, gs_out)
    w_key, w_val = cut(KV, KV + 16), cut(KV + 16, EARLY)
    parts = 4
    for k in range(parts):
        span = src_count // parts
        at = pl.ds(k * span, span)
        kv_out[at, 0:width] = dot(enc[at, :], w_key).astype(LOW)
        kv_out[at, width : 2 * width] = dot(enc[at, :], w_val).astype(LOW)
    for _ in steps:
        pass
    for copy in swaps + [meet] + line:
        copy.wait()
    if gathers:
        for copy in owns[-2:]:
            copy.wait()


def first_part(depth, gathers, seg, pad, pair, dec, enc, tiny, raw, late, whole):
    tok_count, width = dec.shape
    src_count = enc.shape[0]
    lead = (depth, 2, 2, 2) if gathers else (BLOCK // 16,)
    outs = [
        (shape_of((tok_count, width), WIDE), VMEM),
        (shape_of((tok_count, width), LOW), VMEM),
        (shape_of((tok_count, 3 * width), LOW), VMEM),
        (shape_of((tok_count, width), LOW), VMEM),
        (shape_of((tok_count, 128), WIDE), VMEM),
        (shape_of((tok_count, width), WIDE), VMEM),
        (shape_of((tok_count, width), LOW), VMEM),
        (shape_of((tok_count, width), LOW), VMEM),
        (shape_of((tok_count, width), LOW), ANY),
        (shape_of((src_count, 2 * width), LOW), VMEM),
        (shape_of((1, tok_count), jnp.int32), ANY),
    ]
    if gathers:
        outs = [
            (shape_of(lead + (EARLY, BLOCK), LOW), ANY),
            (shape_of(lead + (16, 128), LOW), ANY),
            (shape_of((depth, 160, BLOCK), LOW), ANY),
        ] + outs
    extra = (*tiny, *raw, *late) if gathers else whole
    res = pl.pallas_call(
        partial(first_kernel, depth, gathers),
        name="first_part",
        out_shape=[o for o, _ in outs],
        in_specs=[VMEM, VMEM, SMEM, VMEM, VMEM] + ([VMEM] * 4 + [ANY] * 8 if gathers else [ANY] * 2),
        out_specs=[s for _, s in outs],
        scratch_shapes=[
            pltpu.VMEM(lead + (EARLY, BLOCK), LOW),
            pltpu.VMEM(lead + (16, 128), LOW),
            pltpu.VMEM((1, tok_count), WIDE),
            pltpu.VMEM((1, tok_count), WIDE),
            pltpu.VMEM((tok_count, 128), WIDE),
            pltpu.SemaphoreType.DMA((18,)),
            pltpu.SemaphoreType.DMA((2, 2 * (depth + 3))),
            pltpu.SemaphoreType.DMA((2, 2 * (depth + 3))),
            pltpu.SemaphoreType.DMA((depth + 3,)),
            pltpu.SemaphoreType.DMA((depth + 3,)),
        ],
        compiler_params=pltpu.CompilerParams(
            collective_id=0, has_side_effects=True, vmem_limit_bytes=LIMIT
        ),
    )(seg, pad, pair, dec, enc, *extra)
    if gathers:
        whole, line, res = res[:2], res[2], res[3:]
        return whole, line, res
    return whole, None, res


def segment_ends(lengths, ends):
    total = jnp.int32(0)
    ends[0] = total
    for s in range(2 * SEGS):
        total = total + lengths[0, s]
        ends[s + 1] = total


def block_ranges(seg_s, first_seg, ends, off, src_count, block):
    at = pl.multiple_of(block * 128, 128)
    low = jnp.clip(ends[first_seg + seg_s[0, at]] - off, 0, src_count)
    high = jnp.clip(ends[first_seg + seg_s[0, at + 127] + 1] - off, 0, src_count)
    first = low // TILE
    return first, jnp.where(high > low, (high + TILE - 1) // TILE, first)


def key_bounds(segs, firsts, ends, off):
    rows = []
    for seg, first_seg in zip(segs, firsts):
        low = jnp.zeros(seg.shape, jnp.int32)
        high = jnp.zeros(seg.shape, jnp.int32)
        for s in range(SEGS):
            low = jnp.where(seg == s, ends[first_seg + s] - off, low)
            high = jnp.where(seg == s, ends[first_seg + s + 1] - off, high)
        rows += [low.astype(WIDE), high.astype(WIDE)]
    rows = jnp.concatenate(rows + [jnp.zeros((4, rows[0].shape[1]), WIDE)], axis=0)
    return transposed_rows(rows).astype(jnp.int32)


TILE = 256


def cross_forward_kernel(
    lengths, seg_so, seg_sp, seg_vo, seg_vp, q_own, q_other, kv, o_own, o_other, lse_own, lse_other,
    ends, cols_ref, top_ref, total_ref, acc_ref,
):
    tok_count, width = q_own.shape
    src_count = kv.shape[0]
    pairs = width // 128
    pos = lax.axis_index("src")
    off = pos * src_count
    firsts = (pos * SEGS, (1 - pos) * SEGS)
    segment_ends(lengths, ends)
    cols_ref[...] = key_bounds((seg_vo[...], seg_vp[...]), firsts, ends, off)
    for side, (q, o, lse_ref) in enumerate(((q_own, o_own, lse_own), (q_other, o_other, lse_other))):

        @pl.loop(0, tok_count // 128)
        def _(block):
            at = pl.ds(pl.multiple_of(block * 128, 128), 128)
            first, last = block_ranges((seg_so, seg_sp)[side], firsts[side], ends, off, src_count, block)
            low, high = cols_ref[at, 2 * side : 2 * side + 1], cols_ref[at, 2 * side + 1 : 2 * side + 2]
            top_ref[...] = jnp.full_like(top_ref, FILL)
            total_ref[...] = jnp.zeros_like(total_ref)
            acc_ref[...] = jnp.zeros_like(acc_ref)

            def one(t, carry):
                base = pl.multiple_of(t * TILE, TILE)
                keys = pl.ds(base, TILE)
                index = lanes((128, TILE)) + base
                allowed = twice((index >= low) & (index < high))
                for p in range(pairs):
                    cols = pl.ds(p * 128, 128)
                    k = kv[keys, cols]
                    v = kv[keys, pl.ds(width + p * 128, 128)]
                    scores = dot_nt(both_heads(q[at, cols]), k) * SCALE
                    scores = jnp.where(allowed, scores, FILL)
                    old = top_ref[p]
                    top = jnp.maximum(old, jnp.max(scores, axis=1, keepdims=True))
                    exps = jnp.where(allowed, jnp.exp(scores - top[:, 0:1]), 0.0)
                    fade = jnp.exp(old - top)
                    top_ref[p] = top
                    total_ref[p] = total_ref[p] * fade + jnp.sum(exps, axis=1, keepdims=True)
                    acc_ref[p] = acc_ref[p] * fade + dot(exps.astype(LOW), v)
                return carry

            lax.fori_loop(first, last, one, 0)
            lane = lanes((128, 128))
            stats = jnp.zeros((128, 128), WIDE)
            for p in range(pairs):
                total = total_ref[p]
                safe = jnp.where(total > 0.0, total, 1.0)
                o[at, pl.ds(p * 128, 128)] = join_heads(acc_ref[p] / safe).astype(LOW)
                lse = jnp.where(total > 0.0, top_ref[p] + jnp.log(safe), FILL)
                stats = jnp.where(lane == 2 * p, lse[:128], jnp.where(lane == 2 * p + 1, lse[128:], stats))
            lse_ref[:, at] = stats.T[0:8]


def cross_forward(lengths, seg_own, seg_other, q_own, q_other, kv):
    tok_count, width = q_own.shape
    heads = width // HD
    out = shape_of((tok_count, width), LOW)
    lse = shape_of((heads, tok_count), WIDE)
    return pl.pallas_call(
        cross_forward_kernel,
        name="cross_forward",
        out_shape=[out, out, lse, lse],
        in_specs=[SMEM] * 3 + [VMEM] * 5,
        out_specs=[VMEM] * 4,
        scratch_shapes=[pltpu.SMEM((32,), jnp.int32), pltpu.VMEM((tok_count, 128), jnp.int32)]
        + [pltpu.VMEM((width // 128, 256, 128), WIDE)] * 3,
        compiler_params=pltpu.CompilerParams(vmem_limit_bytes=LIMIT),
    )(lengths, seg_own, seg_other, seg_own, seg_other, q_own, q_other, kv)


def cross_backward_kernel(
    lengths, seg_so, seg_sp, seg_vo, seg_vp, q_own, q_other, g_own, g_other, st_own, st_other, kv,
    dq_own, dq_other, dkv, ends, cols_ref, acc, col_ref, dq_acc,
):
    tok_count, width = q_own.shape
    src_count = kv.shape[0]
    pairs = width // 128
    pos = lax.axis_index("src")
    off = pos * src_count
    firsts = (pos * SEGS, (1 - pos) * SEGS)
    segment_ends(lengths, ends)
    cols_ref[...] = key_bounds((seg_vo[...], seg_vp[...]), firsts, ends, off)
    acc[...] = jnp.zeros_like(acc)
    sides = ((q_own, g_own, st_own, dq_own), (q_other, g_other, st_other, dq_other))
    for side, (q, g, st, dq) in enumerate(sides):

        @pl.loop(0, tok_count // 128)
        def _(block):
            at = pl.ds(pl.multiple_of(block * 128, 128), 128)
            first, last = block_ranges((seg_so, seg_sp)[side], firsts[side], ends, off, src_count, block)
            low, high = cols_ref[at, 2 * side : 2 * side + 1], cols_ref[at, 2 * side + 1 : 2 * side + 2]
            dq_acc[...] = jnp.zeros_like(dq_acc)
            col_ref[...] = jnp.concatenate([st[:, at], jnp.zeros((112, 128), WIDE)], axis=0).T

            def one(t, carry):
                base = pl.multiple_of(t * TILE, TILE)
                keys = pl.ds(base, TILE)
                index = lanes((128, TILE)) + base
                allowed = twice((index >= low) & (index < high))
                for p in range(pairs):
                    cols = pl.ds(p * 128, 128)
                    vals = pl.ds(width + p * 128, 128)
                    k = kv[keys, cols]
                    v = kv[keys, vals]
                    qs = both_heads(q[at, cols])
                    gs = both_heads(g[at, cols])
                    lse = jnp.concatenate([col_ref[:, 2 * p : 2 * p + 1], col_ref[:, 2 * p + 1 : 2 * p + 2]], axis=0)
                    delta = jnp.concatenate(
                        [col_ref[:, 8 + 2 * p : 9 + 2 * p], col_ref[:, 9 + 2 * p : 10 + 2 * p]], axis=0
                    )
                    scores = dot_nt(qs, k) * SCALE
                    probs = jnp.exp(jnp.where(allowed, scores - lse, FILL))
                    gscores = (probs * (dot_nt(gs, v) - delta)).astype(LOW)
                    dq_acc[:, cols] = dq_acc[:, cols] + join_heads(dot(gscores, k))
                    acc[keys, cols] = acc[keys, cols] + dot_tn(gscores, qs)
                    acc[keys, vals] = acc[keys, vals] + dot_tn(probs.astype(LOW), gs)
                return carry

            lax.fori_loop(first, last, one, 0)
            dq[at, :] = (dq_acc[...] * SCALE).astype(dq.dtype)

    @pl.loop(0, src_count // 256)
    def _(t):
        at = pl.ds(pl.multiple_of(t * 256, 256), 256)
        dkv[at, 0:width] = (acc[at, 0:width] * SCALE).astype(LOW)
        dkv[at, width : 2 * width] = acc[at, width : 2 * width].astype(LOW)


def cross_backward(lengths, seg_own, seg_other, q_own, q_other, g_own, g_other, st_own, st_other, kv):
    tok_count, width = q_own.shape
    src_count = kv.shape[0]
    return pl.pallas_call(
        cross_backward_kernel,
        name="cross_backward",
        out_shape=[
            shape_of((tok_count, width), WIDE),
            shape_of((tok_count, width), LOW),
            shape_of((src_count, 2 * width), LOW),
        ],
        in_specs=[SMEM] * 3 + [VMEM] * 9,
        out_specs=[VMEM] * 3,
        scratch_shapes=[
            pltpu.SMEM((32,), jnp.int32),
            pltpu.VMEM((tok_count, 128), jnp.int32),
            pltpu.VMEM((src_count, 2 * width), WIDE),
            pltpu.VMEM((128, 128), WIDE),
            pltpu.VMEM((128, width), WIDE),
        ],
        compiler_params=pltpu.CompilerParams(vmem_limit_bytes=LIMIT),
    )(lengths, seg_own, seg_other, seg_own, seg_other, q_own, q_other, g_own, g_other, st_own, st_other, kv)


def merge_all(parts):
    top = parts[0][0:1]
    for part in parts[1:]:
        top = jnp.maximum(top, part[0:1])
    total = sum(jnp.exp(part[0:1] - top) for part in parts)
    rest = sum(part for part in parts)
    return jnp.where(rows_of(rest.shape) == 0, top + jnp.log(total), rest)


def middle_kernel(depth, split, *refs):
    (
        seg, pad, labels, counts, positions, targets, w_vocab, after_self, o_own, o_other, lse_own, lse_other,
        gs,
    ) = refs[:13]
    parts = refs[13 : 13 + (4 if split else 1)]
    refs = refs[13 + len(parts) :]
    sums = refs[:len(parts)]
    refs = refs[len(parts) :]
    (
        block_out, state_out, g_own, g_other, st_own, st_other, small_rows, small_cols, grad_vocab, token_out, loss_out,
    ) = refs[:11]
    (
        wm, eb, eb_got, w_s, got_o, got_lse, cross_o, cross_low, ac, bs, n3, act, slope, gpre, head,
        lt, gt, pb, rb, got_rc, got_rq, got_rz, st_c, st_q, st_z, gh, load_sem, send, recv,
    ) = refs[11:]
    tok_count, width = after_self.shape
    hidden = act.shape[1]
    masked = positions.shape[1]
    vocab_local = w_vocab.shape[0]
    everyone = depth * 8
    me = Place(depth)
    z, x, c, y = me.z, me.x, me.c, me.y
    greet(me.others() + [me.across_x(), me.across_y(), me.across_both(), me.across_core()])
    used = [0]

    def push(src, dst, peer):
        k = used[0]
        used[0] += 1
        copy = remote(src, dst, send.at[k], recv.at[k], peer)
        copy.start()
        return copy

    pending = []

    def arrive(copies):
        for copy in copies:
            copy.wait_recv()
        pending.extend(copies)

    swap = [push(o_other, got_o, me.across_y()), push(lse_other, got_lse, me.across_y())]
    loads = []

    def load(src, dst):
        copy = pltpu.make_async_copy(src, dst, load_sem.at[len(loads)])
        copy.start()
        loads.append(copy)

    load(gs, w_s)
    shared = []
    if split:
        spots = ((x, y), (1 - x, y), (x, 1 - y), (1 - x, 1 - y))
        for part, (px, py) in zip(parts, spots):
            load(part, wm.at[:, px, c, py])
            shared.append(push(part, wm.at[:, px, c, py], me.across_core()))
    else:
        load(parts[0], wm)

    def cut(lo, hi):
        value = wm[:, :, :, :, lo:hi] if split else wm[:, lo:hi]
        return value.reshape((-1, BLOCK))

    def put(lo, value, first=0, last=None, cols=slice(0, BLOCK)):
        groups, rows, wide = value.shape
        last = depth if last is None else last
        if split:
            eb[first:last, :, :, :, lo : lo + rows, cols] = value.reshape((last - first, 2, 2, 2, rows, wide))
        else:
            step = eb.shape[0] // depth
            eb[first * step : last * step, lo : lo + rows, cols] = value

    segments = seg[...].astype(WIDE)
    keep = 1.0 - pad[...].astype(WIDE)
    lane_row = lanes((1, tok_count))
    inside = lane_row < tok_count - 1

    def following(row):
        return pltpu.roll(jnp.concatenate([row, jnp.zeros((7, tok_count), WIDE)], axis=0), tok_count - 1, 1)[0:1]

    follows = inside & (following(segments) == segments) & (keep > 0.5) & (following(keep) > 0.5)
    valid = jnp.where(follows, 1.0, 0.0)
    rows = [keep, valid, labels[...].astype(WIDE), counts[...].astype(WIDE)]
    columns = transposed_rows(jnp.concatenate(rows + [jnp.zeros((4, tok_count), WIDE)], axis=0))
    col_keep, col_valid = columns[:, 0:1], columns[:, 1:2]
    col_label, col_count = columns[:, 2:3], columns[:, 3:4].astype(jnp.int32)

    for copy in loads:
        copy.wait()
    arrive(shared)
    table = w_s[...].reshape((-1, 128)).astype(WIDE).T

    arrive(swap)
    top = jnp.maximum(lse_own[...], got_lse[...])
    lse = top + jnp.log(jnp.exp(lse_own[...] - top) + jnp.exp(got_lse[...] - top))
    shares = jnp.concatenate([jnp.exp(lse_own[...] - lse), jnp.exp(got_lse[...] - lse)], axis=0)
    shares = transposed_rows(shares)
    low_half = lanes((tok_count, 128)) < HD
    for p in range(width // 128):
        at = slice(p * 128, (p + 1) * 128)
        share_own = jnp.where(low_half, shares[:, 2 * p : 2 * p + 1], shares[:, 2 * p + 1 : 2 * p + 2])
        share_got = jnp.where(low_half, shares[:, 8 + 2 * p : 9 + 2 * p], shares[:, 9 + 2 * p : 10 + 2 * p])
        mixed = o_own[:, at].astype(WIDE) * share_own + got_o[:, at].astype(WIDE) * share_got
        cross_o[:, at] = mixed
        cross_low[:, at] = mixed.astype(LOW)
    weight_co = cut(0, 16)
    after_cross = after_self[...] + dot(cross_low[...], weight_co)
    ac[...] = after_cross
    n3[...] = (normalised(after_cross)[0] * table[2:3] + table[6:7]).astype(LOW)
    bs[...] = after_cross
    blocks = hidden // BLOCK
    flat_fo = cut(80, 144)
    for j in range(blocks):
        at = slice(j * BLOCK, (j + 1) * BLOCK)
        pre = dot(n3[...], cut(16 + 16 * j, 32 + 16 * j))
        square = pre * pre
        bent = jnp.tanh(GELU * pre * (1.0 + CUBIC * square))
        half = 0.5 * (1.0 + bent)
        act[:, at] = (pre * half).astype(LOW)
        slope[:, at] = half + 0.5 * pre * (1.0 - bent * bent) * (GELU * (1.0 + 3.0 * CUBIC * square))
        bs[...] = bs[...] + dot(act[:, at], flat_fo[at])
    state = bs[...]
    block_out[...] = state.astype(LOW)
    head_in = (normalised(state)[0] * table[3:4] + table[7:8]).astype(LOW)
    head[...] = head_in

    picker = (positions[...] == rows_of((tok_count, masked))).astype(LOW)
    picked = dot_tn(picker, head_in).astype(LOW)
    kept = dot(jnp.concatenate([keep, jnp.zeros((7, tok_count), WIDE)], axis=0).astype(LOW), picker)
    code = jnp.where(kept[0:1] > 0.5, targets[...] + 1, 0)
    digits = jnp.concatenate([code >> 8, code & 255, jnp.zeros((6, masked), jnp.int32)], axis=0)
    digits = dot_tn(digits.astype(WIDE).astype(LOW), (rows_of((8, 128)) == lanes((8, 128))).astype(LOW)).astype(LOW)
    pb[z, x, c, y, :, 0:width] = picked
    pb[z, x, c, y, :, width : width + 128] = digits
    mine = pb.at[z, x, c, y]
    flight = [push(mine, mine, peer) for peer in me.others()]

    classes = BLOCK // 2
    flat_in = cut(144, 160).reshape((-1, 16, BLOCK))
    flat_in = jnp.concatenate([flat_in[:, :, :classes], flat_in[:, :, classes:]], axis=1).reshape((-1, classes))
    w_one, w_two = flat_in[:width], flat_in[width:]
    token_row = rows_of((tok_count, classes))
    ahead = pltpu.roll(dot(head_in, w_two), tok_count - 1, 0)
    logits = dot(head_in, w_one) + jnp.where(token_row == tok_count - 1, 0.0, ahead)
    top = jnp.max(logits, axis=1, keepdims=True)
    exps = jnp.exp(logits - top)
    total = jnp.sum(exps, axis=1, keepdims=True)
    hits = lanes((tok_count, classes)) == col_count
    entropy = top + jnp.log(total) - jnp.sum(jnp.where(hits, logits, 0.0), axis=1, keepdims=True)
    loss_col = col_valid * entropy
    grads = col_valid * (exps * (1.0 / total) - jnp.where(hits, 1.0, 0.0))
    g_insert = grads.astype(LOW)
    before = pltpu.roll(g_insert.astype(WIDE), 1, 0)
    g_before = jnp.where(token_row == 0, 0.0, before).astype(LOW)

    arrive(flight)
    column = pb.at[:, x, c, y]
    flight = [push(column, column, peer) for peer in (me.across_x(), me.across_y(), me.across_both())]

    flat_s = w_s[...].reshape((-1, 128))
    two = dot(head_in, flat_s)
    l_zero, l_one = two[:, 16:17], two[:, 17:18]
    top = jnp.maximum(l_zero, l_one)
    e_zero, e_one = jnp.exp(l_zero - top), jnp.exp(l_one - top)
    total = e_zero + e_one
    is_one = col_label > 0.5
    loss_col = loss_col + col_keep * (top + jnp.log(total) - jnp.where(is_one, l_one, l_zero))
    d_zero = col_keep * (e_zero / total - jnp.where(is_one, 0.0, 1.0))
    d_one = col_keep * (e_one / total - jnp.where(is_one, 1.0, 0.0))
    lane = lanes((tok_count, 128))
    g_delete = jnp.where(lane == 16, d_zero, jnp.where(lane == 17, d_one, 0.0)).astype(LOW)
    gh[...] = dot_nt(g_delete, flat_s) + dot_nt(g_insert, w_one) + dot_nt(g_before, w_two)
    arrive(flight)
    plane = pb.at[:, :, c, :]
    flight = [push(plane, plane, me.across_core())]
    small_cols[...] = dot_tn(head_in, g_delete)
    for k, grad in enumerate((g_insert, g_before)):
        pairs = dot_tn(head_in, grad).astype(LOW).reshape((-1, 2, 16, classes))
        for side in range(2):
            cols = slice(side * classes, (side + 1) * classes)
            put(144, pairs[:, side], k * (depth // 2), (k + 1) * (depth // 2), cols)
    arrive(flight)

    gathered = pb[...].reshape((-1, width + 128))
    rows_all = gathered[:, 0:width]
    numbers = gathered[:, width : width + 128].astype(WIDE).T
    code = numbers[0:1] * 256.0 + numbers[1:2]
    weight = jnp.where(code > 0.5, 1.0, 0.0)
    count = rows_all.shape[0]
    pos = lax.axis_index(BOTH)
    place = rows_of((vocab_local, count)) + pos * vocab_local
    hits = place == (code.astype(jnp.int32) - 1)
    lt[...] = dot_nt(w_vocab[...], rows_all)
    logits = lt[...]
    top = jnp.max(logits, axis=0, keepdims=True)
    total = jnp.sum(jnp.exp(logits - top), axis=0, keepdims=True)
    chosen = jnp.sum(jnp.where(hits, logits, 0.0), axis=0, keepdims=True)
    loss_here = jnp.sum(loss_col, axis=0, keepdims=True)
    stat = jnp.concatenate(
        [top + jnp.log(total), chosen, jnp.broadcast_to(loss_here, (1, count)), jnp.zeros((5, count), WIDE)], axis=0
    )
    st_c[0] = stat
    flight = [push(st_c.at[0], st_c.at[1], me.across_core())]
    arrive(flight)
    st_q[x, y] = merge_all([st_c[0], st_c[1]])
    spot = st_q.at[x, y]
    flight = [push(spot, spot, peer) for peer in (me.across_x(), me.across_y(), me.across_both())]
    arrive(flight)
    st_z[z] = merge_all([st_q[0, 0], st_q[0, 1], st_q[1, 0], st_q[1, 1]])
    flight = [push(st_z.at[z], st_z.at[z], peer) for peer in me.others()]
    arrive(flight)
    stat = merge_all([st_z[k] for k in range(depth)])
    tokens = weight * (stat[0:1] - stat[1:2])
    mine = rows_of((masked, count)) + pos * masked == lanes((masked, count))
    own = jnp.sum(jnp.where(mine, tokens, 0.0), axis=1, keepdims=True)
    token_out[...] = jnp.sum(
        jnp.where(rows_of((masked, masked)) == lanes((masked, masked)), own, 0.0), axis=0, keepdims=True
    )
    loss = (stat[2:3, 0:128] + jnp.sum(tokens, axis=1, keepdims=True)) * (1.0 / (tok_count * everyone))
    loss_out[...] = loss[:, 0:1]
    gt[...] = (weight * (jnp.exp(lt[...] - stat[0:1]) - jnp.where(hits, 1.0, 0.0))).astype(LOW)

    rb[...] = dot_tn(gt[...], w_vocab[...]).astype(LOW).reshape(rb.shape)
    flight = [push(rb.at[:, :, 1 - c], got_rc, me.across_core())]
    scale = (tok_count * everyone) ** (-0.5)
    grad_vocab[...] = dot(gt[...], rows_all) * scale
    arrive(flight)
    got_rc[...] = (rb[:, :, c].astype(WIDE) + got_rc[...].astype(WIDE)).astype(LOW)
    flight = [
        push(got_rc.at[:, 1 - x, y], got_rq.at[0], me.across_x()),
        push(got_rc.at[:, x, 1 - y], got_rq.at[1], me.across_y()),
        push(got_rc.at[:, 1 - x, 1 - y], got_rq.at[2], me.across_both()),
    ]
    arrive(flight)
    line = got_rc[:, x, y].astype(WIDE)
    for k in range(3):
        line = line + got_rq[k].astype(WIDE)
    got_rq[3] = line.astype(LOW)
    flight = [
        push(got_rq.at[3, lax.rem(z + k, depth)], got_rz.at[k - 1], me.along(k)) for k in range(1, depth)
    ]
    arrive(flight)
    grad_picked = got_rq[3, z].astype(WIDE)
    for k in range(1, depth):
        grad_picked = grad_picked + got_rz[k - 1].astype(WIDE)
    coarse = grad_picked.astype(LOW)
    fine = (grad_picked - coarse.astype(WIDE)).astype(LOW)
    grad_head = gh[...] + dot(picker, coarse) + dot(picker, fine)

    grad_block, gain_3, bias_3 = norm_back(bs[...], table[3:4], grad_head)
    bs[...] = grad_block
    g_ffn = grad_block.astype(LOW)
    gh[...] = jnp.zeros_like(gh)
    for j in range(blocks):
        at = slice(j * BLOCK, (j + 1) * BLOCK)
        gpre[:, at] = (dot_nt(g_ffn, flat_fo[at]) * slope[:, at]).astype(LOW)
        gh[...] = gh[...] + dot_nt(gpre[:, at], cut(16 + 16 * j, 32 + 16 * j))
    back, gain_2, bias_2 = norm_back(ac[...], table[2:3], gh[...])
    grad_state = grad_block + back
    state_out[...] = grad_state
    g_cross = grad_state.astype(LOW)
    g_attn = dot_nt(g_cross, weight_co).astype(LOW)
    g_own[...] = g_attn
    deltas = jnp.zeros((tok_count, 128), WIDE)
    for p in range(width // 128):
        at = slice(p * 128, (p + 1) * 128)
        product = g_attn[:, at].astype(WIDE) * cross_o[:, at]
        first = jnp.sum(jnp.where(low_half, product, 0.0), axis=1, keepdims=True)
        second = jnp.sum(jnp.where(low_half, 0.0, product), axis=1, keepdims=True)
        deltas = jnp.where(lane == 2 * p, first, jnp.where(lane == 2 * p + 1, second, deltas))
    st_own[...] = jnp.concatenate([lse, deltas.T[0:8]], axis=0)
    swap = [push(g_own, g_other, me.across_y()), push(st_own, st_other, me.across_y())]

    for j in range(blocks):
        at = slice(j * BLOCK, (j + 1) * BLOCK)
        grad = dot_tn(act[:, at], g_ffn).astype(LOW)
        put(80, grad.reshape((-1, 64, BLOCK)), j * depth // blocks, (j + 1) * depth // blocks)
        grad = dot_tn(n3[...], gpre[:, at]).astype(LOW)
        put(16 + 16 * j, grad.reshape((-1, 16, BLOCK)))
    put(0, dot_tn(cross_low[...], g_cross).astype(LOW).reshape((-1, 16, BLOCK)))
    if split:
        halves = [push(eb.at[:, :, 1 - c], eb_got, me.across_core())]
    small_rows[...] = jnp.concatenate([gain_2, gain_3, bias_2, bias_3, jnp.zeros((4, width), WIDE)], axis=0)
    if split:
        arrive(halves)
        for out, (px, py) in zip(sums, spots):

            @pl.loop(0, depth)
            def _(zz):
                total = eb[zz, px, c, py].astype(WIDE) + eb_got[zz, px, py].astype(WIDE)
                out[zz] = total.astype(LOW)

    else:
        sums[0][...] = eb[...]
    arrive(swap)
    for copy in pending:
        copy.wait_send()


def middle_part(depth, split, seg, pad, labels, counts, positions, targets, w_vocab, after_self, attended, gs, parts):
    tok_count, width = after_self.shape
    hidden = 4 * BLOCK
    vocab_local = w_vocab.shape[0]
    everyone = depth * 8
    masked = positions.shape[1]
    count = masked * everyone
    sharded = (depth, 2, 2, 2)
    lead = sharded if split else (BLOCK // 16,)
    own = lead[:1] if split else lead
    sharded = (depth, 2, 2, 2)
    outs = [(shape_of(own + (160, BLOCK), LOW), VMEM)] * len(parts)
    outs += [
        (shape_of((tok_count, width), LOW), VMEM),
        (shape_of((tok_count, width), WIDE), VMEM),
        (shape_of((tok_count, width), LOW), VMEM),
        (shape_of((tok_count, width), LOW), ANY),
        (shape_of((16, tok_count), WIDE), VMEM),
        (shape_of((16, tok_count), WIDE), ANY),
        (shape_of((8, width), WIDE), VMEM),
        (shape_of((width, 128), WIDE), VMEM),
        (shape_of((vocab_local, width), WIDE), VMEM),
        (shape_of((1, masked), WIDE), VMEM),
        (shape_of((1, 1), WIDE), VMEM),
    ]
    copies = 9 + 2 * (depth - 1) + 3 + 1 + 1 + 3 + 1 + 3 + (depth - 1)
    return pl.pallas_call(
        partial(middle_kernel, depth, split),
        name="middle_part",
        out_shape=[o for o, _ in outs],
        in_specs=[VMEM] * 12 + [ANY] * (1 + len(parts)),
        out_specs=[s for _, s in outs],
        scratch_shapes=[
            pltpu.VMEM(lead + (160, BLOCK), LOW),
            pltpu.VMEM(lead + (160, BLOCK), LOW),
            pltpu.VMEM(((depth, 2, 2) if split else (1,)) + (160, BLOCK), LOW),
            pltpu.VMEM(gs.shape, LOW),
            pltpu.VMEM((tok_count, width), LOW),
            pltpu.VMEM((8, tok_count), WIDE),
            pltpu.VMEM((tok_count, width), WIDE),
            pltpu.VMEM((tok_count, width), LOW),
            pltpu.VMEM((tok_count, width), WIDE),
            pltpu.VMEM((tok_count, width), WIDE),
            pltpu.VMEM((tok_count, width), LOW),
            pltpu.VMEM((tok_count, hidden), LOW),
            pltpu.VMEM((tok_count, hidden), WIDE),
            pltpu.VMEM((tok_count, hidden), LOW),
            pltpu.VMEM((tok_count, width), LOW),
            pltpu.VMEM((vocab_local, count), WIDE),
            pltpu.VMEM((vocab_local, count), LOW),
            pltpu.VMEM(sharded + (masked, width + 128), LOW),
            pltpu.VMEM(sharded + (masked, width), LOW),
            pltpu.VMEM((depth, 2, 2, masked, width), LOW),
            pltpu.VMEM((4, depth, masked, width), LOW),
            pltpu.VMEM((max(depth - 1, 1), masked, width), LOW),
            pltpu.VMEM((2, 8, count), WIDE),
            pltpu.VMEM((2, 2, 8, count), WIDE),
            pltpu.VMEM((depth, 8, count), WIDE),
            pltpu.VMEM((tok_count, width), WIDE),
            pltpu.SemaphoreType.DMA((9,)),
            pltpu.SemaphoreType.DMA((copies + depth,)),
            pltpu.SemaphoreType.DMA((copies + depth,)),
        ],
        compiler_params=pltpu.CompilerParams(
            collective_id=1, has_side_effects=True, vmem_limit_bytes=LIMIT
        ),
    )(seg, pad, labels, counts, positions, targets, w_vocab, after_self, *attended, gs, *parts)


def self_backward_start(dk, dv):
    dk[...] = jnp.zeros_like(dk)
    dv[...] = jnp.zeros_like(dv)


def self_backward(blocks, qkv, out, lse_ref, g_ref, dqkv, dk, dv, row_seg, row_keep, col_seg):
    tok_count, width = out.shape
    first, last = blocks
    pairs = width // 128

    def one(t, carry):
        block, pair = first + t // pairs, lax.rem(t, pairs)
        base = pl.multiple_of(pair * 128, 128)
        cols = pl.ds(base, 128)
        at = pl.ds(pl.multiple_of(block * 128, 128), 128)
        low = self_window(block, tok_count)
        keys = pl.ds(low, 384)
        q = both_heads(qkv[at, cols] * SCALE)
        k = qkv[keys, pl.ds(pl.multiple_of(base + width, 128), 128)]
        v = qkv[keys, pl.ds(pl.multiple_of(base + 2 * width, 128), 128)]
        g = both_heads(g_ref[at, cols])
        delta = jnp.sum(g.astype(WIDE) * twice(out[at, cols].astype(WIDE)), axis=1, keepdims=True)
        lane = lanes((128, 128))
        stats = lse_ref[at, :]
        lse_low = jnp.sum(jnp.where(lane == 2 * pair, stats, 0.0), axis=1, keepdims=True)
        lse_high = jnp.sum(jnp.where(lane == 2 * pair + 1, stats, 0.0), axis=1, keepdims=True)
        lse = jnp.concatenate([lse_low, lse_high], axis=0)
        allowed = self_mask(row_seg, row_keep, col_seg, block, low)
        scores = dot_nt(q, k)
        probs = jnp.exp(jnp.where(twice(allowed), scores - lse, FILL))
        gscores = (probs * (dot_nt(g, v) - delta)).astype(LOW)
        dqkv[at, cols] = (join_heads(dot(gscores, k)) * SCALE).astype(LOW)
        dk[keys, cols] = dk[keys, cols] + dot_tn(gscores, q)
        dv[keys, cols] = dv[keys, cols] + dot_tn(probs.astype(LOW), g)
        return carry

    lax.fori_loop(0, (last - first) * pairs, one, 0)


def self_backward_end(dqkv, dk, dv):
    width = dk.shape[1]
    dqkv[:, width : 2 * width] = dk[...].astype(LOW)
    dqkv[:, 2 * width : 3 * width] = dv[...].astype(LOW)


def reduce_steps(me, chunks, send, recv):
    z, x, c, y = me.z, me.x, me.c, me.y
    depth = me.depth
    count = len(chunks)
    started = [[None] * 3 for _ in chunks]
    used = [0] * count

    def launch(k, stage):
        copies = []

        def push(src, dst, peer):
            slot = used[k]
            used[k] += 1
            copy = remote(src, dst, send.at[k, slot], recv.at[k, slot], peer)
            copy.start()
            copies.append(copy)

        for src, got_c, got_q, got_z, at, put in chunks[k]:
            if stage == 0:
                push(src.at[:, :, 1 - c, :, at], got_c.at[:, :, :, at], me.across_core())
            elif stage == 1:
                push(got_c.at[:, 1 - x, y, at], got_q.at[0, :, at], me.across_x())
                push(got_c.at[:, x, 1 - y, at], got_q.at[1, :, at], me.across_y())
                push(got_c.at[:, 1 - x, 1 - y, at], got_q.at[2, :, at], me.across_both())
            else:
                for j in range(1, depth):
                    push(got_c.at[lax.rem(z + j, depth), x, y, at], got_z.at[j - 1, at], me.along(j))
        started[k][stage] = copies

    def absorb(k, stage):
        for copy in started[k][stage]:
            copy.wait_recv()
        for src, got_c, got_q, got_z, at, put in chunks[k]:
            if stage == 0:

                @pl.loop(0, depth)
                def _(zz):
                    for xx in range(2):
                        for yy in range(2):
                            total = src[zz, xx, c, yy, at].astype(WIDE) + got_c[zz, xx, yy, at].astype(WIDE)
                            got_c[zz, xx, yy, at] = total.astype(LOW)

            elif stage == 1:

                @pl.loop(0, depth)
                def _(zz):
                    total = got_c[zz, x, y, at].astype(WIDE)
                    for k in range(3):
                        total = total + got_q[k, zz, at].astype(WIDE)
                    got_c[zz, x, y, at] = total.astype(LOW)

            else:
                total = got_c[z, x, y, at].astype(WIDE)
                for j in range(1, depth):
                    total = total + got_z[j - 1, at].astype(WIDE)
                put(total)

    for step in range(count + 3):
        for stage in range(3, -1, -1):
            k = step - stage
            if not 0 <= k < count:
                continue
            if stage > 0:
                absorb(k, stage - 1)
            if stage < 3:
                launch(k, stage)
        yield step
    for stages in started:
        for copies in stages:
            for copy in copies:
                copy.wait_send()


def last_kernel(depth, reduces, *refs):
    (pair, seg, pad, dkv, enc, dq_own, dq_other) = refs[:7]
    held = refs[7:15]
    (small_rows, small_cols, ga_in, gs_in) = refs[15:19]
    refs = refs[19:]
    if reduces:
        parts, refs = refs[:4], refs[4:]
    grad_input, grad_enc = refs[:2]
    refs = refs[2:]
    outs = refs[:9] if reduces else refs[:2]
    refs = refs[9:] if reduces else refs[2:]
    (start, one, qkv, low, lse, after, two, gstate) = refs[:8]
    (ga, gs, got_dq, g_attn, dqkv, dk, dv, row_seg, row_keep, col_seg, load_sem, sw_send, sw_recv) = refs[8:21]
    refs = refs[21:]
    tok_count, width = dq_own.shape
    src_count = enc.shape[0]
    everyone = depth * 8
    me = Place(depth)
    scale = (tok_count * everyone) ** (-0.5)
    loads = []
    for src, dst in [(gs_in, gs), (ga_in, ga)] + list(zip(held, (start, one, qkv, low, lse, after, two, gstate))):
        copy = pltpu.make_async_copy(src, dst, load_sem.at[len(loads)])
        copy.start()
        loads.append(copy)
    if reduces:
        greet(me.others() + [me.across_x(), me.across_y(), me.across_both(), me.across_core()])
    else:
        greet([me.across_y()])
    halves = 2
    span = tok_count // halves
    swaps = []
    for k in range(halves):
        at = pl.ds(k * span, span)
        swaps.append(remote(dq_other.at[at], got_dq.at[at], sw_send.at[k], sw_recv.at[k], me.across_y()))
        swaps[-1].start()

    if reduces:
        (late, late_s, ez, ez_got, c_a, c_s, q_a, q_s, z_a, z_s, ez_send, ez_recv, send, recv) = refs
        (o_qkv, o_so, o_cq, o_kv, o_co, o_fi, o_fo, o_in, o_s) = outs

        def put_kv(total):
            o_kv[:, 0:BLOCK] = total[0:16] * scale
            o_kv[:, BLOCK : 2 * BLOCK] = total[16:32] * scale

        def put_mid(total):
            o_so[...] = total[0:16] * scale
            o_cq[...] = total[16:32] * scale

        def put_qkv(total):
            for k in range(3):
                o_qkv[:, k * BLOCK : (k + 1) * BLOCK] = total[16 * k : 16 * (k + 1)] * scale

        def put_s(total):
            o_s[...] = total * scale

        def rows(lo, hi, put):
            return (late, c_a, q_a, z_a, pl.ds(lo, hi - lo), put)

        chunks = [
            [rows(KV, EARLY, put_kv)],
            [],
            [rows(SO, KV, put_mid)],
            [rows(QKV, SO, put_qkv), (late_s, c_s, q_s, z_s, pl.ds(0, 16), put_s)],
        ]

        @pl.loop(0, depth)
        def _(zz):
            total = parts[0][zz].astype(WIDE)
            for part in parts[1:]:
                total = total + part[zz].astype(WIDE)
            ez[zz] = total.astype(LOW)

        along = []
        for k in range(1, depth):
            to = lax.rem(me.z + k, depth)
            along.append(remote(ez.at[to], ez_got.at[k - 1], ez_send.at[k - 1], ez_recv.at[k - 1], me.along(k)))
            along[-1].start()

        def settle():
            for copy in along:
                copy.wait()
            total = ez[me.z].astype(WIDE)
            for k in range(depth - 1):
                total = total + ez_got[k].astype(WIDE)
            total = total * scale
            o_co[...] = total[0:16]
            for k in range(4):
                o_fi[:, k * BLOCK : (k + 1) * BLOCK] = total[16 + 16 * k : 32 + 16 * k]
            o_fo[...] = total[80:144]
            half = BLOCK // 2
            for k in range(2):
                o_in[16 * k : 16 * (k + 1)] = total[144:160, half * k : half * (k + 1)]

        steps = reduce_steps(me, chunks, send, recv)

        def keep(lo, value):
            late[:, :, :, :, lo : lo + 16] = value.astype(LOW).reshape(late.shape[:4] + (16, BLOCK))

        def keep_small(value):
            late_s[...] = value.astype(LOW).reshape(late_s.shape)
    else:
        steps = iter(())
        o_late, o_small = outs

        def keep(lo, value):
            o_late[:, lo : lo + 16] = value.astype(LOW).reshape((-1, 16, BLOCK))

        def keep_small(value):
            o_small[...] = value

    def advance():
        return next(steps, None)

    onehot = token_numbers(seg, pad, pair, row_seg, row_keep, col_seg)
    cut = cutter(ga)
    keep(KV, dot_tn(enc[...], dkv[:, 0:width]))
    keep(KV + 16, dot_tn(enc[...], dkv[:, width : 2 * width]))
    advance()
    for copy in loads:
        copy.wait()
    table = cutter(gs)(0, gs.shape[-2]).astype(WIDE).T
    gains = biases = 0.0
    blocks = span // 128
    self_backward_start(dk, dv)
    for k in range(halves):
        at = pl.ds(k * span, span)
        swaps[k].wait()
        g_query = (dq_own[at, :] + got_dq[at, :].astype(WIDE)).astype(LOW)
        got_dq[at, :] = g_query
        back, gain_1, bias_1 = norm_back(after[at, :], table[1:2], dot_nt(g_query, cut(CQ, KV)))
        gains, biases = gains + gain_1, biases + bias_1
        state = gstate[at, :] + back
        gstate[at, :] = state
        g_attn[at, :] = dot_nt(state.astype(LOW), cut(SO, CQ)).astype(LOW)
        if k == halves - 1:
            advance()
        self_backward((k * blocks, (k + 1) * blocks), qkv, low, lse, g_attn, dqkv, dk, dv, row_seg, row_keep, col_seg)
    self_backward_end(dqkv, dk, dv)
    keep(CQ, dot_tn(two[...], got_dq[...]))
    keep(SO, dot_tn(low[...], gstate[...].astype(LOW)))
    advance()
    for k in range(3):
        keep(QKV + 16 * k, dot_tn(one[...], dqkv[:, k * width : (k + 1) * width]))
    upstream = dot_nt(dqkv[:, 0:width], cut(QKV, QKV + 16))
    upstream = upstream + dot_nt(dqkv[:, width : 2 * width], cut(QKV + 16, QKV + 32))
    upstream = upstream + dot_nt(dqkv[:, 2 * width : 3 * width], cut(QKV + 32, SO))
    back, gain_0, bias_0 = norm_back(start[...], table[0:1], upstream)
    grad_start = gstate[...] + back
    grad_input[...] = grad_start.astype(LOW)
    coarse = grad_start.astype(LOW)
    fine = (grad_start - coarse.astype(WIDE)).astype(LOW)
    g_table = (dot_tn(onehot, coarse) + dot_tn(onehot, fine))[8:16]
    mid = small_rows[...]
    stacked = jnp.concatenate([gain_0, gains, mid[0:2], bias_0, biases, mid[2:4], g_table], axis=0)
    keep_small(transposed_rows(stacked) + small_cols[...])
    advance()
    w_key, w_val = cut(KV, KV + 16), cut(KV + 16, EARLY)
    span = src_count // 4
    for k in range(4):
        at = pl.ds(k * span, span)
        grads = dot_nt(dkv[at, 0:width], w_key) + dot_nt(dkv[at, width : 2 * width], w_val)
        grad_enc[at, :] = grads.astype(LOW)
        if k == 0:
            advance()
    advance()
    if reduces:
        settle()
    for _ in steps:
        pass


def last_part(depth, reduces, pair, seg, pad, dq_own, dq_other, dkv, enc, kept, gstate, grads, whole):
    tok_count, width = dq_own.shape
    src_count = enc.shape[0]
    ga, gs = whole
    parts, small_rows, small_cols = grads
    everyone = depth * 8
    rows = BLOCK // everyone
    sharded = (depth, 2, 2, 2)
    held = (*kept, gstate)
    outs = [shape_of((tok_count, width), LOW), shape_of((src_count, width), LOW)]
    scratch = [pltpu.VMEM(a.shape, a.dtype) for a in held]
    scratch += [
        pltpu.VMEM(ga.shape, LOW),
        pltpu.VMEM(gs.shape, LOW),
        pltpu.VMEM((tok_count, width), LOW),
        pltpu.VMEM((tok_count, width), LOW),
        pltpu.VMEM((tok_count, 3 * width), LOW),
        pltpu.VMEM((tok_count, width), WIDE),
        pltpu.VMEM((tok_count, width), WIDE),
        pltpu.VMEM((1, tok_count), WIDE),
        pltpu.VMEM((1, tok_count), WIDE),
        pltpu.VMEM((tok_count, 128), WIDE),
        pltpu.SemaphoreType.DMA((10,)),
        pltpu.SemaphoreType.DMA((2,)),
        pltpu.SemaphoreType.DMA((2,)),
    ]
    if reduces:
        shapes = [(EARLY, BLOCK), (16, 128)]
        outs += [
            shape_of((rows, 3 * BLOCK), WIDE),
            shape_of((rows, BLOCK), WIDE),
            shape_of((rows, BLOCK), WIDE),
            shape_of((rows, 2 * BLOCK), WIDE),
            shape_of((rows, BLOCK), WIDE),
            shape_of((rows, 4 * BLOCK), WIDE),
            shape_of((4 * rows, BLOCK), WIDE),
            shape_of((2 * rows, BLOCK // 2), WIDE),
            shape_of((rows, 128), WIDE),
        ]
        scratch += [pltpu.VMEM(sharded + s, LOW) for s in shapes]
        scratch += [pltpu.VMEM((depth, 160, BLOCK), LOW), pltpu.VMEM((depth - 1, 160, BLOCK), LOW)]
        for lead in ((depth, 2, 2), (3, depth), (depth - 1,)):
            scratch += [pltpu.VMEM(lead + s, LOW) for s in shapes]
        scratch += [pltpu.SemaphoreType.DMA((depth,))] * 2
        slots = 2 * (depth + 3)
        scratch += [pltpu.SemaphoreType.DMA((4, slots)), pltpu.SemaphoreType.DMA((4, slots))]
    else:
        outs += [shape_of((BLOCK // 16, EARLY, BLOCK), LOW), shape_of((BLOCK, 128), WIDE)]
    return pl.pallas_call(
        partial(last_kernel, depth, reduces),
        name="last_part",
        out_shape=outs,
        in_specs=[SMEM] + [VMEM] * 5 + [ANY] * 9 + [VMEM] * 2 + [ANY] * 2 + [VMEM] * len(parts),
        out_specs=[VMEM] * len(outs),
        scratch_shapes=scratch,
        compiler_params=pltpu.CompilerParams(
            collective_id=2, has_side_effects=True, vmem_limit_bytes=LIMIT
        ),
    )(pair, seg, pad, dkv, enc, dq_own, dq_other, *held, small_rows, small_cols, ga, gs, *parts)


def finish_kernel(count, *refs):
    ins, small, loss = refs[:count], refs[count], refs[count + 1]
    refs = refs[count + 2 :]
    outs, (gain, bias, table, delete, loss_out) = refs[:count], refs[count : count + 5]
    held, sems = refs[count + 5 : 2 * count + 5], refs[2 * count + 5]
    first = [pltpu.make_async_copy(ins[k], held[k], sems.at[0, k]) for k in range(count)]
    copies = [pltpu.make_async_copy(held[k], outs[k], sems.at[1, k]) for k in range(count)]
    for copy in first:
        copy.start()
    values = small[...]
    shape = (values.shape[0], values.shape[0])
    turned = jnp.concatenate([values, jnp.zeros((128 - values.shape[0], 128), WIDE)], axis=0).T
    gain[...] = turned[0:4, 0 : shape[0]]
    bias[...] = turned[4:8, 0 : shape[0]]
    table[...] = turned[8:16, 0 : shape[0]]
    delete[...] = values[:, 16:18]
    loss_out[...] = loss[...]
    for before, copy in zip(first, copies):
        before.wait()
        copy.start()
    for copy in copies:
        copy.wait()


def finish(results, small, loss):
    count = len(results)
    rows = small.shape[0]
    outs = [shape_of(a.shape, a.dtype) for a in results]
    outs += [shape_of(s, WIDE) for s in ((4, rows), (4, rows), (PAIRS, rows), (rows, 2), (1, 1))]
    res = pl.pallas_call(
        partial(finish_kernel, count),
        name="finish",
        out_shape=outs,
        in_specs=[ANY] * count + [VMEM] * 2,
        out_specs=[ANY] * count + [VMEM] * 5,
        scratch_shapes=[pltpu.VMEM(a.shape, a.dtype) for a in results] + [pltpu.SemaphoreType.DMA((2, count))],
        compiler_params=pltpu.CompilerParams(vmem_limit_bytes=LIMIT),
    )(*results, small, loss)
    block_out, grad_input, grad_enc, qkv, so, cq, kv, co, fi, fo, insert, vocab, tokens = res[:count]
    gain, bias, table, delete, loss = res[count:]
    return (
        block_out, grad_input, grad_enc, gain, bias, table, qkv, so, cq, kv, co, fi, fo, delete, insert, vocab,
        loss[0, 0], tokens,
    )


def late_blocks(cross_out, ffn_in, ffn_out, insert):
    groups = cross_out.shape[0] // 16
    return jnp.concatenate(
        [
            cross_out.reshape(groups, 16, BLOCK),
            ffn_in.reshape(groups, 16, 4, BLOCK).swapaxes(1, 2).reshape(groups, 64, BLOCK),
            ffn_out.reshape(groups, 64, BLOCK),
            insert.reshape(groups, 2, 16, BLOCK // 2).swapaxes(1, 2).reshape(groups, 16, BLOCK),
        ],
        axis=1,
    )


def gather_by_ops(qkv, self_out, cross_q, cross_kv, small):
    wide = jnp.concatenate([qkv, self_out, cross_q, cross_kv], axis=1)
    ga = lax.all_gather(wide, BOTH, axis=0, tiled=True).reshape(-1, 16, 7, BLOCK).swapaxes(1, 2)
    gs = lax.all_gather(small, BOTH, axis=0, tiled=True)
    return ga.reshape(-1, EARLY, BLOCK), gs.reshape(-1, 16, 128)


def across(depth, arrays):
    res = []
    for array, (dx, dy) in zip(arrays, ((1, 0), (0, 1), (1, 1))):
        pairs = []
        for z in range(depth):
            for x in range(2):
                for c in range(2):
                    for y in range(2):
                        here = ((z * 2 + x) * 2 + c) * 2 + y
                        there = ((z * 2 + (x ^ dx)) * 2 + c) * 2 + (y ^ dy)
                        pairs.append((here, there))
        res.append(lax.ppermute(array, BOTH, pairs))
    return res


def reduce_by_ops(early, small, late, scale):
    groups = late.shape[0]
    gw_f = late[:, 80:144].reshape(groups * 64, BLOCK)
    gw_i = late[:, 144:160].reshape(groups, 16, 2, BLOCK // 2).swapaxes(1, 2).reshape(groups * 32, BLOCK // 2)
    late = late[:, 0:80].reshape(groups, 5, 16, BLOCK).swapaxes(0, 1).reshape(5, BLOCK, BLOCK)
    early = early.reshape(groups, 7, 16, BLOCK).swapaxes(0, 1).reshape(7, BLOCK, BLOCK)
    wide = jnp.concatenate([early, late]).swapaxes(0, 1).reshape(BLOCK, 12 * BLOCK)

    def sums(a):
        return lax.psum_scatter(a.astype(WIDE), BOTH, scatter_dimension=0, tiled=True) * scale

    own = sums(wide)
    edges = (0, 3, 4, 5, 7, 8, 12)
    pieces = [own[:, lo * BLOCK : hi * BLOCK] for lo, hi in zip(edges[:-1], edges[1:])]
    return pieces + [sums(gw_f), sums(gw_i), sums(small)]


def body(
    dec_input, enc_output, segment_ids, padding, pair_ids, src_lengths, delete_labels, insert_counts,
    masked_positions, masked_targets, norm_gain, norm_bias, pair_table, self_qkv, self_out, cross_q, cross_kv,
    cross_out, ffn_in, ffn_out, w_delete, w_insert, w_vocab,
):
    everyone = lax.axis_size(BOTH)
    depth = everyone // 8
    tok_count = dec_input.shape[0]
    aligned = self_qkv.shape[0] == 16
    late = (cross_out, ffn_in, ffn_out, w_insert)
    tiny = (norm_gain, norm_bias, pair_table, w_delete.T)
    raw = (self_qkv, self_out, cross_q, cross_kv)
    whole = None
    if not aligned:
        gathered = late_blocks(*[lax.all_gather(a, BOTH, axis=0, tiled=True) for a in late])
        small = jnp.concatenate([norm_gain, norm_bias, pair_table, w_delete.T], axis=0).T
        small = jnp.pad(small, ((0, 0), (0, 128 - small.shape[1])))
        whole = gather_by_ops(*raw, small)
    whole, line, firsts = first_part(
        depth, aligned, segment_ids, padding, pair_ids, dec_input, enc_output, tiny, raw, late, whole
    )
    start, one, qkv, low, lse, after, two, query, other_query, kv, other_seg = firsts
    parts = (line, *across(depth, (line,) * 3)) if aligned else (gathered,)
    attended = cross_forward(src_lengths, segment_ids, other_seg, query, other_query, kv)
    mids = middle_part(
        depth, aligned, segment_ids, padding, delete_labels, insert_counts, masked_positions, masked_targets,
        w_vocab, after, attended, whole[1], parts,
    )
    parts, mids = mids[: len(parts)], mids[len(parts) :]
    block_out, gstate, g_own, g_other, st_own, st_other, small_rows, small_cols, grad_vocab, tokens, loss = mids
    sums = (parts[0], *across(depth, parts[1:])) if aligned else ()
    dq_own, dq_other, dkv = cross_backward(
        src_lengths, segment_ids, other_seg, query, other_query, g_own, g_other, st_own, st_other, kv
    )
    res = last_part(
        depth, aligned, pair_ids, segment_ids, padding, dq_own, dq_other, dkv, enc_output,
        (start, one, qkv, low, lse, after, two), gstate, (sums, small_rows, small_cols), whole,
    )
    if aligned:
        sums = res[2:]
    else:
        scale = (tok_count * everyone) ** (-0.5)
        sums = reduce_by_ops(res[2], res[3], parts[0], scale)
    return finish((block_out, res[0], res[1], *sums[:8], grad_vocab, tokens), sums[8], loss)


def solution(mesh):
    shared = P(BOTH, None)
    across = P(None, BOTH)
    return jax.shard_map(
        body,
        mesh=mesh,
        in_specs=(shared,) * 5 + (P("batch", None),) + (shared,) * 4 + (across,) * 3 + (shared,) * 10,
        out_specs=(shared,) * 3 + (across,) * 3 + (shared,) * 10 + (P(), shared),
        check_vma=False,
    )
```

```python
from functools import partial

import jax
import jax.numpy as jnp
from jax import lax
from jax.experimental import pallas as pl
from jax.experimental.pallas import tpu as pltpu
from jax.sharding import PartitionSpec as P

HD = 64
PAIRS = 8
SEGS = 8
BLOCK = 512
EPSILON = 1e-05
SCALE = 0.125
FILL = -1e30
GELU = 0.7978845608
CUBIC = 0.044715

MESH = pl.DeviceIdType.MESH
ANY = pl.BlockSpec(memory_space=pl.ANY)
VMEM = pl.BlockSpec(memory_space=pltpu.VMEM)
SMEM = pl.BlockSpec(memory_space=pltpu.SMEM)
BOTH = ("batch", "src")
LOW = jnp.bfloat16
WIDE = jnp.float32
LIMIT = 60 << 20


def shape_of(shape, kind):
    return jax.ShapeDtypeStruct(shape, kind)


def dot(left, right):
    return jnp.dot(left, right, preferred_element_type=WIDE)


def dot_tn(left, right):
    return lax.dot_general(left, right, (((0,), (0,)), ((), ())), preferred_element_type=WIDE)


def dot_nt(left, right):
    return lax.dot_general(left, right, (((1,), (1,)), ((), ())), preferred_element_type=WIDE)


def normalised(v):
    centred = v - jnp.mean(v, axis=-1, keepdims=True)
    r = lax.rsqrt(jnp.mean(centred * centred, axis=-1, keepdims=True) + EPSILON)
    return centred * r, r


def norm_back(v, gain, upstream):
    hat, r = normalised(v)
    scaled = upstream * gain
    first = jnp.mean(scaled, axis=-1, keepdims=True)
    second = jnp.mean(scaled * hat, axis=-1, keepdims=True)
    grad_gain = jnp.sum(upstream * hat, axis=0, keepdims=True)
    grad_bias = jnp.sum(upstream, axis=0, keepdims=True)
    return r * (scaled - first - hat * second), grad_gain, grad_bias


def lanes(shape):
    return lax.broadcasted_iota(jnp.int32, shape, len(shape) - 1)


def rows_of(shape):
    return lax.broadcasted_iota(jnp.int32, shape, len(shape) - 2)


def both_heads(x):
    low = lanes(x.shape) < HD
    zero = jnp.zeros_like(x)
    return jnp.concatenate([jnp.where(low, x, zero), jnp.where(low, zero, x)], axis=0)


def join_heads(x):
    half = x.shape[0] // 2
    return jnp.where(lanes((half, x.shape[1])) < HD, x[:half], x[half:])


def twice(x):
    return jnp.concatenate([x, x], axis=0)


def transposed_rows(rows):
    count, width = rows.shape
    return jnp.concatenate([rows, jnp.zeros((128 - count, width), WIDE)], axis=0).T


def greet(peers):
    barrier = pltpu.get_barrier_semaphore()
    for peer in peers:
        pl.semaphore_signal(barrier, inc=1, device_id=peer, device_id_type=MESH)
    pl.semaphore_wait(barrier, len(peers))


def remote(src, dst, send, recv, peer):
    return pltpu.make_async_remote_copy(
        src_ref=src,
        dst_ref=dst,
        send_sem=send,
        recv_sem=recv,
        device_id=peer,
        device_id_type=MESH,
    )


class Place:
    def __init__(self, depth):
        b = lax.axis_index("batch")
        self.depth = depth
        self.y = lax.axis_index("src")
        self.c = lax.rem(b, 2)
        self.x = lax.rem(b // 2, 2)
        self.z = b // 4

    def at(self, z=None, x=None, c=None, y=None):
        z = self.z if z is None else z
        x = self.x if x is None else x
        c = self.c if c is None else c
        y = self.y if y is None else y
        return ((z * 2 + x) * 2 + c, y)

    def along(self, k):
        return self.at(z=lax.rem(self.z + k, self.depth))

    def others(self):
        return [self.along(k) for k in range(1, self.depth)]

    def across_x(self):
        return self.at(x=1 - self.x)

    def across_y(self):
        return self.at(y=1 - self.y)

    def across_both(self):
        return self.at(x=1 - self.x, y=1 - self.y)

    def across_core(self):
        return self.at(c=1 - self.c)


def gathering(me, chunks, send, recv):
    z, x, c, y = me.z, me.x, me.c, me.y
    started = [[None] * 3 for _ in chunks]
    used = [0] * len(chunks)
    every = slice(None)

    def launch(k, stage):
        copies = []

        def push(block, peer):
            slot = used[k]
            used[k] += 1
            copy = remote(block, block, send.at[k, slot], recv.at[k, slot], peer)
            copy.start()
            copies.append(copy)

        for view in chunks[k]:
            if stage == 0:
                for peer in me.others():
                    push(view(z, x, c, y), peer)
            elif stage == 1:
                for peer in (me.across_x(), me.across_y(), me.across_both()):
                    push(view(every, x, c, y), peer)
            else:
                push(view(every, every, c, every), me.across_core())
        started[k][stage] = copies

    def begin(k):
        launch(k, 0)

    def after(k, stage):
        for copy in started[k][stage]:
            copy.wait_recv()
        if stage < 2:
            launch(k, stage + 1)

    def end():
        for stages in started:
            for copies in stages:
                for copy in copies:
                    copy.wait_send()

    return begin, after, end


def self_window(block, tok_count):
    low = jnp.clip(block * 128 - 128, 0, tok_count - 384)
    return pl.multiple_of(low, 128)


def self_mask(row_seg, row_keep, col_seg, block, low):
    at = pl.ds(low, 384)
    keys = row_seg[0:1, at]
    keep = row_keep[0:1, at]
    queries = col_seg[pl.ds(pl.multiple_of(block * 128, 128), 128), 0:1]
    shape = (128, 384)
    own = (rows_of(shape) + block * 128) == (lanes(shape) + low)
    return (queries == keys) & ((keep > 0.5) | own)


def self_forward(blocks, qkv, out, lse_ref, row_seg, row_keep, col_seg):
    tok_count, width = out.shape
    first, last = blocks
    pairs = width // 128

    def one(block, carry):
        at = pl.ds(pl.multiple_of(block * 128, 128), 128)
        low = self_window(block, tok_count)
        keys = pl.ds(low, 384)
        allowed = twice(self_mask(row_seg, row_keep, col_seg, block, low))
        every = range(pairs)
        q = [both_heads(qkv[at, p * 128 : (p + 1) * 128] * SCALE) for p in every]
        scores = [dot_nt(q[p], qkv[keys, width + p * 128 : width + (p + 1) * 128]) for p in every]
        scores = [jnp.where(allowed, scores[p], FILL) for p in every]
        tops = [jnp.max(scores[p], axis=1, keepdims=True) for p in every]
        exps = [jnp.exp(scores[p] - tops[p]) for p in every]
        totals = [jnp.sum(exps[p], axis=1, keepdims=True) for p in every]
        probs = [(exps[p] * (1.0 / totals[p])).astype(LOW) for p in every]
        mixed = [dot(probs[p], qkv[keys, 2 * width + p * 128 : 2 * width + (p + 1) * 128]) for p in every]
        lane = lanes((128, 128))
        stats = jnp.zeros((128, 128), WIDE)
        for p in every:
            out[at, p * 128 : (p + 1) * 128] = join_heads(mixed[p]).astype(LOW)
            lse = tops[p] + jnp.log(totals[p])
            stats = jnp.where(lane == 2 * p, lse[:128], jnp.where(lane == 2 * p + 1, lse[128:], stats))
        lse_ref[at, :] = stats
        return carry

    lax.fori_loop(first, last, one, 0)


def small_matrix(gain, bias, pair_rows, delete):
    def spot(count, first):
        shape = (count, 128)
        return (rows_of(shape) + first == lanes(shape)).astype(LOW)

    total = dot_tn(gain, spot(4, 0)) + dot_tn(bias, spot(4, 4)) + dot_tn(pair_rows, spot(PAIRS, 8))
    return (total + dot_tn(delete, spot(2, 8 + PAIRS))).astype(LOW)


def token_numbers(seg, pad, pair, row_seg, row_keep, col_seg):
    tok_count = seg.shape[1]
    segments = seg[...].astype(WIDE)
    row_seg[...] = segments
    row_keep[...] = 1.0 - pad[...].astype(WIDE)
    pair_row = jnp.zeros((1, tok_count), WIDE)
    for k in range(SEGS):
        pair_row = jnp.where(segments == k, pair[0, k].astype(WIDE), pair_row)
    columns = transposed_rows(jnp.concatenate([segments, pair_row, jnp.zeros((6, tok_count), WIDE)], axis=0))
    col_seg[...] = columns
    return (lanes((tok_count, 128)) == (columns[:, 1:2].astype(jnp.int32) + 8)).astype(LOW)


def cutter(ref):
    every = (slice(None),) * (len(ref.shape) - 2)

    def cut(lo, hi):
        value = ref[every + (slice(lo, hi),)]
        return value.reshape((-1, value.shape[-1]))

    return cut


QKV, SO, CQ, KV, EARLY = 0, 48, 64, 80, 112
LATE, PERMUTED = 160, 96


def first_kernel(depth, gathers, *refs):
    (seg, pad, pair, dec, enc_in) = refs[:5]
    refs = refs[5:]
    if gathers:
        (gain, bias, pair_rows, delete, raw_qkv, raw_so, raw_cq, raw_kv, raw_co, raw_fi, raw_fo, raw_in) = refs[:12]
        (ga_out, gs_out, gz) = refs[12:15]
        refs = refs[15:]
    else:
        ga_in, gs_in = refs[:2]
        refs = refs[2:]
    results, other_out, seg_out = refs[:9], refs[9], refs[10]
    held = refs[11:20]
    (start_ref, one_ref, qkv, low, lse, after_ref, two_ref, query, kv) = held
    (enc, ga, gs, row_seg, row_keep, col_seg, own_sem, out_sem, send, recv, sw_send, sw_recv) = refs[20:]
    tok_count, width = dec.shape
    src_count = enc.shape[0]
    me = Place(depth)
    z, x, c, y = me.z, me.x, me.c, me.y
    owns = []

    def own(src, dst):
        copy = pltpu.make_async_copy(src, dst, own_sem.at[len(owns)])
        copy.start()
        owns.append(copy)

    if gathers:
        for raw, count, first in ((raw_qkv, 3, QKV), (raw_so, 1, SO), (raw_cq, 1, CQ), (raw_kv, 2, KV)):
            for k in range(count):
                own(raw.at[:, pl.ds(k * BLOCK, BLOCK)], ga.at[z, x, c, y, pl.ds(first + 16 * k, 16)])
        soon = len(owns)
        gz_own = gz.at[y, z]
        own(raw_co, gz_own.at[pl.ds(0, 16)])
        for k in range(4):
            own(raw_fi.at[:, pl.ds(k * BLOCK, BLOCK)], gz_own.at[pl.ds(16 + 16 * k, 16)])
        own(raw_fo, gz_own.at[pl.ds(80, 64)])
        for k in range(2):
            half = BLOCK // 2
            own(raw_in.at[pl.ds(16 * k, 16)], gz_own.at[pl.ds(144, 16), pl.ds(half * k, half)])
        gs[z, x, c, y] = small_matrix(gain[...], bias[...], pair_rows[...], delete[...])
        greet(me.others() + [me.across_x(), me.across_y(), me.across_both(), me.across_core()])
        for copy in owns[:soon]:
            copy.wait()

        def rows(lo, hi):
            return lambda *at: ga.at[at + (pl.ds(lo, hi - lo),)]

        chunks = [[lambda *at: gs.at[at], rows(QKV, SO)], [rows(SO, KV)], [rows(KV, EARLY)]]
        begin, after_stage, end = gathering(me, chunks, send, recv)
    else:
        own(ga_in, ga)
        own(gs_in, gs)
        greet([me.across_y()])
        for copy in owns:
            copy.wait()

        def begin(k):
            return None

        def after_stage(k, stage):
            return None

        def end():
            return None

    outs = []

    def out(k):
        copy = pltpu.make_async_copy(held[k], results[k], out_sem.at[len(outs)])
        copy.start()
        outs.append(copy)

    begin(0)
    if gathers:
        for copy in owns[soon:]:
            copy.wait()
        across = remote(gz_own, gz_own, sw_send.at[3], sw_recv.at[3], me.across_y())
        across.start()
    meet = remote(seg, seg_out, sw_send.at[0], sw_recv.at[0], me.across_y())
    meet.start()
    fetch = pltpu.make_async_copy(enc_in, enc, out_sem.at[11])
    fetch.start()
    onehot = token_numbers(seg, pad, pair, row_seg, row_keep, col_seg)
    cut = cutter(ga)
    after_stage(0, 0)
    begin(1)
    after_stage(0, 1)
    after_stage(1, 0)
    begin(2)
    after_stage(0, 2)
    table = cutter(gs)(0, gs.shape[-2]).astype(WIDE).T
    start = dec[...].astype(WIDE) + dot(onehot, table.astype(LOW))
    start_ref[...] = start
    out(0)
    one = (normalised(start)[0] * table[0:1] + table[4:5]).astype(LOW)
    one_ref[...] = one
    out(1)
    for k in range(3):
        qkv[:, pl.ds(k * BLOCK, BLOCK)] = dot(one, cut(QKV + 16 * k, QKV + 16 * (k + 1))).astype(LOW)
    out(2)
    line = []
    if gathers:
        across.wait()
        for k in range(1, depth):
            both = gz.at[:, z]
            line.append(remote(both, both, sw_send.at[3 + k], sw_recv.at[3 + k], me.along(k)))
            line[-1].start()
    halves = 2
    span = tok_count // halves
    swaps = []
    for k in range(halves):
        at = pl.ds(k * span, span)
        self_forward((k * span // 128, (k + 1) * span // 128), qkv, low, lse, row_seg, row_keep, col_seg)
        if k == 0:
            after_stage(1, 1)
            after_stage(2, 0)
            after_stage(1, 2)
        after = start_ref[at, :] + dot(low[at, :], cut(SO, CQ))
        after_ref[at, :] = after
        two = (normalised(after)[0] * table[1:2] + table[5:6]).astype(LOW)
        two_ref[at, :] = two
        query[at, :] = dot(two, cut(CQ, KV)).astype(LOW)
        swap = remote(query.at[at], other_out.at[at], sw_send.at[1 + k], sw_recv.at[1 + k], me.across_y())
        swap.start()
        swaps.append(swap)
    for k in range(3, 8):
        out(k)
    after_stage(2, 1)
    after_stage(2, 2)
    if gathers:
        own(ga, ga_out)
        own(gs, gs_out)
    fetch.wait()
    w_key, w_val = cut(KV, KV + 16), cut(KV + 16, EARLY)
    parts = 4
    for k in range(parts):
        span = src_count // parts
        at = pl.ds(k * span, span)
        kv[at, 0:width] = dot(enc[at, :], w_key).astype(LOW)
        kv[at, width : 2 * width] = dot(enc[at, :], w_val).astype(LOW)
    out(8)
    for copy in swaps + [meet] + line:
        copy.wait()
    end()
    for copy in outs + (owns[-2:] if gathers else []):
        copy.wait()


def first_part(depth, gathers, seg, pad, pair, dec, enc, tiny, raw, late, whole):
    tok_count, width = dec.shape
    src_count = enc.shape[0]
    lead = (depth, 2, 2, 2) if gathers else (BLOCK // 16,)
    results = [
        shape_of((tok_count, width), WIDE),
        shape_of((tok_count, width), LOW),
        shape_of((tok_count, 3 * width), LOW),
        shape_of((tok_count, width), LOW),
        shape_of((tok_count, 128), WIDE),
        shape_of((tok_count, width), WIDE),
        shape_of((tok_count, width), LOW),
        shape_of((tok_count, width), LOW),
        shape_of((src_count, 2 * width), LOW),
    ]
    outs = results + [shape_of((tok_count, width), LOW), shape_of((1, tok_count), jnp.int32)]
    if gathers:
        outs = [
            shape_of(lead + (EARLY, BLOCK), LOW),
            shape_of(lead + (16, 128), LOW),
            shape_of((2, depth, LATE, BLOCK), LOW),
        ] + outs
    extra = (*tiny, *raw, *late) if gathers else whole
    res = pl.pallas_call(
        partial(first_kernel, depth, gathers),
        name="first_part",
        out_shape=outs,
        in_specs=[VMEM, VMEM, SMEM, VMEM, ANY] + ([VMEM] * 4 + [ANY] * 8 if gathers else [ANY] * 2),
        out_specs=[ANY] * len(outs),
        scratch_shapes=[pltpu.VMEM(a.shape, a.dtype) for a in results]
        + [
            pltpu.VMEM(enc.shape, LOW),
            pltpu.VMEM(lead + (EARLY, BLOCK), LOW),
            pltpu.VMEM(lead + (16, 128), LOW),
            pltpu.VMEM((1, tok_count), WIDE),
            pltpu.VMEM((1, tok_count), WIDE),
            pltpu.VMEM((tok_count, 128), WIDE),
            pltpu.SemaphoreType.DMA((18,)),
            pltpu.SemaphoreType.DMA((12,)),
            pltpu.SemaphoreType.DMA((3, 2 * (depth + 3))),
            pltpu.SemaphoreType.DMA((3, 2 * (depth + 3))),
            pltpu.SemaphoreType.DMA((depth + 3,)),
            pltpu.SemaphoreType.DMA((depth + 3,)),
        ],
        compiler_params=pltpu.CompilerParams(
            collective_id=0, has_side_effects=True, vmem_limit_bytes=LIMIT
        ),
    )(seg, pad, pair, dec, enc, *extra)
    if gathers:
        whole, line, res = res[:2], res[2], res[3:]
    else:
        line = None
    start, one, qkv, low, lse, after, two, query, kv, other_query, other_seg = res
    return whole, line, (start, one, qkv, low, lse, after, two, query, other_query, kv, other_seg)


def segment_ends(lengths, ends):
    total = jnp.int32(0)
    ends[0] = total
    for s in range(2 * SEGS):
        total = total + lengths[0, s]
        ends[s + 1] = total


def block_ranges(seg_s, first_seg, ends, off, src_count, block):
    at = pl.multiple_of(block * 128, 128)
    low = jnp.clip(ends[first_seg + seg_s[0, at]] - off, 0, src_count)
    high = jnp.clip(ends[first_seg + seg_s[0, at + 127] + 1] - off, 0, src_count)
    first = low // TILE
    return first, jnp.where(high > low, (high + TILE - 1) // TILE, first)


def key_bounds(segs, firsts, ends, off):
    rows = []
    for seg, first_seg in zip(segs, firsts):
        low = jnp.zeros(seg.shape, jnp.int32)
        high = jnp.zeros(seg.shape, jnp.int32)
        for s in range(SEGS):
            low = jnp.where(seg == s, ends[first_seg + s] - off, low)
            high = jnp.where(seg == s, ends[first_seg + s + 1] - off, high)
        rows += [low, high]
    return jnp.concatenate(rows + [jnp.zeros((4, rows[0].shape[1]), jnp.int32)], axis=0)


TILE = 256


def side_by_side(x):
    return jnp.concatenate([x, x], axis=1)


def side_by_side_rows(rows, k, at):
    return jnp.concatenate([rows[k : k + 1, at], rows[k + 1 : k + 2, at]], axis=1)


def heads_apart(x):
    n = x.shape[1] // 2
    return jnp.concatenate([x[:HD, :n], x[HD:, n:]], axis=0).T


def cross_forward_kernel(
    lengths, seg_so, seg_sp, seg_vo, seg_vp, q_own, q_other, kv, o_own, o_other, lse_own, lse_other,
    ends, bounds, qs, top_ref, total_ref, acc_ref,
):
    tok_count, width = q_own.shape
    src_count = kv.shape[0]
    pairs = width // 128
    pos = lax.axis_index("src")
    off = pos * src_count
    firsts = (pos * SEGS, (1 - pos) * SEGS)
    segment_ends(lengths, ends)
    bounds[...] = key_bounds((seg_vo[...], seg_vp[...]), firsts, ends, off)
    for side, (q, o, lse_ref) in enumerate(((q_own, o_own, lse_own), (q_other, o_other, lse_other))):

        @pl.loop(0, tok_count // 128)
        def _(block):
            at = pl.ds(pl.multiple_of(block * 128, 128), 128)
            first, last = block_ranges((seg_so, seg_sp)[side], firsts[side], ends, off, src_count, block)
            low, high = bounds[2 * side : 2 * side + 1, at], bounds[2 * side + 1 : 2 * side + 2, at]
            for p in range(pairs):
                qs[p] = both_heads(q[at, p * 128 : (p + 1) * 128] * SCALE)
            top_ref[...] = jnp.full_like(top_ref, FILL)
            total_ref[...] = jnp.zeros_like(total_ref)
            acc_ref[...] = jnp.zeros_like(acc_ref)

            def one(t, carry):
                base = pl.multiple_of(t * TILE, TILE)
                keys = pl.ds(base, TILE)
                index = rows_of((TILE, 128)) + base
                allowed = side_by_side((index >= low) & (index < high))
                every = range(pairs)
                scores = [dot_nt(kv[keys, pl.ds(p * 128, 128)], qs[p]) for p in every]
                scores = [jnp.where(allowed, scores[p], FILL) for p in every]
                olds = [top_ref[p] for p in every]
                tops = [jnp.maximum(olds[p], jnp.max(scores[p], axis=0, keepdims=True)) for p in every]
                exps = [jnp.exp(scores[p] - jnp.maximum(tops[p], 0.1 * FILL)) for p in every]
                fades = [jnp.exp(olds[p] - tops[p]) for p in every]
                sums = [total_ref[p] * fades[p] + jnp.sum(exps[p], axis=0, keepdims=True) for p in every]
                mixed = [dot_tn(kv[keys, pl.ds(width + p * 128, 128)], exps[p].astype(LOW)) for p in every]
                mixed = [acc_ref[p] * fades[p] + mixed[p] for p in every]
                for p in every:
                    top_ref[p] = tops[p]
                    total_ref[p] = sums[p]
                    acc_ref[p] = mixed[p]
                return carry

            lax.fori_loop(first, last, one, 0)
            stats = []
            for p in range(pairs):
                total = total_ref[p]
                safe = jnp.where(total > 0.0, total, 1.0)
                o[at, p * 128 : (p + 1) * 128] = heads_apart(acc_ref[p] * (1.0 / safe)).astype(LOW)
                lse = jnp.where(total > 0.0, top_ref[p] + jnp.log(safe), FILL)
                stats += [lse[:, :128], lse[:, 128:]]
            lse_ref[:, at] = jnp.concatenate(stats, axis=0)


def cross_forward(lengths, seg_own, seg_other, q_own, q_other, kv):
    tok_count, width = q_own.shape
    heads = width // HD
    pairs = width // 128
    out = shape_of((tok_count, width), LOW)
    lse = shape_of((heads, tok_count), WIDE)
    return pl.pallas_call(
        cross_forward_kernel,
        name="cross_forward",
        out_shape=[out, out, lse, lse],
        in_specs=[SMEM] * 3 + [VMEM] * 5,
        out_specs=[VMEM] * 4,
        scratch_shapes=[
            pltpu.SMEM((32,), jnp.int32),
            pltpu.VMEM((8, tok_count), jnp.int32),
            pltpu.VMEM((pairs, 256, 128), LOW),
            pltpu.VMEM((pairs, 1, 256), WIDE),
            pltpu.VMEM((pairs, 1, 256), WIDE),
            pltpu.VMEM((pairs, 128, 256), WIDE),
        ],
        compiler_params=pltpu.CompilerParams(vmem_limit_bytes=LIMIT),
        cost_estimate=pl.CostEstimate(flops=1 << 33, bytes_accessed=8 << 20, transcendentals=0),
    )(lengths, seg_own, seg_other, seg_own, seg_other, q_own, q_other, kv)


def cross_backward_kernel(
    lengths, seg_so, seg_sp, seg_vo, seg_vp, q_own, q_other, g_own, g_other, st_own, st_other, kv, pass_0, pass_1,
    dq_own, dq_other, dkv, given_0, given_1, ends, bounds, acc, qs, gs, dq_acc, held_0, held_1, sems,
):
    ways = ((pass_0, held_0, given_0), (pass_1, held_1, given_1))
    taking = [pltpu.make_async_copy(way[0], way[1], sems.at[0, k]) for k, way in enumerate(ways)]
    giving = [pltpu.make_async_copy(way[1], way[2], sems.at[1, k]) for k, way in enumerate(ways)]
    for copy in taking:
        copy.start()
    tok_count, width = q_own.shape
    src_count = kv.shape[0]
    pairs = width // 128
    pos = lax.axis_index("src")
    off = pos * src_count
    firsts = (pos * SEGS, (1 - pos) * SEGS)
    segment_ends(lengths, ends)
    bounds[...] = key_bounds((seg_vo[...], seg_vp[...]), firsts, ends, off)
    acc[...] = jnp.zeros_like(acc)
    sides = ((q_own, g_own, st_own, dq_own), (q_other, g_other, st_other, dq_other))
    for side, (q, g, st, dq) in enumerate(sides):

        @pl.loop(0, tok_count // 128)
        def _(block):
            at = pl.ds(pl.multiple_of(block * 128, 128), 128)
            first, last = block_ranges((seg_so, seg_sp)[side], firsts[side], ends, off, src_count, block)
            low, high = bounds[2 * side : 2 * side + 1, at], bounds[2 * side + 1 : 2 * side + 2, at]
            for p in range(pairs):
                cols = slice(p * 128, (p + 1) * 128)
                qs[p] = both_heads(q[at, cols] * SCALE)
                gs[p] = both_heads(g[at, cols])
            dq_acc[...] = jnp.zeros_like(dq_acc)
            lses = [side_by_side_rows(st, 2 * p, at) for p in range(pairs)]
            deltas = [side_by_side_rows(st, 8 + 2 * p, at) for p in range(pairs)]

            def one(t, carry):
                base = pl.multiple_of(t * TILE, TILE)
                keys = pl.ds(base, TILE)
                index = rows_of((TILE, 128)) + base
                allowed = side_by_side((index >= low) & (index < high))
                every = range(pairs)
                cols = [pl.ds(p * 128, 128) for p in every]
                vals = [pl.ds(width + p * 128, 128) for p in every]
                scores = [dot_nt(kv[keys, cols[p]], qs[p]) for p in every]
                slopes = [dot_nt(kv[keys, vals[p]], gs[p]) for p in every]
                probs = [jnp.exp(jnp.where(allowed, scores[p] - lses[p], FILL)) for p in every]
                gscores = [(probs[p] * (slopes[p] - deltas[p])).astype(LOW) for p in every]
                grad_k = [acc[keys, cols[p]] + dot(gscores[p], qs[p]) for p in every]
                grad_v = [acc[keys, vals[p]] + dot(probs[p].astype(LOW), gs[p]) for p in every]
                grad_q = [dq_acc[p] + dot_tn(kv[keys, cols[p]], gscores[p]) for p in every]
                for p in every:
                    acc[keys, cols[p]] = grad_k[p]
                    acc[keys, vals[p]] = grad_v[p]
                    dq_acc[p] = grad_q[p]
                return carry

            lax.fori_loop(first, last, one, 0)
            for p in range(pairs):
                dq[at, p * 128 : (p + 1) * 128] = (heads_apart(dq_acc[p]) * SCALE).astype(dq.dtype)

    for first, second in zip(taking, giving):
        first.wait()
        second.start()

    @pl.loop(0, src_count // 256)
    def _(t):
        at = pl.ds(pl.multiple_of(t * 256, 256), 256)
        dkv[at, :] = acc[at, :].astype(LOW)

    for copy in giving:
        copy.wait()


def cross_backward(lengths, seg_own, seg_other, q_own, q_other, g_own, g_other, st_own, st_other, kv, passed):
    tok_count, width = q_own.shape
    src_count = kv.shape[0]
    pairs = width // 128
    return pl.pallas_call(
        cross_backward_kernel,
        name="cross_backward",
        out_shape=[
            shape_of((tok_count, width), WIDE),
            shape_of((tok_count, width), LOW),
            shape_of((src_count, 2 * width), LOW),
        ]
        + [shape_of(a.shape, a.dtype) for a in passed],
        in_specs=[SMEM] * 3 + [VMEM] * 9 + [ANY] * 2,
        out_specs=[VMEM] * 3 + [ANY] * 2,
        scratch_shapes=[
            pltpu.SMEM((32,), jnp.int32),
            pltpu.VMEM((8, tok_count), jnp.int32),
            pltpu.VMEM((src_count, 2 * width), WIDE),
            pltpu.VMEM((pairs, 256, 128), LOW),
            pltpu.VMEM((pairs, 256, 128), LOW),
            pltpu.VMEM((pairs, 128, 256), WIDE),
        ]
        + [pltpu.VMEM(a.shape, a.dtype) for a in passed]
        + [pltpu.SemaphoreType.DMA((2, 2))],
        compiler_params=pltpu.CompilerParams(vmem_limit_bytes=LIMIT),
        cost_estimate=pl.CostEstimate(flops=1 << 34, bytes_accessed=16 << 20, transcendentals=0),
    )(lengths, seg_own, seg_other, seg_own, seg_other, q_own, q_other, g_own, g_other, st_own, st_other, kv, *passed)


def merge_all(parts):
    top = parts[0][0:1]
    for part in parts[1:]:
        top = jnp.maximum(top, part[0:1])
    total = sum(jnp.exp(part[0:1] - top) for part in parts)
    rest = sum(part for part in parts)
    return jnp.where(rows_of(rest.shape) == 0, top + jnp.log(total), rest)


def middle_kernel(depth, split, *refs):
    (
        seg, pad, labels, counts, positions, targets, w_vocab, after_self, o_own, o_other, lse_own, lse_other,
        gs,
    ) = refs[:13]
    parts = refs[13 : 13 + (2 if split else 1)]
    refs = refs[13 + len(parts) :]
    count = 2 if split else 1
    sums = refs[:count]
    refs = refs[count:]
    (
        block_out, state_out, g_own, g_other, st_own, st_other, small_rows, small_cols, grad_vocab, token_out, loss_out,
    ) = refs[:11]
    (
        wm, eb, eb_got, w_s, got_o, got_lse, cross_o, cross_low, ac, bs, n3, act, slope, gpre, head,
        lt, gt, pb, rb, got_rc, got_rq, got_rz, st_c, st_q, st_z, gh, load_sem, send, recv,
    ) = refs[11:]
    tok_count, width = after_self.shape
    hidden = act.shape[1]
    masked = positions.shape[1]
    vocab_local = w_vocab.shape[0]
    everyone = depth * 8
    me = Place(depth)
    z, x, c, y = me.z, me.x, me.c, me.y
    greet(me.others() + [me.across_x(), me.across_y(), me.across_both(), me.across_core()])
    used = [0]

    def push(src, dst, peer):
        k = used[0]
        used[0] += 1
        copy = remote(src, dst, send.at[k], recv.at[k], peer)
        copy.start()
        return copy

    pending = []

    def arrive(copies):
        for copy in copies:
            copy.wait_recv()
        pending.extend(copies)

    loads = []

    def load(src, dst):
        copy = pltpu.make_async_copy(src, dst, load_sem.at[len(loads)])
        copy.start()
        loads.append(copy)

    load(gs, w_s)
    shared = []
    if split:
        rest = pl.ds(PERMUTED, LATE - PERMUTED)
        soon = pl.ds(0, PERMUTED)
        late_part = []
        for py in range(2):
            block = parts[0].at[py, :, rest]
            late_part.append(push(block, wm.at[:, x, c, py, rest], me.across_x()))
        swap = [push(o_other, got_o, me.across_y()), push(lse_other, got_lse, me.across_y())]
        for py in range(2):
            load(parts[0].at[py], wm.at[:, x, c, py])
            shared.append(push(parts[0].at[py], wm.at[:, x, c, py], me.across_core()))
            load(parts[1].at[py], wm.at[:, 1 - x, c, py, soon])
            shared.append(push(parts[1].at[py], wm.at[:, 1 - x, c, py, soon], me.across_core()))
    else:
        swap = [push(o_other, got_o, me.across_y()), push(lse_other, got_lse, me.across_y())]
        load(parts[0], wm)

    def cut(lo, hi):
        value = wm[:, :, :, :, lo:hi] if split else wm[:, lo:hi]
        return value.reshape((-1, BLOCK))

    def put(lo, value, first=0, last=None, cols=slice(0, BLOCK)):
        groups, rows, wide = value.shape
        last = depth if last is None else last
        if split:
            eb[first:last, :, :, :, lo : lo + rows, cols] = value.reshape((last - first, 2, 2, 2, rows, wide))
        else:
            step = eb.shape[0] // depth
            eb[first * step : last * step, lo : lo + rows, cols] = value

    segments = seg[...].astype(WIDE)
    keep = 1.0 - pad[...].astype(WIDE)
    lane_row = lanes((1, tok_count))
    inside = lane_row < tok_count - 1

    def following(row):
        return pltpu.roll(jnp.concatenate([row, jnp.zeros((7, tok_count), WIDE)], axis=0), tok_count - 1, 1)[0:1]

    follows = inside & (following(segments) == segments) & (keep > 0.5) & (following(keep) > 0.5)
    valid = jnp.where(follows, 1.0, 0.0)
    rows = [keep, valid, labels[...].astype(WIDE), counts[...].astype(WIDE)]
    columns = transposed_rows(jnp.concatenate(rows + [jnp.zeros((4, tok_count), WIDE)], axis=0))
    col_keep, col_valid = columns[:, 0:1], columns[:, 1:2]
    col_label, col_count = columns[:, 2:3], columns[:, 3:4].astype(jnp.int32)

    for copy in loads:
        copy.wait()
    arrive(shared)
    table = w_s[...].reshape((-1, 128)).astype(WIDE).T

    arrive(swap)
    if split:
        arrive(late_part)
        block = wm.at[:, 1 - x, c, :, rest]
        late_part = [push(block, block, me.across_core())]
    top = jnp.maximum(lse_own[...], got_lse[...])
    lse = top + jnp.log(jnp.exp(lse_own[...] - top) + jnp.exp(got_lse[...] - top))
    shares = jnp.concatenate([jnp.exp(lse_own[...] - lse), jnp.exp(got_lse[...] - lse)], axis=0)
    shares = transposed_rows(shares)
    low_half = lanes((tok_count, 128)) < HD
    for p in range(width // 128):
        at = slice(p * 128, (p + 1) * 128)
        share_own = jnp.where(low_half, shares[:, 2 * p : 2 * p + 1], shares[:, 2 * p + 1 : 2 * p + 2])
        share_got = jnp.where(low_half, shares[:, 8 + 2 * p : 9 + 2 * p], shares[:, 9 + 2 * p : 10 + 2 * p])
        mixed = o_own[:, at].astype(WIDE) * share_own + got_o[:, at].astype(WIDE) * share_got
        cross_o[:, at] = mixed
        cross_low[:, at] = mixed.astype(LOW)
    weight_co = cut(0, 16)
    after_cross = after_self[...] + dot(cross_low[...], weight_co)
    ac[...] = after_cross
    n3[...] = (normalised(after_cross)[0] * table[2:3] + table[6:7]).astype(LOW)
    bs[...] = after_cross
    if split:
        arrive(late_part)
    blocks = hidden // BLOCK
    flat_fo = cut(80, 144)
    for j in range(blocks):
        at = slice(j * BLOCK, (j + 1) * BLOCK)
        pre = dot(n3[...], cut(16 + 16 * j, 32 + 16 * j))
        square = pre * pre
        bent = jnp.tanh(GELU * pre * (1.0 + CUBIC * square))
        half = 0.5 * (1.0 + bent)
        act[:, at] = (pre * half).astype(LOW)
        slope[:, at] = half + 0.5 * pre * (1.0 - bent * bent) * (GELU * (1.0 + 3.0 * CUBIC * square))
        bs[...] = bs[...] + dot(act[:, at], flat_fo[at])
    state = bs[...]
    block_out[...] = state.astype(LOW)
    head_in = (normalised(state)[0] * table[3:4] + table[7:8]).astype(LOW)
    head[...] = head_in

    picker = (positions[...] == rows_of((tok_count, masked))).astype(LOW)
    picked = dot_tn(picker, head_in).astype(LOW)
    kept = dot(jnp.concatenate([keep, jnp.zeros((7, tok_count), WIDE)], axis=0).astype(LOW), picker)
    code = jnp.where(kept[0:1] > 0.5, targets[...] + 1, 0)
    digits = jnp.concatenate([code >> 8, code & 255, jnp.zeros((6, masked), jnp.int32)], axis=0)
    digits = dot_tn(digits.astype(WIDE).astype(LOW), (rows_of((8, 128)) == lanes((8, 128))).astype(LOW)).astype(LOW)
    pb[z, x, c, y, :, 0:width] = picked
    pb[z, x, c, y, :, width : width + 128] = digits
    mine = pb.at[z, x, c, y]
    flight = [push(mine, mine, peer) for peer in me.others()]

    classes = BLOCK // 2
    flat_in = cut(144, 160).reshape((-1, 16, BLOCK))
    flat_in = jnp.concatenate([flat_in[:, :, :classes], flat_in[:, :, classes:]], axis=1).reshape((-1, classes))
    w_one, w_two = flat_in[:width], flat_in[width:]
    token_row = rows_of((tok_count, classes))
    ahead = pltpu.roll(dot(head_in, w_two), tok_count - 1, 0)
    logits = dot(head_in, w_one) + jnp.where(token_row == tok_count - 1, 0.0, ahead)
    top = jnp.max(logits, axis=1, keepdims=True)
    exps = jnp.exp(logits - top)
    total = jnp.sum(exps, axis=1, keepdims=True)
    hits = lanes((tok_count, classes)) == col_count
    entropy = top + jnp.log(total) - jnp.sum(jnp.where(hits, logits, 0.0), axis=1, keepdims=True)
    loss_col = col_valid * entropy
    grads = col_valid * (exps * (1.0 / total) - jnp.where(hits, 1.0, 0.0))
    g_insert = grads.astype(LOW)
    before = pltpu.roll(g_insert.astype(WIDE), 1, 0)
    g_before = jnp.where(token_row == 0, 0.0, before).astype(LOW)

    arrive(flight)
    column = pb.at[:, x, c, y]
    flight = [push(column, column, peer) for peer in (me.across_x(), me.across_y(), me.across_both())]

    flat_s = w_s[...].reshape((-1, 128))
    two = dot(head_in, flat_s)
    l_zero, l_one = two[:, 16:17], two[:, 17:18]
    top = jnp.maximum(l_zero, l_one)
    e_zero, e_one = jnp.exp(l_zero - top), jnp.exp(l_one - top)
    total = e_zero + e_one
    is_one = col_label > 0.5
    loss_col = loss_col + col_keep * (top + jnp.log(total) - jnp.where(is_one, l_one, l_zero))
    d_zero = col_keep * (e_zero / total - jnp.where(is_one, 0.0, 1.0))
    d_one = col_keep * (e_one / total - jnp.where(is_one, 1.0, 0.0))
    lane = lanes((tok_count, 128))
    g_delete = jnp.where(lane == 16, d_zero, jnp.where(lane == 17, d_one, 0.0)).astype(LOW)
    gh[...] = dot_nt(g_delete, flat_s) + dot_nt(g_insert, w_one) + dot_nt(g_before, w_two)
    arrive(flight)
    plane = pb.at[:, :, c, :]
    flight = [push(plane, plane, me.across_core())]
    small_cols[...] = dot_tn(head_in, g_delete)
    for k, grad in enumerate((g_insert, g_before)):
        pairs = dot_tn(head_in, grad).astype(LOW).reshape((-1, 2, 16, classes))
        for side in range(2):
            cols = slice(side * classes, (side + 1) * classes)
            put(144, pairs[:, side], k * (depth // 2), (k + 1) * (depth // 2), cols)
    arrive(flight)

    gathered = pb[...].reshape((-1, width + 128))
    rows_all = gathered[:, 0:width]
    numbers = gathered[:, width : width + 128].astype(WIDE).T
    code = numbers[0:1] * 256.0 + numbers[1:2]
    weight = jnp.where(code > 0.5, 1.0, 0.0)
    count = rows_all.shape[0]
    pos = lax.axis_index(BOTH)
    place = rows_of((vocab_local, count)) + pos * vocab_local
    hits = place == (code.astype(jnp.int32) - 1)
    lt[...] = dot_nt(w_vocab[...], rows_all)
    logits = lt[...]
    top = jnp.max(logits, axis=0, keepdims=True)
    total = jnp.sum(jnp.exp(logits - top), axis=0, keepdims=True)
    chosen = jnp.sum(jnp.where(hits, logits, 0.0), axis=0, keepdims=True)
    loss_here = jnp.sum(loss_col, axis=0, keepdims=True)
    stat = jnp.concatenate(
        [top + jnp.log(total), chosen, jnp.broadcast_to(loss_here, (1, count)), jnp.zeros((5, count), WIDE)], axis=0
    )
    st_c[0] = stat
    flight = [push(st_c.at[0], st_c.at[1], me.across_core())]
    arrive(flight)
    st_q[x, y] = merge_all([st_c[0], st_c[1]])
    spot = st_q.at[x, y]
    flight = [push(spot, spot, peer) for peer in (me.across_x(), me.across_y(), me.across_both())]
    arrive(flight)
    st_z[z] = merge_all([st_q[0, 0], st_q[0, 1], st_q[1, 0], st_q[1, 1]])
    flight = [push(st_z.at[z], st_z.at[z], peer) for peer in me.others()]
    arrive(flight)
    stat = merge_all([st_z[k] for k in range(depth)])
    tokens = weight * (stat[0:1] - stat[1:2])
    mine = rows_of((masked, count)) + pos * masked == lanes((masked, count))
    own = jnp.sum(jnp.where(mine, tokens, 0.0), axis=1, keepdims=True)
    token_out[...] = jnp.sum(
        jnp.where(rows_of((masked, masked)) == lanes((masked, masked)), own, 0.0), axis=0, keepdims=True
    )
    loss = (stat[2:3, 0:128] + jnp.sum(tokens, axis=1, keepdims=True)) * (1.0 / (tok_count * everyone))
    loss_out[...] = loss[:, 0:1]
    gt[...] = (weight * (jnp.exp(lt[...] - stat[0:1]) - jnp.where(hits, 1.0, 0.0))).astype(LOW)

    rb[...] = dot_tn(gt[...], w_vocab[...]).astype(LOW).reshape(rb.shape)
    flight = [push(rb.at[:, :, 1 - c], got_rc, me.across_core())]
    scale = (tok_count * everyone) ** (-0.5)
    grad_vocab[...] = dot(gt[...], rows_all) * scale
    arrive(flight)
    got_rc[...] = (rb[:, :, c].astype(WIDE) + got_rc[...].astype(WIDE)).astype(LOW)
    flight = [
        push(got_rc.at[:, 1 - x, y], got_rq.at[0], me.across_x()),
        push(got_rc.at[:, x, 1 - y], got_rq.at[1], me.across_y()),
        push(got_rc.at[:, 1 - x, 1 - y], got_rq.at[2], me.across_both()),
    ]
    arrive(flight)
    line = got_rc[:, x, y].astype(WIDE)
    for k in range(3):
        line = line + got_rq[k].astype(WIDE)
    got_rq[3] = line.astype(LOW)
    flight = [
        push(got_rq.at[3, lax.rem(z + k, depth)], got_rz.at[k - 1], me.along(k)) for k in range(1, depth)
    ]
    arrive(flight)
    grad_picked = got_rq[3, z].astype(WIDE)
    for k in range(1, depth):
        grad_picked = grad_picked + got_rz[k - 1].astype(WIDE)
    coarse = grad_picked.astype(LOW)
    fine = (grad_picked - coarse.astype(WIDE)).astype(LOW)
    grad_head = gh[...] + dot(picker, coarse) + dot(picker, fine)

    grad_block, gain_3, bias_3 = norm_back(bs[...], table[3:4], grad_head)
    bs[...] = grad_block
    g_ffn = grad_block.astype(LOW)
    gh[...] = jnp.zeros_like(gh)
    for j in range(blocks):
        at = slice(j * BLOCK, (j + 1) * BLOCK)
        gpre[:, at] = (dot_nt(g_ffn, flat_fo[at]) * slope[:, at]).astype(LOW)
        gh[...] = gh[...] + dot_nt(gpre[:, at], cut(16 + 16 * j, 32 + 16 * j))
    back, gain_2, bias_2 = norm_back(ac[...], table[2:3], gh[...])
    grad_state = grad_block + back
    state_out[...] = grad_state
    g_cross = grad_state.astype(LOW)
    g_attn = dot_nt(g_cross, weight_co).astype(LOW)
    g_own[...] = g_attn
    deltas = jnp.zeros((tok_count, 128), WIDE)
    for p in range(width // 128):
        at = slice(p * 128, (p + 1) * 128)
        product = g_attn[:, at].astype(WIDE) * cross_o[:, at]
        first = jnp.sum(jnp.where(low_half, product, 0.0), axis=1, keepdims=True)
        second = jnp.sum(jnp.where(low_half, 0.0, product), axis=1, keepdims=True)
        deltas = jnp.where(lane == 2 * p, first, jnp.where(lane == 2 * p + 1, second, deltas))
    st_own[...] = jnp.concatenate([lse, deltas.T[0:8]], axis=0)
    swap = [push(g_own, g_other, me.across_y()), push(st_own, st_other, me.across_y())]

    for j in range(blocks):
        at = slice(j * BLOCK, (j + 1) * BLOCK)
        grad = dot_tn(act[:, at], g_ffn).astype(LOW)
        put(80, grad.reshape((-1, 64, BLOCK)), j * depth // blocks, (j + 1) * depth // blocks)
        grad = dot_tn(n3[...], gpre[:, at]).astype(LOW)
        put(16 + 16 * j, grad.reshape((-1, 16, BLOCK)))
    put(0, dot_tn(cross_low[...], g_cross).astype(LOW).reshape((-1, 16, BLOCK)))
    if split:
        halves = [push(eb.at[:, :, 1 - c], eb_got, me.across_core())]
    small_rows[...] = jnp.concatenate([gain_2, gain_3, bias_2, bias_3, jnp.zeros((4, width), WIDE)], axis=0)
    if split:
        arrive(halves)
        for k, py in enumerate((y, 1 - y)):
            for px in range(2):

                @pl.loop(0, depth)
                def _(zz):
                    total = eb[zz, px, c, py].astype(WIDE) + eb_got[zz, px, py].astype(WIDE)
                    sums[k][px, zz] = total.astype(LOW)

    else:
        sums[0][...] = eb[...]
    arrive(swap)
    for copy in pending:
        copy.wait_send()


def middle_part(depth, split, seg, pad, labels, counts, positions, targets, w_vocab, after_self, attended, gs, parts):
    tok_count, width = after_self.shape
    hidden = 4 * BLOCK
    vocab_local = w_vocab.shape[0]
    everyone = depth * 8
    masked = positions.shape[1]
    count = masked * everyone
    sharded = (depth, 2, 2, 2)
    lead = sharded if split else (BLOCK // 16,)
    sharded = (depth, 2, 2, 2)
    outs = [(shape_of(parts[0].shape, LOW), VMEM)] * len(parts)
    outs += [
        (shape_of((tok_count, width), LOW), VMEM),
        (shape_of((tok_count, width), WIDE), VMEM),
        (shape_of((tok_count, width), LOW), VMEM),
        (shape_of((tok_count, width), LOW), ANY),
        (shape_of((16, tok_count), WIDE), VMEM),
        (shape_of((16, tok_count), WIDE), ANY),
        (shape_of((8, width), WIDE), VMEM),
        (shape_of((width, 128), WIDE), VMEM),
        (shape_of((vocab_local, width), WIDE), VMEM),
        (shape_of((1, masked), WIDE), VMEM),
        (shape_of((1, 1), WIDE), VMEM),
    ]
    copies = 16 + 2 * (depth - 1) + 3 + 1 + 1 + 3 + 1 + 3 + (depth - 1)
    return pl.pallas_call(
        partial(middle_kernel, depth, split),
        name="middle_part",
        out_shape=[o for o, _ in outs],
        in_specs=[VMEM] * 12 + [ANY] * (1 + len(parts)),
        out_specs=[s for _, s in outs],
        scratch_shapes=[
            pltpu.VMEM(lead + (160, BLOCK), LOW),
            pltpu.VMEM(lead + (160, BLOCK), LOW),
            pltpu.VMEM(((depth, 2, 2) if split else (1,)) + (160, BLOCK), LOW),
            pltpu.VMEM(gs.shape, LOW),
            pltpu.VMEM((tok_count, width), LOW),
            pltpu.VMEM((8, tok_count), WIDE),
            pltpu.VMEM((tok_count, width), WIDE),
            pltpu.VMEM((tok_count, width), LOW),
            pltpu.VMEM((tok_count, width), WIDE),
            pltpu.VMEM((tok_count, width), WIDE),
            pltpu.VMEM((tok_count, width), LOW),
            pltpu.VMEM((tok_count, hidden), LOW),
            pltpu.VMEM((tok_count, hidden), WIDE),
            pltpu.VMEM((tok_count, hidden), LOW),
            pltpu.VMEM((tok_count, width), LOW),
            pltpu.VMEM((vocab_local, count), WIDE),
            pltpu.VMEM((vocab_local, count), LOW),
            pltpu.VMEM(sharded + (masked, width + 128), LOW),
            pltpu.VMEM(sharded + (masked, width), LOW),
            pltpu.VMEM((depth, 2, 2, masked, width), LOW),
            pltpu.VMEM((4, depth, masked, width), LOW),
            pltpu.VMEM((max(depth - 1, 1), masked, width), LOW),
            pltpu.VMEM((2, 8, count), WIDE),
            pltpu.VMEM((2, 2, 8, count), WIDE),
            pltpu.VMEM((depth, 8, count), WIDE),
            pltpu.VMEM((tok_count, width), WIDE),
            pltpu.SemaphoreType.DMA((10,)),
            pltpu.SemaphoreType.DMA((copies + depth,)),
            pltpu.SemaphoreType.DMA((copies + depth,)),
        ],
        compiler_params=pltpu.CompilerParams(
            collective_id=1, has_side_effects=True, vmem_limit_bytes=LIMIT
        ),
    )(seg, pad, labels, counts, positions, targets, w_vocab, after_self, *attended, gs, *parts)


def self_backward_start(dk, dv):
    dk[...] = jnp.zeros_like(dk)
    dv[...] = jnp.zeros_like(dv)


def self_backward(blocks, qkv, out, lse_ref, g_ref, dqkv, dk, dv, row_seg, row_keep, col_seg):
    tok_count, width = out.shape
    first, last = blocks
    pairs = width // 128

    def one(block, carry):
        at = pl.ds(pl.multiple_of(block * 128, 128), 128)
        low = self_window(block, tok_count)
        keys = pl.ds(low, 384)
        allowed = twice(self_mask(row_seg, row_keep, col_seg, block, low))
        stats = lse_ref[at, :]
        every = range(pairs)
        cols = [slice(p * 128, (p + 1) * 128) for p in every]
        q = [both_heads(qkv[at, cols[p]] * SCALE) for p in every]
        g = [both_heads(g_ref[at, cols[p]]) for p in every]
        keyed = [qkv[keys, width + p * 128 : width + (p + 1) * 128] for p in every]
        scores = [dot_nt(q[p], keyed[p]) for p in every]
        slopes = [dot_nt(g[p], qkv[keys, 2 * width + p * 128 : 2 * width + (p + 1) * 128]) for p in every]
        deltas = [jnp.sum(g[p].astype(WIDE) * twice(out[at, cols[p]].astype(WIDE)), axis=1, keepdims=True) for p in every]
        lses = [jnp.concatenate([stats[:, 2 * p : 2 * p + 1], stats[:, 2 * p + 1 : 2 * p + 2]], axis=0) for p in every]
        probs = [jnp.exp(jnp.where(allowed, scores[p] - lses[p], FILL)) for p in every]
        gscores = [(probs[p] * (slopes[p] - deltas[p])).astype(LOW) for p in every]
        grad_q = [join_heads(dot(gscores[p], keyed[p])) * SCALE for p in every]
        grad_k = [dk[keys, cols[p]] + dot_tn(gscores[p], q[p]) for p in every]
        grad_v = [dv[keys, cols[p]] + dot_tn(probs[p].astype(LOW), g[p]) for p in every]
        for p in every:
            dqkv[at, cols[p]] = grad_q[p].astype(LOW)
            dk[keys, cols[p]] = grad_k[p]
            dv[keys, cols[p]] = grad_v[p]
        return carry

    lax.fori_loop(first, last, one, 0)


def self_backward_end(dqkv, dk, dv):
    width = dk.shape[1]
    dqkv[:, width : 2 * width] = dk[...].astype(LOW)
    dqkv[:, 2 * width : 3 * width] = dv[...].astype(LOW)


def reduction(me, chunks, send, recv):
    z, x, c, y = me.z, me.x, me.c, me.y
    depth = me.depth
    count = len(chunks)
    started = [[None] * 3 for _ in chunks]
    used = [0] * count

    def launch(k, stage):
        copies = []

        def push(src, dst, peer):
            slot = used[k]
            used[k] += 1
            copy = remote(src, dst, send.at[k, slot], recv.at[k, slot], peer)
            copy.start()
            copies.append(copy)

        for src, got_c, got_q, got_z, at, put in chunks[k]:
            if stage == 0:
                push(src.at[:, :, 1 - c, :, at], got_c.at[:, :, :, at], me.across_core())
            elif stage == 1:
                push(got_c.at[:, 1 - x, y, at], got_q.at[0, :, at], me.across_x())
                push(got_c.at[:, x, 1 - y, at], got_q.at[1, :, at], me.across_y())
                push(got_c.at[:, 1 - x, 1 - y, at], got_q.at[2, :, at], me.across_both())
            else:
                for j in range(1, depth):
                    push(got_c.at[lax.rem(z + j, depth), x, y, at], got_z.at[j - 1, at], me.along(j))
        started[k][stage] = copies

    def absorb(k, stage):
        for copy in started[k][stage]:
            copy.wait_recv()
        for src, got_c, got_q, got_z, at, put in chunks[k]:
            if stage == 0:

                @pl.loop(0, depth)
                def _(zz):
                    for xx in range(2):
                        for yy in range(2):
                            total = src[zz, xx, c, yy, at].astype(WIDE) + got_c[zz, xx, yy, at].astype(WIDE)
                            got_c[zz, xx, yy, at] = total.astype(LOW)

            elif stage == 1:

                @pl.loop(0, depth)
                def _(zz):
                    total = got_c[zz, x, y, at].astype(WIDE)
                    for k in range(3):
                        total = total + got_q[k, zz, at].astype(WIDE)
                    got_c[zz, x, y, at] = total.astype(LOW)

            else:
                total = got_c[z, x, y, at].astype(WIDE)
                for j in range(1, depth):
                    total = total + got_z[j - 1, at].astype(WIDE)
                put(total)

    def begin(k):
        launch(k, 0)

    def after(k, stage):
        absorb(k, stage)
        if stage < 2:
            launch(k, stage + 1)

    def end():
        for stages in started:
            for copies in stages:
                for copy in copies:
                    copy.wait_send()

    return begin, after, end


def last_kernel(depth, reduces, *refs):
    (pair, seg, pad, dq_other) = refs[:4]
    held = refs[4:15]
    (small_rows, small_cols, ga_in, gs_in) = refs[15:19]
    refs = refs[19:]
    if reduces:
        parts, refs = refs[:2], refs[2:]
    grad_input, grad_enc = refs[:2]
    refs = refs[2:]
    outs = refs[:9] if reduces else refs[:2]
    refs = refs[9:] if reduces else refs[2:]
    (dkv, enc, dq_own, start, one, qkv, low, lse, after, two, gstate) = refs[:11]
    (ga, gs, g_query, g_attn, dqkv, dk, dv, row_seg, row_keep, col_seg, load_sem, dq_got, sw_send, sw_recv) = refs[11:25]
    refs = refs[25:]
    refs_held = (dkv, enc, dq_own, start, one, qkv, low, lse, after, two, gstate)
    tok_count, width = dq_own.shape
    src_count = enc.shape[0]
    everyone = depth * 8
    me = Place(depth)
    scale = (tok_count * everyone) ** (-0.5)
    loads = []
    for src, dst in list(zip(held, refs_held)) + [(gs_in, gs), (ga_in, ga)]:
        copy = pltpu.make_async_copy(src, dst, load_sem.at[len(loads)])
        copy.start()
        loads.append(copy)
    if reduces:
        greet(me.others() + [me.across_x(), me.across_y(), me.across_both(), me.across_core()])
    else:
        greet([me.across_y()])
    halves = 2
    half = tok_count // halves
    swaps = []
    for k in range(halves):
        at = pl.ds(k * half, half)
        swaps.append(remote(dq_other.at[at], dq_got.at[at], sw_send.at[k], sw_recv.at[k], me.across_y()))
        swaps[-1].start()

    if reduces:
        (late, late_s, ex, ex_got, ez, ez_got, c_a, c_s, q_a, q_s, z_a, z_s, ez_send, ez_recv, send, recv) = refs
        (o_qkv, o_so, o_cq, o_kv, o_co, o_fi, o_fo, o_in, o_s) = outs

        def put_kv(total):
            o_kv[:, 0:BLOCK] = total[0:16] * scale
            o_kv[:, BLOCK : 2 * BLOCK] = total[16:32] * scale

        def put_mid(total):
            o_so[...] = total[0:16] * scale
            o_cq[...] = total[16:32] * scale

        def put_qkv(k, total):
            o_qkv[:, k * BLOCK : (k + 1) * BLOCK] = total * scale

        def put_s(total):
            o_s[...] = total * scale

        def rows(lo, hi, put):
            return (late, c_a, q_a, z_a, pl.ds(lo, hi - lo), put)

        chunks = [
            [rows(KV, EARLY, put_kv)],
            [rows(SO, KV, put_mid)],
            [rows(0, 16, partial(put_qkv, 0))],
            [rows(16, 32, partial(put_qkv, 1))],
            [rows(32, SO, partial(put_qkv, 2))],
            [(late_s, c_s, q_s, z_s, pl.ds(0, 16), put_s)],
        ]

        z, x = me.z, me.x

        @pl.loop(0, depth)
        def _(zz):
            for k in range(2):
                ex[k, zz] = (parts[0][k, zz].astype(WIDE) + parts[1][k, zz].astype(WIDE)).astype(LOW)

        plane = [remote(ex.at[1 - x], ex_got, ez_send.at[0], ez_recv.at[0], me.across_x())]
        plane[0].start()
        along = []

        def onward():
            for copy in plane:
                copy.wait_recv()

            @pl.loop(0, depth)
            def _(zz):
                ez[zz] = (ex[x, zz].astype(WIDE) + ex_got[zz].astype(WIDE)).astype(LOW)

            for k in range(1, depth):
                to = lax.rem(z + k, depth)
                at = 1 + k
                along.append(remote(ez.at[to], ez_got.at[k - 1], ez_send.at[at], ez_recv.at[at], me.along(k)))
                along[-1].start()

        def settle():
            for copy in plane:
                copy.wait_send()
            for copy in along:
                copy.wait()
            total = ez[me.z].astype(WIDE)
            for k in range(depth - 1):
                total = total + ez_got[k].astype(WIDE)
            total = total * scale
            o_co[...] = total[0:16]
            for k in range(4):
                o_fi[:, k * BLOCK : (k + 1) * BLOCK] = total[16 + 16 * k : 32 + 16 * k]
            o_fo[...] = total[80:144]
            half = BLOCK // 2
            for k in range(2):
                o_in[16 * k : 16 * (k + 1)] = total[144:160, half * k : half * (k + 1)]

        begin, after_stage, end = reduction(me, chunks, send, recv)

        def keep(lo, value):
            late[:, :, :, :, lo : lo + 16] = value.astype(LOW).reshape(late.shape[:4] + (16, BLOCK))

        def keep_small(value):
            late_s[...] = value.astype(LOW).reshape(late_s.shape)
    else:
        def begin(k):
            return None

        def after_stage(k, stage):
            return None

        end = onward = settle = lambda: None
        o_late, o_small = outs

        def keep(lo, value):
            o_late[:, lo : lo + 16] = value.astype(LOW).reshape((-1, 16, BLOCK))

        def keep_small(value):
            o_small[...] = value

    chunk_kv, chunk_mid, chunk_q, chunk_k, chunk_v, chunk_s = range(6)
    onehot = token_numbers(seg, pad, pair, row_seg, row_keep, col_seg)
    cut = cutter(ga)
    for copy in loads[:2]:
        copy.wait()
    keep(KV, dot_tn(enc[...], dkv[:, 0:width]))
    keep(KV + 16, dot_tn(enc[...], dkv[:, width : 2 * width]))
    begin(chunk_kv)
    for copy in loads[2:]:
        copy.wait()
    table = cutter(gs)(0, gs.shape[-2]).astype(WIDE).T
    self_backward_start(dk, dv)
    gains = biases = 0.0
    for k in range(halves):
        at = pl.ds(k * half, half)
        swaps[k].wait()
        query = (dq_own[at, :] + dq_got[at, :].astype(WIDE)).astype(LOW)
        g_query[at, :] = query
        back, gain_1, bias_1 = norm_back(after[at, :], table[1:2], dot_nt(query, cut(CQ, KV)))
        gains, biases = gains + gain_1, biases + bias_1
        state = gstate[at, :] + back
        gstate[at, :] = state
        g_attn[at, :] = dot_nt(state.astype(LOW), cut(SO, CQ)).astype(LOW)
        if k == 0:
            after_stage(chunk_kv, 0)
        blocks = (k * half // 128, (k + 1) * half // 128)
        self_backward(blocks, qkv, low, lse, g_attn, dqkv, dk, dv, row_seg, row_keep, col_seg)
        if k == 0:
            onward()
    self_backward_end(dqkv, dk, dv)
    keep(CQ, dot_tn(two[...], g_query[...]))
    keep(SO, dot_tn(low[...], gstate[...].astype(LOW)))
    begin(chunk_mid)
    for k, chunk in enumerate((chunk_q, chunk_k, chunk_v)):
        keep(QKV + 16 * k, dot_tn(one[...], dqkv[:, k * width : (k + 1) * width]))
        begin(chunk)
    after_stage(chunk_mid, 0)
    after_stage(chunk_q, 0)
    after_stage(chunk_k, 0)
    after_stage(chunk_kv, 1)
    upstream = dot_nt(dqkv[:, 0:width], cut(QKV, QKV + 16))
    upstream = upstream + dot_nt(dqkv[:, width : 2 * width], cut(QKV + 16, QKV + 32))
    upstream = upstream + dot_nt(dqkv[:, 2 * width : 3 * width], cut(QKV + 32, SO))
    after_stage(chunk_v, 0)
    back, gain_0, bias_0 = norm_back(start[...], table[0:1], upstream)
    grad_start = gstate[...] + back
    grad_input[...] = grad_start.astype(LOW)
    coarse = grad_start.astype(LOW)
    fine = (grad_start - coarse.astype(WIDE)).astype(LOW)
    g_table = (dot_tn(onehot, coarse) + dot_tn(onehot, fine))[8:16]
    mid = small_rows[...]
    stacked = jnp.concatenate([gain_0, gains, mid[0:2], bias_0, biases, mid[2:4], g_table], axis=0)
    keep_small(transposed_rows(stacked) + small_cols[...])
    begin(chunk_s)
    after_stage(chunk_mid, 1)
    w_key, w_val = cut(KV, KV + 16), cut(KV + 16, EARLY)
    span = src_count // 4

    def source_grads(k):
        at = pl.ds(k * span, span)
        grads = dot_nt(dkv[at, 0:width], w_key) + dot_nt(dkv[at, width : 2 * width], w_val)
        grad_enc[at, :] = grads.astype(LOW)

    source_grads(0)
    after_stage(chunk_s, 0)
    after_stage(chunk_kv, 2)
    after_stage(chunk_q, 1)
    source_grads(1)
    after_stage(chunk_k, 1)
    source_grads(2)
    after_stage(chunk_v, 1)
    after_stage(chunk_s, 1)
    source_grads(3)
    settle()
    for chunk in (chunk_mid, chunk_q, chunk_k, chunk_v, chunk_s):
        after_stage(chunk, 2)
    end()


def last_part(depth, reduces, pair, seg, pad, dq_own, dq_other, dkv, enc, kept, gstate, grads, whole):
    tok_count, width = dq_own.shape
    src_count = enc.shape[0]
    ga, gs = whole
    parts, small_rows, small_cols = grads
    everyone = depth * 8
    rows = BLOCK // everyone
    sharded = (depth, 2, 2, 2)
    held = (dkv, enc, dq_own, *kept, gstate)
    outs = [shape_of((tok_count, width), LOW), shape_of((src_count, width), LOW)]
    scratch = [pltpu.VMEM(a.shape, a.dtype) for a in held]
    scratch += [
        pltpu.VMEM(ga.shape, LOW),
        pltpu.VMEM(gs.shape, LOW),
        pltpu.VMEM((tok_count, width), LOW),
        pltpu.VMEM((tok_count, width), LOW),
        pltpu.VMEM((tok_count, 3 * width), LOW),
        pltpu.VMEM((tok_count, width), WIDE),
        pltpu.VMEM((tok_count, width), WIDE),
        pltpu.VMEM((1, tok_count), WIDE),
        pltpu.VMEM((1, tok_count), WIDE),
        pltpu.VMEM((tok_count, 128), WIDE),
        pltpu.SemaphoreType.DMA((14,)),
        pltpu.VMEM((tok_count, width), LOW),
        pltpu.SemaphoreType.DMA((2,)),
        pltpu.SemaphoreType.DMA((2,)),
    ]
    if reduces:
        shapes = [(EARLY, BLOCK), (16, 128)]
        outs += [
            shape_of((rows, 3 * BLOCK), WIDE),
            shape_of((rows, BLOCK), WIDE),
            shape_of((rows, BLOCK), WIDE),
            shape_of((rows, 2 * BLOCK), WIDE),
            shape_of((rows, BLOCK), WIDE),
            shape_of((rows, 4 * BLOCK), WIDE),
            shape_of((4 * rows, BLOCK), WIDE),
            shape_of((2 * rows, BLOCK // 2), WIDE),
            shape_of((rows, 128), WIDE),
        ]
        scratch += [pltpu.VMEM(sharded + s, LOW) for s in shapes]
        scratch += [pltpu.VMEM(parts[0].shape, LOW), pltpu.VMEM(parts[0].shape[1:], LOW)]
        scratch += [pltpu.VMEM((depth, LATE, BLOCK), LOW), pltpu.VMEM((depth - 1, LATE, BLOCK), LOW)]
        for lead in ((depth, 2, 2), (3, depth), (depth - 1,)):
            scratch += [pltpu.VMEM(lead + s, LOW) for s in shapes]
        scratch += [pltpu.SemaphoreType.DMA((depth + 2,))] * 2
        slots = 2 * (depth + 3)
        scratch += [pltpu.SemaphoreType.DMA((6, slots)), pltpu.SemaphoreType.DMA((6, slots))]
    else:
        outs += [shape_of((BLOCK // 16, EARLY, BLOCK), LOW), shape_of((BLOCK, 128), WIDE)]
    return pl.pallas_call(
        partial(last_kernel, depth, reduces),
        name="last_part",
        out_shape=outs,
        in_specs=[SMEM] + [VMEM] * 2 + [ANY] * 12 + [VMEM] * 2 + [ANY] * 2 + [VMEM] * len(parts),
        out_specs=[VMEM] * len(outs),
        scratch_shapes=scratch,
        compiler_params=pltpu.CompilerParams(
            collective_id=2, has_side_effects=True, vmem_limit_bytes=LIMIT
        ),
    )(pair, seg, pad, dq_other, *held, small_rows, small_cols, ga, gs, *parts)


def finish_kernel(count, *refs):
    ins, small, loss = refs[:count], refs[count], refs[count + 1]
    refs = refs[count + 2 :]
    outs, (gain, bias, table, delete, loss_out) = refs[:count], refs[count : count + 5]
    held, sems = refs[count + 5 : 2 * count + 5], refs[2 * count + 5]
    first = [pltpu.make_async_copy(ins[k], held[k], sems.at[0, k]) for k in range(count)]
    copies = [pltpu.make_async_copy(held[k], outs[k], sems.at[1, k]) for k in range(count)]
    for copy in first:
        copy.start()
    values = small[...]
    shape = (values.shape[0], values.shape[0])
    turned = jnp.concatenate([values, jnp.zeros((128 - values.shape[0], 128), WIDE)], axis=0).T
    gain[...] = turned[0:4, 0 : shape[0]]
    bias[...] = turned[4:8, 0 : shape[0]]
    table[...] = turned[8:16, 0 : shape[0]]
    delete[...] = turned[16:18, 0 : shape[0]]
    loss_out[...] = loss[...]
    for before, copy in zip(first, copies):
        before.wait()
        copy.start()
    for copy in copies:
        copy.wait()


def finish(results, small, loss):
    count = len(results)
    rows = small.shape[0]
    outs = [shape_of(a.shape, a.dtype) for a in results]
    outs += [shape_of(s, WIDE) for s in ((4, rows), (4, rows), (PAIRS, rows), (2, rows), (1, 1))]
    res = pl.pallas_call(
        partial(finish_kernel, count),
        name="finish",
        out_shape=outs,
        in_specs=[ANY] * count + [VMEM] * 2,
        out_specs=[ANY] * count + [VMEM] * 5,
        scratch_shapes=[pltpu.VMEM(a.shape, a.dtype) for a in results] + [pltpu.SemaphoreType.DMA((2, count))],
        compiler_params=pltpu.CompilerParams(vmem_limit_bytes=LIMIT),
    )(*results, small, loss)
    return res[:count], res[count:]


def late_blocks(cross_out, ffn_in, ffn_out, insert):
    groups = cross_out.shape[0] // 16
    return jnp.concatenate(
        [
            cross_out.reshape(groups, 16, BLOCK),
            ffn_in.reshape(groups, 16, 4, BLOCK).swapaxes(1, 2).reshape(groups, 64, BLOCK),
            ffn_out.reshape(groups, 64, BLOCK),
            insert.reshape(groups, 2, 16, BLOCK // 2).swapaxes(1, 2).reshape(groups, 16, BLOCK),
        ],
        axis=1,
    )


def gather_by_ops(qkv, self_out, cross_q, cross_kv, small):
    wide = jnp.concatenate([qkv, self_out, cross_q, cross_kv], axis=1)
    ga = lax.all_gather(wide, BOTH, axis=0, tiled=True).reshape(-1, 16, 7, BLOCK).swapaxes(1, 2)
    gs = lax.all_gather(small, BOTH, axis=0, tiled=True)
    return ga.reshape(-1, EARLY, BLOCK), gs.reshape(-1, 16, 128)


def partner(array, depth, axis):
    dx, dy = (1, 0) if axis == "x" else (0, 1)
    pairs = []
    for z in range(depth):
        for x in range(2):
            for c in range(2):
                for y in range(2):
                    here = ((z * 2 + x) * 2 + c) * 2 + y
                    there = ((z * 2 + (x ^ dx)) * 2 + c) * 2 + (y ^ dy)
                    pairs.append((here, there))
    return lax.ppermute(array, BOTH, pairs)


def reduce_by_ops(early, small, late, scale):
    groups = late.shape[0]
    gw_f = late[:, 80:144].reshape(groups * 64, BLOCK)
    gw_i = late[:, 144:160].reshape(groups, 16, 2, BLOCK // 2).swapaxes(1, 2).reshape(groups * 32, BLOCK // 2)
    late = late[:, 0:80].reshape(groups, 5, 16, BLOCK).swapaxes(0, 1).reshape(5, BLOCK, BLOCK)
    early = early.reshape(groups, 7, 16, BLOCK).swapaxes(0, 1).reshape(7, BLOCK, BLOCK)
    wide = jnp.concatenate([early, late]).swapaxes(0, 1).reshape(BLOCK, 12 * BLOCK)

    def sums(a):
        return lax.psum_scatter(a.astype(WIDE), BOTH, scatter_dimension=0, tiled=True) * scale

    own = sums(wide)
    edges = (0, 3, 4, 5, 7, 8, 12)
    pieces = [own[:, lo * BLOCK : hi * BLOCK] for lo, hi in zip(edges[:-1], edges[1:])]
    return pieces + [sums(gw_f), sums(gw_i), sums(small)]


def body(
    dec_input, enc_output, segment_ids, padding, pair_ids, src_lengths, delete_labels, insert_counts,
    masked_positions, masked_targets, norm_gain, norm_bias, pair_table, self_qkv, self_out, cross_q, cross_kv,
    cross_out, ffn_in, ffn_out, w_delete, w_insert, w_vocab,
):
    everyone = lax.axis_size(BOTH)
    depth = everyone // 8
    tok_count = dec_input.shape[0]
    aligned = self_qkv.shape[0] == 16
    late = (cross_out, ffn_in, ffn_out, w_insert)
    tiny = (norm_gain, norm_bias, pair_table, w_delete.T)
    raw = (self_qkv, self_out, cross_q, cross_kv)
    whole = gathered = None
    if not aligned:
        gathered = late_blocks(*[lax.all_gather(a, BOTH, axis=0, tiled=True) for a in late])
        small = jnp.concatenate([norm_gain, norm_bias, pair_table, w_delete.T], axis=0).T
        small = jnp.pad(small, ((0, 0), (0, 128 - small.shape[1])))
        whole = gather_by_ops(*raw, small)
    whole, line, firsts = first_part(
        depth, aligned, segment_ids, padding, pair_ids, dec_input, enc_output, tiny, raw, late, whole
    )
    start, one, qkv, low, lse, after, two, query, other_query, kv, other_seg = firsts
    parts = (line, partner(line[:, :, :PERMUTED], depth, "x")) if aligned else (gathered,)
    o_own, o_other, lse_own, lse_other = cross_forward(src_lengths, segment_ids, other_seg, query, other_query, kv)
    mids = middle_part(
        depth, aligned, segment_ids, padding, delete_labels, insert_counts, masked_positions, masked_targets,
        w_vocab, after, (o_own, o_other, lse_own, lse_other), whole[1], parts,
    )
    parts, mids = mids[: len(parts)], mids[len(parts) :]
    block_out, gstate, g_own, g_other, st_own, st_other, small_rows, small_cols, grad_vocab, tokens, loss = mids
    sums = (parts[0], partner(parts[1], depth, "y")) if aligned else ()
    dq_own, dq_other, dkv, block_out, grad_vocab = cross_backward(
        src_lengths, segment_ids, other_seg, query, other_query, g_own, g_other, st_own, st_other, kv,
        (block_out, grad_vocab),
    )
    res = last_part(
        depth, aligned, pair_ids, segment_ids, padding, dq_own, dq_other, dkv, enc_output,
        (start, one, qkv, low, lse, after, two), gstate, (sums, small_rows, small_cols), whole,
    )
    if aligned:
        sums = res[2:]
    else:
        scale = (tok_count * everyone) ** (-0.5)
        sums = reduce_by_ops(res[2], res[3], parts[0], scale)
    results, smalls = finish((res[1], res[0], *sums[:8], tokens), sums[8], loss)
    grad_enc, grad_input, qkv, so, cq, kv, co, fi, fo, insert, tokens = results
    gain, bias, table, delete, loss = smalls
    return (
        block_out, grad_input, grad_enc, gain, bias, table, qkv, so, cq, kv, co, fi, fo, delete.T, insert,
        grad_vocab, loss[0, 0], tokens,
    )


def solution(mesh):
    shared = P(BOTH, None)
    across = P(None, BOTH)
    return jax.shard_map(
        body,
        mesh=mesh,
        in_specs=(shared,) * 5 + (P("batch", None),) + (shared,) * 4 + (across,) * 3 + (shared,) * 10,
        out_specs=(shared,) * 3 + (across,) * 3 + (shared,) * 10 + (P(), shared),
        check_vma=False,
    )
```

```python
from functools import partial

import jax
import jax.numpy as jnp
from jax import lax
from jax.experimental import pallas as pl
from jax.experimental.pallas import tpu as pltpu
from jax.sharding import PartitionSpec as P

HD = 64
PAIRS = 8
SEGS = 8
BLOCK = 512
EPSILON = 1e-05
SCALE = 0.125
FILL = -1e30
GELU = 0.7978845608
CUBIC = 0.044715

MESH = pl.DeviceIdType.MESH
ANY = pl.BlockSpec(memory_space=pl.ANY)
VMEM = pl.BlockSpec(memory_space=pltpu.VMEM)
SMEM = pl.BlockSpec(memory_space=pltpu.SMEM)
BOTH = ("batch", "src")
LOW = jnp.bfloat16
WIDE = jnp.float32
LIMIT = 63 << 20


def shape_of(shape, kind):
    return jax.ShapeDtypeStruct(shape, kind)


def dot(left, right):
    return jnp.dot(left, right, preferred_element_type=WIDE)


def dot_tn(left, right):
    return lax.dot_general(left, right, (((0,), (0,)), ((), ())), preferred_element_type=WIDE)


def dot_nt(left, right):
    return lax.dot_general(left, right, (((1,), (1,)), ((), ())), preferred_element_type=WIDE)


def normalised(v):
    centred = v - jnp.mean(v, axis=-1, keepdims=True)
    r = lax.rsqrt(jnp.mean(centred * centred, axis=-1, keepdims=True) + EPSILON)
    return centred * r, r


def norm_back(v, gain, upstream):
    hat, r = normalised(v)
    scaled = upstream * gain
    first = jnp.mean(scaled, axis=-1, keepdims=True)
    second = jnp.mean(scaled * hat, axis=-1, keepdims=True)
    grad_gain = jnp.sum(upstream * hat, axis=0, keepdims=True)
    grad_bias = jnp.sum(upstream, axis=0, keepdims=True)
    return r * (scaled - first - hat * second), grad_gain, grad_bias


def lanes(shape):
    return lax.broadcasted_iota(jnp.int32, shape, len(shape) - 1)


def rows_of(shape):
    return lax.broadcasted_iota(jnp.int32, shape, len(shape) - 2)


def both_heads(x):
    low = lanes(x.shape) < HD
    zero = jnp.zeros_like(x)
    return jnp.concatenate([jnp.where(low, x, zero), jnp.where(low, zero, x)], axis=0)


def join_heads(x):
    half = x.shape[0] // 2
    return jnp.where(lanes((half, x.shape[1])) < HD, x[:half], x[half:])


def twice(x):
    return jnp.concatenate([x, x], axis=0)


def transposed_rows(rows):
    count, width = rows.shape
    return jnp.concatenate([rows, jnp.zeros((128 - count, width), WIDE)], axis=0).T


def greet(peers):
    barrier = pltpu.get_barrier_semaphore()
    for peer in peers:
        pl.semaphore_signal(barrier, inc=1, device_id=peer, device_id_type=MESH)
    pl.semaphore_wait(barrier, len(peers))


def remote(src, dst, send, recv, peer):
    return pltpu.make_async_remote_copy(
        src_ref=src,
        dst_ref=dst,
        send_sem=send,
        recv_sem=recv,
        device_id=peer,
        device_id_type=MESH,
    )


class Place:
    def __init__(self, depth):
        b = lax.axis_index("batch")
        self.depth = depth
        self.y = lax.axis_index("src")
        self.c = lax.rem(b, 2)
        self.x = lax.rem(b // 2, 2)
        self.z = b // 4

    def at(self, z=None, x=None, c=None, y=None):
        z = self.z if z is None else z
        x = self.x if x is None else x
        c = self.c if c is None else c
        y = self.y if y is None else y
        return ((z * 2 + x) * 2 + c, y)

    def along(self, k):
        return self.at(z=lax.rem(self.z + k, self.depth))

    def others(self):
        return [self.along(k) for k in range(1, self.depth)]

    def across_x(self):
        return self.at(x=1 - self.x)

    def across_y(self):
        return self.at(y=1 - self.y)

    def across_both(self):
        return self.at(x=1 - self.x, y=1 - self.y)

    def across_core(self):
        return self.at(c=1 - self.c)

    def plane(self):
        spots = [(dx, dy, dc) for dx in range(2) for dy in range(2) for dc in range(2)][1:]

        def turned(value, flip):
            return 1 - value if flip else value

        return [self.at(x=turned(self.x, dx), y=turned(self.y, dy), c=turned(self.c, dc)) for dx, dy, dc in spots]


def gathering(me, chunks, send, recv):
    z, x, c, y = me.z, me.x, me.c, me.y
    started = [[None] * 3 for _ in chunks]
    used = [0] * len(chunks)
    every = slice(None)

    def launch(k, stage):
        copies = []

        def push(block, peer):
            slot = used[k]
            used[k] += 1
            copy = remote(block, block, send.at[k, slot], recv.at[k, slot], peer)
            copy.start()
            copies.append(copy)

        for view in chunks[k]:
            if stage == 0:
                for peer in me.others():
                    push(view(z, x, c, y), peer)
            elif stage == 1:
                for peer in (me.across_x(), me.across_y(), me.across_both()):
                    push(view(every, x, c, y), peer)
            else:
                push(view(every, every, c, every), me.across_core())
        started[k][stage] = copies

    def begin(k):
        launch(k, 0)

    def after(k, stage):
        for copy in started[k][stage]:
            copy.wait_recv()
        if stage < 2:
            launch(k, stage + 1)

    def end():
        for stages in started:
            for copies in stages:
                for copy in copies:
                    copy.wait_send()

    return begin, after, end


def self_window(block, tok_count):
    low = jnp.clip(block * 128 - 128, 0, tok_count - 384)
    return pl.multiple_of(low, 128)


def self_mask(row_seg, row_keep, col_seg, block, low):
    at = pl.ds(low, 384)
    keys = row_seg[0:1, at]
    keep = row_keep[0:1, at]
    queries = col_seg[pl.ds(pl.multiple_of(block * 128, 128), 128), 0:1]
    shape = (128, 384)
    own = (rows_of(shape) + block * 128) == (lanes(shape) + low)
    return (queries == keys) & ((keep > 0.5) | own)


def self_forward(blocks, qkv, out, lse_ref, row_seg, row_keep, col_seg):
    tok_count, width = out.shape
    first, last = blocks
    pairs = width // 128

    def one(block, carry):
        at = pl.ds(pl.multiple_of(block * 128, 128), 128)
        low = self_window(block, tok_count)
        keys = pl.ds(low, 384)
        allowed = twice(self_mask(row_seg, row_keep, col_seg, block, low))
        every = range(pairs)
        q = [both_heads(qkv[at, p * 128 : (p + 1) * 128] * SCALE) for p in every]
        scores = [dot_nt(q[p], qkv[keys, width + p * 128 : width + (p + 1) * 128]) for p in every]
        scores = [jnp.where(allowed, scores[p], FILL) for p in every]
        tops = [jnp.max(scores[p], axis=1, keepdims=True) for p in every]
        exps = [jnp.exp(scores[p] - tops[p]) for p in every]
        totals = [jnp.sum(exps[p], axis=1, keepdims=True) for p in every]
        probs = [(exps[p] * (1.0 / totals[p])).astype(LOW) for p in every]
        mixed = [dot(probs[p], qkv[keys, 2 * width + p * 128 : 2 * width + (p + 1) * 128]) for p in every]
        lane = lanes((128, 128))
        stats = jnp.zeros((128, 128), WIDE)
        for p in every:
            out[at, p * 128 : (p + 1) * 128] = join_heads(mixed[p]).astype(LOW)
            lse = tops[p] + jnp.log(totals[p])
            stats = jnp.where(lane == 2 * p, lse[:128], jnp.where(lane == 2 * p + 1, lse[128:], stats))
        lse_ref[at, :] = stats
        return carry

    lax.fori_loop(first, last, one, 0)


def small_matrix(gain, bias, pair_rows, delete):
    def spot(count, first):
        shape = (count, 128)
        return (rows_of(shape) + first == lanes(shape)).astype(LOW)

    total = dot_tn(gain, spot(4, 0)) + dot_tn(bias, spot(4, 4)) + dot_tn(pair_rows, spot(PAIRS, 8))
    return (total + dot_tn(delete, spot(2, 8 + PAIRS))).astype(LOW)


def token_numbers(seg, pad, pair, row_seg, row_keep, col_seg):
    tok_count = seg.shape[1]
    segments = seg[...].astype(WIDE)
    row_seg[...] = segments
    row_keep[...] = 1.0 - pad[...].astype(WIDE)
    pair_row = jnp.zeros((1, tok_count), WIDE)
    for k in range(SEGS):
        pair_row = jnp.where(segments == k, pair[0, k].astype(WIDE), pair_row)
    columns = transposed_rows(jnp.concatenate([segments, pair_row, jnp.zeros((6, tok_count), WIDE)], axis=0))
    col_seg[...] = columns
    return (lanes((tok_count, 128)) == (columns[:, 1:2].astype(jnp.int32) + 8)).astype(LOW)


def cutter(ref):
    every = (slice(None),) * (len(ref.shape) - 2)

    def cut(lo, hi):
        value = ref[every + (slice(lo, hi),)]
        return value.reshape((-1, value.shape[-1]))

    return cut


QKV, SO, CQ, KV, EARLY = 0, 48, 64, 80, 112
LATE, PERMUTED, RETURNED = 160, 96, 128


def first_kernel(depth, gathers, *refs):
    (seg, pad, pair, dec, enc_in) = refs[:5]
    refs = refs[5:]
    if gathers:
        (gain, bias, pair_rows, delete, raw_qkv, raw_so, raw_cq, raw_kv, raw_co, raw_fi, raw_fo, raw_in) = refs[:12]
        (ga_out, gs_out, gz1, gz2) = refs[12:16]
        refs = refs[16:]
    else:
        ga_in, gs_in = refs[:2]
        refs = refs[2:]
    results, other_out, seg_out = refs[:9], refs[9], refs[10]
    held = refs[11:20]
    (start_ref, one_ref, qkv, low, lse, after_ref, two_ref, query, kv) = held
    (enc, ga, gs, row_seg, row_keep, col_seg, own_sem, out_sem, send, recv, sw_send, sw_recv, stage1, stage2) = refs[20:]
    tok_count, width = dec.shape
    src_count = enc.shape[0]
    me = Place(depth)
    z, x, c, y = me.z, me.x, me.c, me.y
    owns = []

    def own(src, dst):
        copy = pltpu.make_async_copy(src, dst, own_sem.at[len(owns)])
        copy.start()
        owns.append(copy)

    if gathers:
        for raw, count, first in ((raw_qkv, 3, QKV), (raw_so, 1, SO), (raw_cq, 1, CQ), (raw_kv, 2, KV)):
            for k in range(count):
                own(raw.at[:, pl.ds(k * BLOCK, BLOCK)], ga.at[z, x, c, y, pl.ds(first + 16 * k, 16)])
        soon = len(owns)
        own1, own2 = stage1, stage2
        split_fo = PERMUTED - 80
        own(raw_co, own1.at[pl.ds(0, 16)])
        for k in range(4):
            own(raw_fi.at[:, pl.ds(k * BLOCK, BLOCK)], own1.at[pl.ds(16 + 16 * k, 16)])
        own(raw_fo.at[pl.ds(0, split_fo)], own1.at[pl.ds(80, split_fo)])
        own(raw_fo.at[pl.ds(split_fo, 64 - split_fo)], own2.at[pl.ds(0, 64 - split_fo)])
        for k in range(2):
            half = BLOCK // 2
            place = own2.at[pl.ds(64 - split_fo, 16), pl.ds(half * k, half)]
            own(raw_in.at[pl.ds(16 * k, 16)], place)
        gs[z, x, c, y] = small_matrix(gain[...], bias[...], pair_rows[...], delete[...])
        greet(me.others() + [me.across_x(), me.across_y(), me.across_both(), me.across_core()])
        for copy in owns[:soon]:
            copy.wait()

        def rows(lo, hi):
            return lambda *at: ga.at[at + (pl.ds(lo, hi - lo),)]

        chunks = [[lambda *at: gs.at[at]]]
        chunks += [[rows(lo, hi)] for lo, hi in ((0, 16), (16, 32), (32, SO), (SO, KV), (KV, EARLY))]
        begin, after_stage, end = gathering(me, chunks, send, recv)
    else:
        own(ga_in, ga)
        own(gs_in, gs)
        greet([me.across_y()])
        for copy in owns:
            copy.wait()

        def begin(k):
            return None

        def after_stage(k, stage):
            return None

        def end():
            return None

    outs = []

    def out(k):
        copy = pltpu.make_async_copy(held[k], results[k], out_sem.at[len(outs)])
        copy.start()
        outs.append(copy)

    c_s, c_q, c_k, c_v, c_mid, c_kv = range(6)
    begin(c_s)
    begin(c_q)
    line, crossing = [], []
    if gathers:
        for copy in owns[soon:]:
            copy.wait()
        kept = len(owns)
        for k, (ref, spot) in enumerate(((own1, gz1.at[y, z]), (own2, gz2.at[y, z]))):
            crossing.append(remote(ref, spot, sw_send.at[3 + k], sw_recv.at[3 + k], me.across_y()))
            crossing[-1].start()
            own(ref, spot)
    meet = remote(seg, seg_out, sw_send.at[0], sw_recv.at[0], me.across_y())
    meet.start()
    fetch = pltpu.make_async_copy(enc_in, enc, out_sem.at[11])
    fetch.start()
    onehot = token_numbers(seg, pad, pair, row_seg, row_keep, col_seg)
    cut = cutter(ga)
    after_stage(c_s, 0)
    after_stage(c_q, 0)
    begin(c_k)
    after_stage(c_k, 0)
    begin(c_v)
    after_stage(c_s, 1)
    after_stage(c_q, 1)
    after_stage(c_v, 0)
    begin(c_mid)
    begin(c_kv)
    for copy in crossing:
        copy.wait()
    if gathers:
        for copy in owns[kept:]:
            copy.wait()
        far, near = me.along(depth // 2), me.at(z=z + 1 - 2 * lax.rem(z, 2))
        z_far = lax.rem(z + depth // 2, depth)

        def along(ref, peer):
            at = 5 + len(line)
            line.append(remote(ref, ref, sw_send.at[at], sw_recv.at[at], peer))
            line[-1].start()

        for ref in (gz1.at[:, z], gz2.at[:, z]):
            along(ref, far)
            along(ref, near)
    after_stage(c_s, 2)
    table = cutter(gs)(0, gs.shape[-2]).astype(WIDE).T
    start = dec[...].astype(WIDE) + dot(onehot, table.astype(LOW))
    start_ref[...] = start
    out(0)
    one = (normalised(start)[0] * table[0:1] + table[4:5]).astype(LOW)
    one_ref[...] = one
    out(1)
    after_stage(c_k, 1)
    after_stage(c_mid, 0)
    after_stage(c_q, 2)
    qkv[:, 0:BLOCK] = dot(one, cut(QKV, QKV + 16)).astype(LOW)
    after_stage(c_v, 1)
    after_stage(c_k, 2)
    qkv[:, BLOCK : 2 * BLOCK] = dot(one, cut(QKV + 16, QKV + 32)).astype(LOW)
    after_stage(c_v, 2)
    qkv[:, 2 * BLOCK : 3 * BLOCK] = dot(one, cut(QKV + 32, SO)).astype(LOW)
    out(2)
    halves = 2
    span = tok_count // halves
    swaps = []
    for k in range(halves):
        at = pl.ds(k * span, span)
        self_forward((k * span // 128, (k + 1) * span // 128), qkv, low, lse, row_seg, row_keep, col_seg)
        if k == 0:
            after_stage(c_mid, 1)
            after_stage(c_kv, 0)
            after_stage(c_mid, 2)
        after = start_ref[at, :] + dot(low[at, :], cut(SO, CQ))
        after_ref[at, :] = after
        two = (normalised(after)[0] * table[1:2] + table[5:6]).astype(LOW)
        two_ref[at, :] = two
        query[at, :] = dot(two, cut(CQ, KV)).astype(LOW)
        swap = remote(query.at[at], other_out.at[at], sw_send.at[1 + k], sw_recv.at[1 + k], me.across_y())
        swap.start()
        swaps.append(swap)
        if k == 0 and gathers:
            line[0].wait_recv()
            along(gz1.at[:, z_far], near)
            line[2].wait_recv()
            along(gz2.at[:, z_far], near)
    for k in range(3, 8):
        out(k)
    after_stage(c_kv, 1)
    after_stage(c_kv, 2)
    if gathers:
        own(ga, ga_out)
        own(gs, gs_out)
    fetch.wait()
    w_key, w_val = cut(KV, KV + 16), cut(KV + 16, EARLY)
    parts = 4
    for k in range(parts):
        span = src_count // parts
        at = pl.ds(k * span, span)
        kv[at, 0:width] = dot(enc[at, :], w_key).astype(LOW)
        kv[at, width : 2 * width] = dot(enc[at, :], w_val).astype(LOW)
    out(8)
    for copy in swaps + [meet]:
        copy.wait()
    for k, copy in enumerate(line):
        if k not in (0, 2):
            copy.wait_recv()
        copy.wait_send()
    end()
    for copy in outs + (owns[-2:] if gathers else []):
        copy.wait()


def first_part(depth, gathers, seg, pad, pair, dec, enc, tiny, raw, late, whole):
    tok_count, width = dec.shape
    src_count = enc.shape[0]
    lead = (depth, 2, 2, 2) if gathers else (BLOCK // 16,)
    results = [
        shape_of((tok_count, width), WIDE),
        shape_of((tok_count, width), LOW),
        shape_of((tok_count, 3 * width), LOW),
        shape_of((tok_count, width), LOW),
        shape_of((tok_count, 128), WIDE),
        shape_of((tok_count, width), WIDE),
        shape_of((tok_count, width), LOW),
        shape_of((tok_count, width), LOW),
        shape_of((src_count, 2 * width), LOW),
    ]
    outs = results + [shape_of((tok_count, width), LOW), shape_of((1, tok_count), jnp.int32)]
    if gathers:
        outs = [
            shape_of(lead + (EARLY, BLOCK), LOW),
            shape_of(lead + (16, 128), LOW),
            shape_of((2, depth, PERMUTED, BLOCK), LOW),
            shape_of((2, depth, LATE - PERMUTED, BLOCK), LOW),
        ] + outs
    extra = (*tiny, *raw, *late) if gathers else whole
    res = pl.pallas_call(
        partial(first_kernel, depth, gathers),
        name="first_part",
        out_shape=outs,
        in_specs=[VMEM, VMEM, SMEM, VMEM, ANY] + ([VMEM] * 4 + [ANY] * 8 if gathers else [ANY] * 2),
        out_specs=[ANY] * len(outs),
        scratch_shapes=[pltpu.VMEM(a.shape, a.dtype) for a in results]
        + [
            pltpu.VMEM(enc.shape, LOW),
            pltpu.VMEM(lead + (EARLY, BLOCK), LOW),
            pltpu.VMEM(lead + (16, 128), LOW),
            pltpu.VMEM((1, tok_count), WIDE),
            pltpu.VMEM((1, tok_count), WIDE),
            pltpu.VMEM((tok_count, 128), WIDE),
            pltpu.SemaphoreType.DMA((20,)),
            pltpu.SemaphoreType.DMA((12,)),
            pltpu.SemaphoreType.DMA((6, depth + 3)),
            pltpu.SemaphoreType.DMA((6, depth + 3)),
            pltpu.SemaphoreType.DMA((2 * depth + 3,)),
            pltpu.SemaphoreType.DMA((2 * depth + 3,)),
            pltpu.VMEM((PERMUTED, BLOCK), LOW),
            pltpu.VMEM((LATE - PERMUTED, BLOCK), LOW),
        ],
        compiler_params=pltpu.CompilerParams(
            collective_id=0, has_side_effects=True, vmem_limit_bytes=LIMIT
        ),
    )(seg, pad, pair, dec, enc, *extra)
    if gathers:
        whole, line, res = res[:2], res[2:4], res[4:]
    else:
        line = None
    start, one, qkv, low, lse, after, two, query, kv, other_query, other_seg = res
    return whole, line, (start, one, qkv, low, lse, after, two, query, other_query, kv, other_seg)


def segment_ends(lengths, ends):
    total = jnp.int32(0)
    ends[0] = total
    for s in range(2 * SEGS):
        total = total + lengths[0, s]
        ends[s + 1] = total


def block_ranges(seg_s, first_seg, ends, off, src_count, block):
    at = pl.multiple_of(block * 128, 128)
    low = jnp.clip(ends[first_seg + seg_s[0, at]] - off, 0, src_count)
    high = jnp.clip(ends[first_seg + seg_s[0, at + 127] + 1] - off, 0, src_count)
    first = low // TILE
    return first, jnp.where(high > low, (high + TILE - 1) // TILE, first)


def key_bounds(segs, firsts, ends, off):
    rows = []
    for seg, first_seg in zip(segs, firsts):
        low = jnp.zeros(seg.shape, jnp.int32)
        high = jnp.zeros(seg.shape, jnp.int32)
        for s in range(SEGS):
            low = jnp.where(seg == s, ends[first_seg + s] - off, low)
            high = jnp.where(seg == s, ends[first_seg + s + 1] - off, high)
        rows += [low, high]
    return jnp.concatenate(rows + [jnp.zeros((4, rows[0].shape[1]), jnp.int32)], axis=0)


TILE = 256


def side_by_side(x):
    return jnp.concatenate([x, x], axis=1)


def side_by_side_rows(rows, k, at):
    return jnp.concatenate([rows[k : k + 1, at], rows[k + 1 : k + 2, at]], axis=1)


def heads_apart(x):
    n = x.shape[1] // 2
    return jnp.concatenate([x[:HD, :n], x[HD:, n:]], axis=0).T


def cross_forward_kernel(
    lengths, seg_so, seg_sp, seg_vo, seg_vp, q_own, q_other, kv, o_own, o_other, lse_own, lse_other,
    ends, bounds, qs, top_ref, total_ref, acc_ref,
):
    tok_count, width = q_own.shape
    src_count = kv.shape[0]
    pairs = width // 128
    pos = lax.axis_index("src")
    off = pos * src_count
    firsts = (pos * SEGS, (1 - pos) * SEGS)
    segment_ends(lengths, ends)
    bounds[...] = key_bounds((seg_vo[...], seg_vp[...]), firsts, ends, off)
    for side, (q, o, lse_ref) in enumerate(((q_own, o_own, lse_own), (q_other, o_other, lse_other))):

        @pl.loop(0, tok_count // 128)
        def _(block):
            at = pl.ds(pl.multiple_of(block * 128, 128), 128)
            first, last = block_ranges((seg_so, seg_sp)[side], firsts[side], ends, off, src_count, block)
            low, high = bounds[2 * side : 2 * side + 1, at], bounds[2 * side + 1 : 2 * side + 2, at]
            for p in range(pairs):
                qs[p] = both_heads(q[at, p * 128 : (p + 1) * 128] * SCALE)
            top_ref[...] = jnp.full_like(top_ref, FILL)
            total_ref[...] = jnp.zeros_like(total_ref)
            acc_ref[...] = jnp.zeros_like(acc_ref)

            def one(t, carry):
                base = pl.multiple_of(t * TILE, TILE)
                keys = pl.ds(base, TILE)
                index = rows_of((TILE, 128)) + base
                allowed = side_by_side((index >= low) & (index < high))
                every = range(pairs)
                scores = [dot_nt(kv[keys, pl.ds(p * 128, 128)], qs[p]) for p in every]
                scores = [jnp.where(allowed, scores[p], FILL) for p in every]
                olds = [top_ref[p] for p in every]
                tops = [jnp.maximum(olds[p], jnp.max(scores[p], axis=0, keepdims=True)) for p in every]
                exps = [jnp.exp(scores[p] - jnp.maximum(tops[p], 0.1 * FILL)) for p in every]
                fades = [jnp.exp(olds[p] - tops[p]) for p in every]
                sums = [total_ref[p] * fades[p] + jnp.sum(exps[p], axis=0, keepdims=True) for p in every]
                mixed = [dot_tn(kv[keys, pl.ds(width + p * 128, 128)], exps[p].astype(LOW)) for p in every]
                mixed = [acc_ref[p] * fades[p] + mixed[p] for p in every]
                for p in every:
                    top_ref[p] = tops[p]
                    total_ref[p] = sums[p]
                    acc_ref[p] = mixed[p]
                return carry

            lax.fori_loop(first, last, one, 0)
            stats = []
            for p in range(pairs):
                total = total_ref[p]
                safe = jnp.where(total > 0.0, total, 1.0)
                o[at, p * 128 : (p + 1) * 128] = heads_apart(acc_ref[p] * (1.0 / safe)).astype(LOW)
                lse = jnp.where(total > 0.0, top_ref[p] + jnp.log(safe), FILL)
                stats += [lse[:, :128], lse[:, 128:]]
            lse_ref[:, at] = jnp.concatenate(stats, axis=0)


def cross_forward(lengths, seg_own, seg_other, q_own, q_other, kv):
    tok_count, width = q_own.shape
    heads = width // HD
    pairs = width // 128
    out = shape_of((tok_count, width), LOW)
    lse = shape_of((heads, tok_count), WIDE)
    return pl.pallas_call(
        cross_forward_kernel,
        name="cross_forward",
        out_shape=[out, out, lse, lse],
        in_specs=[SMEM] * 3 + [VMEM] * 5,
        out_specs=[VMEM] * 4,
        scratch_shapes=[
            pltpu.SMEM((32,), jnp.int32),
            pltpu.VMEM((8, tok_count), jnp.int32),
            pltpu.VMEM((pairs, 256, 128), LOW),
            pltpu.VMEM((pairs, 1, 256), WIDE),
            pltpu.VMEM((pairs, 1, 256), WIDE),
            pltpu.VMEM((pairs, 128, 256), WIDE),
        ],
        compiler_params=pltpu.CompilerParams(vmem_limit_bytes=LIMIT),
        cost_estimate=pl.CostEstimate(flops=1 << 33, bytes_accessed=8 << 20, transcendentals=0),
    )(lengths, seg_own, seg_other, seg_own, seg_other, q_own, q_other, kv)


def cross_backward_kernel(
    lengths, seg_so, seg_sp, seg_vo, seg_vp, q_own, q_other, g_own, g_other, st_own, st_other, kv_in, pass_0, pass_1,
    dq_own, dq_other, dkv_out, given_0, given_1, ends, bounds, acc, qs, gs, dq_acc, kv, dkv, held_0, held_1, sems, io_sems,
):
    fetch = pltpu.make_async_copy(kv_in, kv, io_sems.at[0])
    fetch.start()
    ways = ((pass_0, held_0, given_0), (pass_1, held_1, given_1))
    taking = [pltpu.make_async_copy(way[0], way[1], sems.at[0, k]) for k, way in enumerate(ways)]
    giving = [pltpu.make_async_copy(way[1], way[2], sems.at[1, k]) for k, way in enumerate(ways)]
    for copy in taking:
        copy.start()
    tok_count, width = q_own.shape
    src_count = kv.shape[0]
    pairs = width // 128
    pos = lax.axis_index("src")
    off = pos * src_count
    firsts = (pos * SEGS, (1 - pos) * SEGS)
    segment_ends(lengths, ends)
    bounds[...] = key_bounds((seg_vo[...], seg_vp[...]), firsts, ends, off)
    acc[...] = jnp.zeros_like(acc)
    fetch.wait()
    sides = ((q_own, g_own, st_own, dq_own), (q_other, g_other, st_other, dq_other))
    for side, (q, g, st, dq) in enumerate(sides):

        @pl.loop(0, tok_count // 128)
        def _(block):
            at = pl.ds(pl.multiple_of(block * 128, 128), 128)
            first, last = block_ranges((seg_so, seg_sp)[side], firsts[side], ends, off, src_count, block)
            low, high = bounds[2 * side : 2 * side + 1, at], bounds[2 * side + 1 : 2 * side + 2, at]
            for p in range(pairs):
                cols = slice(p * 128, (p + 1) * 128)
                qs[p] = both_heads(q[at, cols] * SCALE)
                gs[p] = both_heads(g[at, cols])
            dq_acc[...] = jnp.zeros_like(dq_acc)
            lses = [side_by_side_rows(st, 2 * p, at) for p in range(pairs)]
            deltas = [side_by_side_rows(st, 8 + 2 * p, at) for p in range(pairs)]

            def one(t, carry):
                base = pl.multiple_of(t * TILE, TILE)
                keys = pl.ds(base, TILE)
                index = rows_of((TILE, 128)) + base
                allowed = side_by_side((index >= low) & (index < high))
                every = range(pairs)
                cols = [pl.ds(p * 128, 128) for p in every]
                vals = [pl.ds(width + p * 128, 128) for p in every]
                scores = [dot_nt(kv[keys, cols[p]], qs[p]) for p in every]
                slopes = [dot_nt(kv[keys, vals[p]], gs[p]) for p in every]
                probs = [jnp.exp(jnp.where(allowed, scores[p] - lses[p], FILL)) for p in every]
                gscores = [(probs[p] * (slopes[p] - deltas[p])).astype(LOW) for p in every]
                grad_k = [acc[keys, cols[p]] + dot(gscores[p], qs[p]) for p in every]
                grad_v = [acc[keys, vals[p]] + dot(probs[p].astype(LOW), gs[p]) for p in every]
                grad_q = [dq_acc[p] + dot_tn(kv[keys, cols[p]], gscores[p]) for p in every]
                for p in every:
                    acc[keys, cols[p]] = grad_k[p]
                    acc[keys, vals[p]] = grad_v[p]
                    dq_acc[p] = grad_q[p]
                return carry

            lax.fori_loop(first, last, one, 0)
            for p in range(pairs):
                dq[at, p * 128 : (p + 1) * 128] = (heads_apart(dq_acc[p]) * SCALE).astype(dq.dtype)

    for first, second in zip(taking, giving):
        first.wait()
        second.start()

    parts = 4
    span = src_count // parts
    stores = []
    for k in range(parts):
        at = pl.ds(k * span, span)
        dkv[at, :] = acc[at, :].astype(LOW)
        stores.append(pltpu.make_async_copy(dkv.at[at], dkv_out.at[at], io_sems.at[1 + k]))
        stores[-1].start()
    for copy in stores:
        copy.wait()
    for copy in giving:
        copy.wait()


def cross_backward(lengths, seg_own, seg_other, q_own, q_other, g_own, g_other, st_own, st_other, kv, passed):
    tok_count, width = q_own.shape
    src_count = kv.shape[0]
    pairs = width // 128
    return pl.pallas_call(
        cross_backward_kernel,
        name="cross_backward",
        out_shape=[
            shape_of((tok_count, width), WIDE),
            shape_of((tok_count, width), LOW),
            shape_of((src_count, 2 * width), LOW),
        ]
        + [shape_of(a.shape, a.dtype) for a in passed],
        in_specs=[SMEM] * 3 + [VMEM] * 8 + [ANY] * 3,
        out_specs=[VMEM] * 2 + [ANY] * 3,
        scratch_shapes=[
            pltpu.SMEM((32,), jnp.int32),
            pltpu.VMEM((8, tok_count), jnp.int32),
            pltpu.VMEM((src_count, 2 * width), WIDE),
            pltpu.VMEM((pairs, 256, 128), LOW),
            pltpu.VMEM((pairs, 256, 128), LOW),
            pltpu.VMEM((pairs, 128, 256), WIDE),
            pltpu.VMEM(kv.shape, LOW),
            pltpu.VMEM(kv.shape, LOW),
        ]
        + [pltpu.VMEM(a.shape, a.dtype) for a in passed]
        + [pltpu.SemaphoreType.DMA((2, 2)), pltpu.SemaphoreType.DMA((5,))],
        compiler_params=pltpu.CompilerParams(vmem_limit_bytes=LIMIT),
        cost_estimate=pl.CostEstimate(flops=1 << 34, bytes_accessed=16 << 20, transcendentals=0),
    )(lengths, seg_own, seg_other, seg_own, seg_other, q_own, q_other, g_own, g_other, st_own, st_other, kv, *passed)


def merge_all(parts, count):
    top = parts[0]
    for part in parts[1:]:
        top = jnp.maximum(top, part)
    total = sum(jnp.exp(part - top) for part in parts)
    return jnp.where(rows_of(top.shape) < count, top + jnp.log(total), sum(parts))


def folded(row):
    return jnp.concatenate([row[:, k : k + 128] for k in range(0, row.shape[1], 128)], axis=0)


def unfolded(rows):
    return jnp.concatenate([rows[k : k + 1] for k in range(rows.shape[0])], axis=1)


def middle_kernel(depth, split, *refs):
    (
        seg, pad, labels, counts, positions, targets, lse_own, lse_other, vocab_in, after_in, o_in, o_other, gs,
    ) = refs[:13]
    parts = refs[13 : 13 + (3 if split else 1)]
    refs = refs[13 + len(parts) :]
    count = 4 if split else 1
    sums = refs[:count]
    refs = refs[count:]
    (
        block_out, state_out, g_own, g_other, st_own, st_other, small_rows, small_cols, grad_vocab, token_out, loss_out,
    ) = refs[:11]
    (
        w_vocab, after_self, o_own, block_ref, state_ref, g_ref, vocab_ref, out_sem,
        wm, eb, eb_got, w_s, got_o, got_lse, cross_o, cross_low, ac, bs, n3, act, slope, gpre, head,
        lt, gt, pb, rb, got_rc, got_rq, got_rz, st_q, st_z, gh, g_ffn, load_sem, send, recv,
    ) = refs[11 : 11 + 37]
    sum_refs = refs[11 + 37 :]
    tok_count, width = after_self.shape
    hidden = act.shape[1]
    masked = positions.shape[1]
    vocab_local = w_vocab.shape[0]
    everyone = depth * 8
    me = Place(depth)
    z, x, c, y = me.z, me.x, me.c, me.y
    greet(me.others() + me.plane())
    used = [0]

    def push(src, dst, peer):
        k = used[0]
        used[0] += 1
        copy = remote(src, dst, send.at[k], recv.at[k], peer)
        copy.start()
        return copy

    pending = []

    def arrive(copies):
        for copy in copies:
            copy.wait_recv()
        pending.extend(copies)

    loads = []

    def load(src, dst):
        copy = pltpu.make_async_copy(src, dst, load_sem.at[len(loads)])
        copy.start()
        loads.append(copy)

    halves = 2
    span = tok_count // halves
    ranges = [pl.ds(k * span, span) for k in range(halves)]

    def swap_outputs():
        copies = [push(lse_other, got_lse, me.across_y())]
        return copies + [push(o_other.at[at], got_o.at[at], me.across_y()) for at in ranges]

    load(gs, w_s)
    load(after_in, after_self)
    load(o_in, o_own)
    load(vocab_in, w_vocab)
    shared = []
    if split:
        rest = pl.ds(PERMUTED, LATE - PERMUTED)
        soon = pl.ds(0, PERMUTED)
        late_part = [push(parts[1].at[py], wm.at[:, x, c, py, rest], me.across_x()) for py in range(2)]
        swap = swap_outputs()
        for py in range(2):
            load(parts[0].at[py], wm.at[:, x, c, py, soon])
            load(parts[1].at[py], wm.at[:, x, c, py, rest])
            load(parts[2].at[py], wm.at[:, 1 - x, c, py, soon])
            shared.append(push(parts[0].at[py], wm.at[:, x, c, py, soon], me.across_core()))
            shared.append(push(parts[1].at[py], wm.at[:, x, c, py, rest], me.across_core()))
            shared.append(push(parts[2].at[py], wm.at[:, 1 - x, c, py, soon], me.across_core()))
    else:
        swap = swap_outputs()
        load(parts[0], wm)

    def cut(lo, hi):
        value = wm[:, :, :, :, lo:hi] if split else wm[:, lo:hi]
        return value.reshape((-1, BLOCK))

    def put(lo, value, first=0, last=None, cols=slice(0, BLOCK)):
        groups, rows, wide = value.shape
        last = depth if last is None else last
        if split:
            eb[first:last, :, :, :, lo : lo + rows, cols] = value.reshape((last - first, 2, 2, 2, rows, wide))
        else:
            step = eb.shape[0] // depth
            eb[first * step : last * step, lo : lo + rows, cols] = value

    segments = seg[...].astype(WIDE)
    keep = 1.0 - pad[...].astype(WIDE)
    lane_row = lanes((1, tok_count))
    inside = lane_row < tok_count - 1

    def following(row):
        return pltpu.roll(jnp.concatenate([row, jnp.zeros((7, tok_count), WIDE)], axis=0), tok_count - 1, 1)[0:1]

    follows = inside & (following(segments) == segments) & (keep > 0.5) & (following(keep) > 0.5)
    valid = jnp.where(follows, 1.0, 0.0)
    rows = [keep, valid, labels[...].astype(WIDE), counts[...].astype(WIDE)]
    columns = transposed_rows(jnp.concatenate(rows + [jnp.zeros((4, tok_count), WIDE)], axis=0))
    col_keep, col_valid = columns[:, 0:1], columns[:, 1:2]
    col_label, col_count = columns[:, 2:3], columns[:, 3:4].astype(jnp.int32)

    for copy in loads:
        copy.wait()
    arrive(shared)
    table = w_s[...].reshape((-1, 128)).astype(WIDE).T

    outs = []

    def out(src, dst):
        copy = pltpu.make_async_copy(src, dst, out_sem.at[len(outs)])
        copy.start()
        outs.append(copy)

    blocks = hidden // BLOCK
    weight_co = cut(0, 16)
    arrive(swap[:1])
    top = jnp.maximum(lse_own[...], got_lse[...])
    lse = top + jnp.log(jnp.exp(lse_own[...] - top) + jnp.exp(got_lse[...] - top))
    shares = jnp.concatenate([jnp.exp(lse_own[...] - lse), jnp.exp(got_lse[...] - lse)], axis=0)
    shares = transposed_rows(shares)
    low_half = lanes((span, 128)) < HD
    for k, at in enumerate(ranges):
        arrive(swap[1 + k : 2 + k])
        mine = shares[k * span : (k + 1) * span]
        for p in range(width // 128):
            cols = slice(p * 128, (p + 1) * 128)
            share_own = jnp.where(low_half, mine[:, 2 * p : 2 * p + 1], mine[:, 2 * p + 1 : 2 * p + 2])
            share_got = jnp.where(low_half, mine[:, 8 + 2 * p : 9 + 2 * p], mine[:, 9 + 2 * p : 10 + 2 * p])
            mixed = o_own[at, cols].astype(WIDE) * share_own + got_o[at, cols].astype(WIDE) * share_got
            cross_o[at, cols] = mixed
            cross_low[at, cols] = mixed.astype(LOW)
        after_cross = after_self[at, :] + dot(cross_low[at, :], weight_co)
        ac[at, :] = after_cross
        normed = (normalised(after_cross)[0] * table[2:3] + table[6:7]).astype(LOW)
        n3[at, :] = normed
        if k == 0 and split:
            arrive(late_part)
            block = wm.at[:, 1 - x, c, :, rest]
            late_part = [push(block, block, me.across_core())]
        for j in range(blocks):
            cols = slice(j * BLOCK, (j + 1) * BLOCK)
            pre = dot(normed, cut(16 + 16 * j, 32 + 16 * j))
            square = pre * pre
            bent = jnp.tanh(GELU * pre * (1.0 + CUBIC * square))
            half = 0.5 * (1.0 + bent)
            act[at, cols] = (pre * half).astype(LOW)
            slope[at, cols] = half + 0.5 * pre * (1.0 - bent * bent) * (GELU * (1.0 + 3.0 * CUBIC * square))
        if k == 0 and split:
            arrive(late_part)
        state = after_cross + dot(act[at, :], cut(80, 144))
        bs[at, :] = state
        block_ref[at, :] = state.astype(LOW)
        head[at, :] = (normalised(state)[0] * table[3:4] + table[7:8]).astype(LOW)
    flat_fo = cut(80, 144)
    out(block_ref, block_out)
    head_in = head[...]

    picker = (positions[...] == rows_of((tok_count, masked))).astype(LOW)
    picked = dot_tn(picker, head_in).astype(LOW)
    kept = dot(jnp.concatenate([keep, jnp.zeros((7, tok_count), WIDE)], axis=0).astype(LOW), picker)
    code = jnp.where(kept[0:1] > 0.5, targets[...] + 1, 0)
    digits = jnp.concatenate([code >> 8, code & 255, jnp.zeros((6, masked), jnp.int32)], axis=0)
    digits = dot_tn(digits.astype(WIDE).astype(LOW), (rows_of((8, 128)) == lanes((8, 128))).astype(LOW)).astype(LOW)
    pb[z, x, c, y, :, 0:width] = picked
    pb[z, x, c, y, :, width : width + 128] = digits
    mine = pb.at[z, x, c, y]
    flight = [push(mine, mine, peer) for peer in me.others()]

    classes = BLOCK // 2
    flat_in = cut(144, 160).reshape((-1, 16, BLOCK))
    flat_in = jnp.concatenate([flat_in[:, :, :classes], flat_in[:, :, classes:]], axis=1).reshape((-1, classes))
    w_one, w_two = flat_in[:width], flat_in[width:]
    token_row = rows_of((tok_count, classes))
    ahead = pltpu.roll(dot(head_in, w_two), tok_count - 1, 0)
    logits = dot(head_in, w_one) + jnp.where(token_row == tok_count - 1, 0.0, ahead)
    top = jnp.max(logits, axis=1, keepdims=True)
    exps = jnp.exp(logits - top)
    total = jnp.sum(exps, axis=1, keepdims=True)
    hits = lanes((tok_count, classes)) == col_count
    entropy = top + jnp.log(total) - jnp.sum(jnp.where(hits, logits, 0.0), axis=1, keepdims=True)
    loss_col = col_valid * entropy
    grads = col_valid * (exps * (1.0 / total) - jnp.where(hits, 1.0, 0.0))
    g_insert = grads.astype(LOW)
    before = pltpu.roll(g_insert.astype(WIDE), 1, 0)
    g_before = jnp.where(token_row == 0, 0.0, before).astype(LOW)

    arrive(flight)
    column = pb.at[:, x, c, y]
    flight = [push(column, column, peer) for peer in (me.across_x(), me.across_y(), me.across_both())]

    flat_s = w_s[...].reshape((-1, 128))
    two = dot(head_in, flat_s)
    l_zero, l_one = two[:, 16:17], two[:, 17:18]
    top = jnp.maximum(l_zero, l_one)
    e_zero, e_one = jnp.exp(l_zero - top), jnp.exp(l_one - top)
    total = e_zero + e_one
    is_one = col_label > 0.5
    loss_col = loss_col + col_keep * (top + jnp.log(total) - jnp.where(is_one, l_one, l_zero))
    d_zero = col_keep * (e_zero / total - jnp.where(is_one, 0.0, 1.0))
    d_one = col_keep * (e_one / total - jnp.where(is_one, 1.0, 0.0))
    lane = lanes((tok_count, 128))
    g_delete = jnp.where(lane == 16, d_zero, jnp.where(lane == 17, d_one, 0.0)).astype(LOW)
    gh[...] = dot_nt(g_delete, flat_s) + dot_nt(g_insert, w_one) + dot_nt(g_before, w_two)
    arrive(flight)
    plane = pb.at[:, :, c, :]
    flight = [push(plane, plane, me.across_core())]
    small_cols[...] = dot_tn(head_in, g_delete)
    for k, grad in enumerate((g_insert, g_before)):
        pairs = dot_tn(head_in, grad).astype(LOW).reshape((-1, 2, 16, classes))
        for side in range(2):
            cols = slice(side * classes, (side + 1) * classes)
            put(144, pairs[:, side], k * (depth // 2), (k + 1) * (depth // 2), cols)
    arrive(flight)

    gathered = pb[...].reshape((-1, width + 128))
    rows_all = gathered[:, 0:width]
    numbers = gathered[:, width : width + 128].astype(WIDE).T
    code = numbers[0:1] * 256.0 + numbers[1:2]
    weight = jnp.where(code > 0.5, 1.0, 0.0)
    count = rows_all.shape[0]
    pos = lax.axis_index(BOTH)
    place = rows_of((vocab_local, count)) + pos * vocab_local
    hits = place == (code.astype(jnp.int32) - 1)
    lt[...] = dot_nt(w_vocab[...], rows_all)
    logits = lt[...]
    top = jnp.max(logits, axis=0, keepdims=True)
    total = jnp.sum(jnp.exp(logits - top), axis=0, keepdims=True)
    chosen = jnp.sum(jnp.where(hits, logits, 0.0), axis=0, keepdims=True)
    loss_here = jnp.sum(loss_col, axis=0, keepdims=True)
    folds = count // 128
    loss_rows = jnp.broadcast_to(loss_here, (8, 128))
    st_q[x, y, c] = jnp.concatenate([folded(top + jnp.log(total)), folded(chosen), loss_rows], axis=0)
    spot = st_q.at[x, y, c]
    flight = [push(spot, spot, peer) for peer in me.plane()]
    arrive(flight)
    st_z[z] = merge_all([st_q[k // 4, (k // 2) % 2, k % 2] for k in range(8)], folds)
    flight = [push(st_z.at[z], st_z.at[z], peer) for peer in me.others()]
    arrive(flight)
    stat = merge_all([st_z[k] for k in range(depth)], folds)
    all_loss = stat[2 * folds : 2 * folds + 1]
    stat = jnp.concatenate([unfolded(stat[0:folds]), unfolded(stat[folds : 2 * folds])], axis=0)
    tokens = weight * (stat[0:1] - stat[1:2])
    mine = rows_of((masked, count)) + pos * masked == lanes((masked, count))
    own = jnp.sum(jnp.where(mine, tokens, 0.0), axis=1, keepdims=True)
    token_out[...] = jnp.sum(
        jnp.where(rows_of((masked, masked)) == lanes((masked, masked)), own, 0.0), axis=0, keepdims=True
    )
    loss = (all_loss + jnp.sum(tokens, axis=1, keepdims=True)) * (1.0 / (tok_count * everyone))
    loss_out[...] = loss[:, 0:1]
    gt[...] = (weight * (jnp.exp(lt[...] - stat[0:1]) - jnp.where(hits, 1.0, 0.0))).astype(LOW)

    rb[...] = dot_tn(gt[...], w_vocab[...]).astype(LOW).reshape(rb.shape)
    flight = [push(rb.at[:, :, 1 - c], got_rc, me.across_core())]
    scale = (tok_count * everyone) ** (-0.5)
    vocab_ref[...] = dot(gt[...], rows_all) * scale
    out(vocab_ref, grad_vocab)
    arrive(flight)
    got_rc[...] = (rb[:, :, c].astype(WIDE) + got_rc[...].astype(WIDE)).astype(LOW)
    flight = [
        push(got_rc.at[:, 1 - x, y], got_rq.at[0], me.across_x()),
        push(got_rc.at[:, x, 1 - y], got_rq.at[1], me.across_y()),
        push(got_rc.at[:, 1 - x, 1 - y], got_rq.at[2], me.across_both()),
    ]
    arrive(flight)
    line = got_rc[:, x, y].astype(WIDE)
    for k in range(3):
        line = line + got_rq[k].astype(WIDE)
    got_rq[3] = line.astype(LOW)
    flight = [
        push(got_rq.at[3, lax.rem(z + k, depth)], got_rz.at[k - 1], me.along(k)) for k in range(1, depth)
    ]
    arrive(flight)
    grad_picked = got_rq[3, z].astype(WIDE)
    for k in range(1, depth):
        grad_picked = grad_picked + got_rz[k - 1].astype(WIDE)
    coarse = grad_picked.astype(LOW)
    fine = (grad_picked - coarse.astype(WIDE)).astype(LOW)
    grad_head = gh[...] + dot(picker, coarse) + dot(picker, fine)

    gh[...] = grad_head
    gain_2 = gain_3 = bias_2 = bias_3 = 0.0
    low_half = lanes((span, 128)) < HD
    lane = lanes((span, 128))
    swap, delta_rows = [], []
    for at in ranges:
        grad_block, gain, bias = norm_back(bs[at, :], table[3:4], gh[at, :])
        gain_3, bias_3 = gain_3 + gain, bias_3 + bias
        g_half = grad_block.astype(LOW)
        g_ffn[at, :] = g_half
        slopes = [dot_nt(g_half, flat_fo[j * BLOCK : (j + 1) * BLOCK]) for j in range(blocks)]
        slopes = [(slopes[j] * slope[at, j * BLOCK : (j + 1) * BLOCK]).astype(LOW) for j in range(blocks)]
        upstream = sum(dot_nt(slopes[j], cut(16 + 16 * j, 32 + 16 * j)) for j in range(blocks))
        for j in range(blocks):
            gpre[at, j * BLOCK : (j + 1) * BLOCK] = slopes[j]
        back, gain, bias = norm_back(ac[at, :], table[2:3], upstream)
        gain_2, bias_2 = gain_2 + gain, bias_2 + bias
        grad_state = grad_block + back
        state_ref[at, :] = grad_state
        g_attn = dot_nt(grad_state.astype(LOW), weight_co).astype(LOW)
        g_ref[at, :] = g_attn
        swap.append(push(g_ref.at[at], g_other.at[at], me.across_y()))
        deltas = jnp.zeros((span, 128), WIDE)
        for p in range(width // 128):
            cols = slice(p * 128, (p + 1) * 128)
            product = g_attn[:, cols].astype(WIDE) * cross_o[at, cols]
            first = jnp.sum(jnp.where(low_half, product, 0.0), axis=1, keepdims=True)
            second = jnp.sum(jnp.where(low_half, 0.0, product), axis=1, keepdims=True)
            deltas = jnp.where(lane == 2 * p, first, jnp.where(lane == 2 * p + 1, second, deltas))
        delta_rows.append(deltas.T[0:8])
    st_own[...] = jnp.concatenate([lse, jnp.concatenate(delta_rows, axis=1)], axis=0)
    swap.append(push(st_own, st_other, me.across_y()))
    out(state_ref, state_out)
    out(g_ref, g_own)
    g_cross = state_ref[...].astype(LOW)

    cores = []

    def to_core(lo, hi):
        if split:
            at = pl.ds(lo, hi - lo)
            cores.append(push(eb.at[:, :, 1 - c, :, at], eb_got.at[:, :, :, at], me.across_core()))

    to_core(144, 160)
    for j in range(blocks):
        grad = dot_tn(act[:, j * BLOCK : (j + 1) * BLOCK], g_ffn[...]).astype(LOW)
        put(80, grad.reshape((-1, 64, BLOCK)), j * depth // blocks, (j + 1) * depth // blocks)
    to_core(80, 144)
    for j in range(blocks):
        grad = dot_tn(n3[...], gpre[:, j * BLOCK : (j + 1) * BLOCK]).astype(LOW)
        put(16 + 16 * j, grad.reshape((-1, 16, BLOCK)))
    to_core(16, 80)
    put(0, dot_tn(cross_low[...], g_cross).astype(LOW).reshape((-1, 16, BLOCK)))
    to_core(0, 16)
    small_rows[...] = jnp.concatenate([gain_2, gain_3, bias_2, bias_3, jnp.zeros((4, width), WIDE)], axis=0)
    if split:
        arrive(cores)
        one, two = pl.ds(0, RETURNED), pl.ds(RETURNED, LATE - RETURNED)
        for k, (at, first, spot) in enumerate(((one, 1 - y, 1), (two, 1 - x, 0), (one, y, 1), (two, x, 0))):
            for other in range(2):
                px, py = (other, first) if spot else (first, other)

                @pl.loop(0, depth)
                def _(zz):
                    total = eb[zz, px, c, py, at].astype(WIDE) + eb_got[zz, px, py, at].astype(WIDE)
                    sum_refs[k][other, zz] = total.astype(LOW)

            out(sum_refs[k], sums[k])
    else:
        sums[0][...] = eb[...]
    arrive(swap)
    for copy in pending:
        copy.wait_send()
    for copy in outs:
        copy.wait()


def middle_part(depth, split, seg, pad, labels, counts, positions, targets, w_vocab, after_self, attended, gs, parts):
    tok_count, width = after_self.shape
    hidden = 4 * BLOCK
    vocab_local = w_vocab.shape[0]
    everyone = depth * 8
    masked = positions.shape[1]
    count = masked * everyone
    sharded = (depth, 2, 2, 2)
    lead = sharded if split else (BLOCK // 16,)
    sharded = (depth, 2, 2, 2)
    if split:
        outs = [(shape_of((2, depth, n, BLOCK), LOW), ANY) for n in (RETURNED, LATE - RETURNED)] * 2
    else:
        outs = [(shape_of(parts[0].shape, LOW), VMEM)]
    outs += [
        (shape_of((tok_count, width), LOW), ANY),
        (shape_of((tok_count, width), WIDE), ANY),
        (shape_of((tok_count, width), LOW), ANY),
        (shape_of((tok_count, width), LOW), ANY),
        (shape_of((16, tok_count), WIDE), VMEM),
        (shape_of((16, tok_count), WIDE), ANY),
        (shape_of((8, width), WIDE), VMEM),
        (shape_of((width, 128), WIDE), VMEM),
        (shape_of((vocab_local, width), WIDE), ANY),
        (shape_of((1, masked), WIDE), VMEM),
        (shape_of((1, 1), WIDE), VMEM),
    ]
    copies = 32 + 2 * (depth - 1) + 3 + 1 + 1 + 3 + 1 + 3 + (depth - 1)
    return pl.pallas_call(
        partial(middle_kernel, depth, split),
        name="middle_part",
        out_shape=[o for o, _ in outs],
        in_specs=[VMEM] * 8 + [ANY] * (5 + len(parts)),
        out_specs=[s for _, s in outs],
        scratch_shapes=[
            pltpu.VMEM((vocab_local, width), LOW),
            pltpu.VMEM((tok_count, width), WIDE),
            pltpu.VMEM((tok_count, width), LOW),
            pltpu.VMEM((tok_count, width), LOW),
            pltpu.VMEM((tok_count, width), WIDE),
            pltpu.VMEM((tok_count, width), LOW),
            pltpu.VMEM((vocab_local, width), WIDE),
            pltpu.SemaphoreType.DMA((10,)),
            pltpu.VMEM(lead + (160, BLOCK), LOW),
            pltpu.VMEM(lead + (160, BLOCK), LOW),
            pltpu.VMEM(((depth, 2, 2) if split else (1,)) + (160, BLOCK), LOW),
            pltpu.VMEM(gs.shape, LOW),
            pltpu.VMEM((tok_count, width), LOW),
            pltpu.VMEM((8, tok_count), WIDE),
            pltpu.VMEM((tok_count, width), WIDE),
            pltpu.VMEM((tok_count, width), LOW),
            pltpu.VMEM((tok_count, width), WIDE),
            pltpu.VMEM((tok_count, width), WIDE),
            pltpu.VMEM((tok_count, width), LOW),
            pltpu.VMEM((tok_count, hidden), LOW),
            pltpu.VMEM((tok_count, hidden), WIDE),
            pltpu.VMEM((tok_count, hidden), LOW),
            pltpu.VMEM((tok_count, width), LOW),
            pltpu.VMEM((vocab_local, count), WIDE),
            pltpu.VMEM((vocab_local, count), LOW),
            pltpu.VMEM(sharded + (masked, width + 128), LOW),
            pltpu.VMEM(sharded + (masked, width), LOW),
            pltpu.VMEM((depth, 2, 2, masked, width), LOW),
            pltpu.VMEM((4, depth, masked, width), LOW),
            pltpu.VMEM((max(depth - 1, 1), masked, width), LOW),
            pltpu.VMEM((2, 2, 2, 2 * (count // 128) + 8, 128), WIDE),
            pltpu.VMEM((depth, 2 * (count // 128) + 8, 128), WIDE),
            pltpu.VMEM((tok_count, width), WIDE),
            pltpu.VMEM((tok_count, width), LOW),
            pltpu.SemaphoreType.DMA((12,)),
            pltpu.SemaphoreType.DMA((copies + depth,)),
            pltpu.SemaphoreType.DMA((copies + depth,)),
        ]
        + ([pltpu.VMEM((2, depth, n, BLOCK), LOW) for n in (RETURNED, LATE - RETURNED)] * 2 if split else []),
        compiler_params=pltpu.CompilerParams(
            collective_id=1, has_side_effects=True, vmem_limit_bytes=LIMIT
        ),
    )(seg, pad, labels, counts, positions, targets, *attended[2:], w_vocab, after_self, *attended[:2], gs, *parts)


def self_backward_start(dk, dv):
    dk[...] = jnp.zeros_like(dk)
    dv[...] = jnp.zeros_like(dv)


def self_backward(blocks, qkv, out, lse_ref, g_ref, dqkv, dk, dv, row_seg, row_keep, col_seg):
    tok_count, width = out.shape
    first, last = blocks
    pairs = width // 128

    def one(block, carry):
        at = pl.ds(pl.multiple_of(block * 128, 128), 128)
        low = self_window(block, tok_count)
        keys = pl.ds(low, 384)
        allowed = twice(self_mask(row_seg, row_keep, col_seg, block, low))
        stats = lse_ref[at, :]
        every = range(pairs)
        cols = [slice(p * 128, (p + 1) * 128) for p in every]
        q = [both_heads(qkv[at, cols[p]] * SCALE) for p in every]
        g = [both_heads(g_ref[at, cols[p]]) for p in every]
        keyed = [qkv[keys, width + p * 128 : width + (p + 1) * 128] for p in every]
        scores = [dot_nt(q[p], keyed[p]) for p in every]
        slopes = [dot_nt(g[p], qkv[keys, 2 * width + p * 128 : 2 * width + (p + 1) * 128]) for p in every]
        deltas = [jnp.sum(g[p].astype(WIDE) * twice(out[at, cols[p]].astype(WIDE)), axis=1, keepdims=True) for p in every]
        lses = [jnp.concatenate([stats[:, 2 * p : 2 * p + 1], stats[:, 2 * p + 1 : 2 * p + 2]], axis=0) for p in every]
        probs = [jnp.exp(jnp.where(allowed, scores[p] - lses[p], FILL)) for p in every]
        gscores = [(probs[p] * (slopes[p] - deltas[p])).astype(LOW) for p in every]
        grad_q = [join_heads(dot(gscores[p], keyed[p])) * SCALE for p in every]
        grad_k = [dk[keys, cols[p]] + dot_tn(gscores[p], q[p]) for p in every]
        grad_v = [dv[keys, cols[p]] + dot_tn(probs[p].astype(LOW), g[p]) for p in every]
        for p in every:
            dqkv[at, cols[p]] = grad_q[p].astype(LOW)
            dk[keys, cols[p]] = grad_k[p]
            dv[keys, cols[p]] = grad_v[p]
        return carry

    lax.fori_loop(first, last, one, 0)


def self_backward_end(dqkv, dk, dv):
    width = dk.shape[1]
    dqkv[:, width : 2 * width] = dk[...].astype(LOW)
    dqkv[:, 2 * width : 3 * width] = dv[...].astype(LOW)


def reduction(me, chunks, send, recv):
    z, x, c, y = me.z, me.x, me.c, me.y
    depth = me.depth
    count = len(chunks)
    started = [[None] * 3 for _ in chunks]
    used = [0] * count

    def launch(k, stage):
        copies = []

        def push(src, dst, peer):
            slot = used[k]
            used[k] += 1
            copy = remote(src, dst, send.at[k, slot], recv.at[k, slot], peer)
            copy.start()
            copies.append(copy)

        for src, got_c, got_q, got_z, at, put in chunks[k]:
            if stage == 0:
                push(src.at[:, :, 1 - c, :, at], got_c.at[:, :, :, at], me.across_core())
            elif stage == 1:
                push(got_c.at[:, 1 - x, y, at], got_q.at[0, :, at], me.across_x())
                push(got_c.at[:, x, 1 - y, at], got_q.at[1, :, at], me.across_y())
                push(got_c.at[:, 1 - x, 1 - y, at], got_q.at[2, :, at], me.across_both())
            else:
                for j in range(1, depth):
                    push(got_c.at[lax.rem(z + j, depth), x, y, at], got_z.at[j - 1, at], me.along(j))
        started[k][stage] = copies

    def absorb(k, stage):
        for copy in started[k][stage]:
            copy.wait_recv()
        for src, got_c, got_q, got_z, at, put in chunks[k]:
            if stage == 0:

                @pl.loop(0, depth)
                def _(zz):
                    for xx in range(2):
                        for yy in range(2):
                            total = src[zz, xx, c, yy, at].astype(WIDE) + got_c[zz, xx, yy, at].astype(WIDE)
                            got_c[zz, xx, yy, at] = total.astype(LOW)

            elif stage == 1:

                @pl.loop(0, depth)
                def _(zz):
                    total = got_c[zz, x, y, at].astype(WIDE)
                    for k in range(3):
                        total = total + got_q[k, zz, at].astype(WIDE)
                    got_c[zz, x, y, at] = total.astype(LOW)

            else:
                total = got_c[z, x, y, at].astype(WIDE)
                for j in range(1, depth):
                    total = total + got_z[j - 1, at].astype(WIDE)
                put(total)

    def begin(k):
        launch(k, 0)

    def after(k, stage):
        absorb(k, stage)
        if stage < 2:
            launch(k, stage + 1)

    def end():
        for stages in started:
            for copies in stages:
                for copy in copies:
                    copy.wait_send()

    return begin, after, end


def last_kernel(depth, reduces, *refs):
    (pair, seg, pad, dq_other) = refs[:4]
    held = refs[4:15]
    (small_rows, small_cols, ga_in, gs_in) = refs[15:19]
    refs = refs[19:]
    if reduces:
        parts, refs = refs[:4], refs[4:]
    grad_input, grad_enc = refs[:2]
    refs = refs[2:]
    outs = refs[:9] if reduces else refs[:2]
    refs = refs[9:] if reduces else refs[2:]
    (dkv, enc, dq_own, start, one, qkv, low, lse, after, two, gstate) = refs[:11]
    (ga, gs, g_query, g_attn, dqkv, dk, dv, row_seg, row_keep, col_seg, load_sem, dq_got, sw_send, sw_recv) = refs[11:25]
    refs = refs[25:]
    refs_held = (dkv, enc, dq_own, start, one, qkv, low, lse, after, two, gstate)
    tok_count, width = dq_own.shape
    src_count = enc.shape[0]
    everyone = depth * 8
    me = Place(depth)
    scale = (tok_count * everyone) ** (-0.5)
    loads = []
    for src, dst in list(zip(held, refs_held)) + [(gs_in, gs), (ga_in, ga)]:
        copy = pltpu.make_async_copy(src, dst, load_sem.at[len(loads)])
        copy.start()
        loads.append(copy)
    if reduces:
        greet(me.others() + [me.across_x(), me.across_y(), me.across_both(), me.across_core()])
    else:
        greet([me.across_y()])
    halves = 2
    half = tok_count // halves
    swaps = []
    for k in range(halves):
        at = pl.ds(k * half, half)
        swaps.append(remote(dq_other.at[at], dq_got.at[at], sw_send.at[k], sw_recv.at[k], me.across_y()))
        swaps[-1].start()

    if reduces:
        (late, late_s, ex, ey, ex_got, ey_got, ez, ez_got, c_a, c_s, q_a, q_s, z_a, z_s, ez_send, ez_recv, send, recv) = refs
        (o_qkv, o_so, o_cq, o_kv, o_co, o_fi, o_fo, o_in, o_s) = outs

        def put_kv(total):
            o_kv[:, 0:BLOCK] = total[0:16] * scale
            o_kv[:, BLOCK : 2 * BLOCK] = total[16:32] * scale

        def put_mid(total):
            o_so[...] = total[0:16] * scale
            o_cq[...] = total[16:32] * scale

        def put_qkv(k, total):
            o_qkv[:, k * BLOCK : (k + 1) * BLOCK] = total * scale

        def put_s(total):
            o_s[...] = total * scale

        def rows(lo, hi, put):
            return (late, c_a, q_a, z_a, pl.ds(lo, hi - lo), put)

        chunks = [
            [rows(KV, EARLY, put_kv)],
            [rows(SO, KV, put_mid)],
            [rows(0, 16, partial(put_qkv, 0))],
            [rows(16, 32, partial(put_qkv, 1))],
            [rows(32, SO, partial(put_qkv, 2))],
            [(late_s, c_s, q_s, z_s, pl.ds(0, 16), put_s)],
        ]

        z, x, y = me.z, me.x, me.y
        for total, own, got in ((ex, parts[0], parts[1]), (ey, parts[2], parts[3])):

            @pl.loop(0, depth)
            def _(zz):
                for k in range(2):
                    total[k, zz] = (own[k, zz].astype(WIDE) + got[k, zz].astype(WIDE)).astype(LOW)

        plane = [
            remote(ex.at[1 - x], ex_got, ez_send.at[0], ez_recv.at[0], me.across_x()),
            remote(ey.at[1 - y], ey_got, ez_send.at[1], ez_recv.at[1], me.across_y()),
        ]
        for copy in plane:
            copy.start()
        along = []

        def onward():
            for copy in plane:
                copy.wait_recv()

            @pl.loop(0, depth)
            def _(zz):
                ez[zz, 0:RETURNED] = (ex[x, zz].astype(WIDE) + ex_got[zz].astype(WIDE)).astype(LOW)
                ez[zz, RETURNED:LATE] = (ey[y, zz].astype(WIDE) + ey_got[zz].astype(WIDE)).astype(LOW)

            for k in range(1, depth):
                to = lax.rem(z + k, depth)
                at = 1 + k
                along.append(remote(ez.at[to], ez_got.at[k - 1], ez_send.at[at], ez_recv.at[at], me.along(k)))
                along[-1].start()

        def settle():
            for copy in plane:
                copy.wait_send()
            for copy in along:
                copy.wait()
            total = ez[me.z].astype(WIDE)
            for k in range(depth - 1):
                total = total + ez_got[k].astype(WIDE)
            total = total * scale
            o_co[...] = total[0:16]
            for k in range(4):
                o_fi[:, k * BLOCK : (k + 1) * BLOCK] = total[16 + 16 * k : 32 + 16 * k]
            o_fo[...] = total[80:144]
            half = BLOCK // 2
            for k in range(2):
                o_in[16 * k : 16 * (k + 1)] = total[144:160, half * k : half * (k + 1)]

        begin, after_stage, end = reduction(me, chunks, send, recv)

        def keep(lo, value):
            late[:, :, :, :, lo : lo + 16] = value.astype(LOW).reshape(late.shape[:4] + (16, BLOCK))

        def keep_small(value):
            late_s[...] = value.astype(LOW).reshape(late_s.shape)
    else:
        def begin(k):
            return None

        def after_stage(k, stage):
            return None

        end = onward = settle = lambda: None
        o_late, o_small = outs

        def keep(lo, value):
            o_late[:, lo : lo + 16] = value.astype(LOW).reshape((-1, 16, BLOCK))

        def keep_small(value):
            o_small[...] = value

    chunk_kv, chunk_mid, chunk_q, chunk_k, chunk_v, chunk_s = range(6)
    onehot = token_numbers(seg, pad, pair, row_seg, row_keep, col_seg)
    cut = cutter(ga)
    for copy in loads[:2]:
        copy.wait()
    keep(KV, dot_tn(enc[...], dkv[:, 0:width]))
    keep(KV + 16, dot_tn(enc[...], dkv[:, width : 2 * width]))
    begin(chunk_kv)
    for copy in loads[2:]:
        copy.wait()
    table = cutter(gs)(0, gs.shape[-2]).astype(WIDE).T
    self_backward_start(dk, dv)
    gains = biases = 0.0
    for k in range(halves):
        at = pl.ds(k * half, half)
        swaps[k].wait()
        query = (dq_own[at, :] + dq_got[at, :].astype(WIDE)).astype(LOW)
        g_query[at, :] = query
        back, gain_1, bias_1 = norm_back(after[at, :], table[1:2], dot_nt(query, cut(CQ, KV)))
        gains, biases = gains + gain_1, biases + bias_1
        state = gstate[at, :] + back
        gstate[at, :] = state
        g_attn[at, :] = dot_nt(state.astype(LOW), cut(SO, CQ)).astype(LOW)
        if k == 0:
            after_stage(chunk_kv, 0)
        if k == halves - 1:
            keep(CQ, dot_tn(two[...], g_query[...]))
            keep(SO, dot_tn(low[...], gstate[...].astype(LOW)))
            begin(chunk_mid)
        blocks = (k * half // 128, (k + 1) * half // 128)
        self_backward(blocks, qkv, low, lse, g_attn, dqkv, dk, dv, row_seg, row_keep, col_seg)
        if k == 0:
            onward()
    after_stage(chunk_mid, 0)
    self_backward_end(dqkv, dk, dv)
    for k, chunk in enumerate((chunk_q, chunk_k, chunk_v)):
        keep(QKV + 16 * k, dot_tn(one[...], dqkv[:, k * width : (k + 1) * width]))
        begin(chunk)
    after_stage(chunk_q, 0)
    after_stage(chunk_k, 0)
    after_stage(chunk_v, 0)
    after_stage(chunk_kv, 1)
    upstream = dot_nt(dqkv[:, 0:width], cut(QKV, QKV + 16))
    upstream = upstream + dot_nt(dqkv[:, width : 2 * width], cut(QKV + 16, QKV + 32))
    upstream = upstream + dot_nt(dqkv[:, 2 * width : 3 * width], cut(QKV + 32, SO))
    back, gain_0, bias_0 = norm_back(start[...], table[0:1], upstream)
    grad_start = gstate[...] + back
    grad_input[...] = grad_start.astype(LOW)
    coarse = grad_start.astype(LOW)
    fine = (grad_start - coarse.astype(WIDE)).astype(LOW)
    g_table = (dot_tn(onehot, coarse) + dot_tn(onehot, fine))[8:16]
    mid = small_rows[...]
    stacked = jnp.concatenate([gain_0, gains, mid[0:2], bias_0, biases, mid[2:4], g_table], axis=0)
    keep_small(transposed_rows(stacked) + small_cols[...])
    begin(chunk_s)
    after_stage(chunk_mid, 1)
    w_key, w_val = cut(KV, KV + 16), cut(KV + 16, EARLY)
    span = src_count // 4

    def source_grads(k):
        at = pl.ds(k * span, span)
        grads = dot_nt(dkv[at, 0:width], w_key) + dot_nt(dkv[at, width : 2 * width], w_val)
        grad_enc[at, :] = grads.astype(LOW)

    source_grads(0)
    after_stage(chunk_s, 0)
    after_stage(chunk_kv, 2)
    after_stage(chunk_q, 1)
    source_grads(1)
    after_stage(chunk_k, 1)
    source_grads(2)
    after_stage(chunk_v, 1)
    after_stage(chunk_s, 1)
    source_grads(3)
    settle()
    for chunk in (chunk_mid, chunk_q, chunk_k, chunk_v, chunk_s):
        after_stage(chunk, 2)
    end()


def last_part(depth, reduces, pair, seg, pad, dq_own, dq_other, dkv, enc, kept, gstate, grads, whole):
    tok_count, width = dq_own.shape
    src_count = enc.shape[0]
    ga, gs = whole
    parts, small_rows, small_cols = grads
    everyone = depth * 8
    rows = BLOCK // everyone
    sharded = (depth, 2, 2, 2)
    held = (dkv, enc, dq_own, *kept, gstate)
    outs = [shape_of((tok_count, width), LOW), shape_of((src_count, width), LOW)]
    scratch = [pltpu.VMEM(a.shape, a.dtype) for a in held]
    scratch += [
        pltpu.VMEM(ga.shape, LOW),
        pltpu.VMEM(gs.shape, LOW),
        pltpu.VMEM((tok_count, width), LOW),
        pltpu.VMEM((tok_count, width), LOW),
        pltpu.VMEM((tok_count, 3 * width), LOW),
        pltpu.VMEM((tok_count, width), WIDE),
        pltpu.VMEM((tok_count, width), WIDE),
        pltpu.VMEM((1, tok_count), WIDE),
        pltpu.VMEM((1, tok_count), WIDE),
        pltpu.VMEM((tok_count, 128), WIDE),
        pltpu.SemaphoreType.DMA((14,)),
        pltpu.VMEM((tok_count, width), LOW),
        pltpu.SemaphoreType.DMA((2,)),
        pltpu.SemaphoreType.DMA((2,)),
    ]
    if reduces:
        shapes = [(EARLY, BLOCK), (16, 128)]
        outs += [
            shape_of((rows, 3 * BLOCK), WIDE),
            shape_of((rows, BLOCK), WIDE),
            shape_of((rows, BLOCK), WIDE),
            shape_of((rows, 2 * BLOCK), WIDE),
            shape_of((rows, BLOCK), WIDE),
            shape_of((rows, 4 * BLOCK), WIDE),
            shape_of((4 * rows, BLOCK), WIDE),
            shape_of((2 * rows, BLOCK // 2), WIDE),
            shape_of((rows, 128), WIDE),
        ]
        scratch += [pltpu.VMEM(sharded + s, LOW) for s in shapes]
        scratch += [pltpu.VMEM(parts[0].shape, LOW), pltpu.VMEM(parts[2].shape, LOW)]
        scratch += [pltpu.VMEM(parts[0].shape[1:], LOW), pltpu.VMEM(parts[2].shape[1:], LOW)]
        scratch += [pltpu.VMEM((depth, LATE, BLOCK), LOW), pltpu.VMEM((depth - 1, LATE, BLOCK), LOW)]
        for lead in ((depth, 2, 2), (3, depth), (depth - 1,)):
            scratch += [pltpu.VMEM(lead + s, LOW) for s in shapes]
        scratch += [pltpu.SemaphoreType.DMA((depth + 2,))] * 2
        slots = 2 * (depth + 3)
        scratch += [pltpu.SemaphoreType.DMA((6, slots)), pltpu.SemaphoreType.DMA((6, slots))]
    else:
        outs += [shape_of((BLOCK // 16, EARLY, BLOCK), LOW), shape_of((BLOCK, 128), WIDE)]
    return pl.pallas_call(
        partial(last_kernel, depth, reduces),
        name="last_part",
        out_shape=outs,
        in_specs=[SMEM] + [VMEM] * 2 + [ANY] * 12 + [VMEM] * 2 + [ANY] * 2 + [VMEM] * len(parts),
        out_specs=[VMEM] * len(outs),
        scratch_shapes=scratch,
        compiler_params=pltpu.CompilerParams(
            collective_id=2, has_side_effects=True, vmem_limit_bytes=LIMIT
        ),
    )(pair, seg, pad, dq_other, *held, small_rows, small_cols, ga, gs, *parts)


def finish_kernel(count, *refs):
    ins, small, loss = refs[:count], refs[count], refs[count + 1]
    refs = refs[count + 2 :]
    outs, (gain, bias, table, delete, loss_out) = refs[:count], refs[count : count + 5]
    held, sems = refs[count + 5 : 2 * count + 5], refs[2 * count + 5]
    first = [pltpu.make_async_copy(ins[k], held[k], sems.at[0, k]) for k in range(count)]
    copies = [pltpu.make_async_copy(held[k], outs[k], sems.at[1, k]) for k in range(count)]
    for copy in first:
        copy.start()
    values = small[...]
    shape = (values.shape[0], values.shape[0])
    turned = jnp.concatenate([values, jnp.zeros((128 - values.shape[0], 128), WIDE)], axis=0).T
    gain[...] = turned[0:4, 0 : shape[0]]
    bias[...] = turned[4:8, 0 : shape[0]]
    table[...] = turned[8:16, 0 : shape[0]]
    delete[...] = turned[16:18, 0 : shape[0]]
    loss_out[...] = loss[...]
    for before, copy in zip(first, copies):
        before.wait()
        copy.start()
    for copy in copies:
        copy.wait()


def finish(results, small, loss):
    count = len(results)
    rows = small.shape[0]
    outs = [shape_of(a.shape, a.dtype) for a in results]
    outs += [shape_of(s, WIDE) for s in ((4, rows), (4, rows), (PAIRS, rows), (2, rows), (1, 1))]
    res = pl.pallas_call(
        partial(finish_kernel, count),
        name="finish",
        out_shape=outs,
        in_specs=[ANY] * count + [VMEM] * 2,
        out_specs=[ANY] * count + [VMEM] * 5,
        scratch_shapes=[pltpu.VMEM(a.shape, a.dtype) for a in results] + [pltpu.SemaphoreType.DMA((2, count))],
        compiler_params=pltpu.CompilerParams(vmem_limit_bytes=LIMIT),
    )(*results, small, loss)
    return res[:count], res[count:]


def late_blocks(cross_out, ffn_in, ffn_out, insert):
    groups = cross_out.shape[0] // 16
    return jnp.concatenate(
        [
            cross_out.reshape(groups, 16, BLOCK),
            ffn_in.reshape(groups, 16, 4, BLOCK).swapaxes(1, 2).reshape(groups, 64, BLOCK),
            ffn_out.reshape(groups, 64, BLOCK),
            insert.reshape(groups, 2, 16, BLOCK // 2).swapaxes(1, 2).reshape(groups, 16, BLOCK),
        ],
        axis=1,
    )


def gather_by_ops(qkv, self_out, cross_q, cross_kv, small):
    wide = jnp.concatenate([qkv, self_out, cross_q, cross_kv], axis=1)
    ga = lax.all_gather(wide, BOTH, axis=0, tiled=True).reshape(-1, 16, 7, BLOCK).swapaxes(1, 2)
    gs = lax.all_gather(small, BOTH, axis=0, tiled=True)
    return ga.reshape(-1, EARLY, BLOCK), gs.reshape(-1, 16, 128)


def partner(array, depth, axis):
    dx, dy = (1, 0) if axis == "x" else (0, 1)
    pairs = []
    for z in range(depth):
        for x in range(2):
            for c in range(2):
                for y in range(2):
                    here = ((z * 2 + x) * 2 + c) * 2 + y
                    there = ((z * 2 + (x ^ dx)) * 2 + c) * 2 + (y ^ dy)
                    pairs.append((here, there))
    return lax.ppermute(array, BOTH, pairs)


def reduce_by_ops(early, small, late, scale):
    groups = late.shape[0]
    gw_f = late[:, 80:144].reshape(groups * 64, BLOCK)
    gw_i = late[:, 144:160].reshape(groups, 16, 2, BLOCK // 2).swapaxes(1, 2).reshape(groups * 32, BLOCK // 2)
    late = late[:, 0:80].reshape(groups, 5, 16, BLOCK).swapaxes(0, 1).reshape(5, BLOCK, BLOCK)
    early = early.reshape(groups, 7, 16, BLOCK).swapaxes(0, 1).reshape(7, BLOCK, BLOCK)
    wide = jnp.concatenate([early, late]).swapaxes(0, 1).reshape(BLOCK, 12 * BLOCK)

    def sums(a):
        return lax.psum_scatter(a.astype(WIDE), BOTH, scatter_dimension=0, tiled=True) * scale

    own = sums(wide)
    edges = (0, 3, 4, 5, 7, 8, 12)
    pieces = [own[:, lo * BLOCK : hi * BLOCK] for lo, hi in zip(edges[:-1], edges[1:])]
    return pieces + [sums(gw_f), sums(gw_i), sums(small)]


def body(
    dec_input, enc_output, segment_ids, padding, pair_ids, src_lengths, delete_labels, insert_counts,
    masked_positions, masked_targets, norm_gain, norm_bias, pair_table, self_qkv, self_out, cross_q, cross_kv,
    cross_out, ffn_in, ffn_out, w_delete, w_insert, w_vocab,
):
    everyone = lax.axis_size(BOTH)
    depth = everyone // 8
    tok_count = dec_input.shape[0]
    aligned = self_qkv.shape[0] == 16
    late = (cross_out, ffn_in, ffn_out, w_insert)
    tiny = (norm_gain, norm_bias, pair_table, w_delete.T)
    raw = (self_qkv, self_out, cross_q, cross_kv)
    whole = gathered = None
    if not aligned:
        gathered = late_blocks(*[lax.all_gather(a, BOTH, axis=0, tiled=True) for a in late])
        small = jnp.concatenate([norm_gain, norm_bias, pair_table, w_delete.T], axis=0).T
        small = jnp.pad(small, ((0, 0), (0, 128 - small.shape[1])))
        whole = gather_by_ops(*raw, small)
    whole, line, firsts = first_part(
        depth, aligned, segment_ids, padding, pair_ids, dec_input, enc_output, tiny, raw, late, whole
    )
    start, one, qkv, low, lse, after, two, query, other_query, kv, other_seg = firsts
    parts = (*line, partner(line[0], depth, "x")) if aligned else (gathered,)
    o_own, o_other, lse_own, lse_other = cross_forward(src_lengths, segment_ids, other_seg, query, other_query, kv)
    mids = middle_part(
        depth, aligned, segment_ids, padding, delete_labels, insert_counts, masked_positions, masked_targets,
        w_vocab, after, (o_own, o_other, lse_own, lse_other), whole[1], parts,
    )
    count = 4 if aligned else 1
    parts, mids = mids[:count], mids[count:]
    block_out, gstate, g_own, g_other, st_own, st_other, small_rows, small_cols, grad_vocab, tokens, loss = mids
    sums = ()
    if aligned:
        sums = (parts[2], partner(parts[0], depth, "y"), parts[3], partner(parts[1], depth, "x"))
    dq_own, dq_other, dkv, block_out, grad_vocab = cross_backward(
        src_lengths, segment_ids, other_seg, query, other_query, g_own, g_other, st_own, st_other, kv,
        (block_out, grad_vocab),
    )
    res = last_part(
        depth, aligned, pair_ids, segment_ids, padding, dq_own, dq_other, dkv, enc_output,
        (start, one, qkv, low, lse, after, two), gstate, (sums, small_rows, small_cols), whole,
    )
    if aligned:
        sums = res[2:]
    else:
        scale = (tok_count * everyone) ** (-0.5)
        sums = reduce_by_ops(res[2], res[3], parts[0], scale)
    results, smalls = finish((res[1], res[0], *sums[:8], tokens), sums[8], loss)
    grad_enc, grad_input, qkv, so, cq, kv, co, fi, fo, insert, tokens = results
    gain, bias, table, delete, loss = smalls
    return (
        block_out, grad_input, grad_enc, gain, bias, table, qkv, so, cq, kv, co, fi, fo, delete.T, insert,
        grad_vocab, loss[0, 0], tokens,
    )


def solution(mesh):
    shared = P(BOTH, None)
    across = P(None, BOTH)
    return jax.shard_map(
        body,
        mesh=mesh,
        in_specs=(shared,) * 5 + (P("batch", None),) + (shared,) * 4 + (across,) * 3 + (shared,) * 10,
        out_specs=(shared,) * 3 + (across,) * 3 + (shared,) * 10 + (P(), shared),
        check_vma=False,
    )
```

```python
from functools import partial

import jax
import jax.numpy as jnp
from jax import lax
from jax.experimental import pallas as pl
from jax.experimental.pallas import tpu as pltpu
from jax.sharding import PartitionSpec as P

HD = 64
PAIRS = 8
SEGS = 8
BLOCK = 512
EPSILON = 1e-05
SCALE = 0.125
FILL = -1e30
GELU = 0.7978845608
CUBIC = 0.044715

MESH = pl.DeviceIdType.MESH
ANY = pl.BlockSpec(memory_space=pl.ANY)
VMEM = pl.BlockSpec(memory_space=pltpu.VMEM)
SMEM = pl.BlockSpec(memory_space=pltpu.SMEM)
BOTH = ("batch", "src")
LOW = jnp.bfloat16
WIDE = jnp.float32
LIMIT = 64 << 20


def shape_of(shape, kind):
    return jax.ShapeDtypeStruct(shape, kind)


def dot(left, right):
    return jnp.dot(left, right, preferred_element_type=WIDE)


def dot_tn(left, right):
    return lax.dot_general(left, right, (((0,), (0,)), ((), ())), preferred_element_type=WIDE)


def dot_nt(left, right):
    return lax.dot_general(left, right, (((1,), (1,)), ((), ())), preferred_element_type=WIDE)


def normalised(v):
    centred = v - jnp.mean(v, axis=-1, keepdims=True)
    r = lax.rsqrt(jnp.mean(centred * centred, axis=-1, keepdims=True) + EPSILON)
    return centred * r, r


def norm_back(v, gain, upstream):
    hat, r = normalised(v)
    scaled = upstream * gain
    first = jnp.mean(scaled, axis=-1, keepdims=True)
    second = jnp.mean(scaled * hat, axis=-1, keepdims=True)
    grad_gain = jnp.sum(upstream * hat, axis=0, keepdims=True)
    grad_bias = jnp.sum(upstream, axis=0, keepdims=True)
    return r * (scaled - first - hat * second), grad_gain, grad_bias


def lanes(shape):
    return lax.broadcasted_iota(jnp.int32, shape, len(shape) - 1)


def rows_of(shape):
    return lax.broadcasted_iota(jnp.int32, shape, len(shape) - 2)


def both_heads(x):
    low = lanes(x.shape) < HD
    zero = jnp.zeros_like(x)
    return jnp.concatenate([jnp.where(low, x, zero), jnp.where(low, zero, x)], axis=0)


def join_heads(x):
    half = x.shape[0] // 2
    return jnp.where(lanes((half, x.shape[1])) < HD, x[:half], x[half:])


def twice(x):
    return jnp.concatenate([x, x], axis=0)


def transposed_rows(rows):
    count, width = rows.shape
    return jnp.concatenate([rows, jnp.zeros((128 - count, width), WIDE)], axis=0).T


def greet(peers):
    barrier = pltpu.get_barrier_semaphore()
    for peer in peers:
        pl.semaphore_signal(barrier, inc=1, device_id=peer, device_id_type=MESH)
    pl.semaphore_wait(barrier, len(peers))


def remote(src, dst, send, recv, peer):
    return pltpu.make_async_remote_copy(
        src_ref=src,
        dst_ref=dst,
        send_sem=send,
        recv_sem=recv,
        device_id=peer,
        device_id_type=MESH,
    )


class Place:
    def __init__(self, depth):
        b = lax.axis_index("batch")
        self.depth = depth
        self.y = lax.axis_index("src")
        self.c = lax.rem(b, 2)
        self.x = lax.rem(b // 2, 2)
        self.z = b // 4

    def at(self, z=None, x=None, c=None, y=None):
        z = self.z if z is None else z
        x = self.x if x is None else x
        c = self.c if c is None else c
        y = self.y if y is None else y
        return ((z * 2 + x) * 2 + c, y)

    def along(self, k):
        return self.at(z=lax.rem(self.z + k, self.depth))

    def others(self):
        return [self.along(k) for k in range(1, self.depth)]

    def across_x(self):
        return self.at(x=1 - self.x)

    def across_y(self):
        return self.at(y=1 - self.y)

    def across_both(self):
        return self.at(x=1 - self.x, y=1 - self.y)

    def across_core(self):
        return self.at(c=1 - self.c)


def gathering(me, chunks, send, recv):
    z, x, c, y = me.z, me.x, me.c, me.y
    started = [[None] * 3 for _ in chunks]
    used = [0] * len(chunks)
    every = slice(None)

    def launch(k, stage):
        copies = []

        def push(block, peer):
            slot = used[k]
            used[k] += 1
            copy = remote(block, block, send.at[k, slot], recv.at[k, slot], peer)
            copy.start()
            copies.append(copy)

        for view in chunks[k]:
            if stage == 0:
                for peer in me.others():
                    push(view(z, x, c, y), peer)
            elif stage == 1:
                for peer in (me.across_x(), me.across_y(), me.across_both()):
                    push(view(every, x, c, y), peer)
            else:
                push(view(every, every, c, every), me.across_core())
        started[k][stage] = copies

    def begin(k):
        launch(k, 0)

    def after(k, stage):
        for copy in started[k][stage]:
            copy.wait_recv()
        if stage < 2:
            launch(k, stage + 1)

    def end():
        for stages in started:
            for copies in stages:
                for copy in copies:
                    copy.wait_send()

    return begin, after, end


def self_window(block, tok_count):
    low = jnp.clip(block * 128 - 128, 0, tok_count - 384)
    return pl.multiple_of(low, 128)


def self_mask(row_seg, row_keep, col_seg, block, low):
    at = pl.ds(low, 384)
    keys = row_seg[0:1, at]
    keep = row_keep[0:1, at]
    queries = col_seg[pl.ds(pl.multiple_of(block * 128, 128), 128), 0:1]
    shape = (128, 384)
    own = (rows_of(shape) + block * 128) == (lanes(shape) + low)
    return (queries == keys) & ((keep > 0.5) | own)


def self_forward(blocks, qkv, out, lse_ref, row_seg, row_keep, col_seg):
    tok_count, width = out.shape
    first, last = blocks
    pairs = width // 128

    def one(block, carry):
        at = pl.ds(pl.multiple_of(block * 128, 128), 128)
        low = self_window(block, tok_count)
        keys = pl.ds(low, 384)
        allowed = twice(self_mask(row_seg, row_keep, col_seg, block, low))
        every = range(pairs)
        q = [both_heads(qkv[at, p * 128 : (p + 1) * 128] * SCALE) for p in every]
        scores = [dot_nt(q[p], qkv[keys, width + p * 128 : width + (p + 1) * 128]) for p in every]
        scores = [jnp.where(allowed, scores[p], FILL) for p in every]
        tops = [jnp.max(scores[p], axis=1, keepdims=True) for p in every]
        exps = [jnp.exp(scores[p] - tops[p]) for p in every]
        totals = [jnp.sum(exps[p], axis=1, keepdims=True) for p in every]
        probs = [(exps[p] * (1.0 / totals[p])).astype(LOW) for p in every]
        mixed = [dot(probs[p], qkv[keys, 2 * width + p * 128 : 2 * width + (p + 1) * 128]) for p in every]
        lane = lanes((128, 128))
        stats = jnp.zeros((128, 128), WIDE)
        for p in every:
            out[at, p * 128 : (p + 1) * 128] = join_heads(mixed[p]).astype(LOW)
            lse = tops[p] + jnp.log(totals[p])
            stats = jnp.where(lane == 2 * p, lse[:128], jnp.where(lane == 2 * p + 1, lse[128:], stats))
        lse_ref[at, :] = stats
        return carry

    lax.fori_loop(first, last, one, 0)


def small_matrix(gain, bias, pair_rows, delete):
    def spot(count, first):
        shape = (count, 128)
        return (rows_of(shape) + first == lanes(shape)).astype(LOW)

    total = dot_tn(gain, spot(4, 0)) + dot_tn(bias, spot(4, 4)) + dot_tn(pair_rows, spot(PAIRS, 8))
    return (total + dot_tn(delete, spot(2, 8 + PAIRS))).astype(LOW)


def token_numbers(seg, pad, pair, row_seg, row_keep, col_seg):
    tok_count = seg.shape[1]
    segments = seg[...].astype(WIDE)
    row_seg[...] = segments
    row_keep[...] = 1.0 - pad[...].astype(WIDE)
    pair_row = jnp.zeros((1, tok_count), WIDE)
    for k in range(SEGS):
        pair_row = jnp.where(segments == k, pair[0, k].astype(WIDE), pair_row)
    columns = transposed_rows(jnp.concatenate([segments, pair_row, jnp.zeros((6, tok_count), WIDE)], axis=0))
    col_seg[...] = columns
    return (lanes((tok_count, 128)) == (columns[:, 1:2].astype(jnp.int32) + 8)).astype(LOW)


def cutter(ref):
    every = (slice(None),) * (len(ref.shape) - 2)

    def cut(lo, hi):
        value = ref[every + (slice(lo, hi),)]
        return value.reshape((-1, value.shape[-1]))

    return cut


QKV, SO, CQ, KV, EARLY = 0, 48, 64, 80, 112
LATE, PERMUTED, RETURNED = 160, 96, 128


def first_kernel(depth, gathers, *refs):
    (seg, pad, pair, dec, enc_in) = refs[:5]
    refs = refs[5:]
    if gathers:
        (gain, bias, pair_rows, delete, raw_qkv, raw_so, raw_cq, raw_kv, raw_co, raw_fi, raw_fo, raw_in) = refs[:12]
        (ga_out, gs_out, gz1, gz2) = refs[12:16]
        refs = refs[16:]
    else:
        ga_in, gs_in = refs[:2]
        refs = refs[2:]
    results, other_out, seg_out = refs[:9], refs[9], refs[10]
    held = refs[11:20]
    (start_ref, one_ref, qkv, low, lse, after_ref, two_ref, query, kv) = held
    (enc, ga, gs, row_seg, row_keep, col_seg, own_sem, out_sem, send, recv, sw_send, sw_recv, stage1, stage2) = refs[20:]
    tok_count, width = dec.shape
    src_count = enc.shape[0]
    me = Place(depth)
    z, x, c, y = me.z, me.x, me.c, me.y
    owns = []

    def own(src, dst):
        copy = pltpu.make_async_copy(src, dst, own_sem.at[len(owns)])
        copy.start()
        owns.append(copy)

    if gathers:
        for raw, count, first in ((raw_qkv, 3, QKV), (raw_so, 1, SO), (raw_cq, 1, CQ), (raw_kv, 2, KV)):
            for k in range(count):
                own(raw.at[:, pl.ds(k * BLOCK, BLOCK)], ga.at[z, x, c, y, pl.ds(first + 16 * k, 16)])
        soon = len(owns)
        own1, own2 = stage1, stage2
        split_fo = PERMUTED - 80
        own(raw_co, own1.at[pl.ds(0, 16)])
        for k in range(4):
            own(raw_fi.at[:, pl.ds(k * BLOCK, BLOCK)], own1.at[pl.ds(16 + 16 * k, 16)])
        own(raw_fo.at[pl.ds(0, split_fo)], own1.at[pl.ds(80, split_fo)])
        own(raw_fo.at[pl.ds(split_fo, 64 - split_fo)], own2.at[pl.ds(0, 64 - split_fo)])
        for k in range(2):
            half = BLOCK // 2
            place = own2.at[pl.ds(64 - split_fo, 16), pl.ds(half * k, half)]
            own(raw_in.at[pl.ds(16 * k, 16)], place)
        gs[z, x, c, y] = small_matrix(gain[...], bias[...], pair_rows[...], delete[...])
        greet(me.others() + [me.across_x(), me.across_y(), me.across_both(), me.across_core()])
        for copy in owns[:soon]:
            copy.wait()

        def rows(lo, hi):
            return lambda *at: ga.at[at + (pl.ds(lo, hi - lo),)]

        chunks = [[lambda *at: gs.at[at]]]
        chunks += [[rows(lo, hi)] for lo, hi in ((0, 16), (16, 32), (32, SO), (SO, KV), (KV, EARLY))]
        begin, after_stage, end = gathering(me, chunks, send, recv)
    else:
        own(ga_in, ga)
        own(gs_in, gs)
        greet([me.across_y()])
        for copy in owns:
            copy.wait()

        def begin(k):
            return None

        def after_stage(k, stage):
            return None

        def end():
            return None

    outs = []

    def out(k):
        copy = pltpu.make_async_copy(held[k], results[k], out_sem.at[len(outs)])
        copy.start()
        outs.append(copy)

    c_s, c_q, c_k, c_v, c_mid, c_kv = range(6)
    begin(c_s)
    begin(c_q)
    line, crossing = [], []
    if gathers:
        for copy in owns[soon:]:
            copy.wait()
        kept = len(owns)
        for k, (ref, spot) in enumerate(((own1, gz1.at[y, z]), (own2, gz2.at[y, z]))):
            crossing.append(remote(ref, spot, sw_send.at[3 + k], sw_recv.at[3 + k], me.across_y()))
            crossing[-1].start()
            own(ref, spot)
    meet = remote(seg, seg_out, sw_send.at[0], sw_recv.at[0], me.across_y())
    meet.start()
    fetch = pltpu.make_async_copy(enc_in, enc, out_sem.at[11])
    fetch.start()
    onehot = token_numbers(seg, pad, pair, row_seg, row_keep, col_seg)
    cut = cutter(ga)
    after_stage(c_s, 0)
    after_stage(c_q, 0)
    begin(c_k)
    after_stage(c_k, 0)
    begin(c_v)
    after_stage(c_s, 1)
    after_stage(c_q, 1)
    after_stage(c_v, 0)
    begin(c_mid)
    begin(c_kv)
    for copy in crossing:
        copy.wait()
    if gathers:
        for copy in owns[kept:]:
            copy.wait()
        far, near = me.along(depth // 2), me.at(z=z + 1 - 2 * lax.rem(z, 2))
        z_far = lax.rem(z + depth // 2, depth)

        def along(ref, peer):
            at = 5 + len(line)
            line.append(remote(ref, ref, sw_send.at[at], sw_recv.at[at], peer))
            line[-1].start()

        for ref in (gz1.at[:, z], gz2.at[:, z]):
            along(ref, far)
            along(ref, near)
    after_stage(c_s, 2)
    table = cutter(gs)(0, gs.shape[-2]).astype(WIDE).T
    start = dec[...].astype(WIDE) + dot(onehot, table.astype(LOW))
    start_ref[...] = start
    out(0)
    one = (normalised(start)[0] * table[0:1] + table[4:5]).astype(LOW)
    one_ref[...] = one
    out(1)
    after_stage(c_k, 1)
    after_stage(c_mid, 0)
    after_stage(c_q, 2)
    qkv[:, 0:BLOCK] = dot(one, cut(QKV, QKV + 16)).astype(LOW)
    after_stage(c_v, 1)
    after_stage(c_k, 2)
    qkv[:, BLOCK : 2 * BLOCK] = dot(one, cut(QKV + 16, QKV + 32)).astype(LOW)
    after_stage(c_v, 2)
    after_stage(c_kv, 0)
    qkv[:, 2 * BLOCK : 3 * BLOCK] = dot(one, cut(QKV + 32, SO)).astype(LOW)
    out(2)
    halves = 2
    span = tok_count // halves
    swaps = []
    for k in range(halves):
        at = pl.ds(k * span, span)
        self_forward((k * span // 128, (k + 1) * span // 128), qkv, low, lse, row_seg, row_keep, col_seg)
        if k == 0:
            after_stage(c_mid, 1)
            after_stage(c_mid, 2)
        after = start_ref[at, :] + dot(low[at, :], cut(SO, CQ))
        after_ref[at, :] = after
        two = (normalised(after)[0] * table[1:2] + table[5:6]).astype(LOW)
        two_ref[at, :] = two
        query[at, :] = dot(two, cut(CQ, KV)).astype(LOW)
        swap = remote(query.at[at], other_out.at[at], sw_send.at[1 + k], sw_recv.at[1 + k], me.across_y())
        swap.start()
        swaps.append(swap)
        if k == 0 and gathers:
            line[0].wait_recv()
            along(gz1.at[:, z_far], near)
            line[2].wait_recv()
            along(gz2.at[:, z_far], near)
    for k in range(3, 8):
        out(k)
    after_stage(c_kv, 1)
    after_stage(c_kv, 2)
    if gathers:
        own(ga, ga_out)
        own(gs, gs_out)
    fetch.wait()
    w_key, w_val = cut(KV, KV + 16), cut(KV + 16, EARLY)
    parts = 4
    for k in range(parts):
        span = src_count // parts
        at = pl.ds(k * span, span)
        kv[at, 0:width] = dot(enc[at, :], w_key).astype(LOW)
        kv[at, width : 2 * width] = dot(enc[at, :], w_val).astype(LOW)
    out(8)
    for copy in swaps + [meet]:
        copy.wait()
    for k, copy in enumerate(line):
        if k not in (0, 2):
            copy.wait_recv()
        copy.wait_send()
    end()
    for copy in outs + (owns[-2:] if gathers else []):
        copy.wait()


def first_part(depth, gathers, seg, pad, pair, dec, enc, tiny, raw, late, whole):
    tok_count, width = dec.shape
    src_count = enc.shape[0]
    lead = (depth, 2, 2, 2) if gathers else (BLOCK // 16,)
    results = [
        shape_of((tok_count, width), WIDE),
        shape_of((tok_count, width), LOW),
        shape_of((tok_count, 3 * width), LOW),
        shape_of((tok_count, width), LOW),
        shape_of((tok_count, 128), WIDE),
        shape_of((tok_count, width), WIDE),
        shape_of((tok_count, width), LOW),
        shape_of((tok_count, width), LOW),
        shape_of((src_count, 2 * width), LOW),
    ]
    outs = results + [shape_of((tok_count, width), LOW), shape_of((1, tok_count), jnp.int32)]
    if gathers:
        outs = [
            shape_of(lead + (EARLY, BLOCK), LOW),
            shape_of(lead + (16, 128), LOW),
            shape_of((2, depth, PERMUTED, BLOCK), LOW),
            shape_of((2, depth, LATE - PERMUTED, BLOCK), LOW),
        ] + outs
    extra = (*tiny, *raw, *late) if gathers else whole
    res = pl.pallas_call(
        partial(first_kernel, depth, gathers),
        name="first_part",
        out_shape=outs,
        in_specs=[VMEM, VMEM, SMEM, VMEM, ANY] + ([VMEM] * 4 + [ANY] * 8 if gathers else [ANY] * 2),
        out_specs=[ANY] * len(outs),
        scratch_shapes=[pltpu.VMEM(a.shape, a.dtype) for a in results]
        + [
            pltpu.VMEM(enc.shape, LOW),
            pltpu.VMEM(lead + (EARLY, BLOCK), LOW),
            pltpu.VMEM(lead + (16, 128), LOW),
            pltpu.VMEM((1, tok_count), WIDE),
            pltpu.VMEM((1, tok_count), WIDE),
            pltpu.VMEM((tok_count, 128), WIDE),
            pltpu.SemaphoreType.DMA((20,)),
            pltpu.SemaphoreType.DMA((12,)),
            pltpu.SemaphoreType.DMA((6, depth + 3)),
            pltpu.SemaphoreType.DMA((6, depth + 3)),
            pltpu.SemaphoreType.DMA((2 * depth + 3,)),
            pltpu.SemaphoreType.DMA((2 * depth + 3,)),
            pltpu.VMEM((PERMUTED, BLOCK), LOW),
            pltpu.VMEM((LATE - PERMUTED, BLOCK), LOW),
        ],
        compiler_params=pltpu.CompilerParams(
            collective_id=0, has_side_effects=True, vmem_limit_bytes=LIMIT
        ),
    )(seg, pad, pair, dec, enc, *extra)
    if gathers:
        whole, line, res = res[:2], res[2:4], res[4:]
    else:
        line = None
    start, one, qkv, low, lse, after, two, query, kv, other_query, other_seg = res
    return whole, line, (start, one, qkv, low, lse, after, two, query, other_query, kv, other_seg)


def segment_ends(lengths, ends):
    total = jnp.int32(0)
    ends[0] = total
    for s in range(2 * SEGS):
        total = total + lengths[0, s]
        ends[s + 1] = total


def block_ranges(seg_s, first_seg, ends, off, src_count, block):
    at = pl.multiple_of(block * 128, 128)
    low = jnp.clip(ends[first_seg + seg_s[0, at]] - off, 0, src_count)
    high = jnp.clip(ends[first_seg + seg_s[0, at + 127] + 1] - off, 0, src_count)
    first = low // TILE
    return first, jnp.where(high > low, (high + TILE - 1) // TILE, first)


def key_bounds(segs, firsts, ends, off):
    rows = []
    for seg, first_seg in zip(segs, firsts):
        low = jnp.zeros(seg.shape, jnp.int32)
        high = jnp.zeros(seg.shape, jnp.int32)
        for s in range(SEGS):
            low = jnp.where(seg == s, ends[first_seg + s] - off, low)
            high = jnp.where(seg == s, ends[first_seg + s + 1] - off, high)
        rows += [low, high]
    return jnp.concatenate(rows + [jnp.zeros((4, rows[0].shape[1]), jnp.int32)], axis=0)


TILE = 256


def side_by_side(x):
    return jnp.concatenate([x, x], axis=1)


def side_by_side_rows(rows, k, at):
    return jnp.concatenate([rows[k : k + 1, at], rows[k + 1 : k + 2, at]], axis=1)


def heads_apart(x):
    n = x.shape[1] // 2
    return jnp.concatenate([x[:HD, :n], x[HD:, n:]], axis=0).T


def cross_forward_kernel(
    lengths, seg_so, seg_sp, seg_vo, seg_vp, q_own, q_other, kv, o_own, o_other, lse_own, lse_other,
    ends, bounds, qs, top_ref, total_ref, acc_ref,
):
    tok_count, width = q_own.shape
    src_count = kv.shape[0]
    pairs = width // 128
    pos = lax.axis_index("src")
    off = pos * src_count
    firsts = (pos * SEGS, (1 - pos) * SEGS)
    segment_ends(lengths, ends)
    bounds[...] = key_bounds((seg_vo[...], seg_vp[...]), firsts, ends, off)
    for side, (q, o, lse_ref) in enumerate(((q_own, o_own, lse_own), (q_other, o_other, lse_other))):

        @pl.loop(0, tok_count // 128)
        def _(block):
            at = pl.ds(pl.multiple_of(block * 128, 128), 128)
            first, last = block_ranges((seg_so, seg_sp)[side], firsts[side], ends, off, src_count, block)
            low, high = bounds[2 * side : 2 * side + 1, at], bounds[2 * side + 1 : 2 * side + 2, at]
            for p in range(pairs):
                qs[p] = both_heads(q[at, p * 128 : (p + 1) * 128] * SCALE)
            top_ref[...] = jnp.full_like(top_ref, FILL)
            total_ref[...] = jnp.zeros_like(total_ref)
            acc_ref[...] = jnp.zeros_like(acc_ref)

            def one(t, carry):
                base = pl.multiple_of(t * TILE, TILE)
                keys = pl.ds(base, TILE)
                index = rows_of((TILE, 128)) + base
                barred = side_by_side(jnp.where((index >= low) & (index < high), 0.0, FILL))
                every = range(pairs)
                scores = [dot_nt(kv[keys, pl.ds(p * 128, 128)], qs[p]) for p in every]
                scores = [scores[p] + barred for p in every]
                olds = [top_ref[p] for p in every]
                tops = [jnp.maximum(olds[p], jnp.max(scores[p], axis=0, keepdims=True)) for p in every]
                exps = [jnp.exp(scores[p] - jnp.maximum(tops[p], 0.1 * FILL)) for p in every]
                fades = [jnp.exp(olds[p] - tops[p]) for p in every]
                sums = [total_ref[p] * fades[p] + jnp.sum(exps[p], axis=0, keepdims=True) for p in every]
                mixed = [dot_tn(kv[keys, pl.ds(width + p * 128, 128)], exps[p].astype(LOW)) for p in every]
                mixed = [acc_ref[p] * fades[p] + mixed[p] for p in every]
                for p in every:
                    top_ref[p] = tops[p]
                    total_ref[p] = sums[p]
                    acc_ref[p] = mixed[p]
                return carry

            lax.fori_loop(first, last, one, 0)
            stats = []
            for p in range(pairs):
                total = total_ref[p]
                safe = jnp.where(total > 0.0, total, 1.0)
                o[at, p * 128 : (p + 1) * 128] = heads_apart(acc_ref[p] * (1.0 / safe)).astype(LOW)
                lse = jnp.where(total > 0.0, top_ref[p] + jnp.log(safe), FILL)
                stats += [lse[:, :128], lse[:, 128:]]
            lse_ref[:, at] = jnp.concatenate(stats, axis=0)


def cross_forward(lengths, seg_own, seg_other, q_own, q_other, kv):
    tok_count, width = q_own.shape
    heads = width // HD
    pairs = width // 128
    out = shape_of((tok_count, width), LOW)
    lse = shape_of((heads, tok_count), WIDE)
    return pl.pallas_call(
        cross_forward_kernel,
        name="cross_forward",
        out_shape=[out, out, lse, lse],
        in_specs=[SMEM] * 3 + [VMEM] * 5,
        out_specs=[VMEM] * 4,
        scratch_shapes=[
            pltpu.SMEM((32,), jnp.int32),
            pltpu.VMEM((8, tok_count), jnp.int32),
            pltpu.VMEM((pairs, 256, 128), LOW),
            pltpu.VMEM((pairs, 1, 256), WIDE),
            pltpu.VMEM((pairs, 1, 256), WIDE),
            pltpu.VMEM((pairs, 128, 256), WIDE),
        ],
        compiler_params=pltpu.CompilerParams(vmem_limit_bytes=LIMIT),
        cost_estimate=pl.CostEstimate(flops=1 << 33, bytes_accessed=8 << 20, transcendentals=0),
    )(lengths, seg_own, seg_other, seg_own, seg_other, q_own, q_other, kv)


def cross_backward_kernel(
    lengths, seg_so, seg_sp, seg_vo, seg_vp, q_own, q_other, g_own, g_other, st_own, st_other, kv_in, pass_0, pass_1,
    dq_own, dq_other, dkv_out, given_0, given_1, ends, bounds, acc, qs, gs, dq_acc, kv, dkv, held_0, held_1, sems, io_sems,
):
    fetch = pltpu.make_async_copy(kv_in, kv, io_sems.at[0])
    fetch.start()
    ways = ((pass_0, held_0, given_0), (pass_1, held_1, given_1))
    taking = [pltpu.make_async_copy(way[0], way[1], sems.at[0, k]) for k, way in enumerate(ways)]
    giving = [pltpu.make_async_copy(way[1], way[2], sems.at[1, k]) for k, way in enumerate(ways)]
    for copy in taking:
        copy.start()
    tok_count, width = q_own.shape
    src_count = kv.shape[0]
    pairs = width // 128
    pos = lax.axis_index("src")
    off = pos * src_count
    firsts = (pos * SEGS, (1 - pos) * SEGS)
    segment_ends(lengths, ends)
    bounds[...] = key_bounds((seg_vo[...], seg_vp[...]), firsts, ends, off)
    acc[...] = jnp.zeros_like(acc)
    fetch.wait()
    sides = ((q_own, g_own, st_own, dq_own), (q_other, g_other, st_other, dq_other))
    for side, (q, g, st, dq) in enumerate(sides):

        @pl.loop(0, tok_count // 128)
        def _(block):
            at = pl.ds(pl.multiple_of(block * 128, 128), 128)
            first, last = block_ranges((seg_so, seg_sp)[side], firsts[side], ends, off, src_count, block)
            low, high = bounds[2 * side : 2 * side + 1, at], bounds[2 * side + 1 : 2 * side + 2, at]
            for p in range(pairs):
                cols = slice(p * 128, (p + 1) * 128)
                qs[p] = both_heads(q[at, cols] * SCALE)
                gs[p] = both_heads(g[at, cols])
            dq_acc[...] = jnp.zeros_like(dq_acc)
            lses = [side_by_side_rows(st, 2 * p, at) for p in range(pairs)]
            deltas = [side_by_side_rows(st, 8 + 2 * p, at) for p in range(pairs)]

            def one(t, carry):
                base = pl.multiple_of(t * TILE, TILE)
                keys = pl.ds(base, TILE)
                index = rows_of((TILE, 128)) + base
                barred = side_by_side(jnp.where((index >= low) & (index < high), 0.0, FILL))
                every = range(pairs)
                cols = [pl.ds(p * 128, 128) for p in every]
                vals = [pl.ds(width + p * 128, 128) for p in every]
                scores = [dot_nt(kv[keys, cols[p]], qs[p]) for p in every]
                slopes = [dot_nt(kv[keys, vals[p]], gs[p]) for p in every]
                probs = [jnp.exp(scores[p] - lses[p] + barred) for p in every]
                gscores = [(probs[p] * (slopes[p] - deltas[p])).astype(LOW) for p in every]
                grad_k = [acc[keys, cols[p]] + dot(gscores[p], qs[p]) for p in every]
                grad_v = [acc[keys, vals[p]] + dot(probs[p].astype(LOW), gs[p]) for p in every]
                grad_q = [dq_acc[p] + dot_tn(kv[keys, cols[p]], gscores[p]) for p in every]
                for p in every:
                    acc[keys, cols[p]] = grad_k[p]
                    acc[keys, vals[p]] = grad_v[p]
                    dq_acc[p] = grad_q[p]
                return carry

            lax.fori_loop(first, last, one, 0)
            for p in range(pairs):
                dq[at, p * 128 : (p + 1) * 128] = (heads_apart(dq_acc[p]) * SCALE).astype(dq.dtype)

    for first, second in zip(taking, giving):
        first.wait()
        second.start()

    parts = 4
    span = src_count // parts
    stores = []
    for k in range(parts):
        at = pl.ds(k * span, span)
        dkv[at, :] = acc[at, :].astype(LOW)
        stores.append(pltpu.make_async_copy(dkv.at[at], dkv_out.at[at], io_sems.at[1 + k]))
        stores[-1].start()
    for copy in stores:
        copy.wait()
    for copy in giving:
        copy.wait()


def cross_backward(lengths, seg_own, seg_other, q_own, q_other, g_own, g_other, st_own, st_other, kv, passed):
    tok_count, width = q_own.shape
    src_count = kv.shape[0]
    pairs = width // 128
    return pl.pallas_call(
        cross_backward_kernel,
        name="cross_backward",
        out_shape=[
            shape_of((tok_count, width), WIDE),
            shape_of((tok_count, width), LOW),
            shape_of((src_count, 2 * width), LOW),
        ]
        + [shape_of(a.shape, a.dtype) for a in passed],
        in_specs=[SMEM] * 3 + [VMEM] * 8 + [ANY] * 3,
        out_specs=[VMEM] * 2 + [ANY] * 3,
        scratch_shapes=[
            pltpu.SMEM((32,), jnp.int32),
            pltpu.VMEM((8, tok_count), jnp.int32),
            pltpu.VMEM((src_count, 2 * width), WIDE),
            pltpu.VMEM((pairs, 256, 128), LOW),
            pltpu.VMEM((pairs, 256, 128), LOW),
            pltpu.VMEM((pairs, 128, 256), WIDE),
            pltpu.VMEM(kv.shape, LOW),
            pltpu.VMEM(kv.shape, LOW),
        ]
        + [pltpu.VMEM(a.shape, a.dtype) for a in passed]
        + [pltpu.SemaphoreType.DMA((2, 2)), pltpu.SemaphoreType.DMA((5,))],
        compiler_params=pltpu.CompilerParams(vmem_limit_bytes=LIMIT),
        cost_estimate=pl.CostEstimate(flops=1 << 34, bytes_accessed=16 << 20, transcendentals=0),
    )(lengths, seg_own, seg_other, seg_own, seg_other, q_own, q_other, g_own, g_other, st_own, st_other, kv, *passed)


def merge_all(parts, count):
    top = parts[0]
    for part in parts[1:]:
        top = jnp.maximum(top, part)
    total = sum(jnp.exp(part - top) for part in parts)
    return jnp.where(rows_of(top.shape) < count, top + jnp.log(total), sum(parts))


def folded(row):
    return jnp.concatenate([row[:, k : k + 128] for k in range(0, row.shape[1], 128)], axis=0)


def unfolded(rows):
    return jnp.concatenate([rows[k : k + 1] for k in range(rows.shape[0])], axis=1)


def middle_kernel(depth, split, *refs):
    (
        seg, pad, labels, counts, positions, targets, lse_own, lse_other, vocab_in, after_in, o_in, o_other, gs,
    ) = refs[:13]
    parts = refs[13 : 13 + (3 if split else 1)]
    refs = refs[13 + len(parts) :]
    count = 4 if split else 1
    sums = refs[:count]
    refs = refs[count:]
    (
        block_out, state_out, g_own, g_other, st_own, st_other, small_rows, small_cols, grad_vocab, token_out, loss_out,
    ) = refs[:11]
    (
        w_vocab, after_self, o_own, block_ref, state_ref, g_ref, vocab_ref, out_sem,
        wm, eb, eb_got, w_s, got_o, got_lse, cross_o, cross_low, ac, bs, n3, act, slope, gpre, head,
        lt, gt, gt_got, pb, pb_got, rb, got_rq, got_rz, st_c, st_q, st_z, gh, g_ffn, load_sem, send, recv,
    ) = refs[11 : 11 + 39]
    sum_refs = refs[11 + 39 :]
    tok_count, width = after_self.shape
    hidden = act.shape[1]
    masked = positions.shape[1]
    vocab_local = w_vocab.shape[1]
    everyone = depth * 8
    me = Place(depth)
    z, x, c, y = me.z, me.x, me.c, me.y
    greet(me.others() + [me.across_x(), me.across_y(), me.across_both(), me.across_core()])
    used = [0]

    def push(src, dst, peer):
        k = used[0]
        used[0] += 1
        copy = remote(src, dst, send.at[k], recv.at[k], peer)
        copy.start()
        return copy

    pending = []

    def arrive(copies):
        for copy in copies:
            copy.wait_recv()
        pending.extend(copies)

    loads = []

    def load(src, dst):
        copy = pltpu.make_async_copy(src, dst, load_sem.at[len(loads)])
        copy.start()
        loads.append(copy)

    halves = 2
    span = tok_count // halves
    ranges = [pl.ds(k * span, span) for k in range(halves)]

    def swap_outputs():
        copies = [push(lse_other, got_lse, me.across_y())]
        return copies + [push(o_other.at[at], got_o.at[at], me.across_y()) for at in ranges]

    load(gs, w_s)
    load(after_in, after_self)
    load(o_in, o_own)
    load(vocab_in, w_vocab.at[c])
    shared = [push(vocab_in, w_vocab.at[c], me.across_core())]
    if split:
        rest = pl.ds(PERMUTED, LATE - PERMUTED)
        soon = pl.ds(0, PERMUTED)
        late_part = [push(parts[1].at[py], wm.at[:, x, c, py, rest], me.across_x()) for py in range(2)]
        swap = swap_outputs()
        for py in range(2):
            load(parts[0].at[py], wm.at[:, x, c, py, soon])
            load(parts[1].at[py], wm.at[:, x, c, py, rest])
            load(parts[2].at[py], wm.at[:, 1 - x, c, py, soon])
            shared.append(push(parts[0].at[py], wm.at[:, x, c, py, soon], me.across_core()))
            shared.append(push(parts[1].at[py], wm.at[:, x, c, py, rest], me.across_core()))
            shared.append(push(parts[2].at[py], wm.at[:, 1 - x, c, py, soon], me.across_core()))
    else:
        swap = swap_outputs()
        load(parts[0], wm)

    def cut(lo, hi):
        value = wm[:, :, :, :, lo:hi] if split else wm[:, lo:hi]
        return value.reshape((-1, BLOCK))

    def put(lo, value, first=0, last=None, cols=slice(0, BLOCK)):
        groups, rows, wide = value.shape
        last = depth if last is None else last
        if split:
            eb[first:last, :, :, :, lo : lo + rows, cols] = value.reshape((last - first, 2, 2, 2, rows, wide))
        else:
            step = eb.shape[0] // depth
            eb[first * step : last * step, lo : lo + rows, cols] = value

    segments = seg[...].astype(WIDE)
    keep = 1.0 - pad[...].astype(WIDE)
    lane_row = lanes((1, tok_count))
    inside = lane_row < tok_count - 1

    def following(row):
        return pltpu.roll(jnp.concatenate([row, jnp.zeros((7, tok_count), WIDE)], axis=0), tok_count - 1, 1)[0:1]

    follows = inside & (following(segments) == segments) & (keep > 0.5) & (following(keep) > 0.5)
    valid = jnp.where(follows, 1.0, 0.0)
    rows = [keep, valid, labels[...].astype(WIDE), counts[...].astype(WIDE)]
    columns = transposed_rows(jnp.concatenate(rows + [jnp.zeros((4, tok_count), WIDE)], axis=0))
    col_keep, col_valid = columns[:, 0:1], columns[:, 1:2]
    col_label, col_count = columns[:, 2:3], columns[:, 3:4].astype(jnp.int32)

    for copy in loads:
        copy.wait()
    arrive(shared)
    table = w_s[...].reshape((-1, 128)).astype(WIDE).T

    outs = []

    def out(src, dst):
        copy = pltpu.make_async_copy(src, dst, out_sem.at[len(outs)])
        copy.start()
        outs.append(copy)

    blocks = hidden // BLOCK
    weight_co = cut(0, 16)
    arrive(swap[:1])
    top = jnp.maximum(lse_own[...], got_lse[...])
    lse = top + jnp.log(jnp.exp(lse_own[...] - top) + jnp.exp(got_lse[...] - top))
    shares = jnp.concatenate([jnp.exp(lse_own[...] - lse), jnp.exp(got_lse[...] - lse)], axis=0)
    shares = transposed_rows(shares)
    low_half = lanes((span, 128)) < HD
    for k, at in enumerate(ranges):
        arrive(swap[1 + k : 2 + k])
        mine = shares[k * span : (k + 1) * span]
        for p in range(width // 128):
            cols = slice(p * 128, (p + 1) * 128)
            share_own = jnp.where(low_half, mine[:, 2 * p : 2 * p + 1], mine[:, 2 * p + 1 : 2 * p + 2])
            share_got = jnp.where(low_half, mine[:, 8 + 2 * p : 9 + 2 * p], mine[:, 9 + 2 * p : 10 + 2 * p])
            mixed = o_own[at, cols].astype(WIDE) * share_own + got_o[at, cols].astype(WIDE) * share_got
            cross_o[at, cols] = mixed
            cross_low[at, cols] = mixed.astype(LOW)
        after_cross = after_self[at, :] + dot(cross_low[at, :], weight_co)
        ac[at, :] = after_cross
        normed = (normalised(after_cross)[0] * table[2:3] + table[6:7]).astype(LOW)
        n3[at, :] = normed
        if k == 0 and split:
            arrive(late_part)
            block = wm.at[:, 1 - x, c, :, rest]
            late_part = [push(block, block, me.across_core())]
        for j in range(blocks):
            cols = slice(j * BLOCK, (j + 1) * BLOCK)
            pre = dot(normed, cut(16 + 16 * j, 32 + 16 * j))
            square = pre * pre
            bent = jnp.tanh(GELU * pre * (1.0 + CUBIC * square))
            half = 0.5 * (1.0 + bent)
            act[at, cols] = (pre * half).astype(LOW)
            slope[at, cols] = half + 0.5 * pre * (1.0 - bent * bent) * (GELU * (1.0 + 3.0 * CUBIC * square))
        if k == 0 and split:
            arrive(late_part)
        state = after_cross + dot(act[at, :], cut(80, 144))
        bs[at, :] = state
        block_ref[at, :] = state.astype(LOW)
        head[at, :] = (normalised(state)[0] * table[3:4] + table[7:8]).astype(LOW)
    flat_fo = cut(80, 144)
    out(block_ref, block_out)
    head_in = head[...]

    picker = (positions[...] == rows_of((tok_count, masked))).astype(LOW)
    picked = dot_tn(picker, head_in).astype(LOW)
    kept = dot(jnp.concatenate([keep, jnp.zeros((7, tok_count), WIDE)], axis=0).astype(LOW), picker)
    code = jnp.where(kept[0:1] > 0.5, targets[...] + 1, 0)
    digits = jnp.concatenate([code >> 8, code & 255, jnp.zeros((6, masked), jnp.int32)], axis=0)
    digits = dot_tn(digits.astype(WIDE).astype(LOW), (rows_of((8, 128)) == lanes((8, 128))).astype(LOW)).astype(LOW)
    pb[z, x, y, :, 0:width] = picked
    pb[z, x, y, :, width : width + 128] = digits
    mine = pb.at[z, x, y]
    flight = [push(mine, mine, peer) for peer in me.others()]

    classes = BLOCK // 2
    flat_in = cut(144, 160).reshape((-1, 16, BLOCK))
    flat_in = jnp.concatenate([flat_in[:, :, :classes], flat_in[:, :, classes:]], axis=1).reshape((-1, classes))
    w_one, w_two = flat_in[:width], flat_in[width:]
    token_row = rows_of((tok_count, classes))
    ahead = pltpu.roll(dot(head_in, w_two), tok_count - 1, 0)
    logits = dot(head_in, w_one) + jnp.where(token_row == tok_count - 1, 0.0, ahead)
    top = jnp.max(logits, axis=1, keepdims=True)
    exps = jnp.exp(logits - top)
    total = jnp.sum(exps, axis=1, keepdims=True)
    hits = lanes((tok_count, classes)) == col_count
    entropy = top + jnp.log(total) - jnp.sum(jnp.where(hits, logits, 0.0), axis=1, keepdims=True)
    loss_col = col_valid * entropy
    grads = col_valid * (exps * (1.0 / total) - jnp.where(hits, 1.0, 0.0))
    g_insert = grads.astype(LOW)
    before = pltpu.roll(g_insert.astype(WIDE), 1, 0)
    g_before = jnp.where(token_row == 0, 0.0, before).astype(LOW)

    arrive(flight)
    column = pb.at[:, x, y]
    flight = [push(column, column, peer) for peer in (me.across_x(), me.across_y(), me.across_both())]

    flat_s = w_s[...].reshape((-1, 128))
    two = dot(head_in, flat_s)
    l_zero, l_one = two[:, 16:17], two[:, 17:18]
    top = jnp.maximum(l_zero, l_one)
    e_zero, e_one = jnp.exp(l_zero - top), jnp.exp(l_one - top)
    total = e_zero + e_one
    is_one = col_label > 0.5
    loss_col = loss_col + col_keep * (top + jnp.log(total) - jnp.where(is_one, l_one, l_zero))
    d_zero = col_keep * (e_zero / total - jnp.where(is_one, 0.0, 1.0))
    d_one = col_keep * (e_one / total - jnp.where(is_one, 1.0, 0.0))
    lane = lanes((tok_count, 128))
    g_delete = jnp.where(lane == 16, d_zero, jnp.where(lane == 17, d_one, 0.0)).astype(LOW)
    gh[...] = dot_nt(g_delete, flat_s) + dot_nt(g_insert, w_one) + dot_nt(g_before, w_two)
    arrive(flight)
    sibling = [push(pb, pb_got, me.across_core())]
    def rows_from(ref):
        return ref[...].reshape((-1, width + 128))

    gathered = rows_from(pb)
    rows_all = gathered[:, 0:width]
    numbers = gathered[:, width : width + 128].astype(WIDE).T
    code = numbers[0:1] * 256.0 + numbers[1:2]
    weight = jnp.where(code > 0.5, 1.0, 0.0)
    count = rows_all.shape[0]
    target = code.astype(jnp.int32) - 1
    place = rows_of((vocab_local, count))
    lt[...] = dot_nt(w_vocab[...].reshape((-1, width)), rows_all)
    hits = []
    for k in range(2):
        first = lax.axis_index(BOTH) + 2 * (k - c)
        hits.append(place + first * vocab_local == target)
    hits = jnp.concatenate(hits, axis=0)
    logits = lt[...]
    top = jnp.max(logits, axis=0, keepdims=True)
    total = jnp.sum(jnp.exp(logits - top), axis=0, keepdims=True)
    chosen = jnp.sum(jnp.where(hits, logits, 0.0), axis=0, keepdims=True)
    loss_here = jnp.sum(loss_col, axis=0, keepdims=True)
    folds = count // 128
    loss_rows = jnp.broadcast_to(loss_here, (st_z.shape[1] - 2 * folds, 128))
    st_q[x, y] = jnp.concatenate([folded(top + jnp.log(total)), folded(chosen), loss_rows], axis=0)
    spot = st_q.at[x, y]
    flight = [push(spot, spot, peer) for peer in (me.across_x(), me.across_y(), me.across_both())]
    small_cols[...] = dot_tn(head_in, g_delete)
    for k, grad in enumerate((g_insert, g_before)):
        pairs = dot_tn(head_in, grad).astype(LOW).reshape((-1, 2, 16, classes))
        for side in range(2):
            cols = slice(side * classes, (side + 1) * classes)
            put(144, pairs[:, side], k * (depth // 2), (k + 1) * (depth // 2), cols)
    arrive(flight)
    st_z[z] = merge_all([st_q[0, 0], st_q[0, 1], st_q[1, 0], st_q[1, 1]], folds)
    flight = [push(st_z.at[z], st_z.at[z], peer) for peer in me.others()]
    arrive(flight)
    stat = merge_all([st_z[k] for k in range(depth)], folds)
    all_loss = stat[2 * folds : 2 * folds + 1]
    stat = jnp.concatenate([unfolded(stat[0:folds]), unfolded(stat[folds : 2 * folds])], axis=0)
    gt[...] = (weight * (jnp.exp(lt[...] - stat[0:1]) - jnp.where(hits, 1.0, 0.0))).astype(LOW)
    rb[...] = dot_tn(gt[...], w_vocab[...].reshape((-1, width))).astype(LOW).reshape(rb.shape)
    flight = [
        push(rb.at[:, 1 - x, y], got_rq.at[0], me.across_x()),
        push(rb.at[:, x, 1 - y], got_rq.at[1], me.across_y()),
        push(rb.at[:, 1 - x, 1 - y], got_rq.at[2], me.across_both()),
    ]
    sibling.append(push(gt.at[pl.ds((1 - c) * vocab_local, vocab_local)], gt_got, me.across_core()))
    tokens = weight * (stat[0:1] - stat[1:2])
    mine = rows_of((masked, count)) + ((z * 2 + x) * 2 + y) * masked == lanes((masked, count))
    own = jnp.sum(jnp.where(mine, tokens, 0.0), axis=1, keepdims=True)
    token_out[...] = jnp.sum(
        jnp.where(rows_of((masked, masked)) == lanes((masked, masked)), own, 0.0), axis=0, keepdims=True
    )
    loss = (all_loss + jnp.sum(tokens, axis=1, keepdims=True)) * (1.0 / (tok_count * everyone))
    st_c[0] = jnp.broadcast_to(loss, (8, 128))
    sibling.append(push(st_c.at[0], st_c.at[1], me.across_core()))
    arrive(flight)
    line = rb[:, x, y].astype(WIDE)
    for k in range(3):
        line = line + got_rq[k].astype(WIDE)
    got_rq[3] = line.astype(LOW)
    flight = [
        push(got_rq.at[3, lax.rem(z + k, depth)], got_rz.at[k - 1], me.along(k)) for k in range(1, depth)
    ]
    arrive(sibling)
    loss_out[...] = st_c[0, 0:1, 0:1] + st_c[1, 0:1, 0:1]
    scale = (tok_count * everyone) ** (-0.5)
    mine = gt[pl.ds(pl.multiple_of(c * vocab_local, vocab_local), vocab_local), :]
    vocab_ref[...] = (dot(mine, rows_all) + dot(gt_got[...], rows_from(pb_got)[:, 0:width])) * scale
    out(vocab_ref, grad_vocab)
    arrive(flight)
    grad_picked = got_rq[3, z].astype(WIDE)
    for k in range(1, depth):
        grad_picked = grad_picked + got_rz[k - 1].astype(WIDE)
    coarse = grad_picked.astype(LOW)
    fine = (grad_picked - coarse.astype(WIDE)).astype(LOW)
    grad_head = gh[...] + dot(picker, coarse) + dot(picker, fine)

    gh[...] = grad_head
    gain_2 = gain_3 = bias_2 = bias_3 = 0.0
    low_half = lanes((span, 128)) < HD
    lane = lanes((span, 128))
    swap, delta_rows = [], []
    for at in ranges:
        grad_block, gain, bias = norm_back(bs[at, :], table[3:4], gh[at, :])
        gain_3, bias_3 = gain_3 + gain, bias_3 + bias
        g_half = grad_block.astype(LOW)
        g_ffn[at, :] = g_half
        slopes = [dot_nt(g_half, flat_fo[j * BLOCK : (j + 1) * BLOCK]) for j in range(blocks)]
        slopes = [(slopes[j] * slope[at, j * BLOCK : (j + 1) * BLOCK]).astype(LOW) for j in range(blocks)]
        upstream = sum(dot_nt(slopes[j], cut(16 + 16 * j, 32 + 16 * j)) for j in range(blocks))
        for j in range(blocks):
            gpre[at, j * BLOCK : (j + 1) * BLOCK] = slopes[j]
        back, gain, bias = norm_back(ac[at, :], table[2:3], upstream)
        gain_2, bias_2 = gain_2 + gain, bias_2 + bias
        grad_state = grad_block + back
        state_ref[at, :] = grad_state
        g_attn = dot_nt(grad_state.astype(LOW), weight_co).astype(LOW)
        g_ref[at, :] = g_attn
        swap.append(push(g_ref.at[at], g_other.at[at], me.across_y()))
        deltas = jnp.zeros((span, 128), WIDE)
        for p in range(width // 128):
            cols = slice(p * 128, (p + 1) * 128)
            product = g_attn[:, cols].astype(WIDE) * cross_o[at, cols]
            first = jnp.sum(jnp.where(low_half, product, 0.0), axis=1, keepdims=True)
            second = jnp.sum(jnp.where(low_half, 0.0, product), axis=1, keepdims=True)
            deltas = jnp.where(lane == 2 * p, first, jnp.where(lane == 2 * p + 1, second, deltas))
        delta_rows.append(deltas.T[0:8])
    st_own[...] = jnp.concatenate([lse, jnp.concatenate(delta_rows, axis=1)], axis=0)
    swap.append(push(st_own, st_other, me.across_y()))
    out(state_ref, state_out)
    out(g_ref, g_own)
    g_cross = state_ref[...].astype(LOW)

    cores = []

    def to_core(lo, hi):
        if split:
            at = pl.ds(lo, hi - lo)
            cores.append(push(eb.at[:, :, 1 - c, :, at], eb_got.at[:, :, :, at], me.across_core()))

    to_core(144, 160)
    for j in range(blocks):
        grad = dot_tn(act[:, j * BLOCK : (j + 1) * BLOCK], g_ffn[...]).astype(LOW)
        put(80, grad.reshape((-1, 64, BLOCK)), j * depth // blocks, (j + 1) * depth // blocks)
    to_core(80, 144)
    for j in range(blocks):
        grad = dot_tn(n3[...], gpre[:, j * BLOCK : (j + 1) * BLOCK]).astype(LOW)
        put(16 + 16 * j, grad.reshape((-1, 16, BLOCK)))
    to_core(16, 80)
    put(0, dot_tn(cross_low[...], g_cross).astype(LOW).reshape((-1, 16, BLOCK)))
    to_core(0, 16)
    small_rows[...] = jnp.concatenate([gain_2, gain_3, bias_2, bias_3, jnp.zeros((4, width), WIDE)], axis=0)
    if split:
        arrive(cores)
        one, two = pl.ds(0, RETURNED), pl.ds(RETURNED, LATE - RETURNED)
        for k, (at, first, spot) in enumerate(((one, 1 - y, 1), (two, 1 - x, 0), (one, y, 1), (two, x, 0))):
            for other in range(2):
                px, py = (other, first) if spot else (first, other)

                @pl.loop(0, depth)
                def _(zz):
                    total = eb[zz, px, c, py, at].astype(WIDE) + eb_got[zz, px, py, at].astype(WIDE)
                    sum_refs[k][other, zz] = total.astype(LOW)

            out(sum_refs[k], sums[k])
    else:
        sums[0][...] = eb[...]
    arrive(swap)
    for copy in pending:
        copy.wait_send()
    for copy in outs:
        copy.wait()


def middle_part(depth, split, seg, pad, labels, counts, positions, targets, w_vocab, after_self, attended, gs, parts):
    tok_count, width = after_self.shape
    hidden = 4 * BLOCK
    vocab_local = w_vocab.shape[0]
    everyone = depth * 8
    masked = positions.shape[1]
    count = masked * everyone // 2
    stat_rows = (2 * (count // 128) + 15) // 8 * 8
    sharded = (depth, 2, 2, 2)
    lead = sharded if split else (BLOCK // 16,)
    sharded = (depth, 2, 2, 2)
    if split:
        outs = [(shape_of((2, depth, n, BLOCK), LOW), ANY) for n in (RETURNED, LATE - RETURNED)] * 2
    else:
        outs = [(shape_of(parts[0].shape, LOW), VMEM)]
    outs += [
        (shape_of((tok_count, width), LOW), ANY),
        (shape_of((tok_count, width), WIDE), ANY),
        (shape_of((tok_count, width), LOW), ANY),
        (shape_of((tok_count, width), LOW), ANY),
        (shape_of((16, tok_count), WIDE), VMEM),
        (shape_of((16, tok_count), WIDE), ANY),
        (shape_of((8, width), WIDE), VMEM),
        (shape_of((width, 128), WIDE), VMEM),
        (shape_of((vocab_local, width), WIDE), ANY),
        (shape_of((1, masked), WIDE), VMEM),
        (shape_of((1, 1), WIDE), VMEM),
    ]
    copies = 32 + 2 * (depth - 1) + 3 + 1 + 1 + 3 + 1 + 3 + (depth - 1)
    return pl.pallas_call(
        partial(middle_kernel, depth, split),
        name="middle_part",
        out_shape=[o for o, _ in outs],
        in_specs=[VMEM] * 8 + [ANY] * (5 + len(parts)),
        out_specs=[s for _, s in outs],
        scratch_shapes=[
            pltpu.VMEM((2, vocab_local, width), LOW),
            pltpu.VMEM((tok_count, width), WIDE),
            pltpu.VMEM((tok_count, width), LOW),
            pltpu.VMEM((tok_count, width), LOW),
            pltpu.VMEM((tok_count, width), WIDE),
            pltpu.VMEM((tok_count, width), LOW),
            pltpu.VMEM((vocab_local, width), WIDE),
            pltpu.SemaphoreType.DMA((10,)),
            pltpu.VMEM(lead + (160, BLOCK), LOW),
            pltpu.VMEM(lead + (160, BLOCK), LOW),
            pltpu.VMEM(((depth, 2, 2) if split else (1,)) + (160, BLOCK), LOW),
            pltpu.VMEM(gs.shape, LOW),
            pltpu.VMEM((tok_count, width), LOW),
            pltpu.VMEM((8, tok_count), WIDE),
            pltpu.VMEM((tok_count, width), WIDE),
            pltpu.VMEM((tok_count, width), LOW),
            pltpu.VMEM((tok_count, width), WIDE),
            pltpu.VMEM((tok_count, width), WIDE),
            pltpu.VMEM((tok_count, width), LOW),
            pltpu.VMEM((tok_count, hidden), LOW),
            pltpu.VMEM((tok_count, hidden), WIDE),
            pltpu.VMEM((tok_count, hidden), LOW),
            pltpu.VMEM((tok_count, width), LOW),
            pltpu.VMEM((2 * vocab_local, count), WIDE),
            pltpu.VMEM((2 * vocab_local, count), LOW),
            pltpu.VMEM((vocab_local, count), LOW),
            pltpu.VMEM((depth, 2, 2, masked, width + 128), LOW),
            pltpu.VMEM((depth, 2, 2, masked, width + 128), LOW),
            pltpu.VMEM((depth, 2, 2, masked, width), LOW),
            pltpu.VMEM((4, depth, masked, width), LOW),
            pltpu.VMEM((max(depth - 1, 1), masked, width), LOW),
            pltpu.VMEM((2, 8, 128), WIDE),
            pltpu.VMEM((2, 2, stat_rows, 128), WIDE),
            pltpu.VMEM((depth, stat_rows, 128), WIDE),
            pltpu.VMEM((tok_count, width), WIDE),
            pltpu.VMEM((tok_count, width), LOW),
            pltpu.SemaphoreType.DMA((12,)),
            pltpu.SemaphoreType.DMA((copies + depth,)),
            pltpu.SemaphoreType.DMA((copies + depth,)),
        ]
        + ([pltpu.VMEM((2, depth, n, BLOCK), LOW) for n in (RETURNED, LATE - RETURNED)] * 2 if split else []),
        compiler_params=pltpu.CompilerParams(
            collective_id=1, has_side_effects=True, vmem_limit_bytes=LIMIT
        ),
    )(seg, pad, labels, counts, positions, targets, *attended[2:], w_vocab, after_self, *attended[:2], gs, *parts)


def self_backward_start(dk, dv):
    dk[...] = jnp.zeros_like(dk)
    dv[...] = jnp.zeros_like(dv)


def self_backward(blocks, qkv, out, lse_ref, g_ref, dqkv, dk, dv, row_seg, row_keep, col_seg):
    tok_count, width = out.shape
    first, last = blocks
    pairs = width // 128

    def one(block, carry):
        at = pl.ds(pl.multiple_of(block * 128, 128), 128)
        low = self_window(block, tok_count)
        keys = pl.ds(low, 384)
        allowed = twice(self_mask(row_seg, row_keep, col_seg, block, low))
        stats = lse_ref[at, :]
        every = range(pairs)
        cols = [slice(p * 128, (p + 1) * 128) for p in every]
        q = [both_heads(qkv[at, cols[p]] * SCALE) for p in every]
        g = [both_heads(g_ref[at, cols[p]]) for p in every]
        keyed = [qkv[keys, width + p * 128 : width + (p + 1) * 128] for p in every]
        scores = [dot_nt(q[p], keyed[p]) for p in every]
        slopes = [dot_nt(g[p], qkv[keys, 2 * width + p * 128 : 2 * width + (p + 1) * 128]) for p in every]
        deltas = [jnp.sum(g[p].astype(WIDE) * twice(out[at, cols[p]].astype(WIDE)), axis=1, keepdims=True) for p in every]
        lses = [jnp.concatenate([stats[:, 2 * p : 2 * p + 1], stats[:, 2 * p + 1 : 2 * p + 2]], axis=0) for p in every]
        probs = [jnp.exp(jnp.where(allowed, scores[p] - lses[p], FILL)) for p in every]
        gscores = [(probs[p] * (slopes[p] - deltas[p])).astype(LOW) for p in every]
        grad_q = [join_heads(dot(gscores[p], keyed[p])) * SCALE for p in every]
        grad_k = [dk[keys, cols[p]] + dot_tn(gscores[p], q[p]) for p in every]
        grad_v = [dv[keys, cols[p]] + dot_tn(probs[p].astype(LOW), g[p]) for p in every]
        for p in every:
            dqkv[at, cols[p]] = grad_q[p].astype(LOW)
            dk[keys, cols[p]] = grad_k[p]
            dv[keys, cols[p]] = grad_v[p]
        return carry

    lax.fori_loop(first, last, one, 0)


def self_backward_end(dqkv, dk, dv):
    width = dk.shape[1]
    dqkv[:, width : 2 * width] = dk[...].astype(LOW)
    dqkv[:, 2 * width : 3 * width] = dv[...].astype(LOW)


def reduction(me, chunks, send, recv):
    z, x, c, y = me.z, me.x, me.c, me.y
    depth = me.depth
    count = len(chunks)
    started = [[None] * 3 for _ in chunks]
    used = [0] * count

    def launch(k, stage):
        copies = []

        def push(src, dst, peer):
            slot = used[k]
            used[k] += 1
            copy = remote(src, dst, send.at[k, slot], recv.at[k, slot], peer)
            copy.start()
            copies.append(copy)

        for src, got_c, got_q, got_z, at, put in chunks[k]:
            if stage == 0:
                push(src.at[:, :, 1 - c, :, at], got_c.at[:, :, :, at], me.across_core())
            elif stage == 1:
                push(got_c.at[:, 1 - x, y, at], got_q.at[0, :, at], me.across_x())
                push(got_c.at[:, x, 1 - y, at], got_q.at[1, :, at], me.across_y())
                push(got_c.at[:, 1 - x, 1 - y, at], got_q.at[2, :, at], me.across_both())
            else:
                for j in range(1, depth):
                    push(got_c.at[lax.rem(z + j, depth), x, y, at], got_z.at[j - 1, at], me.along(j))
        started[k][stage] = copies

    def absorb(k, stage):
        for copy in started[k][stage]:
            copy.wait_recv()
        for src, got_c, got_q, got_z, at, put in chunks[k]:
            if stage == 0:

                @pl.loop(0, depth)
                def _(zz):
                    for xx in range(2):
                        for yy in range(2):
                            total = src[zz, xx, c, yy, at].astype(WIDE) + got_c[zz, xx, yy, at].astype(WIDE)
                            got_c[zz, xx, yy, at] = total.astype(LOW)

            elif stage == 1:

                @pl.loop(0, depth)
                def _(zz):
                    total = got_c[zz, x, y, at].astype(WIDE)
                    for k in range(3):
                        total = total + got_q[k, zz, at].astype(WIDE)
                    got_c[zz, x, y, at] = total.astype(LOW)

            else:
                total = got_c[z, x, y, at].astype(WIDE)
                for j in range(1, depth):
                    total = total + got_z[j - 1, at].astype(WIDE)
                put(total)

    def begin(k):
        launch(k, 0)

    def after(k, stage):
        absorb(k, stage)
        if stage < 2:
            launch(k, stage + 1)

    def end():
        for stages in started:
            for copies in stages:
                for copy in copies:
                    copy.wait_send()

    return begin, after, end


def last_kernel(depth, reduces, *refs):
    (pair, seg, pad, dq_other) = refs[:4]
    held = refs[4:15]
    (small_rows, small_cols, ga_in, gs_in) = refs[15:19]
    refs = refs[19:]
    if reduces:
        parts, refs = refs[:4], refs[4:]
    grad_input, grad_enc = refs[:2]
    refs = refs[2:]
    outs = refs[:9] if reduces else refs[:2]
    refs = refs[9:] if reduces else refs[2:]
    (dkv, enc, dq_own, start, one, qkv, low, lse, after, two, gstate) = refs[:11]
    (ga, gs, g_query, g_attn, dqkv, dk, dv, row_seg, row_keep, col_seg, load_sem, dq_got, sw_send, sw_recv) = refs[11:25]
    refs = refs[25:]
    refs_held = (dkv, enc, dq_own, start, one, qkv, low, lse, after, two, gstate)
    tok_count, width = dq_own.shape
    src_count = enc.shape[0]
    everyone = depth * 8
    me = Place(depth)
    scale = (tok_count * everyone) ** (-0.5)
    loads = []
    for src, dst in list(zip(held, refs_held)) + [(gs_in, gs), (ga_in, ga)]:
        copy = pltpu.make_async_copy(src, dst, load_sem.at[len(loads)])
        copy.start()
        loads.append(copy)
    if reduces:
        greet(me.others() + [me.across_x(), me.across_y(), me.across_both(), me.across_core()])
    else:
        greet([me.across_y()])
    halves = 2
    half = tok_count // halves
    swaps = []
    for k in range(halves):
        at = pl.ds(k * half, half)
        swaps.append(remote(dq_other.at[at], dq_got.at[at], sw_send.at[k], sw_recv.at[k], me.across_y()))
        swaps[-1].start()

    if reduces:
        (late, late_s, ex, ey, ex_got, ey_got, ez, ez_got, c_a, c_s, q_a, q_s, z_a, z_s, ez_send, ez_recv, send, recv) = refs
        (o_qkv, o_so, o_cq, o_kv, o_co, o_fi, o_fo, o_in, o_s) = outs

        def put_kv(total):
            o_kv[:, 0:BLOCK] = total[0:16] * scale
            o_kv[:, BLOCK : 2 * BLOCK] = total[16:32] * scale

        def put_mid(total):
            o_so[...] = total[0:16] * scale
            o_cq[...] = total[16:32] * scale

        def put_qkv(k, total):
            o_qkv[:, k * BLOCK : (k + 1) * BLOCK] = total * scale

        def put_s(total):
            o_s[...] = total * scale

        def rows(lo, hi, put):
            return (late, c_a, q_a, z_a, pl.ds(lo, hi - lo), put)

        chunks = [
            [rows(KV, EARLY, put_kv)],
            [rows(SO, KV, put_mid)],
            [rows(0, 16, partial(put_qkv, 0))],
            [rows(16, 32, partial(put_qkv, 1))],
            [rows(32, SO, partial(put_qkv, 2))],
            [(late_s, c_s, q_s, z_s, pl.ds(0, 16), put_s)],
        ]

        z, x, y = me.z, me.x, me.y
        for total, own, got in ((ex, parts[0], parts[1]), (ey, parts[2], parts[3])):

            @pl.loop(0, depth)
            def _(zz):
                for k in range(2):
                    total[k, zz] = (own[k, zz].astype(WIDE) + got[k, zz].astype(WIDE)).astype(LOW)

        plane = [
            remote(ex.at[1 - x], ex_got, ez_send.at[0], ez_recv.at[0], me.across_x()),
            remote(ey.at[1 - y], ey_got, ez_send.at[1], ez_recv.at[1], me.across_y()),
        ]
        for copy in plane:
            copy.start()
        along = []

        def onward():
            for copy in plane:
                copy.wait_recv()

            @pl.loop(0, depth)
            def _(zz):
                ez[zz, 0:RETURNED] = (ex[x, zz].astype(WIDE) + ex_got[zz].astype(WIDE)).astype(LOW)
                ez[zz, RETURNED:LATE] = (ey[y, zz].astype(WIDE) + ey_got[zz].astype(WIDE)).astype(LOW)

            for k in range(1, depth):
                to = lax.rem(z + k, depth)
                at = 1 + k
                along.append(remote(ez.at[to], ez_got.at[k - 1], ez_send.at[at], ez_recv.at[at], me.along(k)))
                along[-1].start()

        def settle():
            for copy in plane:
                copy.wait_send()
            for copy in along:
                copy.wait()
            total = ez[me.z].astype(WIDE)
            for k in range(depth - 1):
                total = total + ez_got[k].astype(WIDE)
            total = total * scale
            o_co[...] = total[0:16]
            for k in range(4):
                o_fi[:, k * BLOCK : (k + 1) * BLOCK] = total[16 + 16 * k : 32 + 16 * k]
            o_fo[...] = total[80:144]
            half = BLOCK // 2
            for k in range(2):
                o_in[16 * k : 16 * (k + 1)] = total[144:160, half * k : half * (k + 1)]

        begin, after_stage, end = reduction(me, chunks, send, recv)

        def keep(lo, value):
            late[:, :, :, :, lo : lo + 16] = value.astype(LOW).reshape(late.shape[:4] + (16, BLOCK))

        def keep_small(value):
            late_s[...] = value.astype(LOW).reshape(late_s.shape)
    else:
        def begin(k):
            return None

        def after_stage(k, stage):
            return None

        end = onward = settle = lambda: None
        o_late, o_small = outs

        def keep(lo, value):
            o_late[:, lo : lo + 16] = value.astype(LOW).reshape((-1, 16, BLOCK))

        def keep_small(value):
            o_small[...] = value

    chunk_kv, chunk_mid, chunk_q, chunk_k, chunk_v, chunk_s = range(6)
    onehot = token_numbers(seg, pad, pair, row_seg, row_keep, col_seg)
    cut = cutter(ga)
    for copy in loads[:2]:
        copy.wait()
    keep(KV, dot_tn(enc[...], dkv[:, 0:width]))
    keep(KV + 16, dot_tn(enc[...], dkv[:, width : 2 * width]))
    begin(chunk_kv)
    for copy in loads[2:]:
        copy.wait()
    table = cutter(gs)(0, gs.shape[-2]).astype(WIDE).T
    self_backward_start(dk, dv)
    gains = biases = 0.0
    for k in range(halves):
        at = pl.ds(k * half, half)
        swaps[k].wait()
        query = (dq_own[at, :] + dq_got[at, :].astype(WIDE)).astype(LOW)
        g_query[at, :] = query
        back, gain_1, bias_1 = norm_back(after[at, :], table[1:2], dot_nt(query, cut(CQ, KV)))
        gains, biases = gains + gain_1, biases + bias_1
        state = gstate[at, :] + back
        gstate[at, :] = state
        g_attn[at, :] = dot_nt(state.astype(LOW), cut(SO, CQ)).astype(LOW)
        if k == 0:
            after_stage(chunk_kv, 0)
        if k == halves - 1:
            keep(CQ, dot_tn(two[...], g_query[...]))
            keep(SO, dot_tn(low[...], gstate[...].astype(LOW)))
            begin(chunk_mid)
        blocks = (k * half // 128, (k + 1) * half // 128)
        self_backward(blocks, qkv, low, lse, g_attn, dqkv, dk, dv, row_seg, row_keep, col_seg)
        if k == 0:
            onward()
    after_stage(chunk_mid, 0)
    self_backward_end(dqkv, dk, dv)
    for k, chunk in enumerate((chunk_q, chunk_k, chunk_v)):
        keep(QKV + 16 * k, dot_tn(one[...], dqkv[:, k * width : (k + 1) * width]))
        begin(chunk)
    after_stage(chunk_q, 0)
    after_stage(chunk_k, 0)
    after_stage(chunk_v, 0)
    after_stage(chunk_kv, 1)
    upstream = dot_nt(dqkv[:, 0:width], cut(QKV, QKV + 16))
    upstream = upstream + dot_nt(dqkv[:, width : 2 * width], cut(QKV + 16, QKV + 32))
    upstream = upstream + dot_nt(dqkv[:, 2 * width : 3 * width], cut(QKV + 32, SO))
    back, gain_0, bias_0 = norm_back(start[...], table[0:1], upstream)
    grad_start = gstate[...] + back
    grad_input[...] = grad_start.astype(LOW)
    coarse = grad_start.astype(LOW)
    fine = (grad_start - coarse.astype(WIDE)).astype(LOW)
    g_table = (dot_tn(onehot, coarse) + dot_tn(onehot, fine))[8:16]
    mid = small_rows[...]
    stacked = jnp.concatenate([gain_0, gains, mid[0:2], bias_0, biases, mid[2:4], g_table], axis=0)
    keep_small(transposed_rows(stacked) + small_cols[...])
    begin(chunk_s)
    after_stage(chunk_mid, 1)
    w_key, w_val = cut(KV, KV + 16), cut(KV + 16, EARLY)
    span = src_count // 4

    def source_grads(k):
        at = pl.ds(k * span, span)
        grads = dot_nt(dkv[at, 0:width], w_key) + dot_nt(dkv[at, width : 2 * width], w_val)
        grad_enc[at, :] = grads.astype(LOW)

    source_grads(0)
    after_stage(chunk_s, 0)
    after_stage(chunk_kv, 2)
    after_stage(chunk_q, 1)
    source_grads(1)
    after_stage(chunk_k, 1)
    source_grads(2)
    after_stage(chunk_v, 1)
    after_stage(chunk_s, 1)
    source_grads(3)
    settle()
    for chunk in (chunk_mid, chunk_q, chunk_k, chunk_v, chunk_s):
        after_stage(chunk, 2)
    end()


def last_part(depth, reduces, pair, seg, pad, dq_own, dq_other, dkv, enc, kept, gstate, grads, whole):
    tok_count, width = dq_own.shape
    src_count = enc.shape[0]
    ga, gs = whole
    parts, small_rows, small_cols = grads
    everyone = depth * 8
    rows = BLOCK // everyone
    sharded = (depth, 2, 2, 2)
    held = (dkv, enc, dq_own, *kept, gstate)
    outs = [shape_of((tok_count, width), LOW), shape_of((src_count, width), LOW)]
    scratch = [pltpu.VMEM(a.shape, a.dtype) for a in held]
    scratch += [
        pltpu.VMEM(ga.shape, LOW),
        pltpu.VMEM(gs.shape, LOW),
        pltpu.VMEM((tok_count, width), LOW),
        pltpu.VMEM((tok_count, width), LOW),
        pltpu.VMEM((tok_count, 3 * width), LOW),
        pltpu.VMEM((tok_count, width), WIDE),
        pltpu.VMEM((tok_count, width), WIDE),
        pltpu.VMEM((1, tok_count), WIDE),
        pltpu.VMEM((1, tok_count), WIDE),
        pltpu.VMEM((tok_count, 128), WIDE),
        pltpu.SemaphoreType.DMA((14,)),
        pltpu.VMEM((tok_count, width), LOW),
        pltpu.SemaphoreType.DMA((2,)),
        pltpu.SemaphoreType.DMA((2,)),
    ]
    if reduces:
        shapes = [(EARLY, BLOCK), (16, 128)]
        outs += [
            shape_of((rows, 3 * BLOCK), WIDE),
            shape_of((rows, BLOCK), WIDE),
            shape_of((rows, BLOCK), WIDE),
            shape_of((rows, 2 * BLOCK), WIDE),
            shape_of((rows, BLOCK), WIDE),
            shape_of((rows, 4 * BLOCK), WIDE),
            shape_of((4 * rows, BLOCK), WIDE),
            shape_of((2 * rows, BLOCK // 2), WIDE),
            shape_of((rows, 128), WIDE),
        ]
        scratch += [pltpu.VMEM(sharded + s, LOW) for s in shapes]
        scratch += [pltpu.VMEM(parts[0].shape, LOW), pltpu.VMEM(parts[2].shape, LOW)]
        scratch += [pltpu.VMEM(parts[0].shape[1:], LOW), pltpu.VMEM(parts[2].shape[1:], LOW)]
        scratch += [pltpu.VMEM((depth, LATE, BLOCK), LOW), pltpu.VMEM((depth - 1, LATE, BLOCK), LOW)]
        for lead in ((depth, 2, 2), (3, depth), (depth - 1,)):
            scratch += [pltpu.VMEM(lead + s, LOW) for s in shapes]
        scratch += [pltpu.SemaphoreType.DMA((depth + 2,))] * 2
        slots = 2 * (depth + 3)
        scratch += [pltpu.SemaphoreType.DMA((6, slots)), pltpu.SemaphoreType.DMA((6, slots))]
    else:
        outs += [shape_of((BLOCK // 16, EARLY, BLOCK), LOW), shape_of((BLOCK, 128), WIDE)]
    return pl.pallas_call(
        partial(last_kernel, depth, reduces),
        name="last_part",
        out_shape=outs,
        in_specs=[SMEM] + [VMEM] * 2 + [ANY] * 12 + [VMEM] * 2 + [ANY] * 2 + [VMEM] * len(parts),
        out_specs=[VMEM] * len(outs),
        scratch_shapes=scratch,
        compiler_params=pltpu.CompilerParams(
            collective_id=2, has_side_effects=True, vmem_limit_bytes=LIMIT
        ),
    )(pair, seg, pad, dq_other, *held, small_rows, small_cols, ga, gs, *parts)


def finish_kernel(count, *refs):
    ins, (small_in, loss_in) = refs[:count], refs[count : count + 2]
    outs, tiny_outs = refs[count + 2 : 2 * count + 2], refs[2 * count + 2 : 2 * count + 7]
    refs = refs[2 * count + 7 :]
    held, (small, loss) = refs[:count], refs[count : count + 2]
    tiny, sems = refs[count + 2 : count + 7], refs[count + 7]
    ahead = [pltpu.make_async_copy(small_in, small, sems.at[0, count]), pltpu.make_async_copy(loss_in, loss, sems.at[0, count + 1])]
    first = [pltpu.make_async_copy(ins[k], held[k], sems.at[0, k]) for k in range(count)]
    copies = [pltpu.make_async_copy(held[k], outs[k], sems.at[1, k]) for k in range(count)]
    for copy in ahead + first:
        copy.start()
    for copy in ahead:
        copy.wait()
    values = small[...]
    rows = values.shape[0]
    turned = jnp.concatenate([values, jnp.zeros((128 - rows, 128), WIDE)], axis=0).T
    for ref, lo, hi in zip(tiny[:4], (0, 4, 8, 16), (4, 8, 16, 18)):
        ref[...] = turned[lo:hi, 0:rows]
    tiny[4][...] = loss[...]
    for k in range(5):
        copies.append(pltpu.make_async_copy(tiny[k], tiny_outs[k], sems.at[1, count + k]))
        copies[-1].start()
    for k in range(count):
        first[k].wait()
        copies[k].start()
    for copy in copies:
        copy.wait()


def finish(results, small, loss):
    count = len(results)
    rows = small.shape[0]
    tiny = [shape_of(s, WIDE) for s in ((4, rows), (4, rows), (PAIRS, rows), (2, rows), (1, 1))]
    outs = [shape_of(a.shape, a.dtype) for a in results] + tiny
    held = list(results) + [small, loss] + tiny
    res = pl.pallas_call(
        partial(finish_kernel, count),
        name="finish",
        out_shape=outs,
        in_specs=[ANY] * (count + 2),
        out_specs=[ANY] * len(outs),
        scratch_shapes=[pltpu.VMEM(a.shape, a.dtype) for a in held]
        + [pltpu.SemaphoreType.DMA((2, count + 5))],
        compiler_params=pltpu.CompilerParams(vmem_limit_bytes=LIMIT),
    )(*results, small, loss)
    return res[:count], res[count:]


def late_blocks(cross_out, ffn_in, ffn_out, insert):
    groups = cross_out.shape[0] // 16
    return jnp.concatenate(
        [
            cross_out.reshape(groups, 16, BLOCK),
            ffn_in.reshape(groups, 16, 4, BLOCK).swapaxes(1, 2).reshape(groups, 64, BLOCK),
            ffn_out.reshape(groups, 64, BLOCK),
            insert.reshape(groups, 2, 16, BLOCK // 2).swapaxes(1, 2).reshape(groups, 16, BLOCK),
        ],
        axis=1,
    )


def gather_by_ops(qkv, self_out, cross_q, cross_kv, small):
    wide = jnp.concatenate([qkv, self_out, cross_q, cross_kv], axis=1)
    ga = lax.all_gather(wide, BOTH, axis=0, tiled=True).reshape(-1, 16, 7, BLOCK).swapaxes(1, 2)
    gs = lax.all_gather(small, BOTH, axis=0, tiled=True)
    return ga.reshape(-1, EARLY, BLOCK), gs.reshape(-1, 16, 128)


def partner(array, depth, axis):
    dx, dy = (1, 0) if axis == "x" else (0, 1)
    pairs = []
    for z in range(depth):
        for x in range(2):
            for c in range(2):
                for y in range(2):
                    here = ((z * 2 + x) * 2 + c) * 2 + y
                    there = ((z * 2 + (x ^ dx)) * 2 + c) * 2 + (y ^ dy)
                    pairs.append((here, there))
    return lax.ppermute(array, BOTH, pairs)


def reduce_by_ops(early, small, late, scale):
    groups = late.shape[0]
    gw_f = late[:, 80:144].reshape(groups * 64, BLOCK)
    gw_i = late[:, 144:160].reshape(groups, 16, 2, BLOCK // 2).swapaxes(1, 2).reshape(groups * 32, BLOCK // 2)
    late = late[:, 0:80].reshape(groups, 5, 16, BLOCK).swapaxes(0, 1).reshape(5, BLOCK, BLOCK)
    early = early.reshape(groups, 7, 16, BLOCK).swapaxes(0, 1).reshape(7, BLOCK, BLOCK)
    wide = jnp.concatenate([early, late]).swapaxes(0, 1).reshape(BLOCK, 12 * BLOCK)

    def sums(a):
        return lax.psum_scatter(a.astype(WIDE), BOTH, scatter_dimension=0, tiled=True) * scale

    own = sums(wide)
    edges = (0, 3, 4, 5, 7, 8, 12)
    pieces = [own[:, lo * BLOCK : hi * BLOCK] for lo, hi in zip(edges[:-1], edges[1:])]
    return pieces + [sums(gw_f), sums(gw_i), sums(small)]


def body(
    dec_input, enc_output, segment_ids, padding, pair_ids, src_lengths, delete_labels, insert_counts,
    masked_positions, masked_targets, norm_gain, norm_bias, pair_table, self_qkv, self_out, cross_q, cross_kv,
    cross_out, ffn_in, ffn_out, w_delete, w_insert, w_vocab,
):
    everyone = lax.axis_size(BOTH)
    depth = everyone // 8
    tok_count = dec_input.shape[0]
    aligned = self_qkv.shape[0] == 16
    late = (cross_out, ffn_in, ffn_out, w_insert)
    tiny = (norm_gain, norm_bias, pair_table, w_delete.T)
    raw = (self_qkv, self_out, cross_q, cross_kv)
    whole = gathered = None
    if not aligned:
        gathered = late_blocks(*[lax.all_gather(a, BOTH, axis=0, tiled=True) for a in late])
        small = jnp.concatenate([norm_gain, norm_bias, pair_table, w_delete.T], axis=0).T
        small = jnp.pad(small, ((0, 0), (0, 128 - small.shape[1])))
        whole = gather_by_ops(*raw, small)
    whole, line, firsts = first_part(
        depth, aligned, segment_ids, padding, pair_ids, dec_input, enc_output, tiny, raw, late, whole
    )
    start, one, qkv, low, lse, after, two, query, other_query, kv, other_seg = firsts
    parts = (*line, partner(line[0], depth, "x")) if aligned else (gathered,)
    o_own, o_other, lse_own, lse_other = cross_forward(src_lengths, segment_ids, other_seg, query, other_query, kv)
    mids = middle_part(
        depth, aligned, segment_ids, padding, delete_labels, insert_counts, masked_positions, masked_targets,
        w_vocab, after, (o_own, o_other, lse_own, lse_other), whole[1], parts,
    )
    count = 4 if aligned else 1
    parts, mids = mids[:count], mids[count:]
    block_out, gstate, g_own, g_other, st_own, st_other, small_rows, small_cols, grad_vocab, tokens, loss = mids
    sums = ()
    if aligned:
        sums = (parts[2], partner(parts[0], depth, "y"), parts[3], partner(parts[1], depth, "x"))
    dq_own, dq_other, dkv, block_out, grad_vocab = cross_backward(
        src_lengths, segment_ids, other_seg, query, other_query, g_own, g_other, st_own, st_other, kv,
        (block_out, grad_vocab),
    )
    res = last_part(
        depth, aligned, pair_ids, segment_ids, padding, dq_own, dq_other, dkv, enc_output,
        (start, one, qkv, low, lse, after, two), gstate, (sums, small_rows, small_cols), whole,
    )
    if aligned:
        sums = res[2:]
    else:
        scale = (tok_count * everyone) ** (-0.5)
        sums = reduce_by_ops(res[2], res[3], parts[0], scale)
    results, smalls = finish((res[1], res[0], *sums[:8], tokens), sums[8], loss)
    grad_enc, grad_input, qkv, so, cq, kv, co, fi, fo, insert, tokens = results
    gain, bias, table, delete, loss = smalls
    return (
        block_out, grad_input, grad_enc, gain, bias, table, qkv, so, cq, kv, co, fi, fo, delete.T, insert,
        grad_vocab, loss[0, 0], tokens,
    )


def solution(mesh):
    shared = P(BOTH, None)
    across = P(None, BOTH)
    return jax.shard_map(
        body,
        mesh=mesh,
        in_specs=(shared,) * 5 + (P("batch", None),) + (shared,) * 4 + (across,) * 3 + (shared,) * 10,
        out_specs=(shared,) * 3 + (across,) * 3 + (shared,) * 10 + (P(), shared),
        check_vma=False,
    )
```

```python
from functools import partial

import jax
import jax.numpy as jnp
from jax import lax
from jax.experimental import pallas as pl
from jax.experimental.pallas import tpu as pltpu
from jax.sharding import PartitionSpec as P

HD = 64
PAIRS = 8
SEGS = 8
BLOCK = 512
EPSILON = 1e-05
SCALE = 0.125
FILL = -1e30
GELU = 0.7978845608
CUBIC = 0.044715

MESH = pl.DeviceIdType.MESH
ANY = pl.BlockSpec(memory_space=pl.ANY)
VMEM = pl.BlockSpec(memory_space=pltpu.VMEM)
SMEM = pl.BlockSpec(memory_space=pltpu.SMEM)
BOTH = ("batch", "src")
LOW = jnp.bfloat16
WIDE = jnp.float32
LIMIT = 64 << 20


def shape_of(shape, kind):
    return jax.ShapeDtypeStruct(shape, kind)


def dot(left, right):
    return jnp.dot(left, right, preferred_element_type=WIDE)


def dot_tn(left, right):
    return lax.dot_general(left, right, (((0,), (0,)), ((), ())), preferred_element_type=WIDE)


def dot_nt(left, right):
    return lax.dot_general(left, right, (((1,), (1,)), ((), ())), preferred_element_type=WIDE)


def normalised(v):
    centred = v - jnp.mean(v, axis=-1, keepdims=True)
    r = lax.rsqrt(jnp.mean(centred * centred, axis=-1, keepdims=True) + EPSILON)
    return centred * r, r


def norm_back(v, gain, upstream):
    hat, r = normalised(v)
    scaled = upstream * gain
    first = jnp.mean(scaled, axis=-1, keepdims=True)
    second = jnp.mean(scaled * hat, axis=-1, keepdims=True)
    grad_gain = jnp.sum(upstream * hat, axis=0, keepdims=True)
    grad_bias = jnp.sum(upstream, axis=0, keepdims=True)
    return r * (scaled - first - hat * second), grad_gain, grad_bias


def lanes(shape):
    return lax.broadcasted_iota(jnp.int32, shape, len(shape) - 1)


def rows_of(shape):
    return lax.broadcasted_iota(jnp.int32, shape, len(shape) - 2)


def both_heads(x):
    low = lanes(x.shape) < HD
    zero = jnp.zeros_like(x)
    return jnp.concatenate([jnp.where(low, x, zero), jnp.where(low, zero, x)], axis=0)


def join_heads(x):
    half = x.shape[0] // 2
    return jnp.where(lanes((half, x.shape[1])) < HD, x[:half], x[half:])


def twice(x):
    return jnp.concatenate([x, x], axis=0)


def transposed_rows(rows):
    count, width = rows.shape
    return jnp.concatenate([rows, jnp.zeros((128 - count, width), WIDE)], axis=0).T


def greet(peers):
    barrier = pltpu.get_barrier_semaphore()
    for peer in peers:
        pl.semaphore_signal(barrier, inc=1, device_id=peer, device_id_type=MESH)
    pl.semaphore_wait(barrier, len(peers))


def remote(src, dst, send, recv, peer):
    return pltpu.make_async_remote_copy(
        src_ref=src,
        dst_ref=dst,
        send_sem=send,
        recv_sem=recv,
        device_id=peer,
        device_id_type=MESH,
    )


class Place:
    def __init__(self, depth):
        b = lax.axis_index("batch")
        self.depth = depth
        self.y = lax.axis_index("src")
        self.c = lax.rem(b, 2)
        self.x = lax.rem(b // 2, 2)
        self.z = b // 4

    def at(self, z=None, x=None, c=None, y=None):
        z = self.z if z is None else z
        x = self.x if x is None else x
        c = self.c if c is None else c
        y = self.y if y is None else y
        return ((z * 2 + x) * 2 + c, y)

    def along(self, k):
        return self.at(z=lax.rem(self.z + k, self.depth))

    def others(self):
        return [self.along(k) for k in range(1, self.depth)]

    def across_x(self):
        return self.at(x=1 - self.x)

    def across_y(self):
        return self.at(y=1 - self.y)

    def across_both(self):
        return self.at(x=1 - self.x, y=1 - self.y)

    def across_core(self):
        return self.at(c=1 - self.c)


def gathering(me, chunks, send, recv):
    z, x, c, y = me.z, me.x, me.c, me.y
    started = [[None] * 3 for _ in chunks]
    used = [0] * len(chunks)
    every = slice(None)

    def launch(k, stage):
        copies = []

        def push(block, peer):
            slot = used[k]
            used[k] += 1
            copy = remote(block, block, send.at[k, slot], recv.at[k, slot], peer)
            copy.start()
            copies.append(copy)

        for view in chunks[k]:
            if stage == 0:
                for peer in me.others():
                    push(view(z, x, c, y), peer)
            elif stage == 1:
                for peer in (me.across_x(), me.across_y(), me.across_both()):
                    push(view(every, x, c, y), peer)
            else:
                push(view(every, every, c, every), me.across_core())
        started[k][stage] = copies

    def begin(k):
        launch(k, 0)

    def after(k, stage):
        for copy in started[k][stage]:
            copy.wait_recv()
        if stage < 2:
            launch(k, stage + 1)

    def end():
        for stages in started:
            for copies in stages:
                for copy in copies:
                    copy.wait_send()

    return begin, after, end


def self_window(block, tok_count):
    low = jnp.clip(block * 128 - 128, 0, tok_count - 384)
    return pl.multiple_of(low, 128)


def self_mask(row_seg, row_keep, col_seg, block, low):
    at = pl.ds(low, 384)
    keys = row_seg[0:1, at]
    keep = row_keep[0:1, at]
    queries = col_seg[pl.ds(pl.multiple_of(block * 128, 128), 128), 0:1]
    shape = (128, 384)
    own = (rows_of(shape) + block * 128) == (lanes(shape) + low)
    return (queries == keys) & ((keep > 0.5) | own)


def self_forward(blocks, qkv, out, lse_ref, row_seg, row_keep, col_seg):
    tok_count, width = out.shape
    first, last = blocks
    pairs = width // 128

    def one(block, carry):
        at = pl.ds(pl.multiple_of(block * 128, 128), 128)
        low = self_window(block, tok_count)
        keys = pl.ds(low, 384)
        allowed = twice(self_mask(row_seg, row_keep, col_seg, block, low))
        every = range(pairs)
        q = [both_heads(qkv[at, p * 128 : (p + 1) * 128] * SCALE) for p in every]
        scores = [dot_nt(q[p], qkv[keys, width + p * 128 : width + (p + 1) * 128]) for p in every]
        scores = [jnp.where(allowed, scores[p], FILL) for p in every]
        tops = [jnp.max(scores[p], axis=1, keepdims=True) for p in every]
        exps = [jnp.exp(scores[p] - tops[p]) for p in every]
        totals = [jnp.sum(exps[p], axis=1, keepdims=True) for p in every]
        probs = [(exps[p] * (1.0 / totals[p])).astype(LOW) for p in every]
        mixed = [dot(probs[p], qkv[keys, 2 * width + p * 128 : 2 * width + (p + 1) * 128]) for p in every]
        lane = lanes((128, 128))
        stats = jnp.zeros((128, 128), WIDE)
        for p in every:
            out[at, p * 128 : (p + 1) * 128] = join_heads(mixed[p]).astype(LOW)
            lse = tops[p] + jnp.log(totals[p])
            stats = jnp.where(lane == 2 * p, lse[:128], jnp.where(lane == 2 * p + 1, lse[128:], stats))
        lse_ref[at, :] = stats
        return carry

    lax.fori_loop(first, last, one, 0)


def small_matrix(gain, bias, pair_rows, delete):
    def spot(count, first):
        shape = (count, 128)
        return (rows_of(shape) + first == lanes(shape)).astype(LOW)

    total = dot_tn(gain, spot(4, 0)) + dot_tn(bias, spot(4, 4)) + dot_tn(pair_rows, spot(PAIRS, 8))
    return (total + dot_tn(delete, spot(2, 8 + PAIRS))).astype(LOW)


def token_numbers(seg, pad, pair, row_seg, row_keep, col_seg):
    tok_count = seg.shape[1]
    segments = seg[...].astype(WIDE)
    row_seg[...] = segments
    row_keep[...] = 1.0 - pad[...].astype(WIDE)
    pair_row = jnp.zeros((1, tok_count), WIDE)
    for k in range(SEGS):
        pair_row = jnp.where(segments == k, pair[0, k].astype(WIDE), pair_row)
    columns = transposed_rows(jnp.concatenate([segments, pair_row, jnp.zeros((6, tok_count), WIDE)], axis=0))
    col_seg[...] = columns
    return (lanes((tok_count, 128)) == (columns[:, 1:2].astype(jnp.int32) + 8)).astype(LOW)


def cutter(ref):
    every = (slice(None),) * (len(ref.shape) - 2)

    def cut(lo, hi):
        value = ref[every + (slice(lo, hi),)]
        return value.reshape((-1, value.shape[-1]))

    return cut


QKV, SO, CQ, KV, EARLY = 0, 48, 64, 80, 112
LATE, PERMUTED, RETURNED = 160, 96, 128


def first_kernel(depth, gathers, *refs):
    (seg, pad, pair, dec, enc_in) = refs[:5]
    refs = refs[5:]
    if gathers:
        (gain, bias, pair_rows, delete, raw_qkv, raw_so, raw_cq, raw_kv, raw_co, raw_fi, raw_fo, raw_in) = refs[:12]
        (ga_out, gs_out, gz1, gz2) = refs[12:16]
        refs = refs[16:]
    else:
        ga_in, gs_in = refs[:2]
        refs = refs[2:]
    results, other_out, seg_out = refs[:9], refs[9], refs[10]
    held = refs[11:20]
    (start_ref, one_ref, qkv, low, lse, after_ref, two_ref, query, kv) = held
    (enc, ga, gs, row_seg, row_keep, col_seg, own_sem, out_sem, send, recv, sw_send, sw_recv, stage1, stage2) = refs[20:]
    tok_count, width = dec.shape
    src_count = enc.shape[0]
    me = Place(depth)
    z, x, c, y = me.z, me.x, me.c, me.y
    owns = []

    def own(src, dst):
        copy = pltpu.make_async_copy(src, dst, own_sem.at[len(owns)])
        copy.start()
        owns.append(copy)

    if gathers:
        for raw, count, first in ((raw_qkv, 3, QKV), (raw_so, 1, SO), (raw_cq, 1, CQ), (raw_kv, 2, KV)):
            for k in range(count):
                own(raw.at[:, pl.ds(k * BLOCK, BLOCK)], ga.at[z, x, c, y, pl.ds(first + 16 * k, 16)])
        soon = len(owns)
        own1, own2 = stage1, stage2
        split_fo = PERMUTED - 80
        own(raw_co, own1.at[pl.ds(0, 16)])
        for k in range(4):
            own(raw_fi.at[:, pl.ds(k * BLOCK, BLOCK)], own1.at[pl.ds(16 + 16 * k, 16)])
        own(raw_fo.at[pl.ds(0, split_fo)], own1.at[pl.ds(80, split_fo)])
        own(raw_fo.at[pl.ds(split_fo, 64 - split_fo)], own2.at[pl.ds(0, 64 - split_fo)])
        for k in range(2):
            half = BLOCK // 2
            place = own2.at[pl.ds(64 - split_fo, 16), pl.ds(half * k, half)]
            own(raw_in.at[pl.ds(16 * k, 16)], place)
        gs[z, x, c, y] = small_matrix(gain[...], bias[...], pair_rows[...], delete[...])
        greet(me.others() + [me.across_x(), me.across_y(), me.across_both(), me.across_core()])
        for copy in owns[:soon]:
            copy.wait()

        def rows(lo, hi):
            return lambda *at: ga.at[at + (pl.ds(lo, hi - lo),)]

        chunks = [[lambda *at: gs.at[at]]]
        chunks += [[rows(lo, hi)] for lo, hi in ((0, 16), (16, 32), (32, SO), (SO, KV), (KV, EARLY))]
        begin, after_stage, end = gathering(me, chunks, send, recv)
    else:
        own(ga_in, ga)
        own(gs_in, gs)
        greet([me.across_y()])
        for copy in owns:
            copy.wait()

        def begin(k):
            return None

        def after_stage(k, stage):
            return None

        def end():
            return None

    outs = []

    def out(k):
        copy = pltpu.make_async_copy(held[k], results[k], out_sem.at[len(outs)])
        copy.start()
        outs.append(copy)

    c_s, c_q, c_k, c_v, c_mid, c_kv = range(6)
    begin(c_s)
    begin(c_q)
    line, crossing = [], []
    if gathers:
        for copy in owns[soon:]:
            copy.wait()
        kept = len(owns)
        for k, (ref, spot) in enumerate(((own1, gz1.at[y, z]), (own2, gz2.at[y, z]))):
            crossing.append(remote(ref, spot, sw_send.at[3 + k], sw_recv.at[3 + k], me.across_y()))
            crossing[-1].start()
            own(ref, spot)
    meet = remote(seg, seg_out, sw_send.at[0], sw_recv.at[0], me.across_y())
    meet.start()
    fetch = pltpu.make_async_copy(enc_in, enc, out_sem.at[11])
    fetch.start()
    onehot = token_numbers(seg, pad, pair, row_seg, row_keep, col_seg)
    cut = cutter(ga)
    after_stage(c_s, 0)
    after_stage(c_q, 0)
    begin(c_k)
    after_stage(c_k, 0)
    begin(c_v)
    after_stage(c_s, 1)
    after_stage(c_q, 1)
    after_stage(c_v, 0)
    begin(c_mid)
    begin(c_kv)
    for copy in crossing:
        copy.wait()
    if gathers:
        for copy in owns[kept:]:
            copy.wait()
        far, near = me.along(depth // 2), me.at(z=z + 1 - 2 * lax.rem(z, 2))
        z_far = lax.rem(z + depth // 2, depth)

        def along(ref, peer):
            at = 5 + len(line)
            line.append(remote(ref, ref, sw_send.at[at], sw_recv.at[at], peer))
            line[-1].start()

        for ref in (gz1.at[:, z], gz2.at[:, z]):
            along(ref, far)
            along(ref, near)
    after_stage(c_s, 2)
    table = cutter(gs)(0, gs.shape[-2]).astype(WIDE).T
    start = dec[...].astype(WIDE) + dot(onehot, table.astype(LOW))
    start_ref[...] = start
    out(0)
    one = (normalised(start)[0] * table[0:1] + table[4:5]).astype(LOW)
    one_ref[...] = one
    out(1)
    after_stage(c_k, 1)
    after_stage(c_mid, 0)
    after_stage(c_q, 2)
    qkv[:, 0:BLOCK] = dot(one, cut(QKV, QKV + 16)).astype(LOW)
    after_stage(c_v, 1)
    after_stage(c_k, 2)
    qkv[:, BLOCK : 2 * BLOCK] = dot(one, cut(QKV + 16, QKV + 32)).astype(LOW)
    after_stage(c_v, 2)
    after_stage(c_kv, 0)
    qkv[:, 2 * BLOCK : 3 * BLOCK] = dot(one, cut(QKV + 32, SO)).astype(LOW)
    out(2)
    halves = 2
    span = tok_count // halves
    swaps = []
    for k in range(halves):
        at = pl.ds(k * span, span)
        self_forward((k * span // 128, (k + 1) * span // 128), qkv, low, lse, row_seg, row_keep, col_seg)
        if k == 0:
            after_stage(c_mid, 1)
            after_stage(c_mid, 2)
        after = start_ref[at, :] + dot(low[at, :], cut(SO, CQ))
        after_ref[at, :] = after
        two = (normalised(after)[0] * table[1:2] + table[5:6]).astype(LOW)
        two_ref[at, :] = two
        query[at, :] = dot(two, cut(CQ, KV)).astype(LOW)
        swap = remote(query.at[at], other_out.at[at], sw_send.at[1 + k], sw_recv.at[1 + k], me.across_y())
        swap.start()
        swaps.append(swap)
        if k == 0 and gathers:
            line[0].wait_recv()
            along(gz1.at[:, z_far], near)
            line[2].wait_recv()
            along(gz2.at[:, z_far], near)
    for k in range(3, 8):
        out(k)
    after_stage(c_kv, 1)
    after_stage(c_kv, 2)
    if gathers:
        own(ga, ga_out)
        own(gs, gs_out)
    fetch.wait()
    w_key, w_val = cut(KV, KV + 16), cut(KV + 16, EARLY)
    parts = 4
    for k in range(parts):
        span = src_count // parts
        at = pl.ds(k * span, span)
        kv[at, 0:width] = dot(enc[at, :], w_key).astype(LOW)
        kv[at, width : 2 * width] = dot(enc[at, :], w_val).astype(LOW)
    out(8)
    for copy in swaps + [meet]:
        copy.wait()
    for k, copy in enumerate(line):
        if k not in (0, 2):
            copy.wait_recv()
        copy.wait_send()
    end()
    for copy in outs + (owns[-2:] if gathers else []):
        copy.wait()


def first_part(depth, gathers, seg, pad, pair, dec, enc, tiny, raw, late, whole):
    tok_count, width = dec.shape
    src_count = enc.shape[0]
    lead = (depth, 2, 2, 2) if gathers else (BLOCK // 16,)
    results = [
        shape_of((tok_count, width), WIDE),
        shape_of((tok_count, width), LOW),
        shape_of((tok_count, 3 * width), LOW),
        shape_of((tok_count, width), LOW),
        shape_of((tok_count, 128), WIDE),
        shape_of((tok_count, width), WIDE),
        shape_of((tok_count, width), LOW),
        shape_of((tok_count, width), LOW),
        shape_of((src_count, 2 * width), LOW),
    ]
    outs = results + [shape_of((tok_count, width), LOW), shape_of((1, tok_count), jnp.int32)]
    if gathers:
        outs = [
            shape_of(lead + (EARLY, BLOCK), LOW),
            shape_of(lead + (16, 128), LOW),
            shape_of((2, depth, PERMUTED, BLOCK), LOW),
            shape_of((2, depth, LATE - PERMUTED, BLOCK), LOW),
        ] + outs
    extra = (*tiny, *raw, *late) if gathers else whole
    res = pl.pallas_call(
        partial(first_kernel, depth, gathers),
        name="first_part",
        out_shape=outs,
        in_specs=[VMEM, VMEM, SMEM, VMEM, ANY] + ([VMEM] * 4 + [ANY] * 8 if gathers else [ANY] * 2),
        out_specs=[ANY] * len(outs),
        scratch_shapes=[pltpu.VMEM(a.shape, a.dtype) for a in results]
        + [
            pltpu.VMEM(enc.shape, LOW),
            pltpu.VMEM(lead + (EARLY, BLOCK), LOW),
            pltpu.VMEM(lead + (16, 128), LOW),
            pltpu.VMEM((1, tok_count), WIDE),
            pltpu.VMEM((1, tok_count), WIDE),
            pltpu.VMEM((tok_count, 128), WIDE),
            pltpu.SemaphoreType.DMA((20,)),
            pltpu.SemaphoreType.DMA((12,)),
            pltpu.SemaphoreType.DMA((6, depth + 3)),
            pltpu.SemaphoreType.DMA((6, depth + 3)),
            pltpu.SemaphoreType.DMA((2 * depth + 3,)),
            pltpu.SemaphoreType.DMA((2 * depth + 3,)),
            pltpu.VMEM((PERMUTED, BLOCK), LOW),
            pltpu.VMEM((LATE - PERMUTED, BLOCK), LOW),
        ],
        compiler_params=pltpu.CompilerParams(
            collective_id=0, has_side_effects=True, vmem_limit_bytes=LIMIT
        ),
    )(seg, pad, pair, dec, enc, *extra)
    if gathers:
        whole, line, res = res[:2], res[2:4], res[4:]
    else:
        line = None
    start, one, qkv, low, lse, after, two, query, kv, other_query, other_seg = res
    return whole, line, (start, one, qkv, low, lse, after, two, query, other_query, kv, other_seg)


def segment_ends(lengths, ends):
    total = jnp.int32(0)
    ends[0] = total
    for s in range(2 * SEGS):
        total = total + lengths[0, s]
        ends[s + 1] = total


def block_ranges(seg_s, first_seg, ends, off, src_count, block):
    at = pl.multiple_of(block * 128, 128)
    low = jnp.clip(ends[first_seg + seg_s[0, at]] - off, 0, src_count)
    high = jnp.clip(ends[first_seg + seg_s[0, at + 127] + 1] - off, 0, src_count)
    first = low // TILE
    return first, jnp.where(high > low, (high + TILE - 1) // TILE, first)


def key_bounds(segs, firsts, ends, off):
    rows = []
    for seg, first_seg in zip(segs, firsts):
        low = jnp.zeros(seg.shape, jnp.int32)
        high = jnp.zeros(seg.shape, jnp.int32)
        for s in range(SEGS):
            low = jnp.where(seg == s, ends[first_seg + s] - off, low)
            high = jnp.where(seg == s, ends[first_seg + s + 1] - off, high)
        rows += [low, high]
    return jnp.concatenate(rows + [jnp.zeros((4, rows[0].shape[1]), jnp.int32)], axis=0)


TILE = 256


def side_by_side(x):
    return jnp.concatenate([x, x], axis=1)


def side_by_side_rows(rows, k, at):
    return jnp.concatenate([rows[k : k + 1, at], rows[k + 1 : k + 2, at]], axis=1)


def heads_apart(x):
    n = x.shape[1] // 2
    return jnp.concatenate([x[:HD, :n], x[HD:, n:]], axis=0).T


def cross_forward_kernel(
    lengths, seg_so, seg_sp, seg_vo, seg_vp, q_own, q_other, kv, o_own, o_other, lse_own, lse_other,
    ends, bounds, qs, top_ref, total_ref, acc_ref,
):
    tok_count, width = q_own.shape
    src_count = kv.shape[0]
    pairs = width // 128
    pos = lax.axis_index("src")
    off = pos * src_count
    firsts = (pos * SEGS, (1 - pos) * SEGS)
    segment_ends(lengths, ends)
    bounds[...] = key_bounds((seg_vo[...], seg_vp[...]), firsts, ends, off)
    for side, (q, o, lse_ref) in enumerate(((q_own, o_own, lse_own), (q_other, o_other, lse_other))):

        @pl.loop(0, tok_count // 128)
        def _(block):
            at = pl.ds(pl.multiple_of(block * 128, 128), 128)
            first, last = block_ranges((seg_so, seg_sp)[side], firsts[side], ends, off, src_count, block)
            low, high = bounds[2 * side : 2 * side + 1, at], bounds[2 * side + 1 : 2 * side + 2, at]
            for p in range(pairs):
                qs[p] = both_heads(q[at, p * 128 : (p + 1) * 128] * SCALE)
            top_ref[...] = jnp.full_like(top_ref, FILL)
            total_ref[...] = jnp.zeros_like(total_ref)
            acc_ref[...] = jnp.zeros_like(acc_ref)

            def one(t, carry):
                base = pl.multiple_of(t * TILE, TILE)
                keys = pl.ds(base, TILE)
                index = rows_of((TILE, 128)) + base
                barred = side_by_side(jnp.where((index >= low) & (index < high), 0.0, FILL))
                every = range(pairs)
                scores = [dot_nt(kv[keys, pl.ds(p * 128, 128)], qs[p]) for p in every]
                scores = [scores[p] + barred for p in every]
                olds = [top_ref[p] for p in every]
                tops = [jnp.maximum(olds[p], jnp.max(scores[p], axis=0, keepdims=True)) for p in every]
                exps = [jnp.exp(scores[p] - jnp.maximum(tops[p], 0.1 * FILL)) for p in every]
                fades = [jnp.exp(olds[p] - tops[p]) for p in every]
                sums = [total_ref[p] * fades[p] + jnp.sum(exps[p], axis=0, keepdims=True) for p in every]
                mixed = [dot_tn(kv[keys, pl.ds(width + p * 128, 128)], exps[p].astype(LOW)) for p in every]
                mixed = [acc_ref[p] * fades[p] + mixed[p] for p in every]
                for p in every:
                    top_ref[p] = tops[p]
                    total_ref[p] = sums[p]
                    acc_ref[p] = mixed[p]
                return carry

            lax.fori_loop(first, last, one, 0)
            stats = []
            for p in range(pairs):
                total = total_ref[p]
                safe = jnp.where(total > 0.0, total, 1.0)
                o[at, p * 128 : (p + 1) * 128] = heads_apart(acc_ref[p] * (1.0 / safe)).astype(LOW)
                lse = jnp.where(total > 0.0, top_ref[p] + jnp.log(safe), FILL)
                stats += [lse[:, :128], lse[:, 128:]]
            lse_ref[:, at] = jnp.concatenate(stats, axis=0)


def cross_forward(lengths, seg_own, seg_other, q_own, q_other, kv):
    tok_count, width = q_own.shape
    heads = width // HD
    pairs = width // 128
    out = shape_of((tok_count, width), LOW)
    lse = shape_of((heads, tok_count), WIDE)
    return pl.pallas_call(
        cross_forward_kernel,
        name="cross_forward",
        out_shape=[out, out, lse, lse],
        in_specs=[SMEM] * 3 + [VMEM] * 5,
        out_specs=[VMEM] * 4,
        scratch_shapes=[
            pltpu.SMEM((32,), jnp.int32),
            pltpu.VMEM((8, tok_count), jnp.int32),
            pltpu.VMEM((pairs, 256, 128), LOW),
            pltpu.VMEM((pairs, 1, 256), WIDE),
            pltpu.VMEM((pairs, 1, 256), WIDE),
            pltpu.VMEM((pairs, 128, 256), WIDE),
        ],
        compiler_params=pltpu.CompilerParams(vmem_limit_bytes=LIMIT),
        cost_estimate=pl.CostEstimate(flops=1 << 33, bytes_accessed=8 << 20, transcendentals=0),
    )(lengths, seg_own, seg_other, seg_own, seg_other, q_own, q_other, kv)


def cross_backward_kernel(
    lengths, seg_so, seg_sp, seg_vo, seg_vp, q_in, q_in_2, g_in, g_in_2, st_in, st_in_2, kv_in, pass_0, pass_1,
    dq_out, dq_out_2, dkv_out, given_0, given_1, ends, bounds, acc, qs, gs, dq_acc, kv, dkv, held_0, held_1,
    q_own, q_other, g_own, g_other, st_own, st_other, dq_own, dq_other, sems, io_sems, in_sems,
):
    fetch = [pltpu.make_async_copy(kv_in, kv, io_sems.at[0])]
    given = (q_in, q_in_2, g_in, g_in_2, st_in, st_in_2)
    for k, (src, dst) in enumerate(zip(given, (q_own, q_other, g_own, g_other, st_own, st_other))):
        fetch.append(pltpu.make_async_copy(src, dst, in_sems.at[k]))
    for copy in fetch:
        copy.start()
    ways = ((pass_0, held_0, given_0), (pass_1, held_1, given_1))
    taking = [pltpu.make_async_copy(way[0], way[1], sems.at[0, k]) for k, way in enumerate(ways)]
    giving = [pltpu.make_async_copy(way[1], way[2], sems.at[1, k]) for k, way in enumerate(ways)]
    for copy in taking:
        copy.start()
    tok_count, width = q_own.shape
    src_count = kv.shape[0]
    pairs = width // 128
    pos = lax.axis_index("src")
    off = pos * src_count
    firsts = (pos * SEGS, (1 - pos) * SEGS)
    segment_ends(lengths, ends)
    bounds[...] = key_bounds((seg_vo[...], seg_vp[...]), firsts, ends, off)
    acc[...] = jnp.zeros_like(acc)
    for copy in fetch:
        copy.wait()
    stores = []
    sides = ((q_own, g_own, st_own, dq_own), (q_other, g_other, st_other, dq_other))
    for side, (q, g, st, dq) in enumerate(sides):

        @pl.loop(0, tok_count // 128)
        def _(block):
            at = pl.ds(pl.multiple_of(block * 128, 128), 128)
            first, last = block_ranges((seg_so, seg_sp)[side], firsts[side], ends, off, src_count, block)
            low, high = bounds[2 * side : 2 * side + 1, at], bounds[2 * side + 1 : 2 * side + 2, at]
            for p in range(pairs):
                cols = slice(p * 128, (p + 1) * 128)
                qs[p] = both_heads(q[at, cols] * SCALE)
                gs[p] = both_heads(g[at, cols])
            dq_acc[...] = jnp.zeros_like(dq_acc)
            lses = [side_by_side_rows(st, 2 * p, at) for p in range(pairs)]
            deltas = [side_by_side_rows(st, 8 + 2 * p, at) for p in range(pairs)]

            def one(t, carry):
                base = pl.multiple_of(t * TILE, TILE)
                keys = pl.ds(base, TILE)
                index = rows_of((TILE, 128)) + base
                barred = side_by_side(jnp.where((index >= low) & (index < high), 0.0, FILL))
                every = range(pairs)
                cols = [pl.ds(p * 128, 128) for p in every]
                vals = [pl.ds(width + p * 128, 128) for p in every]
                scores = [dot_nt(kv[keys, cols[p]], qs[p]) for p in every]
                slopes = [dot_nt(kv[keys, vals[p]], gs[p]) for p in every]
                probs = [jnp.exp(scores[p] - lses[p] + barred) for p in every]
                gscores = [(probs[p] * (slopes[p] - deltas[p])).astype(LOW) for p in every]
                grad_k = [acc[keys, cols[p]] + dot(gscores[p], qs[p]) for p in every]
                grad_v = [acc[keys, vals[p]] + dot(probs[p].astype(LOW), gs[p]) for p in every]
                grad_q = [dq_acc[p] + dot_tn(kv[keys, cols[p]], gscores[p]) for p in every]
                for p in every:
                    acc[keys, cols[p]] = grad_k[p]
                    acc[keys, vals[p]] = grad_v[p]
                    dq_acc[p] = grad_q[p]
                return carry

            lax.fori_loop(first, last, one, 0)
            for p in range(pairs):
                dq[at, p * 128 : (p + 1) * 128] = (heads_apart(dq_acc[p]) * SCALE).astype(dq.dtype)

        stores.append(pltpu.make_async_copy(dq, (dq_out, dq_out_2)[side], io_sems.at[5 + side]))
        stores[-1].start()

    for first, second in zip(taking, giving):
        first.wait()
        second.start()

    parts = 4
    span = src_count // parts
    for k in range(parts):
        at = pl.ds(k * span, span)
        dkv[at, :] = acc[at, :].astype(LOW)
        stores.append(pltpu.make_async_copy(dkv.at[at], dkv_out.at[at], io_sems.at[1 + k]))
        stores[-1].start()
    for copy in stores:
        copy.wait()
    for copy in giving:
        copy.wait()


def cross_backward(lengths, seg_own, seg_other, q_own, q_other, g_own, g_other, st_own, st_other, kv, passed):
    tok_count, width = q_own.shape
    src_count = kv.shape[0]
    pairs = width // 128
    return pl.pallas_call(
        cross_backward_kernel,
        name="cross_backward",
        out_shape=[
            shape_of((tok_count, width), WIDE),
            shape_of((tok_count, width), LOW),
            shape_of((src_count, 2 * width), LOW),
        ]
        + [shape_of(a.shape, a.dtype) for a in passed],
        in_specs=[SMEM] * 3 + [VMEM] * 2 + [ANY] * 9,
        out_specs=[ANY] * 5,
        scratch_shapes=[
            pltpu.SMEM((32,), jnp.int32),
            pltpu.VMEM((8, tok_count), jnp.int32),
            pltpu.VMEM((src_count, 2 * width), WIDE),
            pltpu.VMEM((pairs, 256, 128), LOW),
            pltpu.VMEM((pairs, 256, 128), LOW),
            pltpu.VMEM((pairs, 128, 256), WIDE),
            pltpu.VMEM(kv.shape, LOW),
            pltpu.VMEM(kv.shape, LOW),
        ]
        + [pltpu.VMEM(a.shape, a.dtype) for a in (*passed, q_own, q_other, g_own, g_other, st_own, st_other)]
        + [pltpu.VMEM((tok_count, width), WIDE), pltpu.VMEM((tok_count, width), LOW)]
        + [pltpu.SemaphoreType.DMA((2, 2)), pltpu.SemaphoreType.DMA((7,)), pltpu.SemaphoreType.DMA((6,))],
        compiler_params=pltpu.CompilerParams(vmem_limit_bytes=LIMIT),
        cost_estimate=pl.CostEstimate(flops=1 << 34, bytes_accessed=16 << 20, transcendentals=0),
    )(lengths, seg_own, seg_other, seg_own, seg_other, q_own, q_other, g_own, g_other, st_own, st_other, kv, *passed)


def merge_all(parts, count):
    top = parts[0]
    for part in parts[1:]:
        top = jnp.maximum(top, part)
    total = sum(jnp.exp(part - top) for part in parts)
    return jnp.where(rows_of(top.shape) < count, top + jnp.log(total), sum(parts))


def folded(row):
    return jnp.concatenate([row[:, k : k + 128] for k in range(0, row.shape[1], 128)], axis=0)


def unfolded(rows):
    return jnp.concatenate([rows[k : k + 1] for k in range(rows.shape[0])], axis=1)


def middle_kernel(depth, split, *refs):
    (
        seg, pad, labels, counts, positions, targets, lse_own, lse_other, vocab_in, after_in, o_in, o_other, gs,
    ) = refs[:13]
    parts = refs[13 : 13 + (3 if split else 1)]
    refs = refs[13 + len(parts) :]
    count = 4 if split else 1
    sums = refs[:count]
    refs = refs[count:]
    (
        block_out, state_out, g_own, g_other, st_own, st_other, small_rows, small_cols, grad_vocab, token_out, loss_out,
    ) = refs[:11]
    (
        w_vocab, after_self, o_own, block_ref, state_ref, g_ref, vocab_ref, out_sem,
        wm, eb, eb_got, w_s, got_o, got_lse, cross_o, cross_low, ac, bs, n3, act, slope, gpre, head,
        lt, gt, gt_got, ew, hw, pb, pb_got, rb, got_rq, got_rz, st_c, st_q, st_z, gh, g_ffn, load_sem, send, recv,
    ) = refs[11 : 11 + 41]
    sum_refs = refs[11 + 41 :]
    tok_count, width = after_self.shape
    hidden = act.shape[1]
    masked = positions.shape[1]
    vocab_local = w_vocab.shape[1]
    everyone = depth * 8
    me = Place(depth)
    z, x, c, y = me.z, me.x, me.c, me.y
    greet(me.others() + [me.across_x(), me.across_y(), me.across_both(), me.across_core()])
    used = [0]

    def push(src, dst, peer):
        k = used[0]
        used[0] += 1
        copy = remote(src, dst, send.at[k], recv.at[k], peer)
        copy.start()
        return copy

    pending = []

    def arrive(copies):
        for copy in copies:
            copy.wait_recv()
        pending.extend(copies)

    loads = []

    def load(src, dst):
        copy = pltpu.make_async_copy(src, dst, load_sem.at[len(loads)])
        copy.start()
        loads.append(copy)

    halves = 2
    span = tok_count // halves
    ranges = [pl.ds(k * span, span) for k in range(halves)]

    def swap_outputs():
        copies = [push(lse_other, got_lse, me.across_y())]
        return copies + [push(o_other.at[at], got_o.at[at], me.across_y()) for at in ranges]

    load(gs, w_s)
    load(after_in, after_self)
    load(o_in, o_own)
    load(vocab_in, w_vocab.at[c])
    shared = [push(vocab_in, w_vocab.at[c], me.across_core())]
    if split:
        rest = pl.ds(PERMUTED, LATE - PERMUTED)
        soon = pl.ds(0, PERMUTED)
        late_part = [push(parts[1].at[py], wm.at[:, x, c, py, rest], me.across_x()) for py in range(2)]
        swap = swap_outputs()
        for py in range(2):
            load(parts[0].at[py], wm.at[:, x, c, py, soon])
            load(parts[1].at[py], wm.at[:, x, c, py, rest])
            load(parts[2].at[py], wm.at[:, 1 - x, c, py, soon])
            shared.append(push(parts[0].at[py], wm.at[:, x, c, py, soon], me.across_core()))
            shared.append(push(parts[1].at[py], wm.at[:, x, c, py, rest], me.across_core()))
            shared.append(push(parts[2].at[py], wm.at[:, 1 - x, c, py, soon], me.across_core()))
    else:
        swap = swap_outputs()
        load(parts[0], wm)

    def cut(lo, hi):
        value = wm[:, :, :, :, lo:hi] if split else wm[:, lo:hi]
        return value.reshape((-1, BLOCK))

    def put(lo, value, first=0, last=None, cols=slice(0, BLOCK)):
        groups, rows, wide = value.shape
        last = depth if last is None else last
        if split:
            eb[first:last, :, :, :, lo : lo + rows, cols] = value.reshape((last - first, 2, 2, 2, rows, wide))
        else:
            step = eb.shape[0] // depth
            eb[first * step : last * step, lo : lo + rows, cols] = value

    segments = seg[...].astype(WIDE)
    keep = 1.0 - pad[...].astype(WIDE)
    lane_row = lanes((1, tok_count))
    inside = lane_row < tok_count - 1

    def following(row):
        return pltpu.roll(jnp.concatenate([row, jnp.zeros((7, tok_count), WIDE)], axis=0), tok_count - 1, 1)[0:1]

    follows = inside & (following(segments) == segments) & (keep > 0.5) & (following(keep) > 0.5)
    valid = jnp.where(follows, 1.0, 0.0)
    rows = [keep, valid, labels[...].astype(WIDE), counts[...].astype(WIDE)]
    columns = transposed_rows(jnp.concatenate(rows + [jnp.zeros((4, tok_count), WIDE)], axis=0))
    col_keep, col_valid = columns[:, 0:1], columns[:, 1:2]
    col_label, col_count = columns[:, 2:3], columns[:, 3:4].astype(jnp.int32)

    for copy in loads:
        copy.wait()
    arrive(shared)
    table = w_s[...].reshape((-1, 128)).astype(WIDE).T

    outs = []

    def out(src, dst):
        copy = pltpu.make_async_copy(src, dst, out_sem.at[len(outs)])
        copy.start()
        outs.append(copy)

    blocks = hidden // BLOCK
    weight_co = cut(0, 16)
    arrive(swap[:1])
    top = jnp.maximum(lse_own[...], got_lse[...])
    lse = top + jnp.log(jnp.exp(lse_own[...] - top) + jnp.exp(got_lse[...] - top))
    shares = jnp.concatenate([jnp.exp(lse_own[...] - lse), jnp.exp(got_lse[...] - lse)], axis=0)
    shares = transposed_rows(shares)
    low_half = lanes((span, 128)) < HD
    for k, at in enumerate(ranges):
        arrive(swap[1 + k : 2 + k])
        mine = shares[k * span : (k + 1) * span]
        for p in range(width // 128):
            cols = slice(p * 128, (p + 1) * 128)
            share_own = jnp.where(low_half, mine[:, 2 * p : 2 * p + 1], mine[:, 2 * p + 1 : 2 * p + 2])
            share_got = jnp.where(low_half, mine[:, 8 + 2 * p : 9 + 2 * p], mine[:, 9 + 2 * p : 10 + 2 * p])
            mixed = o_own[at, cols].astype(WIDE) * share_own + got_o[at, cols].astype(WIDE) * share_got
            cross_o[at, cols] = mixed
            cross_low[at, cols] = mixed.astype(LOW)
        after_cross = after_self[at, :] + dot(cross_low[at, :], weight_co)
        ac[at, :] = after_cross
        normed = (normalised(after_cross)[0] * table[2:3] + table[6:7]).astype(LOW)
        n3[at, :] = normed
        if k == 0 and split:
            arrive(late_part)
            block = wm.at[:, 1 - x, c, :, rest]
            late_part = [push(block, block, me.across_core())]
        for j in range(blocks):
            cols = slice(j * BLOCK, (j + 1) * BLOCK)
            pre = dot(normed, cut(16 + 16 * j, 32 + 16 * j))
            square = pre * pre
            bent = jnp.tanh(GELU * pre * (1.0 + CUBIC * square))
            half = 0.5 * (1.0 + bent)
            act[at, cols] = (pre * half).astype(LOW)
            slope[at, cols] = half + 0.5 * pre * (1.0 - bent * bent) * (GELU * (1.0 + 3.0 * CUBIC * square))
        if k == 0 and split:
            arrive(late_part)
        state = after_cross + dot(act[at, :], cut(80, 144))
        bs[at, :] = state
        block_ref[at, :] = state.astype(LOW)
        head[at, :] = (normalised(state)[0] * table[3:4] + table[7:8]).astype(LOW)
    flat_fo = cut(80, 144)
    out(block_ref, block_out)
    head_in = head[...]

    picker = (positions[...] == rows_of((tok_count, masked))).astype(LOW)
    picked = dot_tn(picker, head_in).astype(LOW)
    kept = dot(jnp.concatenate([keep, jnp.zeros((7, tok_count), WIDE)], axis=0).astype(LOW), picker)
    code = jnp.where(kept[0:1] > 0.5, targets[...] + 1, 0)
    digits = jnp.concatenate([code >> 8, code & 255, jnp.zeros((6, masked), jnp.int32)], axis=0)
    digits = dot_tn(digits.astype(WIDE).astype(LOW), (rows_of((8, 128)) == lanes((8, 128))).astype(LOW)).astype(LOW)
    pb[z, x, y, :, 0:width] = picked
    pb[z, x, y, :, width : width + 128] = digits
    mine = pb.at[z, x, y]
    flight = [push(mine, mine, peer) for peer in me.others()]

    classes = BLOCK // 2
    flat_in = cut(144, 160).reshape((-1, 16, BLOCK))
    flat_in = jnp.concatenate([flat_in[:, :, :classes], flat_in[:, :, classes:]], axis=1).reshape((-1, classes))
    w_one, w_two = flat_in[:width], flat_in[width:]
    token_row = rows_of((tok_count, classes))
    ahead = pltpu.roll(dot(head_in, w_two), tok_count - 1, 0)
    logits = dot(head_in, w_one) + jnp.where(token_row == tok_count - 1, 0.0, ahead)
    top = jnp.max(logits, axis=1, keepdims=True)
    exps = jnp.exp(logits - top)
    total = jnp.sum(exps, axis=1, keepdims=True)
    hits = lanes((tok_count, classes)) == col_count
    entropy = top + jnp.log(total) - jnp.sum(jnp.where(hits, logits, 0.0), axis=1, keepdims=True)
    loss_col = col_valid * entropy
    grads = col_valid * (exps * (1.0 / total) - jnp.where(hits, 1.0, 0.0))
    g_insert = grads.astype(LOW)
    before = pltpu.roll(g_insert.astype(WIDE), 1, 0)
    g_before = jnp.where(token_row == 0, 0.0, before).astype(LOW)

    arrive(flight)
    column = pb.at[:, x, y]
    flight = [push(column, column, peer) for peer in (me.across_x(), me.across_y(), me.across_both())]

    flat_s = w_s[...].reshape((-1, 128))
    two = dot(head_in, flat_s)
    l_zero, l_one = two[:, 16:17], two[:, 17:18]
    top = jnp.maximum(l_zero, l_one)
    e_zero, e_one = jnp.exp(l_zero - top), jnp.exp(l_one - top)
    total = e_zero + e_one
    is_one = col_label > 0.5
    loss_col = loss_col + col_keep * (top + jnp.log(total) - jnp.where(is_one, l_one, l_zero))
    d_zero = col_keep * (e_zero / total - jnp.where(is_one, 0.0, 1.0))
    d_one = col_keep * (e_one / total - jnp.where(is_one, 1.0, 0.0))
    lane = lanes((tok_count, 128))
    g_delete = jnp.where(lane == 16, d_zero, jnp.where(lane == 17, d_one, 0.0)).astype(LOW)
    gh[...] = dot_nt(g_delete, flat_s) + dot_nt(g_insert, w_one) + dot_nt(g_before, w_two)
    arrive(flight)
    sibling = [push(pb, pb_got, me.across_core())]
    def rows_from(ref):
        return ref[...].reshape((-1, width + 128))

    gathered = rows_from(pb)
    rows_all = gathered[:, 0:width]
    numbers = gathered[:, width : width + 128].astype(WIDE).T
    code = numbers[0:1] * 256.0 + numbers[1:2]
    weight = jnp.where(code > 0.5, 1.0, 0.0)
    count = rows_all.shape[0]
    target = code.astype(jnp.int32) - 1
    place = rows_of((vocab_local, count))
    lt[...] = dot_nt(w_vocab[...].reshape((-1, width)), rows_all)
    hits = []
    for k in range(2):
        first = lax.axis_index(BOTH) + 2 * (k - c)
        hits.append(place + first * vocab_local == target)
    hits = jnp.concatenate(hits, axis=0)
    logits = lt[...]
    top = jnp.max(logits, axis=0, keepdims=True)
    exps = jnp.exp(logits - top)
    gt[...] = exps.astype(LOW)
    total = jnp.sum(exps, axis=0, keepdims=True)
    chosen = jnp.sum(jnp.where(hits, logits, 0.0), axis=0, keepdims=True)
    loss_here = jnp.sum(loss_col, axis=0, keepdims=True)
    folds = count // 128
    loss_rows = jnp.broadcast_to(loss_here, (st_z.shape[1] - 2 * folds, 128))
    st_q[x, y] = jnp.concatenate([folded(top + jnp.log(total)), folded(chosen), loss_rows], axis=0)
    spot = st_q.at[x, y]
    flight = [push(spot, spot, peer) for peer in (me.across_x(), me.across_y(), me.across_both())]
    small_cols[...] = dot_tn(head_in, g_delete)
    for k, grad in enumerate((g_insert, g_before)):
        pairs = dot_tn(head_in, grad).astype(LOW).reshape((-1, 2, 16, classes))
        for side in range(2):
            cols = slice(side * classes, (side + 1) * classes)
            put(144, pairs[:, side], k * (depth // 2), (k + 1) * (depth // 2), cols)
    arrive(flight)
    st_z[z] = merge_all([st_q[0, 0], st_q[0, 1], st_q[1, 0], st_q[1, 1]], folds)
    flight = [push(st_z.at[z], st_z.at[z], peer) for peer in me.others()]
    flat_vocab = w_vocab[...].reshape((-1, width))
    ew[...] = dot_tn(gt[...], flat_vocab)
    hw[...] = dot_tn(jnp.where(hits, 1.0, 0.0).astype(LOW), flat_vocab).astype(LOW)
    arrive(flight)
    stat = merge_all([st_z[k] for k in range(depth)], folds)
    all_loss = stat[2 * folds : 2 * folds + 1]
    stat = jnp.concatenate([unfolded(stat[0:folds]), unfolded(stat[folds : 2 * folds])], axis=0)
    factors = [weight * jnp.exp(top - stat[0:1]), weight, jnp.zeros((6, count), WIDE)]
    factors = transposed_rows(jnp.concatenate(factors, axis=0))
    mixed = ew[...] * factors[:, 0:1] - hw[...].astype(WIDE) * factors[:, 1:2]
    rb[...] = mixed.astype(LOW).reshape(rb.shape)
    flight = [
        push(rb.at[:, 1 - x, y], got_rq.at[0], me.across_x()),
        push(rb.at[:, x, 1 - y], got_rq.at[1], me.across_y()),
        push(rb.at[:, 1 - x, 1 - y], got_rq.at[2], me.across_both()),
    ]
    gt[...] = (weight * (jnp.exp(lt[...] - stat[0:1]) - jnp.where(hits, 1.0, 0.0))).astype(LOW)
    sibling.append(push(gt.at[pl.ds((1 - c) * vocab_local, vocab_local)], gt_got, me.across_core()))
    tokens = weight * (stat[0:1] - stat[1:2])
    mine = rows_of((masked, count)) + ((z * 2 + x) * 2 + y) * masked == lanes((masked, count))
    own = jnp.sum(jnp.where(mine, tokens, 0.0), axis=1, keepdims=True)
    token_out[...] = jnp.sum(
        jnp.where(rows_of((masked, masked)) == lanes((masked, masked)), own, 0.0), axis=0, keepdims=True
    )
    loss = (all_loss + jnp.sum(tokens, axis=1, keepdims=True)) * (1.0 / (tok_count * everyone))
    st_c[0] = jnp.broadcast_to(loss, (8, 128))
    sibling.append(push(st_c.at[0], st_c.at[1], me.across_core()))
    arrive(flight)
    line = rb[:, x, y].astype(WIDE)
    for k in range(3):
        line = line + got_rq[k].astype(WIDE)
    got_rq[3] = line.astype(LOW)
    flight = [
        push(got_rq.at[3, lax.rem(z + k, depth)], got_rz.at[k - 1], me.along(k)) for k in range(1, depth)
    ]
    arrive(sibling)
    loss_out[...] = st_c[0, 0:1, 0:1] + st_c[1, 0:1, 0:1]
    scale = (tok_count * everyone) ** (-0.5)
    mine = gt[pl.ds(pl.multiple_of(c * vocab_local, vocab_local), vocab_local), :]
    vocab_ref[...] = (dot(mine, rows_all) + dot(gt_got[...], rows_from(pb_got)[:, 0:width])) * scale
    out(vocab_ref, grad_vocab)
    arrive(flight)
    grad_picked = got_rq[3, z].astype(WIDE)
    for k in range(1, depth):
        grad_picked = grad_picked + got_rz[k - 1].astype(WIDE)
    coarse = grad_picked.astype(LOW)
    fine = (grad_picked - coarse.astype(WIDE)).astype(LOW)
    grad_head = gh[...] + dot(picker, coarse) + dot(picker, fine)

    gh[...] = grad_head
    gain_2 = gain_3 = bias_2 = bias_3 = 0.0
    low_half = lanes((span, 128)) < HD
    lane = lanes((span, 128))
    swap, delta_rows = [], []
    for at in ranges:
        grad_block, gain, bias = norm_back(bs[at, :], table[3:4], gh[at, :])
        gain_3, bias_3 = gain_3 + gain, bias_3 + bias
        g_half = grad_block.astype(LOW)
        g_ffn[at, :] = g_half
        slopes = [dot_nt(g_half, flat_fo[j * BLOCK : (j + 1) * BLOCK]) for j in range(blocks)]
        slopes = [(slopes[j] * slope[at, j * BLOCK : (j + 1) * BLOCK]).astype(LOW) for j in range(blocks)]
        upstream = sum(dot_nt(slopes[j], cut(16 + 16 * j, 32 + 16 * j)) for j in range(blocks))
        for j in range(blocks):
            gpre[at, j * BLOCK : (j + 1) * BLOCK] = slopes[j]
        back, gain, bias = norm_back(ac[at, :], table[2:3], upstream)
        gain_2, bias_2 = gain_2 + gain, bias_2 + bias
        grad_state = grad_block + back
        state_ref[at, :] = grad_state
        g_attn = dot_nt(grad_state.astype(LOW), weight_co).astype(LOW)
        g_ref[at, :] = g_attn
        swap.append(push(g_ref.at[at], g_other.at[at], me.across_y()))
        deltas = jnp.zeros((span, 128), WIDE)
        for p in range(width // 128):
            cols = slice(p * 128, (p + 1) * 128)
            product = g_attn[:, cols].astype(WIDE) * cross_o[at, cols]
            first = jnp.sum(jnp.where(low_half, product, 0.0), axis=1, keepdims=True)
            second = jnp.sum(jnp.where(low_half, 0.0, product), axis=1, keepdims=True)
            deltas = jnp.where(lane == 2 * p, first, jnp.where(lane == 2 * p + 1, second, deltas))
        delta_rows.append(deltas.T[0:8])
    st_own[...] = jnp.concatenate([lse, jnp.concatenate(delta_rows, axis=1)], axis=0)
    swap.append(push(st_own, st_other, me.across_y()))
    out(state_ref, state_out)
    out(g_ref, g_own)
    g_cross = state_ref[...].astype(LOW)

    cores = []

    def to_core(lo, hi):
        if split:
            at = pl.ds(lo, hi - lo)
            cores.append(push(eb.at[:, :, 1 - c, :, at], eb_got.at[:, :, :, at], me.across_core()))

    to_core(144, 160)
    for j in range(blocks):
        grad = dot_tn(act[:, j * BLOCK : (j + 1) * BLOCK], g_ffn[...]).astype(LOW)
        put(80, grad.reshape((-1, 64, BLOCK)), j * depth // blocks, (j + 1) * depth // blocks)
    to_core(80, 144)
    for j in range(blocks):
        grad = dot_tn(n3[...], gpre[:, j * BLOCK : (j + 1) * BLOCK]).astype(LOW)
        put(16 + 16 * j, grad.reshape((-1, 16, BLOCK)))
    to_core(16, 80)
    put(0, dot_tn(cross_low[...], g_cross).astype(LOW).reshape((-1, 16, BLOCK)))
    to_core(0, 16)
    small_rows[...] = jnp.concatenate([gain_2, gain_3, bias_2, bias_3, jnp.zeros((4, width), WIDE)], axis=0)
    if split:
        arrive(cores)
        one, two = pl.ds(0, RETURNED), pl.ds(RETURNED, LATE - RETURNED)
        for k, (at, first, spot) in enumerate(((one, 1 - y, 1), (two, 1 - x, 0), (one, y, 1), (two, x, 0))):
            for other in range(2):
                px, py = (other, first) if spot else (first, other)

                @pl.loop(0, depth)
                def _(zz):
                    total = eb[zz, px, c, py, at].astype(WIDE) + eb_got[zz, px, py, at].astype(WIDE)
                    sum_refs[k][other, zz] = total.astype(LOW)

            out(sum_refs[k], sums[k])
    else:
        sums[0][...] = eb[...]
    arrive(swap)
    for copy in pending:
        copy.wait_send()
    for copy in outs:
        copy.wait()


def middle_part(depth, split, seg, pad, labels, counts, positions, targets, w_vocab, after_self, attended, gs, parts):
    tok_count, width = after_self.shape
    hidden = 4 * BLOCK
    vocab_local = w_vocab.shape[0]
    everyone = depth * 8
    masked = positions.shape[1]
    count = masked * everyone // 2
    stat_rows = (2 * (count // 128) + 15) // 8 * 8
    sharded = (depth, 2, 2, 2)
    lead = sharded if split else (BLOCK // 16,)
    sharded = (depth, 2, 2, 2)
    if split:
        outs = [(shape_of((2, depth, n, BLOCK), LOW), ANY) for n in (RETURNED, LATE - RETURNED)] * 2
    else:
        outs = [(shape_of(parts[0].shape, LOW), VMEM)]
    outs += [
        (shape_of((tok_count, width), LOW), ANY),
        (shape_of((tok_count, width), WIDE), ANY),
        (shape_of((tok_count, width), LOW), ANY),
        (shape_of((tok_count, width), LOW), ANY),
        (shape_of((16, tok_count), WIDE), VMEM),
        (shape_of((16, tok_count), WIDE), ANY),
        (shape_of((8, width), WIDE), VMEM),
        (shape_of((width, 128), WIDE), VMEM),
        (shape_of((vocab_local, width), WIDE), ANY),
        (shape_of((1, masked), WIDE), VMEM),
        (shape_of((1, 1), WIDE), VMEM),
    ]
    copies = 32 + 2 * (depth - 1) + 3 + 1 + 1 + 3 + 1 + 3 + (depth - 1)
    return pl.pallas_call(
        partial(middle_kernel, depth, split),
        name="middle_part",
        out_shape=[o for o, _ in outs],
        in_specs=[VMEM] * 8 + [ANY] * (5 + len(parts)),
        out_specs=[s for _, s in outs],
        scratch_shapes=[
            pltpu.VMEM((2, vocab_local, width), LOW),
            pltpu.VMEM((tok_count, width), WIDE),
            pltpu.VMEM((tok_count, width), LOW),
            pltpu.VMEM((tok_count, width), LOW),
            pltpu.VMEM((tok_count, width), WIDE),
            pltpu.VMEM((tok_count, width), LOW),
            pltpu.VMEM((vocab_local, width), WIDE),
            pltpu.SemaphoreType.DMA((10,)),
            pltpu.VMEM(lead + (160, BLOCK), LOW),
            pltpu.VMEM(lead + (160, BLOCK), LOW),
            pltpu.VMEM(((depth, 2, 2) if split else (1,)) + (160, BLOCK), LOW),
            pltpu.VMEM(gs.shape, LOW),
            pltpu.VMEM((tok_count, width), LOW),
            pltpu.VMEM((8, tok_count), WIDE),
            pltpu.VMEM((tok_count, width), WIDE),
            pltpu.VMEM((tok_count, width), LOW),
            pltpu.VMEM((tok_count, width), WIDE),
            pltpu.VMEM((tok_count, width), WIDE),
            pltpu.VMEM((tok_count, width), LOW),
            pltpu.VMEM((tok_count, hidden), LOW),
            pltpu.VMEM((tok_count, hidden), WIDE),
            pltpu.VMEM((tok_count, hidden), LOW),
            pltpu.VMEM((tok_count, width), LOW),
            pltpu.VMEM((2 * vocab_local, count), WIDE),
            pltpu.VMEM((2 * vocab_local, count), LOW),
            pltpu.VMEM((vocab_local, count), LOW),
            pltpu.VMEM((count, width), WIDE),
            pltpu.VMEM((count, width), LOW),
            pltpu.VMEM((depth, 2, 2, masked, width + 128), LOW),
            pltpu.VMEM((depth, 2, 2, masked, width + 128), LOW),
            pltpu.VMEM((depth, 2, 2, masked, width), LOW),
            pltpu.VMEM((4, depth, masked, width), LOW),
            pltpu.VMEM((max(depth - 1, 1), masked, width), LOW),
            pltpu.VMEM((2, 8, 128), WIDE),
            pltpu.VMEM((2, 2, stat_rows, 128), WIDE),
            pltpu.VMEM((depth, stat_rows, 128), WIDE),
            pltpu.VMEM((tok_count, width), WIDE),
            pltpu.VMEM((tok_count, width), LOW),
            pltpu.SemaphoreType.DMA((12,)),
            pltpu.SemaphoreType.DMA((copies + depth,)),
            pltpu.SemaphoreType.DMA((copies + depth,)),
        ]
        + ([pltpu.VMEM((2, depth, n, BLOCK), LOW) for n in (RETURNED, LATE - RETURNED)] * 2 if split else []),
        compiler_params=pltpu.CompilerParams(
            collective_id=1, has_side_effects=True, vmem_limit_bytes=LIMIT
        ),
    )(seg, pad, labels, counts, positions, targets, *attended[2:], w_vocab, after_self, *attended[:2], gs, *parts)


def self_backward_start(dk, dv):
    dk[...] = jnp.zeros_like(dk)
    dv[...] = jnp.zeros_like(dv)


def self_backward(blocks, qkv, out, lse_ref, g_ref, dqkv, dk, dv, row_seg, row_keep, col_seg):
    tok_count, width = out.shape
    first, last = blocks
    pairs = width // 128

    def one(block, carry):
        at = pl.ds(pl.multiple_of(block * 128, 128), 128)
        low = self_window(block, tok_count)
        keys = pl.ds(low, 384)
        allowed = twice(self_mask(row_seg, row_keep, col_seg, block, low))
        stats = lse_ref[at, :]
        every = range(pairs)
        cols = [slice(p * 128, (p + 1) * 128) for p in every]
        q = [both_heads(qkv[at, cols[p]] * SCALE) for p in every]
        g = [both_heads(g_ref[at, cols[p]]) for p in every]
        keyed = [qkv[keys, width + p * 128 : width + (p + 1) * 128] for p in every]
        scores = [dot_nt(q[p], keyed[p]) for p in every]
        slopes = [dot_nt(g[p], qkv[keys, 2 * width + p * 128 : 2 * width + (p + 1) * 128]) for p in every]
        deltas = [jnp.sum(g[p].astype(WIDE) * twice(out[at, cols[p]].astype(WIDE)), axis=1, keepdims=True) for p in every]
        lses = [jnp.concatenate([stats[:, 2 * p : 2 * p + 1], stats[:, 2 * p + 1 : 2 * p + 2]], axis=0) for p in every]
        probs = [jnp.exp(jnp.where(allowed, scores[p] - lses[p], FILL)) for p in every]
        gscores = [(probs[p] * (slopes[p] - deltas[p])).astype(LOW) for p in every]
        grad_q = [join_heads(dot(gscores[p], keyed[p])) * SCALE for p in every]
        grad_k = [dk[keys, cols[p]] + dot_tn(gscores[p], q[p]) for p in every]
        grad_v = [dv[keys, cols[p]] + dot_tn(probs[p].astype(LOW), g[p]) for p in every]
        for p in every:
            dqkv[at, cols[p]] = grad_q[p].astype(LOW)
            dk[keys, cols[p]] = grad_k[p]
            dv[keys, cols[p]] = grad_v[p]
        return carry

    lax.fori_loop(first, last, one, 0)


def self_backward_end(dqkv, dk, dv):
    width = dk.shape[1]
    dqkv[:, width : 2 * width] = dk[...].astype(LOW)
    dqkv[:, 2 * width : 3 * width] = dv[...].astype(LOW)


def reduction(me, chunks, send, recv):
    z, x, c, y = me.z, me.x, me.c, me.y
    depth = me.depth
    count = len(chunks)
    started = [[None] * 3 for _ in chunks]
    used = [0] * count

    def launch(k, stage):
        copies = []

        def push(src, dst, peer):
            slot = used[k]
            used[k] += 1
            copy = remote(src, dst, send.at[k, slot], recv.at[k, slot], peer)
            copy.start()
            copies.append(copy)

        for src, got_c, got_q, got_z, at, put in chunks[k]:
            if stage == 0:
                push(src.at[:, :, 1 - c, :, at], got_c.at[:, :, :, at], me.across_core())
            elif stage == 1:
                push(got_c.at[:, 1 - x, y, at], got_q.at[0, :, at], me.across_x())
                push(got_c.at[:, x, 1 - y, at], got_q.at[1, :, at], me.across_y())
                push(got_c.at[:, 1 - x, 1 - y, at], got_q.at[2, :, at], me.across_both())
            else:
                for j in range(1, depth):
                    push(got_c.at[lax.rem(z + j, depth), x, y, at], got_z.at[j - 1, at], me.along(j))
        started[k][stage] = copies

    def absorb(k, stage):
        for copy in started[k][stage]:
            copy.wait_recv()
        for src, got_c, got_q, got_z, at, put in chunks[k]:
            if stage == 0:

                @pl.loop(0, depth)
                def _(zz):
                    for xx in range(2):
                        for yy in range(2):
                            total = src[zz, xx, c, yy, at].astype(WIDE) + got_c[zz, xx, yy, at].astype(WIDE)
                            got_c[zz, xx, yy, at] = total.astype(LOW)

            elif stage == 1:

                @pl.loop(0, depth)
                def _(zz):
                    total = got_c[zz, x, y, at].astype(WIDE)
                    for k in range(3):
                        total = total + got_q[k, zz, at].astype(WIDE)
                    got_c[zz, x, y, at] = total.astype(LOW)

            else:
                total = got_c[z, x, y, at].astype(WIDE)
                for j in range(1, depth):
                    total = total + got_z[j - 1, at].astype(WIDE)
                put(total)

    def begin(k):
        launch(k, 0)

    def after(k, stage):
        absorb(k, stage)
        if stage < 2:
            launch(k, stage + 1)

    def end():
        for stages in started:
            for copies in stages:
                for copy in copies:
                    copy.wait_send()

    return begin, after, end


def last_kernel(depth, reduces, *refs):
    (pair, seg, pad, dq_other) = refs[:4]
    held = refs[4:15]
    (small_rows, small_cols, ga_in, gs_in) = refs[15:19]
    refs = refs[19:]
    if reduces:
        parts_in, refs = refs[:4], refs[4:]
    input_out, enc_out = refs[:2]
    refs = refs[2:]
    outs = refs[:9] if reduces else refs[:2]
    refs = refs[9:] if reduces else refs[2:]
    (dkv, enc, dq_own, start, one, qkv, low, lse, after, two, gstate) = refs[:11]
    (ga, gs, g_query, g_attn, dqkv, dk, dv, row_seg, row_keep, col_seg, load_sem, dq_got, sw_send, sw_recv) = refs[11:25]
    grad_input, grad_enc, out_sem = refs[25:28]
    refs = refs[28:]
    if reduces:
        parts, part_sem, refs = refs[:4], refs[4], refs[5:]
        fetched = [pltpu.make_async_copy(parts_in[k], parts[k], part_sem.at[k]) for k in range(4)]
        for copy in fetched:
            copy.start()
    refs_held = (dkv, enc, dq_own, start, one, qkv, low, lse, after, two, gstate)
    tok_count, width = dq_own.shape
    src_count = enc.shape[0]
    everyone = depth * 8
    me = Place(depth)
    scale = (tok_count * everyone) ** (-0.5)
    loads = []
    for src, dst in list(zip(held, refs_held)) + [(gs_in, gs), (ga_in, ga)]:
        copy = pltpu.make_async_copy(src, dst, load_sem.at[len(loads)])
        copy.start()
        loads.append(copy)
    if reduces:
        greet(me.others() + [me.across_x(), me.across_y(), me.across_both(), me.across_core()])
    else:
        greet([me.across_y()])
    halves = 2
    half = tok_count // halves
    swaps = []
    for k in range(halves):
        at = pl.ds(k * half, half)
        swaps.append(remote(dq_other.at[at], dq_got.at[at], sw_send.at[k], sw_recv.at[k], me.across_y()))
        swaps[-1].start()

    if reduces:
        (late, late_s, ex, ey, ex_got, ey_got, ez, ez_got, c_a, c_s, q_a, q_s, z_a, z_s, ez_send, ez_recv, send, recv) = refs
        (o_qkv, o_so, o_cq, o_kv, o_co, o_fi, o_fo, o_in, o_s) = outs

        def put_kv(total):
            o_kv[:, 0:BLOCK] = total[0:16] * scale
            o_kv[:, BLOCK : 2 * BLOCK] = total[16:32] * scale

        def put_mid(total):
            o_so[...] = total[0:16] * scale
            o_cq[...] = total[16:32] * scale

        def put_qkv(k, total):
            o_qkv[:, k * BLOCK : (k + 1) * BLOCK] = total * scale

        def put_s(total):
            o_s[...] = total * scale

        def rows(lo, hi, put):
            return (late, c_a, q_a, z_a, pl.ds(lo, hi - lo), put)

        chunks = [
            [rows(KV, EARLY, put_kv)],
            [rows(SO, KV, put_mid)],
            [rows(0, 16, partial(put_qkv, 0))],
            [rows(16, 32, partial(put_qkv, 1))],
            [rows(32, SO, partial(put_qkv, 2))],
            [(late_s, c_s, q_s, z_s, pl.ds(0, 16), put_s)],
        ]

        z, x, y = me.z, me.x, me.y
        for copy in fetched:
            copy.wait()
        for total, own, got in ((ex, parts[0], parts[1]), (ey, parts[2], parts[3])):

            @pl.loop(0, depth)
            def _(zz):
                for k in range(2):
                    total[k, zz] = (own[k, zz].astype(WIDE) + got[k, zz].astype(WIDE)).astype(LOW)

        plane = [
            remote(ex.at[1 - x], ex_got, ez_send.at[0], ez_recv.at[0], me.across_x()),
            remote(ey.at[1 - y], ey_got, ez_send.at[1], ez_recv.at[1], me.across_y()),
        ]
        for copy in plane:
            copy.start()
        along = []

        def onward():
            for copy in plane:
                copy.wait_recv()

            @pl.loop(0, depth)
            def _(zz):
                ez[zz, 0:RETURNED] = (ex[x, zz].astype(WIDE) + ex_got[zz].astype(WIDE)).astype(LOW)
                ez[zz, RETURNED:LATE] = (ey[y, zz].astype(WIDE) + ey_got[zz].astype(WIDE)).astype(LOW)

            for k in range(1, depth):
                to = lax.rem(z + k, depth)
                at = 1 + k
                along.append(remote(ez.at[to], ez_got.at[k - 1], ez_send.at[at], ez_recv.at[at], me.along(k)))
                along[-1].start()

        def settle():
            for copy in plane:
                copy.wait_send()
            for copy in along:
                copy.wait()
            total = ez[me.z].astype(WIDE)
            for k in range(depth - 1):
                total = total + ez_got[k].astype(WIDE)
            total = total * scale
            o_co[...] = total[0:16]
            for k in range(4):
                o_fi[:, k * BLOCK : (k + 1) * BLOCK] = total[16 + 16 * k : 32 + 16 * k]
            o_fo[...] = total[80:144]
            half = BLOCK // 2
            for k in range(2):
                o_in[16 * k : 16 * (k + 1)] = total[144:160, half * k : half * (k + 1)]

        begin, after_stage, end = reduction(me, chunks, send, recv)

        def keep(lo, value):
            late[:, :, :, :, lo : lo + 16] = value.astype(LOW).reshape(late.shape[:4] + (16, BLOCK))

        def keep_small(value):
            late_s[...] = value.astype(LOW).reshape(late_s.shape)
    else:
        def begin(k):
            return None

        def after_stage(k, stage):
            return None

        end = onward = settle = lambda: None
        o_late, o_small = outs

        def keep(lo, value):
            o_late[:, lo : lo + 16] = value.astype(LOW).reshape((-1, 16, BLOCK))

        def keep_small(value):
            o_small[...] = value

    chunk_kv, chunk_mid, chunk_q, chunk_k, chunk_v, chunk_s = range(6)
    onehot = token_numbers(seg, pad, pair, row_seg, row_keep, col_seg)
    cut = cutter(ga)
    for copy in loads[:2]:
        copy.wait()
    keep(KV, dot_tn(enc[...], dkv[:, 0:width]))
    keep(KV + 16, dot_tn(enc[...], dkv[:, width : 2 * width]))
    begin(chunk_kv)
    for copy in loads[2:]:
        copy.wait()
    table = cutter(gs)(0, gs.shape[-2]).astype(WIDE).T
    self_backward_start(dk, dv)
    gains = biases = 0.0
    for k in range(halves):
        at = pl.ds(k * half, half)
        swaps[k].wait()
        query = (dq_own[at, :] + dq_got[at, :].astype(WIDE)).astype(LOW)
        g_query[at, :] = query
        back, gain_1, bias_1 = norm_back(after[at, :], table[1:2], dot_nt(query, cut(CQ, KV)))
        gains, biases = gains + gain_1, biases + bias_1
        state = gstate[at, :] + back
        gstate[at, :] = state
        g_attn[at, :] = dot_nt(state.astype(LOW), cut(SO, CQ)).astype(LOW)
        if k == 0:
            after_stage(chunk_kv, 0)
        if k == halves - 1:
            keep(CQ, dot_tn(two[...], g_query[...]))
            keep(SO, dot_tn(low[...], gstate[...].astype(LOW)))
            begin(chunk_mid)
        blocks = (k * half // 128, (k + 1) * half // 128)
        self_backward(blocks, qkv, low, lse, g_attn, dqkv, dk, dv, row_seg, row_keep, col_seg)
        if k == 0:
            onward()
    after_stage(chunk_mid, 0)
    self_backward_end(dqkv, dk, dv)
    for k, chunk in enumerate((chunk_q, chunk_k, chunk_v)):
        keep(QKV + 16 * k, dot_tn(one[...], dqkv[:, k * width : (k + 1) * width]))
        begin(chunk)
    after_stage(chunk_q, 0)
    after_stage(chunk_k, 0)
    after_stage(chunk_v, 0)
    after_stage(chunk_kv, 1)
    upstream = dot_nt(dqkv[:, 0:width], cut(QKV, QKV + 16))
    upstream = upstream + dot_nt(dqkv[:, width : 2 * width], cut(QKV + 16, QKV + 32))
    upstream = upstream + dot_nt(dqkv[:, 2 * width : 3 * width], cut(QKV + 32, SO))
    back, gain_0, bias_0 = norm_back(start[...], table[0:1], upstream)
    grad_start = gstate[...] + back
    grad_input[...] = grad_start.astype(LOW)
    stores = [pltpu.make_async_copy(grad_input, input_out, out_sem.at[4])]
    stores[0].start()
    coarse = grad_start.astype(LOW)
    fine = (grad_start - coarse.astype(WIDE)).astype(LOW)
    g_table = (dot_tn(onehot, coarse) + dot_tn(onehot, fine))[8:16]
    mid = small_rows[...]
    stacked = jnp.concatenate([gain_0, gains, mid[0:2], bias_0, biases, mid[2:4], g_table], axis=0)
    keep_small(transposed_rows(stacked) + small_cols[...])
    begin(chunk_s)
    after_stage(chunk_mid, 1)
    w_key, w_val = cut(KV, KV + 16), cut(KV + 16, EARLY)
    span = src_count // 4

    def source_grads(k):
        at = pl.ds(k * span, span)
        grads = dot_nt(dkv[at, 0:width], w_key) + dot_nt(dkv[at, width : 2 * width], w_val)
        grad_enc[at, :] = grads.astype(LOW)
        stores.append(pltpu.make_async_copy(grad_enc.at[at], enc_out.at[at], out_sem.at[k]))
        stores[-1].start()

    source_grads(0)
    after_stage(chunk_s, 0)
    after_stage(chunk_kv, 2)
    after_stage(chunk_q, 1)
    source_grads(1)
    after_stage(chunk_k, 1)
    source_grads(2)
    after_stage(chunk_v, 1)
    after_stage(chunk_s, 1)
    source_grads(3)
    settle()
    for chunk in (chunk_mid, chunk_q, chunk_k, chunk_v, chunk_s):
        after_stage(chunk, 2)
    end()
    for copy in stores:
        copy.wait()


def last_part(depth, reduces, pair, seg, pad, dq_own, dq_other, dkv, enc, kept, gstate, grads, whole):
    tok_count, width = dq_own.shape
    src_count = enc.shape[0]
    ga, gs = whole
    parts, small_rows, small_cols = grads
    everyone = depth * 8
    rows = BLOCK // everyone
    sharded = (depth, 2, 2, 2)
    held = (dkv, enc, dq_own, *kept, gstate)
    outs = [shape_of((tok_count, width), LOW), shape_of((src_count, width), LOW)]
    scratch = [pltpu.VMEM(a.shape, a.dtype) for a in held]
    scratch += [
        pltpu.VMEM(ga.shape, LOW),
        pltpu.VMEM(gs.shape, LOW),
        pltpu.VMEM((tok_count, width), LOW),
        pltpu.VMEM((tok_count, width), LOW),
        pltpu.VMEM((tok_count, 3 * width), LOW),
        pltpu.VMEM((tok_count, width), WIDE),
        pltpu.VMEM((tok_count, width), WIDE),
        pltpu.VMEM((1, tok_count), WIDE),
        pltpu.VMEM((1, tok_count), WIDE),
        pltpu.VMEM((tok_count, 128), WIDE),
        pltpu.SemaphoreType.DMA((14,)),
        pltpu.VMEM((tok_count, width), LOW),
        pltpu.SemaphoreType.DMA((2,)),
        pltpu.SemaphoreType.DMA((2,)),
        pltpu.VMEM((tok_count, width), LOW),
        pltpu.VMEM((src_count, width), LOW),
        pltpu.SemaphoreType.DMA((5,)),
    ]
    if reduces:
        shapes = [(EARLY, BLOCK), (16, 128)]
        outs += [
            shape_of((rows, 3 * BLOCK), WIDE),
            shape_of((rows, BLOCK), WIDE),
            shape_of((rows, BLOCK), WIDE),
            shape_of((rows, 2 * BLOCK), WIDE),
            shape_of((rows, BLOCK), WIDE),
            shape_of((rows, 4 * BLOCK), WIDE),
            shape_of((4 * rows, BLOCK), WIDE),
            shape_of((2 * rows, BLOCK // 2), WIDE),
            shape_of((rows, 128), WIDE),
        ]
        scratch += [pltpu.VMEM(a.shape, LOW) for a in parts] + [pltpu.SemaphoreType.DMA((4,))]
        scratch += [pltpu.VMEM(sharded + s, LOW) for s in shapes]
        scratch += [pltpu.VMEM(parts[0].shape, LOW), pltpu.VMEM(parts[2].shape, LOW)]
        scratch += [pltpu.VMEM(parts[0].shape[1:], LOW), pltpu.VMEM(parts[2].shape[1:], LOW)]
        scratch += [pltpu.VMEM((depth, LATE, BLOCK), LOW), pltpu.VMEM((depth - 1, LATE, BLOCK), LOW)]
        for lead in ((depth, 2, 2), (3, depth), (depth - 1,)):
            scratch += [pltpu.VMEM(lead + s, LOW) for s in shapes]
        scratch += [pltpu.SemaphoreType.DMA((depth + 2,))] * 2
        slots = 2 * (depth + 3)
        scratch += [pltpu.SemaphoreType.DMA((6, slots)), pltpu.SemaphoreType.DMA((6, slots))]
    else:
        outs += [shape_of((BLOCK // 16, EARLY, BLOCK), LOW), shape_of((BLOCK, 128), WIDE)]
    return pl.pallas_call(
        partial(last_kernel, depth, reduces),
        name="last_part",
        out_shape=outs,
        in_specs=[SMEM] + [VMEM] * 2 + [ANY] * 12 + [VMEM] * 2 + [ANY] * (2 + len(parts)),
        out_specs=[ANY] * 2 + [VMEM] * (len(outs) - 2),
        scratch_shapes=scratch,
        compiler_params=pltpu.CompilerParams(
            collective_id=2, has_side_effects=True, vmem_limit_bytes=LIMIT
        ),
    )(pair, seg, pad, dq_other, *held, small_rows, small_cols, ga, gs, *parts)


def finish_kernel(count, *refs):
    ins, (small_in, loss_in) = refs[:count], refs[count : count + 2]
    outs, tiny_outs = refs[count + 2 : 2 * count + 2], refs[2 * count + 2 : 2 * count + 7]
    refs = refs[2 * count + 7 :]
    held, (small, loss) = refs[:count], refs[count : count + 2]
    tiny, sems = refs[count + 2 : count + 7], refs[count + 7]
    ahead = [pltpu.make_async_copy(small_in, small, sems.at[0, count]), pltpu.make_async_copy(loss_in, loss, sems.at[0, count + 1])]
    first = [pltpu.make_async_copy(ins[k], held[k], sems.at[0, k]) for k in range(count)]
    copies = [pltpu.make_async_copy(held[k], outs[k], sems.at[1, k]) for k in range(count)]
    for copy in ahead + first:
        copy.start()
    for copy in ahead:
        copy.wait()
    values = small[...]
    rows = values.shape[0]
    turned = jnp.concatenate([values, jnp.zeros((128 - rows, 128), WIDE)], axis=0).T
    for ref, lo, hi in zip(tiny[:4], (0, 4, 8, 16), (4, 8, 16, 18)):
        ref[...] = turned[lo:hi, 0:rows]
    tiny[4][...] = loss[...]
    for k in range(5):
        copies.append(pltpu.make_async_copy(tiny[k], tiny_outs[k], sems.at[1, count + k]))
        copies[-1].start()
    for k in range(count):
        first[k].wait()
        copies[k].start()
    for copy in copies:
        copy.wait()


def finish(results, small, loss):
    count = len(results)
    rows = small.shape[0]
    tiny = [shape_of(s, WIDE) for s in ((4, rows), (4, rows), (PAIRS, rows), (2, rows), (1, 1))]
    outs = [shape_of(a.shape, a.dtype) for a in results] + tiny
    held = list(results) + [small, loss] + tiny
    res = pl.pallas_call(
        partial(finish_kernel, count),
        name="finish",
        out_shape=outs,
        in_specs=[ANY] * (count + 2),
        out_specs=[ANY] * len(outs),
        scratch_shapes=[pltpu.VMEM(a.shape, a.dtype) for a in held]
        + [pltpu.SemaphoreType.DMA((2, count + 5))],
        compiler_params=pltpu.CompilerParams(vmem_limit_bytes=LIMIT),
    )(*results, small, loss)
    return res[:count], res[count:]


def late_blocks(cross_out, ffn_in, ffn_out, insert):
    groups = cross_out.shape[0] // 16
    return jnp.concatenate(
        [
            cross_out.reshape(groups, 16, BLOCK),
            ffn_in.reshape(groups, 16, 4, BLOCK).swapaxes(1, 2).reshape(groups, 64, BLOCK),
            ffn_out.reshape(groups, 64, BLOCK),
            insert.reshape(groups, 2, 16, BLOCK // 2).swapaxes(1, 2).reshape(groups, 16, BLOCK),
        ],
        axis=1,
    )


def gather_by_ops(qkv, self_out, cross_q, cross_kv, small):
    wide = jnp.concatenate([qkv, self_out, cross_q, cross_kv], axis=1)
    ga = lax.all_gather(wide, BOTH, axis=0, tiled=True).reshape(-1, 16, 7, BLOCK).swapaxes(1, 2)
    gs = lax.all_gather(small, BOTH, axis=0, tiled=True)
    return ga.reshape(-1, EARLY, BLOCK), gs.reshape(-1, 16, 128)


def partner(array, depth, axis):
    dx, dy = (1, 0) if axis == "x" else (0, 1)
    pairs = []
    for z in range(depth):
        for x in range(2):
            for c in range(2):
                for y in range(2):
                    here = ((z * 2 + x) * 2 + c) * 2 + y
                    there = ((z * 2 + (x ^ dx)) * 2 + c) * 2 + (y ^ dy)
                    pairs.append((here, there))
    return lax.ppermute(array, BOTH, pairs)


def reduce_by_ops(early, small, late, scale):
    groups = late.shape[0]
    gw_f = late[:, 80:144].reshape(groups * 64, BLOCK)
    gw_i = late[:, 144:160].reshape(groups, 16, 2, BLOCK // 2).swapaxes(1, 2).reshape(groups * 32, BLOCK // 2)
    late = late[:, 0:80].reshape(groups, 5, 16, BLOCK).swapaxes(0, 1).reshape(5, BLOCK, BLOCK)
    early = early.reshape(groups, 7, 16, BLOCK).swapaxes(0, 1).reshape(7, BLOCK, BLOCK)
    wide = jnp.concatenate([early, late]).swapaxes(0, 1).reshape(BLOCK, 12 * BLOCK)

    def sums(a):
        return lax.psum_scatter(a.astype(WIDE), BOTH, scatter_dimension=0, tiled=True) * scale

    own = sums(wide)
    edges = (0, 3, 4, 5, 7, 8, 12)
    pieces = [own[:, lo * BLOCK : hi * BLOCK] for lo, hi in zip(edges[:-1], edges[1:])]
    return pieces + [sums(gw_f), sums(gw_i), sums(small)]


def body(
    dec_input, enc_output, segment_ids, padding, pair_ids, src_lengths, delete_labels, insert_counts,
    masked_positions, masked_targets, norm_gain, norm_bias, pair_table, self_qkv, self_out, cross_q, cross_kv,
    cross_out, ffn_in, ffn_out, w_delete, w_insert, w_vocab,
):
    everyone = lax.axis_size(BOTH)
    depth = everyone // 8
    tok_count = dec_input.shape[0]
    aligned = self_qkv.shape[0] == 16
    late = (cross_out, ffn_in, ffn_out, w_insert)
    tiny = (norm_gain, norm_bias, pair_table, w_delete.T)
    raw = (self_qkv, self_out, cross_q, cross_kv)
    whole = gathered = None
    if not aligned:
        gathered = late_blocks(*[lax.all_gather(a, BOTH, axis=0, tiled=True) for a in late])
        small = jnp.concatenate([norm_gain, norm_bias, pair_table, w_delete.T], axis=0).T
        small = jnp.pad(small, ((0, 0), (0, 128 - small.shape[1])))
        whole = gather_by_ops(*raw, small)
    whole, line, firsts = first_part(
        depth, aligned, segment_ids, padding, pair_ids, dec_input, enc_output, tiny, raw, late, whole
    )
    start, one, qkv, low, lse, after, two, query, other_query, kv, other_seg = firsts
    parts = (*line, partner(line[0], depth, "x")) if aligned else (gathered,)
    o_own, o_other, lse_own, lse_other = cross_forward(src_lengths, segment_ids, other_seg, query, other_query, kv)
    mids = middle_part(
        depth, aligned, segment_ids, padding, delete_labels, insert_counts, masked_positions, masked_targets,
        w_vocab, after, (o_own, o_other, lse_own, lse_other), whole[1], parts,
    )
    count = 4 if aligned else 1
    parts, mids = mids[:count], mids[count:]
    block_out, gstate, g_own, g_other, st_own, st_other, small_rows, small_cols, grad_vocab, tokens, loss = mids
    sums = ()
    if aligned:
        sums = (parts[2], partner(parts[0], depth, "y"), parts[3], partner(parts[1], depth, "x"))
    dq_own, dq_other, dkv, block_out, grad_vocab = cross_backward(
        src_lengths, segment_ids, other_seg, query, other_query, g_own, g_other, st_own, st_other, kv,
        (block_out, grad_vocab),
    )
    res = last_part(
        depth, aligned, pair_ids, segment_ids, padding, dq_own, dq_other, dkv, enc_output,
        (start, one, qkv, low, lse, after, two), gstate, (sums, small_rows, small_cols), whole,
    )
    if aligned:
        sums = res[2:]
    else:
        scale = (tok_count * everyone) ** (-0.5)
        sums = reduce_by_ops(res[2], res[3], parts[0], scale)
    results, smalls = finish((res[1], res[0], *sums[:8], tokens), sums[8], loss)
    grad_enc, grad_input, qkv, so, cq, kv, co, fi, fo, insert, tokens = results
    gain, bias, table, delete, loss = smalls
    return (
        block_out, grad_input, grad_enc, gain, bias, table, qkv, so, cq, kv, co, fi, fo, delete.T, insert,
        grad_vocab, loss[0, 0], tokens,
    )


def solution(mesh):
    shared = P(BOTH, None)
    across = P(None, BOTH)
    return jax.shard_map(
        body,
        mesh=mesh,
        in_specs=(shared,) * 5 + (P("batch", None),) + (shared,) * 4 + (across,) * 3 + (shared,) * 10,
        out_specs=(shared,) * 3 + (across,) * 3 + (shared,) * 10 + (P(), shared),
        check_vma=False,
    )
```

```python
from functools import partial

import jax
import jax.numpy as jnp
from jax import lax
from jax.experimental import pallas as pl
from jax.experimental.pallas import tpu as pltpu
from jax.sharding import PartitionSpec as P

HD = 64
PAIRS = 8
SEGS = 8
BLOCK = 512
EPSILON = 1e-05
SCALE = 0.125
FILL = -1e30
GELU = 0.7978845608
CUBIC = 0.044715

MESH = pl.DeviceIdType.MESH
ANY = pl.BlockSpec(memory_space=pl.ANY)
VMEM = pl.BlockSpec(memory_space=pltpu.VMEM)
SMEM = pl.BlockSpec(memory_space=pltpu.SMEM)
BOTH = ("batch", "src")
LOW = jnp.bfloat16
WIDE = jnp.float32
LIMIT = 64 << 20


def shape_of(shape, kind):
    return jax.ShapeDtypeStruct(shape, kind)


def dot(left, right):
    return jnp.dot(left, right, preferred_element_type=WIDE)


def dot_tn(left, right):
    return lax.dot_general(left, right, (((0,), (0,)), ((), ())), preferred_element_type=WIDE)


def dot_nt(left, right):
    return lax.dot_general(left, right, (((1,), (1,)), ((), ())), preferred_element_type=WIDE)


def normalised(v):
    centred = v - jnp.mean(v, axis=-1, keepdims=True)
    r = lax.rsqrt(jnp.mean(centred * centred, axis=-1, keepdims=True) + EPSILON)
    return centred * r, r


def norm_back(v, gain, upstream):
    hat, r = normalised(v)
    scaled = upstream * gain
    first = jnp.mean(scaled, axis=-1, keepdims=True)
    second = jnp.mean(scaled * hat, axis=-1, keepdims=True)
    grad_gain = jnp.sum(upstream * hat, axis=0, keepdims=True)
    grad_bias = jnp.sum(upstream, axis=0, keepdims=True)
    return r * (scaled - first - hat * second), grad_gain, grad_bias


def lanes(shape):
    return lax.broadcasted_iota(jnp.int32, shape, len(shape) - 1)


def rows_of(shape):
    return lax.broadcasted_iota(jnp.int32, shape, len(shape) - 2)


def both_heads(x):
    low = lanes(x.shape) < HD
    zero = jnp.zeros_like(x)
    return jnp.concatenate([jnp.where(low, x, zero), jnp.where(low, zero, x)], axis=0)


def join_heads(x):
    half = x.shape[0] // 2
    return jnp.where(lanes((half, x.shape[1])) < HD, x[:half], x[half:])


def twice(x):
    return jnp.concatenate([x, x], axis=0)


def transposed_rows(rows):
    count, width = rows.shape
    return jnp.concatenate([rows, jnp.zeros((128 - count, width), WIDE)], axis=0).T


def bring(sources, places, sems):
    copies = [pltpu.make_async_copy(src, dst, sems.at[k]) for k, (src, dst) in enumerate(zip(sources, places))]
    for copy in copies:
        copy.start()
    return copies


def greet(peers):
    barrier = pltpu.get_barrier_semaphore()
    for peer in peers:
        pl.semaphore_signal(barrier, inc=1, device_id=peer, device_id_type=MESH)
    pl.semaphore_wait(barrier, len(peers))


def remote(src, dst, send, recv, peer):
    return pltpu.make_async_remote_copy(
        src_ref=src,
        dst_ref=dst,
        send_sem=send,
        recv_sem=recv,
        device_id=peer,
        device_id_type=MESH,
    )


class Place:
    def __init__(self, depth):
        b = lax.axis_index("batch")
        self.depth = depth
        self.y = lax.axis_index("src")
        self.c = lax.rem(b, 2)
        self.x = lax.rem(b // 2, 2)
        self.z = b // 4

    def at(self, z=None, x=None, c=None, y=None):
        z = self.z if z is None else z
        x = self.x if x is None else x
        c = self.c if c is None else c
        y = self.y if y is None else y
        return ((z * 2 + x) * 2 + c, y)

    def along(self, k):
        return self.at(z=lax.rem(self.z + k, self.depth))

    def others(self):
        return [self.along(k) for k in range(1, self.depth)]

    def across_x(self):
        return self.at(x=1 - self.x)

    def across_y(self):
        return self.at(y=1 - self.y)

    def across_both(self):
        return self.at(x=1 - self.x, y=1 - self.y)

    def across_core(self):
        return self.at(c=1 - self.c)


def gathering(me, chunks, send, recv):
    z, x, c, y = me.z, me.x, me.c, me.y
    started = [[None] * 3 for _ in chunks]
    used = [0] * len(chunks)
    every = slice(None)

    def launch(k, stage):
        copies = []

        def push(block, peer):
            slot = used[k]
            used[k] += 1
            copy = remote(block, block, send.at[k, slot], recv.at[k, slot], peer)
            copy.start()
            copies.append(copy)

        for view in chunks[k]:
            if stage == 0:
                for peer in me.others():
                    push(view(z, x, c, y), peer)
            elif stage == 1:
                for peer in (me.across_x(), me.across_y(), me.across_both()):
                    push(view(every, x, c, y), peer)
            else:
                push(view(every, every, c, every), me.across_core())
        started[k][stage] = copies

    def begin(k):
        launch(k, 0)

    def after(k, stage):
        for copy in started[k][stage]:
            copy.wait_recv()
        if stage < 2:
            launch(k, stage + 1)

    def end():
        for stages in started:
            for copies in stages:
                for copy in copies:
                    copy.wait_send()

    return begin, after, end


def self_window(block, tok_count):
    low = jnp.clip(block * 128 - 128, 0, tok_count - 384)
    return pl.multiple_of(low, 128)


def self_bar(row_seg, col_seg, block, low):
    keys = pl.ds(low, 384)
    queries = row_seg[0:1, pl.ds(pl.multiple_of(block * 128, 128), 128)]
    shape = (384, 128)
    own = (rows_of(shape) + low) == (lanes(shape) + block * 128)
    allowed = (col_seg[keys, 0:1] == queries) & ((col_seg[keys, 2:3] > 0.5) | own)
    return side_by_side(jnp.where(allowed, 0.0, FILL))


def self_forward(blocks, qkv, out, lse_ref, row_seg, col_seg):
    tok_count, width = out.shape
    first, last = blocks
    pairs = width // 128

    def one(block, carry):
        at = pl.ds(pl.multiple_of(block * 128, 128), 128)
        low = self_window(block, tok_count)
        keys = pl.ds(low, 384)
        barred = self_bar(row_seg, col_seg, block, low)
        every = range(pairs)
        q = [both_heads(qkv[at, p * 128 : (p + 1) * 128] * SCALE) for p in every]
        scores = [dot_nt(qkv[keys, width + p * 128 : width + (p + 1) * 128], q[p]) + barred for p in every]
        tops = [jnp.max(scores[p], axis=0, keepdims=True) for p in every]
        exps = [jnp.exp(scores[p] - tops[p]) for p in every]
        totals = [jnp.sum(exps[p], axis=0, keepdims=True) for p in every]
        values = [qkv[keys, 2 * width + p * 128 : 2 * width + (p + 1) * 128] for p in every]
        mixed = [dot_tn(values[p], exps[p].astype(LOW)) * (1.0 / totals[p]) for p in every]
        stats = []
        for p in every:
            out[at, p * 128 : (p + 1) * 128] = heads_apart(mixed[p]).astype(LOW)
            lse = tops[p] + jnp.log(totals[p])
            stats += [lse[:, :128], lse[:, 128:]]
        lse_ref[:, at] = jnp.concatenate(stats, axis=0)
        return carry

    lax.fori_loop(first, last, one, 0)


def small_matrix(gain, bias, pair_rows, delete):
    def spot(count, first):
        shape = (count, 128)
        return (rows_of(shape) + first == lanes(shape)).astype(LOW)

    total = dot_tn(gain, spot(4, 0)) + dot_tn(bias, spot(4, 4)) + dot_tn(pair_rows, spot(PAIRS, 8))
    return (total + dot_tn(delete, spot(2, 8 + PAIRS))).astype(LOW)


def token_numbers(seg, pad, pair, row_seg, row_keep, col_seg):
    tok_count = seg.shape[1]
    segments = seg[...].astype(WIDE)
    row_seg[...] = segments
    row_keep[...] = 1.0 - pad[...].astype(WIDE)
    pair_row = jnp.zeros((1, tok_count), WIDE)
    for k in range(SEGS):
        pair_row = jnp.where(segments == k, pair[0:1, k : k + 1].astype(WIDE), pair_row)
    columns = [segments, pair_row, row_keep[...], jnp.zeros((5, tok_count), WIDE)]
    columns = transposed_rows(jnp.concatenate(columns, axis=0))
    col_seg[...] = columns
    return (lanes((tok_count, 128)) == (columns[:, 1:2].astype(jnp.int32) + 8)).astype(LOW)


def cutter(ref):
    every = (slice(None),) * (len(ref.shape) - 2)

    def cut(lo, hi):
        value = ref[every + (slice(lo, hi),)]
        return value.reshape((-1, value.shape[-1]))

    return cut


QKV, SO, CQ, KV, EARLY = 0, 48, 64, 80, 112
LATE, PERMUTED, RETURNED = 160, 96, 128


def first_kernel(depth, gathers, *refs):
    (seg_in, pad_in, pair_in, dec_in, enc_in) = refs[:5]
    refs = refs[5:]
    if gathers:
        tiny_in, refs = refs[:4], refs[4:]
        (raw_qkv, raw_so, raw_cq, raw_kv, raw_co, raw_fi, raw_fo, raw_in) = refs[:8]
        (ga_out, gs_out, gz1, gz2) = refs[8:12]
        refs = refs[12:]
    else:
        ga_in, gs_in = refs[:2]
        refs = refs[2:]
    results, other_out, seg_out = refs[:9], refs[9], refs[10]
    held = refs[11:20]
    (start_ref, one_ref, qkv, low, lse, after_ref, two_ref, query, kv) = held
    (enc, ga, gs, row_seg, row_keep, col_seg, own_sem, out_sem, send, recv, sw_send, sw_recv, stage1, stage2) = refs[20:34]
    (seg, pad, pair, dec, few_sem) = refs[34:39]
    few = bring((seg_in, pad_in, pair_in, dec_in), (seg, pad, pair, dec), few_sem)
    if gathers:
        (gain, bias, pair_rows, delete, tiny_sem) = refs[39:]
        tiny = bring(tiny_in, (gain, bias, pair_rows, delete), tiny_sem)
    tok_count, width = dec.shape
    src_count = enc.shape[0]
    me = Place(depth)
    z, x, c, y = me.z, me.x, me.c, me.y
    owns = []

    def own(src, dst):
        copy = pltpu.make_async_copy(src, dst, own_sem.at[len(owns)])
        copy.start()
        owns.append(copy)

    if gathers:
        for raw, count, first in ((raw_qkv, 3, QKV), (raw_so, 1, SO), (raw_cq, 1, CQ), (raw_kv, 2, KV)):
            for k in range(count):
                own(raw.at[:, pl.ds(k * BLOCK, BLOCK)], ga.at[z, x, c, y, pl.ds(first + 16 * k, 16)])
        soon = len(owns)
        own1, own2 = stage1, stage2
        split_fo = PERMUTED - 80
        own(raw_co, own1.at[pl.ds(0, 16)])
        for k in range(4):
            own(raw_fi.at[:, pl.ds(k * BLOCK, BLOCK)], own1.at[pl.ds(16 + 16 * k, 16)])
        own(raw_fo.at[pl.ds(0, split_fo)], own1.at[pl.ds(80, split_fo)])
        own(raw_fo.at[pl.ds(split_fo, 64 - split_fo)], own2.at[pl.ds(0, 64 - split_fo)])
        for k in range(2):
            half = BLOCK // 2
            place = own2.at[pl.ds(64 - split_fo, 16), pl.ds(half * k, half)]
            own(raw_in.at[pl.ds(16 * k, 16)], place)
        for copy in tiny:
            copy.wait()
        gs[z, x, c, y] = small_matrix(gain[...], bias[...], pair_rows[...], delete[...])
        greet(me.others() + [me.across_x(), me.across_y(), me.across_both(), me.across_core()])
        for copy in owns[:soon]:
            copy.wait()

        def rows(lo, hi):
            return lambda *at: ga.at[at + (pl.ds(lo, hi - lo),)]

        chunks = [[lambda *at: gs.at[at]]]
        chunks += [[rows(lo, hi)] for lo, hi in ((0, 16), (16, 32), (32, SO), (SO, KV), (KV, EARLY))]
        begin, after_stage, end = gathering(me, chunks, send, recv)
    else:
        own(ga_in, ga)
        own(gs_in, gs)
        greet([me.across_y()])
        for copy in owns:
            copy.wait()

        def begin(k):
            return None

        def after_stage(k, stage):
            return None

        def end():
            return None

    outs = []

    def out(k):
        copy = pltpu.make_async_copy(held[k], results[k], out_sem.at[len(outs)])
        copy.start()
        outs.append(copy)

    c_s, c_q, c_k, c_v, c_mid, c_kv = range(6)
    begin(c_s)
    begin(c_q)
    line, crossing = [], []
    if gathers:
        for copy in owns[soon:]:
            copy.wait()
        kept = len(owns)
        for k, (ref, spot) in enumerate(((own1, gz1.at[y, z]), (own2, gz2.at[y, z]))):
            crossing.append(remote(ref, spot, sw_send.at[3 + k], sw_recv.at[3 + k], me.across_y()))
            crossing[-1].start()
            own(ref, spot)
    meet = remote(seg_in, seg_out, sw_send.at[0], sw_recv.at[0], me.across_y())
    meet.start()
    fetch = pltpu.make_async_copy(enc_in, enc, out_sem.at[11])
    fetch.start()
    for copy in few:
        copy.wait()
    onehot = token_numbers(seg, pad, pair, row_seg, row_keep, col_seg)
    cut = cutter(ga)
    after_stage(c_s, 0)
    after_stage(c_q, 0)
    begin(c_k)
    after_stage(c_k, 0)
    begin(c_v)
    after_stage(c_s, 1)
    after_stage(c_q, 1)
    after_stage(c_v, 0)
    begin(c_mid)
    begin(c_kv)
    for copy in crossing:
        copy.wait()
    if gathers:
        for copy in owns[kept:]:
            copy.wait()
        far, near = me.along(depth // 2), me.at(z=z + 1 - 2 * lax.rem(z, 2))
        z_far = lax.rem(z + depth // 2, depth)

        def along(ref, peer):
            at = 5 + len(line)
            line.append(remote(ref, ref, sw_send.at[at], sw_recv.at[at], peer))
            line[-1].start()

        for ref in (gz1.at[:, z], gz2.at[:, z]):
            along(ref, far)
            along(ref, near)
    after_stage(c_s, 2)
    table = cutter(gs)(0, gs.shape[-2]).astype(WIDE).T
    start = dec[...].astype(WIDE) + dot(onehot, table.astype(LOW))
    start_ref[...] = start
    out(0)
    one = (normalised(start)[0] * table[0:1] + table[4:5]).astype(LOW)
    one_ref[...] = one
    out(1)
    after_stage(c_k, 1)
    after_stage(c_mid, 0)
    after_stage(c_q, 2)
    qkv[:, 0:BLOCK] = dot(one, cut(QKV, QKV + 16)).astype(LOW)
    after_stage(c_v, 1)
    after_stage(c_k, 2)
    qkv[:, BLOCK : 2 * BLOCK] = dot(one, cut(QKV + 16, QKV + 32)).astype(LOW)
    after_stage(c_v, 2)
    after_stage(c_kv, 0)
    qkv[:, 2 * BLOCK : 3 * BLOCK] = dot(one, cut(QKV + 32, SO)).astype(LOW)
    out(2)
    halves = 2
    span = tok_count // halves
    swaps = []
    for k in range(halves):
        at = pl.ds(k * span, span)
        self_forward((k * span // 128, (k + 1) * span // 128), qkv, low, lse, row_seg, col_seg)
        if k == 0:
            after_stage(c_mid, 1)
            after_stage(c_mid, 2)
        after = start_ref[at, :] + dot(low[at, :], cut(SO, CQ))
        after_ref[at, :] = after
        two = (normalised(after)[0] * table[1:2] + table[5:6]).astype(LOW)
        two_ref[at, :] = two
        query[at, :] = dot(two, cut(CQ, KV)).astype(LOW)
        swap = remote(query.at[at], other_out.at[at], sw_send.at[1 + k], sw_recv.at[1 + k], me.across_y())
        swap.start()
        swaps.append(swap)
        if k == 0 and gathers:
            line[0].wait_recv()
            along(gz1.at[:, z_far], near)
            line[2].wait_recv()
            along(gz2.at[:, z_far], near)
    for k in range(3, 8):
        out(k)
    after_stage(c_kv, 1)
    after_stage(c_kv, 2)
    if gathers:
        own(ga, ga_out)
        own(gs, gs_out)
    fetch.wait()
    w_key, w_val = cut(KV, KV + 16), cut(KV + 16, EARLY)
    parts = 4
    for k in range(parts):
        span = src_count // parts
        at = pl.ds(k * span, span)
        kv[at, 0:width] = dot(enc[at, :], w_key).astype(LOW)
        kv[at, width : 2 * width] = dot(enc[at, :], w_val).astype(LOW)
    out(8)
    for copy in swaps + [meet]:
        copy.wait()
    for k, copy in enumerate(line):
        if k not in (0, 2):
            copy.wait_recv()
        copy.wait_send()
    end()
    for copy in outs + (owns[-2:] if gathers else []):
        copy.wait()


def first_part(depth, gathers, seg, pad, pair, dec, enc, tiny, raw, late, whole):
    tok_count, width = dec.shape
    src_count = enc.shape[0]
    lead = (depth, 2, 2, 2) if gathers else (BLOCK // 16,)
    results = [
        shape_of((tok_count, width), WIDE),
        shape_of((tok_count, width), LOW),
        shape_of((tok_count, 3 * width), LOW),
        shape_of((tok_count, width), LOW),
        shape_of((width // HD, tok_count), WIDE),
        shape_of((tok_count, width), WIDE),
        shape_of((tok_count, width), LOW),
        shape_of((tok_count, width), LOW),
        shape_of((src_count, 2 * width), LOW),
    ]
    outs = results + [shape_of((tok_count, width), LOW), shape_of((1, tok_count), jnp.int32)]
    if gathers:
        outs = [
            shape_of(lead + (EARLY, BLOCK), LOW),
            shape_of(lead + (16, 128), LOW),
            shape_of((2, depth, PERMUTED, BLOCK), LOW),
            shape_of((2, depth, LATE - PERMUTED, BLOCK), LOW),
        ] + outs
    extra = (*tiny, *raw, *late) if gathers else whole
    res = pl.pallas_call(
        partial(first_kernel, depth, gathers),
        name="first_part",
        out_shape=outs,
        in_specs=[ANY] * (5 + len(extra)),
        out_specs=[ANY] * len(outs),
        scratch_shapes=[pltpu.VMEM(a.shape, a.dtype) for a in results]
        + [
            pltpu.VMEM(enc.shape, LOW),
            pltpu.VMEM(lead + (EARLY, BLOCK), LOW),
            pltpu.VMEM(lead + (16, 128), LOW),
            pltpu.VMEM((1, tok_count), WIDE),
            pltpu.VMEM((1, tok_count), WIDE),
            pltpu.VMEM((tok_count, 128), WIDE),
            pltpu.SemaphoreType.DMA((20,)),
            pltpu.SemaphoreType.DMA((12,)),
            pltpu.SemaphoreType.DMA((6, depth + 3)),
            pltpu.SemaphoreType.DMA((6, depth + 3)),
            pltpu.SemaphoreType.DMA((2 * depth + 3,)),
            pltpu.SemaphoreType.DMA((2 * depth + 3,)),
            pltpu.VMEM((PERMUTED, BLOCK), LOW),
            pltpu.VMEM((LATE - PERMUTED, BLOCK), LOW),
            *[pltpu.VMEM(a.shape, a.dtype) for a in (seg, pad, pair, dec)],
            pltpu.SemaphoreType.DMA((4,)),
        ]
        + ([pltpu.VMEM(a.shape, a.dtype) for a in tiny] + [pltpu.SemaphoreType.DMA((4,))] if gathers else []),
        compiler_params=pltpu.CompilerParams(
            collective_id=0, has_side_effects=True, vmem_limit_bytes=LIMIT
        ),
    )(seg, pad, pair, dec, enc, *extra)
    if gathers:
        whole, line, res = res[:2], res[2:4], res[4:]
    else:
        line = None
    start, one, qkv, low, lse, after, two, query, kv, other_query, other_seg = res
    return whole, line, (start, one, qkv, low, lse, after, two, query, other_query, kv, other_seg)


def segment_ends(lengths, ends):
    total = jnp.int32(0)
    ends[0] = total
    for s in range(2 * SEGS):
        total = total + lengths[0, s]
        ends[s + 1] = total


def block_ranges(seg_s, first_seg, ends, off, src_count, block):
    at = pl.multiple_of(block * 128, 128)
    low = jnp.clip(ends[first_seg + seg_s[0, at]] - off, 0, src_count)
    high = jnp.clip(ends[first_seg + seg_s[0, at + 127] + 1] - off, 0, src_count)
    first = low // TILE
    return first, jnp.where(high > low, (high + TILE - 1) // TILE, first)


def key_bounds(segs, firsts, ends, off):
    rows = []
    for seg, first_seg in zip(segs, firsts):
        low = jnp.zeros(seg.shape, jnp.int32)
        high = jnp.zeros(seg.shape, jnp.int32)
        for s in range(SEGS):
            low = jnp.where(seg == s, ends[first_seg + s] - off, low)
            high = jnp.where(seg == s, ends[first_seg + s + 1] - off, high)
        rows += [low, high]
    return jnp.concatenate(rows + [jnp.zeros((4, rows[0].shape[1]), jnp.int32)], axis=0)


TILE = 256


def side_by_side(x):
    return jnp.concatenate([x, x], axis=1)


def side_by_side_rows(rows, k, at):
    return jnp.concatenate([rows[k : k + 1, at], rows[k + 1 : k + 2, at]], axis=1)


def heads_apart(x):
    n = x.shape[1] // 2
    return jnp.concatenate([x[:HD, :n], x[HD:, n:]], axis=0).T


def cross_forward_kernel(
    lengths, seg_so, seg_sp, seg_vo, seg_vp, q_own, q_other, kv, o_own, o_other, lse_own, lse_other,
    ends, bounds, qs, top_ref, total_ref, acc_ref,
):
    tok_count, width = q_own.shape
    src_count = kv.shape[0]
    pairs = width // 128
    pos = lax.axis_index("src")
    off = pos * src_count
    firsts = (pos * SEGS, (1 - pos) * SEGS)
    segment_ends(lengths, ends)
    bounds[...] = key_bounds((seg_vo[...], seg_vp[...]), firsts, ends, off)
    for side, (q, o, lse_ref) in enumerate(((q_own, o_own, lse_own), (q_other, o_other, lse_other))):

        @pl.loop(0, tok_count // 128)
        def _(block):
            at = pl.ds(pl.multiple_of(block * 128, 128), 128)
            first, last = block_ranges((seg_so, seg_sp)[side], firsts[side], ends, off, src_count, block)
            low, high = bounds[2 * side : 2 * side + 1, at], bounds[2 * side + 1 : 2 * side + 2, at]
            for p in range(pairs):
                qs[p] = both_heads(q[at, p * 128 : (p + 1) * 128] * SCALE)
            top_ref[...] = jnp.full_like(top_ref, FILL)
            total_ref[...] = jnp.zeros_like(total_ref)
            acc_ref[...] = jnp.zeros_like(acc_ref)

            def one(t, carry):
                base = pl.multiple_of(t * TILE, TILE)
                keys = pl.ds(base, TILE)
                index = rows_of((TILE, 128)) + base
                barred = side_by_side(jnp.where((index >= low) & (index < high), 0.0, FILL))
                every = range(pairs)
                scores = [dot_nt(kv[keys, pl.ds(p * 128, 128)], qs[p]) for p in every]
                scores = [scores[p] + barred for p in every]
                olds = [top_ref[p] for p in every]
                tops = [jnp.maximum(olds[p], jnp.max(scores[p], axis=0, keepdims=True)) for p in every]
                exps = [jnp.exp(scores[p] - jnp.maximum(tops[p], 0.1 * FILL)) for p in every]
                fades = [jnp.exp(olds[p] - tops[p]) for p in every]
                sums = [total_ref[p] * fades[p] + jnp.sum(exps[p], axis=0, keepdims=True) for p in every]
                mixed = [dot_tn(kv[keys, pl.ds(width + p * 128, 128)], exps[p].astype(LOW)) for p in every]
                mixed = [acc_ref[p] * fades[p] + mixed[p] for p in every]
                for p in every:
                    top_ref[p] = tops[p]
                    total_ref[p] = sums[p]
                    acc_ref[p] = mixed[p]
                return carry

            lax.fori_loop(first, last, one, 0)
            stats = []
            for p in range(pairs):
                total = total_ref[p]
                safe = jnp.where(total > 0.0, total, 1.0)
                o[at, p * 128 : (p + 1) * 128] = heads_apart(acc_ref[p] * (1.0 / safe)).astype(LOW)
                lse = jnp.where(total > 0.0, top_ref[p] + jnp.log(safe), FILL)
                stats += [lse[:, :128], lse[:, 128:]]
            lse_ref[:, at] = jnp.concatenate(stats, axis=0)


def cross_forward(lengths, seg_own, seg_other, q_own, q_other, kv):
    tok_count, width = q_own.shape
    heads = width // HD
    pairs = width // 128
    out = shape_of((tok_count, width), LOW)
    lse = shape_of((heads, tok_count), WIDE)
    return pl.pallas_call(
        cross_forward_kernel,
        name="cross_forward",
        out_shape=[out, out, lse, lse],
        in_specs=[SMEM] * 3 + [VMEM] * 5,
        out_specs=[VMEM] * 4,
        scratch_shapes=[
            pltpu.SMEM((32,), jnp.int32),
            pltpu.VMEM((8, tok_count), jnp.int32),
            pltpu.VMEM((pairs, 256, 128), LOW),
            pltpu.VMEM((pairs, 1, 256), WIDE),
            pltpu.VMEM((pairs, 1, 256), WIDE),
            pltpu.VMEM((pairs, 128, 256), WIDE),
        ],
        compiler_params=pltpu.CompilerParams(vmem_limit_bytes=LIMIT),
        cost_estimate=pl.CostEstimate(flops=1 << 33, bytes_accessed=8 << 20, transcendentals=0),
    )(lengths, seg_own, seg_other, seg_own, seg_other, q_own, q_other, kv)


def cross_backward_kernel(
    lengths, seg_so, seg_sp, seg_vo, seg_vp, q_in, q_in_2, g_in, g_in_2, st_in, st_in_2, kv_in, pass_0, pass_1,
    dq_out, dq_out_2, dkv_out, given_0, given_1, ends, bounds, acc, qs, gs, dq_acc, kv, dkv, held_0, held_1,
    q_own, q_other, g_own, g_other, st_own, st_other, dq_own, dq_other, sems, io_sems, in_sems,
):
    fetch = [pltpu.make_async_copy(kv_in, kv, io_sems.at[0])]
    given = (q_in, q_in_2, g_in, g_in_2, st_in, st_in_2)
    for k, (src, dst) in enumerate(zip(given, (q_own, q_other, g_own, g_other, st_own, st_other))):
        fetch.append(pltpu.make_async_copy(src, dst, in_sems.at[k]))
    for copy in fetch:
        copy.start()
    ways = ((pass_0, held_0, given_0), (pass_1, held_1, given_1))
    taking = [pltpu.make_async_copy(way[0], way[1], sems.at[0, k]) for k, way in enumerate(ways)]
    giving = [pltpu.make_async_copy(way[1], way[2], sems.at[1, k]) for k, way in enumerate(ways)]
    for copy in taking:
        copy.start()
    tok_count, width = q_own.shape
    src_count = kv.shape[0]
    pairs = width // 128
    pos = lax.axis_index("src")
    off = pos * src_count
    firsts = (pos * SEGS, (1 - pos) * SEGS)
    segment_ends(lengths, ends)
    bounds[...] = key_bounds((seg_vo[...], seg_vp[...]), firsts, ends, off)
    acc[...] = jnp.zeros_like(acc)
    for copy in fetch:
        copy.wait()
    stores = []
    sides = ((q_own, g_own, st_own, dq_own), (q_other, g_other, st_other, dq_other))
    for side, (q, g, st, dq) in enumerate(sides):

        @pl.loop(0, tok_count // 128)
        def _(block):
            at = pl.ds(pl.multiple_of(block * 128, 128), 128)
            first, last = block_ranges((seg_so, seg_sp)[side], firsts[side], ends, off, src_count, block)
            low, high = bounds[2 * side : 2 * side + 1, at], bounds[2 * side + 1 : 2 * side + 2, at]
            for p in range(pairs):
                cols = slice(p * 128, (p + 1) * 128)
                qs[p] = both_heads(q[at, cols] * SCALE)
                gs[p] = both_heads(g[at, cols])
            dq_acc[...] = jnp.zeros_like(dq_acc)
            lses = [side_by_side_rows(st, 2 * p, at) for p in range(pairs)]
            deltas = [side_by_side_rows(st, 8 + 2 * p, at) for p in range(pairs)]

            def one(t, carry):
                base = pl.multiple_of(t * TILE, TILE)
                keys = pl.ds(base, TILE)
                index = rows_of((TILE, 128)) + base
                barred = side_by_side(jnp.where((index >= low) & (index < high), 0.0, FILL))
                every = range(pairs)
                cols = [pl.ds(p * 128, 128) for p in every]
                vals = [pl.ds(width + p * 128, 128) for p in every]
                scores = [dot_nt(kv[keys, cols[p]], qs[p]) for p in every]
                slopes = [dot_nt(kv[keys, vals[p]], gs[p]) for p in every]
                probs = [jnp.exp(scores[p] - lses[p] + barred) for p in every]
                gscores = [(probs[p] * (slopes[p] - deltas[p])).astype(LOW) for p in every]
                grad_k = [acc[keys, cols[p]] + dot(gscores[p], qs[p]) for p in every]
                grad_v = [acc[keys, vals[p]] + dot(probs[p].astype(LOW), gs[p]) for p in every]
                grad_q = [dq_acc[p] + dot_tn(kv[keys, cols[p]], gscores[p]) for p in every]
                for p in every:
                    acc[keys, cols[p]] = grad_k[p]
                    acc[keys, vals[p]] = grad_v[p]
                    dq_acc[p] = grad_q[p]
                return carry

            lax.fori_loop(first, last, one, 0)
            for p in range(pairs):
                dq[at, p * 128 : (p + 1) * 128] = (heads_apart(dq_acc[p]) * SCALE).astype(dq.dtype)

        stores.append(pltpu.make_async_copy(dq, (dq_out, dq_out_2)[side], io_sems.at[5 + side]))
        stores[-1].start()

    for first, second in zip(taking, giving):
        first.wait()
        second.start()

    parts = 4
    span = src_count // parts
    for k in range(parts):
        at = pl.ds(k * span, span)
        dkv[at, :] = acc[at, :].astype(LOW)
        stores.append(pltpu.make_async_copy(dkv.at[at], dkv_out.at[at], io_sems.at[1 + k]))
        stores[-1].start()
    for copy in stores:
        copy.wait()
    for copy in giving:
        copy.wait()


def cross_backward(lengths, seg_own, seg_other, q_own, q_other, g_own, g_other, st_own, st_other, kv, passed):
    tok_count, width = q_own.shape
    src_count = kv.shape[0]
    pairs = width // 128
    return pl.pallas_call(
        cross_backward_kernel,
        name="cross_backward",
        out_shape=[
            shape_of((tok_count, width), WIDE),
            shape_of((tok_count, width), LOW),
            shape_of((src_count, 2 * width), LOW),
        ]
        + [shape_of(a.shape, a.dtype) for a in passed],
        in_specs=[SMEM] * 3 + [VMEM] * 2 + [ANY] * 9,
        out_specs=[ANY] * 5,
        scratch_shapes=[
            pltpu.SMEM((32,), jnp.int32),
            pltpu.VMEM((8, tok_count), jnp.int32),
            pltpu.VMEM((src_count, 2 * width), WIDE),
            pltpu.VMEM((pairs, 256, 128), LOW),
            pltpu.VMEM((pairs, 256, 128), LOW),
            pltpu.VMEM((pairs, 128, 256), WIDE),
            pltpu.VMEM(kv.shape, LOW),
            pltpu.VMEM(kv.shape, LOW),
        ]
        + [pltpu.VMEM(a.shape, a.dtype) for a in (*passed, q_own, q_other, g_own, g_other, st_own, st_other)]
        + [pltpu.VMEM((tok_count, width), WIDE), pltpu.VMEM((tok_count, width), LOW)]
        + [pltpu.SemaphoreType.DMA((2, 2)), pltpu.SemaphoreType.DMA((7,)), pltpu.SemaphoreType.DMA((6,))],
        compiler_params=pltpu.CompilerParams(vmem_limit_bytes=LIMIT),
        cost_estimate=pl.CostEstimate(flops=1 << 34, bytes_accessed=16 << 20, transcendentals=0),
    )(lengths, seg_own, seg_other, seg_own, seg_other, q_own, q_other, g_own, g_other, st_own, st_other, kv, *passed)


def merge_all(parts, count):
    top = parts[0]
    for part in parts[1:]:
        top = jnp.maximum(top, part)
    total = sum(jnp.exp(part - top) for part in parts)
    return jnp.where(rows_of(top.shape) < count, top + jnp.log(total), sum(parts))


def folded(row):
    return jnp.concatenate([row[:, k : k + 128] for k in range(0, row.shape[1], 128)], axis=0)


def unfolded(rows):
    return jnp.concatenate([rows[k : k + 1] for k in range(rows.shape[0])], axis=1)


def middle_kernel(depth, split, *refs):
    (
        seg_in, pad_in, labels_in, counts_in, positions_in, targets_in, lse_in, lse_other, vocab_in, after_in, o_in,
        o_other, gs,
    ) = refs[:13]
    parts = refs[13 : 13 + (3 if split else 1)]
    refs = refs[13 + len(parts) :]
    count = 4 if split else 1
    sums = refs[:count]
    refs = refs[count:]
    (
        block_out, state_out, g_own, g_other, st_own, st_other, small_rows, small_cols, grad_vocab, token_out, loss_out,
    ) = refs[:11]
    numbers = refs[11:18]
    (seg, pad, labels, counts, positions, targets, lse_own) = numbers
    few_sem = refs[18]
    refs = refs[:11] + refs[19:]
    given = (seg_in, pad_in, labels_in, counts_in, positions_in, targets_in, lse_in)
    few = bring(given, numbers, few_sem)
    (
        w_vocab, after_self, o_own, block_ref, state_ref, g_ref, vocab_ref, out_sem,
        wm, eb, eb_got, w_s, got_o, got_lse, cross_o, cross_low, ac, bs, n3, act, slope, gpre, head,
        lt, gt, gt_got, ew, hw, pb, pb_got, rb, got_rq, got_rz, st_c, st_q, st_z, gh, g_ffn, load_sem, send, recv,
    ) = refs[11 : 11 + 41]
    sum_refs = refs[11 + 41 :]
    tok_count, width = after_self.shape
    hidden = act.shape[1]
    masked = positions.shape[1]
    vocab_local = w_vocab.shape[1]
    everyone = depth * 8
    me = Place(depth)
    z, x, c, y = me.z, me.x, me.c, me.y
    greet(me.others() + [me.across_x(), me.across_y(), me.across_both(), me.across_core()])
    used = [0]

    def push(src, dst, peer):
        k = used[0]
        used[0] += 1
        copy = remote(src, dst, send.at[k], recv.at[k], peer)
        copy.start()
        return copy

    pending = []

    def arrive(copies):
        for copy in copies:
            copy.wait_recv()
        pending.extend(copies)

    loads = []

    def load(src, dst):
        copy = pltpu.make_async_copy(src, dst, load_sem.at[len(loads)])
        copy.start()
        loads.append(copy)

    halves = 2
    span = tok_count // halves
    ranges = [pl.ds(k * span, span) for k in range(halves)]

    def swap_outputs():
        copies = [push(lse_other, got_lse, me.across_y())]
        return copies + [push(o_other.at[at], got_o.at[at], me.across_y()) for at in ranges]

    load(gs, w_s)
    load(after_in, after_self)
    load(o_in, o_own)
    load(vocab_in, w_vocab.at[c])
    shared = [push(vocab_in, w_vocab.at[c], me.across_core())]
    if split:
        rest = pl.ds(PERMUTED, LATE - PERMUTED)
        soon = pl.ds(0, PERMUTED)
        late_part = [push(parts[1].at[py], wm.at[:, x, c, py, rest], me.across_x()) for py in range(2)]
        swap = swap_outputs()
        for py in range(2):
            load(parts[0].at[py], wm.at[:, x, c, py, soon])
            load(parts[1].at[py], wm.at[:, x, c, py, rest])
            load(parts[2].at[py], wm.at[:, 1 - x, c, py, soon])
            shared.append(push(parts[0].at[py], wm.at[:, x, c, py, soon], me.across_core()))
            shared.append(push(parts[1].at[py], wm.at[:, x, c, py, rest], me.across_core()))
            shared.append(push(parts[2].at[py], wm.at[:, 1 - x, c, py, soon], me.across_core()))
    else:
        swap = swap_outputs()
        load(parts[0], wm)

    def cut(lo, hi):
        value = wm[:, :, :, :, lo:hi] if split else wm[:, lo:hi]
        return value.reshape((-1, BLOCK))

    def put(lo, value, first=0, last=None, cols=slice(0, BLOCK)):
        groups, rows, wide = value.shape
        last = depth if last is None else last
        if split:
            eb[first:last, :, :, :, lo : lo + rows, cols] = value.reshape((last - first, 2, 2, 2, rows, wide))
        else:
            step = eb.shape[0] // depth
            eb[first * step : last * step, lo : lo + rows, cols] = value

    for copy in few:
        copy.wait()
    segments = seg[...].astype(WIDE)
    keep = 1.0 - pad[...].astype(WIDE)
    lane_row = lanes((1, tok_count))
    inside = lane_row < tok_count - 1

    def following(row):
        return pltpu.roll(jnp.concatenate([row, jnp.zeros((7, tok_count), WIDE)], axis=0), tok_count - 1, 1)[0:1]

    follows = inside & (following(segments) == segments) & (keep > 0.5) & (following(keep) > 0.5)
    valid = jnp.where(follows, 1.0, 0.0)
    rows = [keep, valid, labels[...].astype(WIDE), counts[...].astype(WIDE)]
    columns = transposed_rows(jnp.concatenate(rows + [jnp.zeros((4, tok_count), WIDE)], axis=0))
    col_keep, col_valid = columns[:, 0:1], columns[:, 1:2]
    col_label, col_count = columns[:, 2:3], columns[:, 3:4].astype(jnp.int32)

    for copy in loads:
        copy.wait()
    arrive(shared)
    table = w_s[...].reshape((-1, 128)).astype(WIDE).T

    outs = []

    def out(src, dst):
        copy = pltpu.make_async_copy(src, dst, out_sem.at[len(outs)])
        copy.start()
        outs.append(copy)

    blocks = hidden // BLOCK
    weight_co = cut(0, 16)
    arrive(swap[:1])
    top = jnp.maximum(lse_own[...], got_lse[...])
    lse = top + jnp.log(jnp.exp(lse_own[...] - top) + jnp.exp(got_lse[...] - top))
    shares = jnp.concatenate([jnp.exp(lse_own[...] - lse), jnp.exp(got_lse[...] - lse)], axis=0)
    shares = transposed_rows(shares)
    low_half = lanes((span, 128)) < HD
    for k, at in enumerate(ranges):
        arrive(swap[1 + k : 2 + k])
        mine = shares[k * span : (k + 1) * span]
        for p in range(width // 128):
            cols = slice(p * 128, (p + 1) * 128)
            share_own = jnp.where(low_half, mine[:, 2 * p : 2 * p + 1], mine[:, 2 * p + 1 : 2 * p + 2])
            share_got = jnp.where(low_half, mine[:, 8 + 2 * p : 9 + 2 * p], mine[:, 9 + 2 * p : 10 + 2 * p])
            mixed = o_own[at, cols].astype(WIDE) * share_own + got_o[at, cols].astype(WIDE) * share_got
            cross_o[at, cols] = mixed
            cross_low[at, cols] = mixed.astype(LOW)
        after_cross = after_self[at, :] + dot(cross_low[at, :], weight_co)
        ac[at, :] = after_cross
        normed = (normalised(after_cross)[0] * table[2:3] + table[6:7]).astype(LOW)
        n3[at, :] = normed
        if k == 0 and split:
            arrive(late_part)
            block = wm.at[:, 1 - x, c, :, rest]
            late_part = [push(block, block, me.across_core())]
        for j in range(blocks):
            cols = slice(j * BLOCK, (j + 1) * BLOCK)
            pre = dot(normed, cut(16 + 16 * j, 32 + 16 * j))
            square = pre * pre
            bent = jnp.tanh(GELU * pre * (1.0 + CUBIC * square))
            half = 0.5 * (1.0 + bent)
            act[at, cols] = (pre * half).astype(LOW)
            slope[at, cols] = half + 0.5 * pre * (1.0 - bent * bent) * (GELU * (1.0 + 3.0 * CUBIC * square))
        if k == 0 and split:
            arrive(late_part)
        state = after_cross + dot(act[at, :], cut(80, 144))
        bs[at, :] = state
        block_ref[at, :] = state.astype(LOW)
        head[at, :] = (normalised(state)[0] * table[3:4] + table[7:8]).astype(LOW)
    flat_fo = cut(80, 144)
    out(block_ref, block_out)
    head_in = head[...]

    picker = (positions[...] == rows_of((tok_count, masked))).astype(LOW)
    picked = dot_tn(picker, head_in).astype(LOW)
    kept = dot(jnp.concatenate([keep, jnp.zeros((7, tok_count), WIDE)], axis=0).astype(LOW), picker)
    code = jnp.where(kept[0:1] > 0.5, targets[...] + 1, 0)
    digits = jnp.concatenate([code >> 8, code & 255, jnp.zeros((6, masked), jnp.int32)], axis=0)
    digits = dot_tn(digits.astype(WIDE).astype(LOW), (rows_of((8, 128)) == lanes((8, 128))).astype(LOW)).astype(LOW)
    pb[z, x, y, :, 0:width] = picked
    pb[z, x, y, :, width : width + 128] = digits
    mine = pb.at[z, x, y]
    flight = [push(mine, mine, peer) for peer in me.others()]

    classes = BLOCK // 2
    flat_in = cut(144, 160).reshape((-1, 16, BLOCK))
    flat_in = jnp.concatenate([flat_in[:, :, :classes], flat_in[:, :, classes:]], axis=1).reshape((-1, classes))
    w_one, w_two = flat_in[:width], flat_in[width:]
    token_row = rows_of((tok_count, classes))
    ahead = pltpu.roll(dot(head_in, w_two), tok_count - 1, 0)
    logits = dot(head_in, w_one) + jnp.where(token_row == tok_count - 1, 0.0, ahead)
    top = jnp.max(logits, axis=1, keepdims=True)
    exps = jnp.exp(logits - top)
    total = jnp.sum(exps, axis=1, keepdims=True)
    hits = lanes((tok_count, classes)) == col_count
    entropy = top + jnp.log(total) - jnp.sum(jnp.where(hits, logits, 0.0), axis=1, keepdims=True)
    loss_col = col_valid * entropy
    grads = col_valid * (exps * (1.0 / total) - jnp.where(hits, 1.0, 0.0))
    g_insert = grads.astype(LOW)
    before = pltpu.roll(g_insert.astype(WIDE), 1, 0)
    g_before = jnp.where(token_row == 0, 0.0, before).astype(LOW)

    arrive(flight)
    column = pb.at[:, x, y]
    flight = [push(column, column, peer) for peer in (me.across_x(), me.across_y(), me.across_both())]

    flat_s = w_s[...].reshape((-1, 128))
    two = dot(head_in, flat_s)
    l_zero, l_one = two[:, 16:17], two[:, 17:18]
    top = jnp.maximum(l_zero, l_one)
    e_zero, e_one = jnp.exp(l_zero - top), jnp.exp(l_one - top)
    total = e_zero + e_one
    is_one = col_label > 0.5
    loss_col = loss_col + col_keep * (top + jnp.log(total) - jnp.where(is_one, l_one, l_zero))
    d_zero = col_keep * (e_zero / total - jnp.where(is_one, 0.0, 1.0))
    d_one = col_keep * (e_one / total - jnp.where(is_one, 1.0, 0.0))
    lane = lanes((tok_count, 128))
    g_delete = jnp.where(lane == 16, d_zero, jnp.where(lane == 17, d_one, 0.0)).astype(LOW)
    gh[...] = dot_nt(g_delete, flat_s) + dot_nt(g_insert, w_one) + dot_nt(g_before, w_two)
    arrive(flight)
    sibling = [push(pb, pb_got, me.across_core())]
    def rows_from(ref):
        return ref[...].reshape((-1, width + 128))

    gathered = rows_from(pb)
    rows_all = gathered[:, 0:width]
    numbers = gathered[:, width : width + 128].astype(WIDE).T
    code = numbers[0:1] * 256.0 + numbers[1:2]
    weight = jnp.where(code > 0.5, 1.0, 0.0)
    count = rows_all.shape[0]
    target = code.astype(jnp.int32) - 1
    place = rows_of((vocab_local, count))
    lt[...] = dot_nt(w_vocab[...].reshape((-1, width)), rows_all)
    hits = []
    for k in range(2):
        first = lax.axis_index(BOTH) + 2 * (k - c)
        hits.append(place + first * vocab_local == target)
    hits = jnp.concatenate(hits, axis=0)
    logits = lt[...]
    top = jnp.max(logits, axis=0, keepdims=True)
    exps = jnp.exp(logits - top)
    gt[...] = exps.astype(LOW)
    total = jnp.sum(exps, axis=0, keepdims=True)
    chosen = jnp.sum(jnp.where(hits, logits, 0.0), axis=0, keepdims=True)
    loss_here = jnp.sum(loss_col, axis=0, keepdims=True)
    folds = count // 128
    loss_rows = jnp.broadcast_to(loss_here, (st_z.shape[1] - 2 * folds, 128))
    st_q[x, y] = jnp.concatenate([folded(top + jnp.log(total)), folded(chosen), loss_rows], axis=0)
    spot = st_q.at[x, y]
    flight = [push(spot, spot, peer) for peer in (me.across_x(), me.across_y(), me.across_both())]
    small_cols[...] = dot_tn(head_in, g_delete)
    for k, grad in enumerate((g_insert, g_before)):
        pairs = dot_tn(head_in, grad).astype(LOW).reshape((-1, 2, 16, classes))
        for side in range(2):
            cols = slice(side * classes, (side + 1) * classes)
            put(144, pairs[:, side], k * (depth // 2), (k + 1) * (depth // 2), cols)
    arrive(flight)
    st_z[z] = merge_all([st_q[0, 0], st_q[0, 1], st_q[1, 0], st_q[1, 1]], folds)
    flight = [push(st_z.at[z], st_z.at[z], peer) for peer in me.others()]
    flat_vocab = w_vocab[...].reshape((-1, width))
    ew[...] = dot_tn(gt[...], flat_vocab)
    hw[...] = dot_tn(jnp.where(hits, 1.0, 0.0).astype(LOW), flat_vocab).astype(LOW)
    arrive(flight)
    stat = merge_all([st_z[k] for k in range(depth)], folds)
    all_loss = stat[2 * folds : 2 * folds + 1]
    stat = jnp.concatenate([unfolded(stat[0:folds]), unfolded(stat[folds : 2 * folds])], axis=0)
    factors = [weight * jnp.exp(top - stat[0:1]), weight, jnp.zeros((6, count), WIDE)]
    factors = transposed_rows(jnp.concatenate(factors, axis=0))
    mixed = ew[...] * factors[:, 0:1] - hw[...].astype(WIDE) * factors[:, 1:2]
    rb[...] = mixed.astype(LOW).reshape(rb.shape)
    flight = [
        push(rb.at[:, 1 - x, y], got_rq.at[0], me.across_x()),
        push(rb.at[:, x, 1 - y], got_rq.at[1], me.across_y()),
        push(rb.at[:, 1 - x, 1 - y], got_rq.at[2], me.across_both()),
    ]
    gt[...] = (weight * (jnp.exp(lt[...] - stat[0:1]) - jnp.where(hits, 1.0, 0.0))).astype(LOW)
    sibling.append(push(gt.at[pl.ds((1 - c) * vocab_local, vocab_local)], gt_got, me.across_core()))
    tokens = weight * (stat[0:1] - stat[1:2])
    mine = rows_of((masked, count)) + ((z * 2 + x) * 2 + y) * masked == lanes((masked, count))
    own = jnp.sum(jnp.where(mine, tokens, 0.0), axis=1, keepdims=True)
    token_out[...] = jnp.sum(
        jnp.where(rows_of((masked, masked)) == lanes((masked, masked)), own, 0.0), axis=0, keepdims=True
    )
    loss = (all_loss + jnp.sum(tokens, axis=1, keepdims=True)) * (1.0 / (tok_count * everyone))
    st_c[0] = jnp.broadcast_to(loss, (8, 128))
    sibling.append(push(st_c.at[0], st_c.at[1], me.across_core()))
    arrive(flight)
    line = rb[:, x, y].astype(WIDE)
    for k in range(3):
        line = line + got_rq[k].astype(WIDE)
    got_rq[3] = line.astype(LOW)
    flight = [
        push(got_rq.at[3, lax.rem(z + k, depth)], got_rz.at[k - 1], me.along(k)) for k in range(1, depth)
    ]
    arrive(sibling)
    loss_out[...] = st_c[0, 0:1, 0:1] + st_c[1, 0:1, 0:1]
    scale = (tok_count * everyone) ** (-0.5)
    mine = gt[pl.ds(pl.multiple_of(c * vocab_local, vocab_local), vocab_local), :]
    vocab_ref[...] = (dot(mine, rows_all) + dot(gt_got[...], rows_from(pb_got)[:, 0:width])) * scale
    out(vocab_ref, grad_vocab)
    arrive(flight)
    grad_picked = got_rq[3, z].astype(WIDE)
    for k in range(1, depth):
        grad_picked = grad_picked + got_rz[k - 1].astype(WIDE)
    coarse = grad_picked.astype(LOW)
    fine = (grad_picked - coarse.astype(WIDE)).astype(LOW)
    grad_head = gh[...] + dot(picker, coarse) + dot(picker, fine)

    gh[...] = grad_head
    gain_2 = gain_3 = bias_2 = bias_3 = 0.0
    low_half = lanes((span, 128)) < HD
    lane = lanes((span, 128))
    swap, delta_rows = [], []
    for at in ranges:
        grad_block, gain, bias = norm_back(bs[at, :], table[3:4], gh[at, :])
        gain_3, bias_3 = gain_3 + gain, bias_3 + bias
        g_half = grad_block.astype(LOW)
        g_ffn[at, :] = g_half
        slopes = [dot_nt(g_half, flat_fo[j * BLOCK : (j + 1) * BLOCK]) for j in range(blocks)]
        slopes = [(slopes[j] * slope[at, j * BLOCK : (j + 1) * BLOCK]).astype(LOW) for j in range(blocks)]
        upstream = sum(dot_nt(slopes[j], cut(16 + 16 * j, 32 + 16 * j)) for j in range(blocks))
        for j in range(blocks):
            gpre[at, j * BLOCK : (j + 1) * BLOCK] = slopes[j]
        back, gain, bias = norm_back(ac[at, :], table[2:3], upstream)
        gain_2, bias_2 = gain_2 + gain, bias_2 + bias
        grad_state = grad_block + back
        state_ref[at, :] = grad_state
        g_attn = dot_nt(grad_state.astype(LOW), weight_co).astype(LOW)
        g_ref[at, :] = g_attn
        swap.append(push(g_ref.at[at], g_other.at[at], me.across_y()))
        deltas = jnp.zeros((span, 128), WIDE)
        for p in range(width // 128):
            cols = slice(p * 128, (p + 1) * 128)
            product = g_attn[:, cols].astype(WIDE) * cross_o[at, cols]
            first = jnp.sum(jnp.where(low_half, product, 0.0), axis=1, keepdims=True)
            second = jnp.sum(jnp.where(low_half, 0.0, product), axis=1, keepdims=True)
            deltas = jnp.where(lane == 2 * p, first, jnp.where(lane == 2 * p + 1, second, deltas))
        delta_rows.append(deltas.T[0:8])
    st_own[...] = jnp.concatenate([lse, jnp.concatenate(delta_rows, axis=1)], axis=0)
    swap.append(push(st_own, st_other, me.across_y()))
    out(state_ref, state_out)
    out(g_ref, g_own)
    g_cross = state_ref[...].astype(LOW)

    cores = []

    def to_core(lo, hi):
        if split:
            at = pl.ds(lo, hi - lo)
            cores.append(push(eb.at[:, :, 1 - c, :, at], eb_got.at[:, :, :, at], me.across_core()))

    to_core(144, 160)
    for j in range(blocks):
        grad = dot_tn(act[:, j * BLOCK : (j + 1) * BLOCK], g_ffn[...]).astype(LOW)
        put(80, grad.reshape((-1, 64, BLOCK)), j * depth // blocks, (j + 1) * depth // blocks)
    to_core(80, 144)
    for j in range(blocks):
        grad = dot_tn(n3[...], gpre[:, j * BLOCK : (j + 1) * BLOCK]).astype(LOW)
        put(16 + 16 * j, grad.reshape((-1, 16, BLOCK)))
    to_core(16, 80)
    put(0, dot_tn(cross_low[...], g_cross).astype(LOW).reshape((-1, 16, BLOCK)))
    to_core(0, 16)
    small_rows[...] = jnp.concatenate([gain_2, gain_3, bias_2, bias_3, jnp.zeros((4, width), WIDE)], axis=0)
    if split:
        arrive(cores)
        one, two = pl.ds(0, RETURNED), pl.ds(RETURNED, LATE - RETURNED)
        for k, (at, first, spot) in enumerate(((one, 1 - y, 1), (two, 1 - x, 0), (one, y, 1), (two, x, 0))):
            for other in range(2):
                px, py = (other, first) if spot else (first, other)

                @pl.loop(0, depth)
                def _(zz):
                    total = eb[zz, px, c, py, at].astype(WIDE) + eb_got[zz, px, py, at].astype(WIDE)
                    sum_refs[k][other, zz] = total.astype(LOW)

            out(sum_refs[k], sums[k])
    else:
        sums[0][...] = eb[...]
    arrive(swap)
    for copy in pending:
        copy.wait_send()
    for copy in outs:
        copy.wait()


def middle_part(depth, split, seg, pad, labels, counts, positions, targets, w_vocab, after_self, attended, gs, parts):
    tok_count, width = after_self.shape
    hidden = 4 * BLOCK
    vocab_local = w_vocab.shape[0]
    everyone = depth * 8
    masked = positions.shape[1]
    count = masked * everyone // 2
    stat_rows = (2 * (count // 128) + 15) // 8 * 8
    sharded = (depth, 2, 2, 2)
    lead = sharded if split else (BLOCK // 16,)
    sharded = (depth, 2, 2, 2)
    if split:
        outs = [(shape_of((2, depth, n, BLOCK), LOW), ANY) for n in (RETURNED, LATE - RETURNED)] * 2
    else:
        outs = [(shape_of(parts[0].shape, LOW), VMEM)]
    outs += [
        (shape_of((tok_count, width), LOW), ANY),
        (shape_of((tok_count, width), WIDE), ANY),
        (shape_of((tok_count, width), LOW), ANY),
        (shape_of((tok_count, width), LOW), ANY),
        (shape_of((16, tok_count), WIDE), VMEM),
        (shape_of((16, tok_count), WIDE), ANY),
        (shape_of((8, width), WIDE), VMEM),
        (shape_of((width, 128), WIDE), VMEM),
        (shape_of((vocab_local, width), WIDE), ANY),
        (shape_of((1, masked), WIDE), VMEM),
        (shape_of((1, 1), WIDE), VMEM),
    ]
    copies = 32 + 2 * (depth - 1) + 3 + 1 + 1 + 3 + 1 + 3 + (depth - 1)
    return pl.pallas_call(
        partial(middle_kernel, depth, split),
        name="middle_part",
        out_shape=[o for o, _ in outs],
        in_specs=[ANY] * (13 + len(parts)),
        out_specs=[s for _, s in outs],
        scratch_shapes=[
            *[pltpu.VMEM(a.shape, a.dtype) for a in (seg, pad, labels, counts, positions, targets, attended[2])],
            pltpu.SemaphoreType.DMA((7,)),
            pltpu.VMEM((2, vocab_local, width), LOW),
            pltpu.VMEM((tok_count, width), WIDE),
            pltpu.VMEM((tok_count, width), LOW),
            pltpu.VMEM((tok_count, width), LOW),
            pltpu.VMEM((tok_count, width), WIDE),
            pltpu.VMEM((tok_count, width), LOW),
            pltpu.VMEM((vocab_local, width), WIDE),
            pltpu.SemaphoreType.DMA((10,)),
            pltpu.VMEM(lead + (160, BLOCK), LOW),
            pltpu.VMEM(lead + (160, BLOCK), LOW),
            pltpu.VMEM(((depth, 2, 2) if split else (1,)) + (160, BLOCK), LOW),
            pltpu.VMEM(gs.shape, LOW),
            pltpu.VMEM((tok_count, width), LOW),
            pltpu.VMEM((8, tok_count), WIDE),
            pltpu.VMEM((tok_count, width), WIDE),
            pltpu.VMEM((tok_count, width), LOW),
            pltpu.VMEM((tok_count, width), WIDE),
            pltpu.VMEM((tok_count, width), WIDE),
            pltpu.VMEM((tok_count, width), LOW),
            pltpu.VMEM((tok_count, hidden), LOW),
            pltpu.VMEM((tok_count, hidden), WIDE),
            pltpu.VMEM((tok_count, hidden), LOW),
            pltpu.VMEM((tok_count, width), LOW),
            pltpu.VMEM((2 * vocab_local, count), WIDE),
            pltpu.VMEM((2 * vocab_local, count), LOW),
            pltpu.VMEM((vocab_local, count), LOW),
            pltpu.VMEM((count, width), WIDE),
            pltpu.VMEM((count, width), LOW),
            pltpu.VMEM((depth, 2, 2, masked, width + 128), LOW),
            pltpu.VMEM((depth, 2, 2, masked, width + 128), LOW),
            pltpu.VMEM((depth, 2, 2, masked, width), LOW),
            pltpu.VMEM((4, depth, masked, width), LOW),
            pltpu.VMEM((max(depth - 1, 1), masked, width), LOW),
            pltpu.VMEM((2, 8, 128), WIDE),
            pltpu.VMEM((2, 2, stat_rows, 128), WIDE),
            pltpu.VMEM((depth, stat_rows, 128), WIDE),
            pltpu.VMEM((tok_count, width), WIDE),
            pltpu.VMEM((tok_count, width), LOW),
            pltpu.SemaphoreType.DMA((12,)),
            pltpu.SemaphoreType.DMA((copies + depth,)),
            pltpu.SemaphoreType.DMA((copies + depth,)),
        ]
        + ([pltpu.VMEM((2, depth, n, BLOCK), LOW) for n in (RETURNED, LATE - RETURNED)] * 2 if split else []),
        compiler_params=pltpu.CompilerParams(
            collective_id=1, has_side_effects=True, vmem_limit_bytes=LIMIT
        ),
    )(seg, pad, labels, counts, positions, targets, *attended[2:], w_vocab, after_self, *attended[:2], gs, *parts)


def self_backward_start(dk, dv):
    dk[...] = jnp.zeros_like(dk)
    dv[...] = jnp.zeros_like(dv)


def self_backward(blocks, qkv, out, lse_ref, g_ref, dqkv, dk, dv, row_seg, col_seg):
    tok_count, width = out.shape
    first, last = blocks
    pairs = width // 128

    def one(block, carry):
        at = pl.ds(pl.multiple_of(block * 128, 128), 128)
        low = self_window(block, tok_count)
        keys = pl.ds(low, 384)
        barred = self_bar(row_seg, col_seg, block, low)
        shape = (8, 128)
        halves = (rows_of(shape) == lanes(shape) // HD).astype(LOW)
        every = range(pairs)
        cols = [slice(p * 128, (p + 1) * 128) for p in every]
        q = [both_heads(qkv[at, cols[p]] * SCALE) for p in every]
        g = [both_heads(g_ref[at, cols[p]]) for p in every]
        keyed = [qkv[keys, width + p * 128 : width + (p + 1) * 128] for p in every]
        scores = [dot_nt(keyed[p], q[p]) + barred for p in every]
        slopes = [dot_nt(qkv[keys, 2 * width + p * 128 : 2 * width + (p + 1) * 128], g[p]) for p in every]
        products = [g_ref[at, cols[p]].astype(WIDE) * out[at, cols[p]].astype(WIDE) for p in every]
        coarse = [products[p].astype(LOW) for p in every]
        fine = [(products[p] - coarse[p].astype(WIDE)).astype(LOW) for p in every]
        deltas = [dot_nt(halves, coarse[p]) + dot_nt(halves, fine[p]) for p in every]
        deltas = [jnp.concatenate([deltas[p][0:1], deltas[p][1:2]], axis=1) for p in every]
        lses = [side_by_side_rows(lse_ref, 2 * p, at) for p in every]
        probs = [jnp.exp(scores[p] - lses[p]) for p in every]
        gscores = [(probs[p] * (slopes[p] - deltas[p])).astype(LOW) for p in every]
        grad_q = [heads_apart(dot_tn(keyed[p], gscores[p])) * SCALE for p in every]
        grad_k = [dk[keys, cols[p]] + dot(gscores[p], q[p]) for p in every]
        grad_v = [dv[keys, cols[p]] + dot(probs[p].astype(LOW), g[p]) for p in every]
        for p in every:
            dqkv[at, cols[p]] = grad_q[p].astype(LOW)
            dk[keys, cols[p]] = grad_k[p]
            dv[keys, cols[p]] = grad_v[p]
        return carry

    lax.fori_loop(first, last, one, 0)


def self_backward_end(dqkv, dk, dv):
    width = dk.shape[1]
    dqkv[:, width : 2 * width] = dk[...].astype(LOW)
    dqkv[:, 2 * width : 3 * width] = dv[...].astype(LOW)


def reduction(me, chunks, send, recv):
    z, x, c, y = me.z, me.x, me.c, me.y
    depth = me.depth
    count = len(chunks)
    started = [[None] * 3 for _ in chunks]
    used = [0] * count

    def launch(k, stage):
        copies = []

        def push(src, dst, peer):
            slot = used[k]
            used[k] += 1
            copy = remote(src, dst, send.at[k, slot], recv.at[k, slot], peer)
            copy.start()
            copies.append(copy)

        for src, got_c, got_q, got_z, at, put in chunks[k]:
            if stage == 0:
                push(src.at[:, :, 1 - c, :, at], got_c.at[:, :, :, at], me.across_core())
            elif stage == 1:
                push(got_c.at[:, 1 - x, y, at], got_q.at[0, :, at], me.across_x())
                push(got_c.at[:, x, 1 - y, at], got_q.at[1, :, at], me.across_y())
                push(got_c.at[:, 1 - x, 1 - y, at], got_q.at[2, :, at], me.across_both())
            else:
                for j in range(1, depth):
                    push(got_c.at[lax.rem(z + j, depth), x, y, at], got_z.at[j - 1, at], me.along(j))
        started[k][stage] = copies

    def absorb(k, stage):
        for copy in started[k][stage]:
            copy.wait_recv()
        for src, got_c, got_q, got_z, at, put in chunks[k]:
            if stage == 0:

                @pl.loop(0, depth)
                def _(zz):
                    for xx in range(2):
                        for yy in range(2):
                            total = src[zz, xx, c, yy, at].astype(WIDE) + got_c[zz, xx, yy, at].astype(WIDE)
                            got_c[zz, xx, yy, at] = total.astype(LOW)

            elif stage == 1:

                @pl.loop(0, depth)
                def _(zz):
                    total = got_c[zz, x, y, at].astype(WIDE)
                    for k in range(3):
                        total = total + got_q[k, zz, at].astype(WIDE)
                    got_c[zz, x, y, at] = total.astype(LOW)

            else:
                total = got_c[z, x, y, at].astype(WIDE)
                for j in range(1, depth):
                    total = total + got_z[j - 1, at].astype(WIDE)
                put(total)

    def begin(k):
        launch(k, 0)

    def after(k, stage):
        absorb(k, stage)
        if stage < 2:
            launch(k, stage + 1)

    def end():
        for stages in started:
            for copies in stages:
                for copy in copies:
                    copy.wait_send()

    return begin, after, end


def last_kernel(depth, reduces, *refs):
    given, dq_other = refs[:3], refs[3]
    held = refs[4:15]
    given += refs[15:17]
    (ga_in, gs_in) = refs[17:19]
    refs = refs[19:]
    if reduces:
        parts_in, refs = refs[:4], refs[4:]
    input_out, enc_out = refs[:2]
    refs = refs[2:]
    outs = refs[:9] if reduces else refs[:2]
    refs = refs[9:] if reduces else refs[2:]
    (dkv, enc, dq_own, start, one, qkv, low, lse, after, two, gstate) = refs[:11]
    (ga, gs, g_query, g_attn, dqkv, dk, dv, row_seg, row_keep, col_seg, load_sem, dq_got, sw_send, sw_recv) = refs[11:25]
    grad_input, grad_enc, out_sem = refs[25:28]
    (pair, seg, pad, small_rows, small_cols, few_sem) = refs[28:34]
    refs = refs[34:]
    few = bring(given, (pair, seg, pad, small_rows, small_cols), few_sem)
    if reduces:
        parts, part_sem, refs = refs[:4], refs[4], refs[5:]
        fetched = [pltpu.make_async_copy(parts_in[k], parts[k], part_sem.at[k]) for k in range(4)]
        for copy in fetched:
            copy.start()
    refs_held = (dkv, enc, dq_own, start, one, qkv, low, lse, after, two, gstate)
    tok_count, width = dq_own.shape
    src_count = enc.shape[0]
    everyone = depth * 8
    me = Place(depth)
    scale = (tok_count * everyone) ** (-0.5)
    loads = []
    for src, dst in list(zip(held, refs_held)) + [(gs_in, gs), (ga_in, ga)]:
        copy = pltpu.make_async_copy(src, dst, load_sem.at[len(loads)])
        copy.start()
        loads.append(copy)
    if reduces:
        greet(me.others() + [me.across_x(), me.across_y(), me.across_both(), me.across_core()])
    else:
        greet([me.across_y()])
    halves = 2
    half = tok_count // halves
    swaps = []
    for k in range(halves):
        at = pl.ds(k * half, half)
        swaps.append(remote(dq_other.at[at], dq_got.at[at], sw_send.at[k], sw_recv.at[k], me.across_y()))
        swaps[-1].start()

    if reduces:
        (late, late_s, ex, ey, ex_got, ey_got, ez, ez_got, c_a, c_s, q_a, q_s, z_a, z_s, ez_send, ez_recv, send, recv) = refs
        (o_qkv, o_so, o_cq, o_kv, o_co, o_fi, o_fo, o_in, o_s) = outs

        def put_kv(total):
            o_kv[:, 0:BLOCK] = total[0:16] * scale
            o_kv[:, BLOCK : 2 * BLOCK] = total[16:32] * scale

        def put_mid(total):
            o_so[...] = total[0:16] * scale
            o_cq[...] = total[16:32] * scale

        def put_qkv(k, total):
            o_qkv[:, k * BLOCK : (k + 1) * BLOCK] = total * scale

        def put_s(total):
            o_s[...] = total * scale

        def rows(lo, hi, put):
            return (late, c_a, q_a, z_a, pl.ds(lo, hi - lo), put)

        chunks = [
            [rows(KV, EARLY, put_kv)],
            [rows(SO, KV, put_mid)],
            [rows(0, 16, partial(put_qkv, 0))],
            [rows(16, 32, partial(put_qkv, 1))],
            [rows(32, SO, partial(put_qkv, 2))],
            [(late_s, c_s, q_s, z_s, pl.ds(0, 16), put_s)],
        ]

        z, x, y = me.z, me.x, me.y
        for copy in fetched:
            copy.wait()
        for total, own, got in ((ex, parts[0], parts[1]), (ey, parts[2], parts[3])):

            @pl.loop(0, depth)
            def _(zz):
                for k in range(2):
                    total[k, zz] = (own[k, zz].astype(WIDE) + got[k, zz].astype(WIDE)).astype(LOW)

        plane = [
            remote(ex.at[1 - x], ex_got, ez_send.at[0], ez_recv.at[0], me.across_x()),
            remote(ey.at[1 - y], ey_got, ez_send.at[1], ez_recv.at[1], me.across_y()),
        ]
        for copy in plane:
            copy.start()
        along = []

        def onward():
            for copy in plane:
                copy.wait_recv()

            @pl.loop(0, depth)
            def _(zz):
                ez[zz, 0:RETURNED] = (ex[x, zz].astype(WIDE) + ex_got[zz].astype(WIDE)).astype(LOW)
                ez[zz, RETURNED:LATE] = (ey[y, zz].astype(WIDE) + ey_got[zz].astype(WIDE)).astype(LOW)

            for k in range(1, depth):
                to = lax.rem(z + k, depth)
                at = 1 + k
                along.append(remote(ez.at[to], ez_got.at[k - 1], ez_send.at[at], ez_recv.at[at], me.along(k)))
                along[-1].start()

        def settle():
            for copy in plane:
                copy.wait_send()
            for copy in along:
                copy.wait()
            total = ez[me.z].astype(WIDE)
            for k in range(depth - 1):
                total = total + ez_got[k].astype(WIDE)
            total = total * scale
            o_co[...] = total[0:16]
            for k in range(4):
                o_fi[:, k * BLOCK : (k + 1) * BLOCK] = total[16 + 16 * k : 32 + 16 * k]
            o_fo[...] = total[80:144]
            half = BLOCK // 2
            for k in range(2):
                o_in[16 * k : 16 * (k + 1)] = total[144:160, half * k : half * (k + 1)]

        begin, after_stage, end = reduction(me, chunks, send, recv)

        def keep(lo, value):
            late[:, :, :, :, lo : lo + 16] = value.astype(LOW).reshape(late.shape[:4] + (16, BLOCK))

        def keep_small(value):
            late_s[...] = value.astype(LOW).reshape(late_s.shape)
    else:
        def begin(k):
            return None

        def after_stage(k, stage):
            return None

        end = onward = settle = lambda: None
        o_late, o_small = outs

        def keep(lo, value):
            o_late[:, lo : lo + 16] = value.astype(LOW).reshape((-1, 16, BLOCK))

        def keep_small(value):
            o_small[...] = value

    chunk_kv, chunk_mid, chunk_q, chunk_k, chunk_v, chunk_s = range(6)
    for copy in few:
        copy.wait()
    onehot = token_numbers(seg, pad, pair, row_seg, row_keep, col_seg)
    cut = cutter(ga)
    for copy in loads[:2]:
        copy.wait()
    keep(KV, dot_tn(enc[...], dkv[:, 0:width]))
    keep(KV + 16, dot_tn(enc[...], dkv[:, width : 2 * width]))
    begin(chunk_kv)
    for copy in loads[2:]:
        copy.wait()
    table = cutter(gs)(0, gs.shape[-2]).astype(WIDE).T
    self_backward_start(dk, dv)
    gains = biases = 0.0
    for k in range(halves):
        at = pl.ds(k * half, half)
        swaps[k].wait()
        query = (dq_own[at, :] + dq_got[at, :].astype(WIDE)).astype(LOW)
        g_query[at, :] = query
        back, gain_1, bias_1 = norm_back(after[at, :], table[1:2], dot_nt(query, cut(CQ, KV)))
        gains, biases = gains + gain_1, biases + bias_1
        state = gstate[at, :] + back
        gstate[at, :] = state
        g_attn[at, :] = dot_nt(state.astype(LOW), cut(SO, CQ)).astype(LOW)
        if k == 0:
            after_stage(chunk_kv, 0)
        if k == halves - 1:
            keep(CQ, dot_tn(two[...], g_query[...]))
            keep(SO, dot_tn(low[...], gstate[...].astype(LOW)))
            begin(chunk_mid)
        blocks = (k * half // 128, (k + 1) * half // 128)
        self_backward(blocks, qkv, low, lse, g_attn, dqkv, dk, dv, row_seg, col_seg)
        if k == 0:
            onward()
    after_stage(chunk_mid, 0)
    self_backward_end(dqkv, dk, dv)
    for k, chunk in enumerate((chunk_q, chunk_k, chunk_v)):
        keep(QKV + 16 * k, dot_tn(one[...], dqkv[:, k * width : (k + 1) * width]))
        begin(chunk)
    after_stage(chunk_q, 0)
    after_stage(chunk_k, 0)
    after_stage(chunk_v, 0)
    after_stage(chunk_kv, 1)
    upstream = dot_nt(dqkv[:, 0:width], cut(QKV, QKV + 16))
    upstream = upstream + dot_nt(dqkv[:, width : 2 * width], cut(QKV + 16, QKV + 32))
    upstream = upstream + dot_nt(dqkv[:, 2 * width : 3 * width], cut(QKV + 32, SO))
    back, gain_0, bias_0 = norm_back(start[...], table[0:1], upstream)
    grad_start = gstate[...] + back
    grad_input[...] = grad_start.astype(LOW)
    stores = [pltpu.make_async_copy(grad_input, input_out, out_sem.at[4])]
    stores[0].start()
    coarse = grad_start.astype(LOW)
    fine = (grad_start - coarse.astype(WIDE)).astype(LOW)
    g_table = (dot_tn(onehot, coarse) + dot_tn(onehot, fine))[8:16]
    mid = small_rows[...]
    stacked = jnp.concatenate([gain_0, gains, mid[0:2], bias_0, biases, mid[2:4], g_table], axis=0)
    keep_small(transposed_rows(stacked) + small_cols[...])
    begin(chunk_s)
    after_stage(chunk_mid, 1)
    w_key, w_val = cut(KV, KV + 16), cut(KV + 16, EARLY)
    span = src_count // 4

    def source_grads(k):
        at = pl.ds(k * span, span)
        grads = dot_nt(dkv[at, 0:width], w_key) + dot_nt(dkv[at, width : 2 * width], w_val)
        grad_enc[at, :] = grads.astype(LOW)
        stores.append(pltpu.make_async_copy(grad_enc.at[at], enc_out.at[at], out_sem.at[k]))
        stores[-1].start()

    source_grads(0)
    after_stage(chunk_s, 0)
    after_stage(chunk_kv, 2)
    after_stage(chunk_q, 1)
    source_grads(1)
    after_stage(chunk_k, 1)
    source_grads(2)
    after_stage(chunk_v, 1)
    after_stage(chunk_s, 1)
    source_grads(3)
    settle()
    for chunk in (chunk_mid, chunk_q, chunk_k, chunk_v, chunk_s):
        after_stage(chunk, 2)
    end()
    for copy in stores:
        copy.wait()


def last_part(depth, reduces, pair, seg, pad, dq_own, dq_other, dkv, enc, kept, gstate, grads, whole):
    tok_count, width = dq_own.shape
    src_count = enc.shape[0]
    ga, gs = whole
    parts, small_rows, small_cols = grads
    everyone = depth * 8
    rows = BLOCK // everyone
    sharded = (depth, 2, 2, 2)
    held = (dkv, enc, dq_own, *kept, gstate)
    outs = [shape_of((tok_count, width), LOW), shape_of((src_count, width), LOW)]
    scratch = [pltpu.VMEM(a.shape, a.dtype) for a in held]
    scratch += [
        pltpu.VMEM(ga.shape, LOW),
        pltpu.VMEM(gs.shape, LOW),
        pltpu.VMEM((tok_count, width), LOW),
        pltpu.VMEM((tok_count, width), LOW),
        pltpu.VMEM((tok_count, 3 * width), LOW),
        pltpu.VMEM((tok_count, width), WIDE),
        pltpu.VMEM((tok_count, width), WIDE),
        pltpu.VMEM((1, tok_count), WIDE),
        pltpu.VMEM((1, tok_count), WIDE),
        pltpu.VMEM((tok_count, 128), WIDE),
        pltpu.SemaphoreType.DMA((14,)),
        pltpu.VMEM((tok_count, width), LOW),
        pltpu.SemaphoreType.DMA((2,)),
        pltpu.SemaphoreType.DMA((2,)),
        pltpu.VMEM((tok_count, width), LOW),
        pltpu.VMEM((src_count, width), LOW),
        pltpu.SemaphoreType.DMA((5,)),
        *[pltpu.VMEM(a.shape, a.dtype) for a in (pair, seg, pad, small_rows, small_cols)],
        pltpu.SemaphoreType.DMA((5,)),
    ]
    if reduces:
        shapes = [(EARLY, BLOCK), (16, 128)]
        outs += [
            shape_of((rows, 3 * BLOCK), WIDE),
            shape_of((rows, BLOCK), WIDE),
            shape_of((rows, BLOCK), WIDE),
            shape_of((rows, 2 * BLOCK), WIDE),
            shape_of((rows, BLOCK), WIDE),
            shape_of((rows, 4 * BLOCK), WIDE),
            shape_of((4 * rows, BLOCK), WIDE),
            shape_of((2 * rows, BLOCK // 2), WIDE),
            shape_of((rows, 128), WIDE),
        ]
        scratch += [pltpu.VMEM(a.shape, LOW) for a in parts] + [pltpu.SemaphoreType.DMA((4,))]
        scratch += [pltpu.VMEM(sharded + s, LOW) for s in shapes]
        scratch += [pltpu.VMEM(parts[0].shape, LOW), pltpu.VMEM(parts[2].shape, LOW)]
        scratch += [pltpu.VMEM(parts[0].shape[1:], LOW), pltpu.VMEM(parts[2].shape[1:], LOW)]
        scratch += [pltpu.VMEM((depth, LATE, BLOCK), LOW), pltpu.VMEM((depth - 1, LATE, BLOCK), LOW)]
        for lead in ((depth, 2, 2), (3, depth), (depth - 1,)):
            scratch += [pltpu.VMEM(lead + s, LOW) for s in shapes]
        scratch += [pltpu.SemaphoreType.DMA((depth + 2,))] * 2
        slots = 2 * (depth + 3)
        scratch += [pltpu.SemaphoreType.DMA((6, slots)), pltpu.SemaphoreType.DMA((6, slots))]
    else:
        outs += [shape_of((BLOCK // 16, EARLY, BLOCK), LOW), shape_of((BLOCK, 128), WIDE)]
    return pl.pallas_call(
        partial(last_kernel, depth, reduces),
        name="last_part",
        out_shape=outs,
        in_specs=[ANY] * (19 + len(parts)),
        out_specs=[ANY] * 2 + [VMEM] * (len(outs) - 2),
        scratch_shapes=scratch,
        compiler_params=pltpu.CompilerParams(
            collective_id=2, has_side_effects=True, vmem_limit_bytes=LIMIT
        ),
    )(pair, seg, pad, dq_other, *held, small_rows, small_cols, ga, gs, *parts)


def finish_kernel(count, *refs):
    ins, (small_in, loss_in) = refs[:count], refs[count : count + 2]
    outs, tiny_outs = refs[count + 2 : 2 * count + 2], refs[2 * count + 2 : 2 * count + 7]
    refs = refs[2 * count + 7 :]
    held, (small, loss) = refs[:count], refs[count : count + 2]
    tiny, sems = refs[count + 2 : count + 7], refs[count + 7]
    ahead = [pltpu.make_async_copy(small_in, small, sems.at[0, count]), pltpu.make_async_copy(loss_in, loss, sems.at[0, count + 1])]
    first = [pltpu.make_async_copy(ins[k], held[k], sems.at[0, k]) for k in range(count)]
    copies = [pltpu.make_async_copy(held[k], outs[k], sems.at[1, k]) for k in range(count)]
    for copy in ahead + first:
        copy.start()
    for copy in ahead:
        copy.wait()
    values = small[...]
    rows = values.shape[0]
    turned = jnp.concatenate([values, jnp.zeros((128 - rows, 128), WIDE)], axis=0).T
    for ref, lo, hi in zip(tiny[:4], (0, 4, 8, 16), (4, 8, 16, 18)):
        ref[...] = turned[lo:hi, 0:rows]
    tiny[4][...] = loss[...]
    for k in range(5):
        copies.append(pltpu.make_async_copy(tiny[k], tiny_outs[k], sems.at[1, count + k]))
        copies[-1].start()
    for k in range(count):
        first[k].wait()
        copies[k].start()
    for copy in copies:
        copy.wait()


def finish(results, small, loss):
    count = len(results)
    rows = small.shape[0]
    tiny = [shape_of(s, WIDE) for s in ((4, rows), (4, rows), (PAIRS, rows), (2, rows), (1, 1))]
    outs = [shape_of(a.shape, a.dtype) for a in results] + tiny
    held = list(results) + [small, loss] + tiny
    res = pl.pallas_call(
        partial(finish_kernel, count),
        name="finish",
        out_shape=outs,
        in_specs=[ANY] * (count + 2),
        out_specs=[ANY] * len(outs),
        scratch_shapes=[pltpu.VMEM(a.shape, a.dtype) for a in held]
        + [pltpu.SemaphoreType.DMA((2, count + 5))],
        compiler_params=pltpu.CompilerParams(vmem_limit_bytes=LIMIT),
    )(*results, small, loss)
    return res[:count], res[count:]


def late_blocks(cross_out, ffn_in, ffn_out, insert):
    groups = cross_out.shape[0] // 16
    return jnp.concatenate(
        [
            cross_out.reshape(groups, 16, BLOCK),
            ffn_in.reshape(groups, 16, 4, BLOCK).swapaxes(1, 2).reshape(groups, 64, BLOCK),
            ffn_out.reshape(groups, 64, BLOCK),
            insert.reshape(groups, 2, 16, BLOCK // 2).swapaxes(1, 2).reshape(groups, 16, BLOCK),
        ],
        axis=1,
    )


def gather_by_ops(qkv, self_out, cross_q, cross_kv, small):
    wide = jnp.concatenate([qkv, self_out, cross_q, cross_kv], axis=1)
    ga = lax.all_gather(wide, BOTH, axis=0, tiled=True).reshape(-1, 16, 7, BLOCK).swapaxes(1, 2)
    gs = lax.all_gather(small, BOTH, axis=0, tiled=True)
    return ga.reshape(-1, EARLY, BLOCK), gs.reshape(-1, 16, 128)


def partner(array, depth, axis):
    dx, dy = (1, 0) if axis == "x" else (0, 1)
    pairs = []
    for z in range(depth):
        for x in range(2):
            for c in range(2):
                for y in range(2):
                    here = ((z * 2 + x) * 2 + c) * 2 + y
                    there = ((z * 2 + (x ^ dx)) * 2 + c) * 2 + (y ^ dy)
                    pairs.append((here, there))
    return lax.ppermute(array, BOTH, pairs)


def reduce_by_ops(early, small, late, scale):
    groups = late.shape[0]
    gw_f = late[:, 80:144].reshape(groups * 64, BLOCK)
    gw_i = late[:, 144:160].reshape(groups, 16, 2, BLOCK // 2).swapaxes(1, 2).reshape(groups * 32, BLOCK // 2)
    late = late[:, 0:80].reshape(groups, 5, 16, BLOCK).swapaxes(0, 1).reshape(5, BLOCK, BLOCK)
    early = early.reshape(groups, 7, 16, BLOCK).swapaxes(0, 1).reshape(7, BLOCK, BLOCK)
    wide = jnp.concatenate([early, late]).swapaxes(0, 1).reshape(BLOCK, 12 * BLOCK)

    def sums(a):
        return lax.psum_scatter(a.astype(WIDE), BOTH, scatter_dimension=0, tiled=True) * scale

    own = sums(wide)
    edges = (0, 3, 4, 5, 7, 8, 12)
    pieces = [own[:, lo * BLOCK : hi * BLOCK] for lo, hi in zip(edges[:-1], edges[1:])]
    return pieces + [sums(gw_f), sums(gw_i), sums(small)]


def body(
    dec_input, enc_output, segment_ids, padding, pair_ids, src_lengths, delete_labels, insert_counts,
    masked_positions, masked_targets, norm_gain, norm_bias, pair_table, self_qkv, self_out, cross_q, cross_kv,
    cross_out, ffn_in, ffn_out, w_delete, w_insert, w_vocab,
):
    everyone = lax.axis_size(BOTH)
    depth = everyone // 8
    tok_count = dec_input.shape[0]
    aligned = self_qkv.shape[0] == 16
    late = (cross_out, ffn_in, ffn_out, w_insert)
    tiny = (norm_gain, norm_bias, pair_table, w_delete.T)
    raw = (self_qkv, self_out, cross_q, cross_kv)
    whole = gathered = None
    if not aligned:
        gathered = late_blocks(*[lax.all_gather(a, BOTH, axis=0, tiled=True) for a in late])
        small = jnp.concatenate([norm_gain, norm_bias, pair_table, w_delete.T], axis=0).T
        small = jnp.pad(small, ((0, 0), (0, 128 - small.shape[1])))
        whole = gather_by_ops(*raw, small)
    whole, line, firsts = first_part(
        depth, aligned, segment_ids, padding, pair_ids, dec_input, enc_output, tiny, raw, late, whole
    )
    start, one, qkv, low, lse, after, two, query, other_query, kv, other_seg = firsts
    parts = (*line, partner(line[0], depth, "x")) if aligned else (gathered,)
    o_own, o_other, lse_own, lse_other = cross_forward(src_lengths, segment_ids, other_seg, query, other_query, kv)
    mids = middle_part(
        depth, aligned, segment_ids, padding, delete_labels, insert_counts, masked_positions, masked_targets,
        w_vocab, after, (o_own, o_other, lse_own, lse_other), whole[1], parts,
    )
    count = 4 if aligned else 1
    parts, mids = mids[:count], mids[count:]
    block_out, gstate, g_own, g_other, st_own, st_other, small_rows, small_cols, grad_vocab, tokens, loss = mids
    sums = ()
    if aligned:
        sums = (parts[2], partner(parts[0], depth, "y"), parts[3], partner(parts[1], depth, "x"))
    dq_own, dq_other, dkv, block_out, grad_vocab = cross_backward(
        src_lengths, segment_ids, other_seg, query, other_query, g_own, g_other, st_own, st_other, kv,
        (block_out, grad_vocab),
    )
    res = last_part(
        depth, aligned, pair_ids, segment_ids, padding, dq_own, dq_other, dkv, enc_output,
        (start, one, qkv, low, lse, after, two), gstate, (sums, small_rows, small_cols), whole,
    )
    if aligned:
        sums = res[2:]
    else:
        scale = (tok_count * everyone) ** (-0.5)
        sums = reduce_by_ops(res[2], res[3], parts[0], scale)
    results, smalls = finish((res[1], res[0], *sums[:8], tokens), sums[8], loss)
    grad_enc, grad_input, qkv, so, cq, kv, co, fi, fo, insert, tokens = results
    gain, bias, table, delete, loss = smalls
    return (
        block_out, grad_input, grad_enc, gain, bias, table, qkv, so, cq, kv, co, fi, fo, delete.T, insert,
        grad_vocab, loss[0, 0], tokens,
    )


def solution(mesh):
    shared = P(BOTH, None)
    across = P(None, BOTH)
    return jax.shard_map(
        body,
        mesh=mesh,
        in_specs=(shared,) * 5 + (P("batch", None),) + (shared,) * 4 + (across,) * 3 + (shared,) * 10,
        out_specs=(shared,) * 3 + (across,) * 3 + (shared,) * 10 + (P(), shared),
        check_vma=False,
    )
```

```python
from functools import partial

import jax
import jax.numpy as jnp
from jax import lax
from jax.experimental import pallas as pl
from jax.experimental.pallas import tpu as pltpu
from jax.sharding import PartitionSpec as P

HD = 64
PAIRS = 8
SEGS = 8
BLOCK = 512
EPSILON = 1e-05
SCALE = 0.125
FILL = -1e30
GELU = 0.7978845608
CUBIC = 0.044715

MESH = pl.DeviceIdType.MESH
ANY = pl.BlockSpec(memory_space=pl.ANY)
VMEM = pl.BlockSpec(memory_space=pltpu.VMEM)
SMEM = pl.BlockSpec(memory_space=pltpu.SMEM)
BOTH = ("batch", "src")
LOW = jnp.bfloat16
WIDE = jnp.float32
LIMIT = 64 << 20


def shape_of(shape, kind):
    return jax.ShapeDtypeStruct(shape, kind)


def dot(left, right):
    return jnp.dot(left, right, preferred_element_type=WIDE)


def dot_tn(left, right):
    return lax.dot_general(left, right, (((0,), (0,)), ((), ())), preferred_element_type=WIDE)


def dot_nt(left, right):
    return lax.dot_general(left, right, (((1,), (1,)), ((), ())), preferred_element_type=WIDE)


def normalised(v):
    centred = v - jnp.mean(v, axis=-1, keepdims=True)
    r = lax.rsqrt(jnp.mean(centred * centred, axis=-1, keepdims=True) + EPSILON)
    return centred * r, r


def norm_back(v, gain, upstream):
    hat, r = normalised(v)
    scaled = upstream * gain
    first = jnp.mean(scaled, axis=-1, keepdims=True)
    second = jnp.mean(scaled * hat, axis=-1, keepdims=True)
    grad_gain = jnp.sum(upstream * hat, axis=0, keepdims=True)
    grad_bias = jnp.sum(upstream, axis=0, keepdims=True)
    return r * (scaled - first - hat * second), grad_gain, grad_bias


def lanes(shape):
    return lax.broadcasted_iota(jnp.int32, shape, len(shape) - 1)


def rows_of(shape):
    return lax.broadcasted_iota(jnp.int32, shape, len(shape) - 2)


def both_heads(x):
    low = lanes(x.shape) < HD
    zero = jnp.zeros_like(x)
    return jnp.concatenate([jnp.where(low, x, zero), jnp.where(low, zero, x)], axis=0)


def join_heads(x):
    half = x.shape[0] // 2
    return jnp.where(lanes((half, x.shape[1])) < HD, x[:half], x[half:])


def twice(x):
    return jnp.concatenate([x, x], axis=0)


def transposed_rows(rows):
    count, width = rows.shape
    return jnp.concatenate([rows, jnp.zeros((128 - count, width), WIDE)], axis=0).T


def bring(sources, places, sems):
    copies = [pltpu.make_async_copy(src, dst, sems.at[k]) for k, (src, dst) in enumerate(zip(sources, places))]
    for copy in copies:
        copy.start()
    return copies


def greet(peers):
    barrier = pltpu.get_barrier_semaphore()
    for peer in peers:
        pl.semaphore_signal(barrier, inc=1, device_id=peer, device_id_type=MESH)
    pl.semaphore_wait(barrier, len(peers))


def remote(src, dst, send, recv, peer):
    return pltpu.make_async_remote_copy(
        src_ref=src,
        dst_ref=dst,
        send_sem=send,
        recv_sem=recv,
        device_id=peer,
        device_id_type=MESH,
    )


class Place:
    def __init__(self, depth):
        b = lax.axis_index("batch")
        self.depth = depth
        self.y = lax.axis_index("src")
        self.c = lax.rem(b, 2)
        self.x = lax.rem(b // 2, 2)
        self.z = b // 4

    def at(self, z=None, x=None, c=None, y=None):
        z = self.z if z is None else z
        x = self.x if x is None else x
        c = self.c if c is None else c
        y = self.y if y is None else y
        return ((z * 2 + x) * 2 + c, y)

    def along(self, k):
        return self.at(z=lax.rem(self.z + k, self.depth))

    def others(self):
        return [self.along(k) for k in range(1, self.depth)]

    def across_x(self):
        return self.at(x=1 - self.x)

    def across_y(self):
        return self.at(y=1 - self.y)

    def across_both(self):
        return self.at(x=1 - self.x, y=1 - self.y)

    def across_core(self):
        return self.at(c=1 - self.c)


def gathering(me, chunks, send, recv):
    z, x, c, y = me.z, me.x, me.c, me.y
    started = [[None] * 3 for _ in chunks]
    used = [0] * len(chunks)
    every = slice(None)

    def launch(k, stage):
        copies = []

        def push(block, peer):
            slot = used[k]
            used[k] += 1
            copy = remote(block, block, send.at[k, slot], recv.at[k, slot], peer)
            copy.start()
            copies.append(copy)

        for view in chunks[k]:
            if stage == 0:
                for peer in me.others():
                    push(view(z, x, c, y), peer)
            elif stage == 1:
                for peer in (me.across_x(), me.across_y(), me.across_both()):
                    push(view(every, x, c, y), peer)
            else:
                push(view(every, every, c, every), me.across_core())
        started[k][stage] = copies

    def begin(k):
        launch(k, 0)

    def after(k, stage):
        for copy in started[k][stage]:
            copy.wait_recv()
        if stage < 2:
            launch(k, stage + 1)

    def end():
        for stages in started:
            for copies in stages:
                for copy in copies:
                    copy.wait_send()

    return begin, after, end


def self_window(block, tok_count):
    low = jnp.clip(block * 128 - 128, 0, tok_count - 384)
    return pl.multiple_of(low, 128)


def self_bar(row_seg, col_seg, block, low):
    keys = pl.ds(low, 384)
    queries = row_seg[0:1, pl.ds(pl.multiple_of(block * 128, 128), 128)]
    shape = (384, 128)
    own = (rows_of(shape) + low) == (lanes(shape) + block * 128)
    allowed = (col_seg[keys, 0:1] == queries) & ((col_seg[keys, 2:3] > 0.5) | own)
    return side_by_side(jnp.where(allowed, 0.0, FILL))


def self_forward(blocks, qkv, out, lse_ref, row_seg, col_seg):
    tok_count, width = out.shape
    first, last = blocks
    pairs = width // 128

    def one(block, carry):
        at = pl.ds(pl.multiple_of(block * 128, 128), 128)
        low = self_window(block, tok_count)
        keys = pl.ds(low, 384)
        barred = self_bar(row_seg, col_seg, block, low)
        every = range(pairs)
        q = [both_heads(qkv[at, p * 128 : (p + 1) * 128] * SCALE) for p in every]
        scores = [dot_nt(qkv[keys, width + p * 128 : width + (p + 1) * 128], q[p]) + barred for p in every]
        tops = [jnp.max(scores[p], axis=0, keepdims=True) for p in every]
        exps = [jnp.exp(scores[p] - tops[p]) for p in every]
        totals = [jnp.sum(exps[p], axis=0, keepdims=True) for p in every]
        values = [qkv[keys, 2 * width + p * 128 : 2 * width + (p + 1) * 128] for p in every]
        mixed = [dot_tn(values[p], exps[p].astype(LOW)) * (1.0 / totals[p]) for p in every]
        stats = []
        for p in every:
            out[at, p * 128 : (p + 1) * 128] = heads_apart(mixed[p]).astype(LOW)
            lse = tops[p] + jnp.log(totals[p])
            stats += [lse[:, :128], lse[:, 128:]]
        lse_ref[:, at] = jnp.concatenate(stats, axis=0)
        return carry

    lax.fori_loop(first, last, one, 0)


def small_matrix(gain, bias, pair_rows, delete):
    def spot(count, first):
        shape = (count, 128)
        return (rows_of(shape) + first == lanes(shape)).astype(LOW)

    total = dot_tn(gain, spot(4, 0)) + dot_tn(bias, spot(4, 4)) + dot_tn(pair_rows, spot(PAIRS, 8))
    return (total + dot_tn(delete, spot(2, 8 + PAIRS))).astype(LOW)


def token_numbers(seg, pad, pair, row_seg, row_keep, col_seg):
    tok_count = seg.shape[1]
    segments = seg[...].astype(WIDE)
    row_seg[...] = segments
    row_keep[...] = 1.0 - pad[...].astype(WIDE)
    pair_row = jnp.zeros((1, tok_count), WIDE)
    for k in range(SEGS):
        pair_row = jnp.where(segments == k, pair[0:1, k : k + 1].astype(WIDE), pair_row)
    columns = [segments, pair_row, row_keep[...], jnp.zeros((5, tok_count), WIDE)]
    columns = transposed_rows(jnp.concatenate(columns, axis=0))
    col_seg[...] = columns
    return (lanes((tok_count, 128)) == (columns[:, 1:2].astype(jnp.int32) + 8)).astype(LOW)


def cutter(ref):
    every = (slice(None),) * (len(ref.shape) - 2)

    def cut(lo, hi):
        value = ref[every + (slice(lo, hi),)]
        return value.reshape((-1, value.shape[-1]))

    return cut


QKV, SO, CQ, KV, EARLY = 0, 48, 64, 80, 112
LATE, PERMUTED, RETURNED = 160, 96, 128


def first_kernel(depth, gathers, *refs):
    (seg_in, pad_in, pair_in, dec_in, enc_in) = refs[:5]
    refs = refs[5:]
    if gathers:
        tiny_in, refs = refs[:4], refs[4:]
        (raw_qkv, raw_so, raw_cq, raw_kv, raw_co, raw_fi, raw_fo, raw_in) = refs[:8]
        (ga_out, gs_out, gz1, gz2) = refs[8:12]
        refs = refs[12:]
    else:
        ga_in, gs_in = refs[:2]
        refs = refs[2:]
    results, other_out, seg_out = refs[:9], refs[9], refs[10]
    held = refs[11:20]
    (start_ref, one_ref, qkv, low, lse, after_ref, two_ref, query, kv) = held
    (enc, ga, gs, row_seg, row_keep, col_seg, own_sem, out_sem, send, recv, sw_send, sw_recv, stage1, stage2) = refs[20:34]
    (seg, pad, pair, dec, few_sem) = refs[34:39]
    few = bring((seg_in, pad_in, pair_in, dec_in), (seg, pad, pair, dec), few_sem)
    if gathers:
        (gain, bias, pair_rows, delete, tiny_sem) = refs[39:]
        tiny = bring(tiny_in, (gain, bias, pair_rows, delete), tiny_sem)
    tok_count, width = dec.shape
    src_count = enc.shape[0]
    me = Place(depth)
    z, x, c, y = me.z, me.x, me.c, me.y
    owns = []

    def own(src, dst):
        copy = pltpu.make_async_copy(src, dst, own_sem.at[len(owns)])
        copy.start()
        owns.append(copy)

    if gathers:
        for raw, count, first in ((raw_qkv, 3, QKV), (raw_so, 1, SO), (raw_cq, 1, CQ), (raw_kv, 2, KV)):
            for k in range(count):
                own(raw.at[:, pl.ds(k * BLOCK, BLOCK)], ga.at[z, x, c, y, pl.ds(first + 16 * k, 16)])
        soon = len(owns)
        own1, own2 = stage1, stage2
        split_fo = PERMUTED - 80
        own(raw_co, own1.at[pl.ds(0, 16)])
        for k in range(4):
            own(raw_fi.at[:, pl.ds(k * BLOCK, BLOCK)], own1.at[pl.ds(16 + 16 * k, 16)])
        own(raw_fo.at[pl.ds(0, split_fo)], own1.at[pl.ds(80, split_fo)])
        own(raw_fo.at[pl.ds(split_fo, 64 - split_fo)], own2.at[pl.ds(0, 64 - split_fo)])
        for k in range(2):
            half = BLOCK // 2
            place = own2.at[pl.ds(64 - split_fo, 16), pl.ds(half * k, half)]
            own(raw_in.at[pl.ds(16 * k, 16)], place)
        for copy in tiny:
            copy.wait()
        gs[z, x, c, y] = small_matrix(gain[...], bias[...], pair_rows[...], delete[...])
        greet(me.others() + [me.across_x(), me.across_y(), me.across_both(), me.across_core()])
        for copy in owns[:soon]:
            copy.wait()

        def rows(lo, hi):
            return lambda *at: ga.at[at + (pl.ds(lo, hi - lo),)]

        chunks = [[lambda *at: gs.at[at]]]
        chunks += [[rows(lo, hi)] for lo, hi in ((0, 16), (16, 32), (32, SO), (SO, KV), (KV, EARLY))]
        begin, after_stage, end = gathering(me, chunks, send, recv)
    else:
        own(ga_in, ga)
        own(gs_in, gs)
        greet([me.across_y()])
        for copy in owns:
            copy.wait()

        def begin(k):
            return None

        def after_stage(k, stage):
            return None

        def end():
            return None

    outs = []

    def out(k):
        copy = pltpu.make_async_copy(held[k], results[k], out_sem.at[len(outs)])
        copy.start()
        outs.append(copy)

    c_s, c_q, c_k, c_v, c_mid, c_kv = range(6)
    begin(c_s)
    begin(c_q)
    line, crossing = [], []
    if gathers:
        for copy in owns[soon:]:
            copy.wait()
        kept = len(owns)
        for k, (ref, spot) in enumerate(((own1, gz1.at[y, z]), (own2, gz2.at[y, z]))):
            crossing.append(remote(ref, spot, sw_send.at[3 + k], sw_recv.at[3 + k], me.across_y()))
            crossing[-1].start()
            own(ref, spot)
    meet = remote(seg_in, seg_out, sw_send.at[0], sw_recv.at[0], me.across_y())
    meet.start()
    fetch = pltpu.make_async_copy(enc_in, enc, out_sem.at[11])
    fetch.start()
    for copy in few:
        copy.wait()
    onehot = token_numbers(seg, pad, pair, row_seg, row_keep, col_seg)
    cut = cutter(ga)
    after_stage(c_s, 0)
    after_stage(c_q, 0)
    begin(c_k)
    after_stage(c_k, 0)
    begin(c_v)
    after_stage(c_s, 1)
    after_stage(c_q, 1)
    after_stage(c_v, 0)
    begin(c_mid)
    begin(c_kv)
    for copy in crossing:
        copy.wait()
    if gathers:
        for copy in owns[kept:]:
            copy.wait()
        far, near = me.along(depth // 2), me.at(z=z + 1 - 2 * lax.rem(z, 2))
        z_far = lax.rem(z + depth // 2, depth)

        def along(ref, peer):
            at = 5 + len(line)
            line.append(remote(ref, ref, sw_send.at[at], sw_recv.at[at], peer))
            line[-1].start()

        for ref in (gz1.at[:, z], gz2.at[:, z]):
            along(ref, far)
            along(ref, near)
    after_stage(c_s, 2)
    table = cutter(gs)(0, gs.shape[-2]).astype(WIDE).T
    start = dec[...].astype(WIDE) + dot(onehot, table.astype(LOW))
    start_ref[...] = start
    out(0)
    one = (normalised(start)[0] * table[0:1] + table[4:5]).astype(LOW)
    one_ref[...] = one
    out(1)
    after_stage(c_k, 1)
    after_stage(c_mid, 0)
    after_stage(c_q, 2)
    qkv[:, 0:BLOCK] = dot(one, cut(QKV, QKV + 16)).astype(LOW)
    after_stage(c_v, 1)
    after_stage(c_k, 2)
    qkv[:, BLOCK : 2 * BLOCK] = dot(one, cut(QKV + 16, QKV + 32)).astype(LOW)
    after_stage(c_v, 2)
    after_stage(c_kv, 0)
    qkv[:, 2 * BLOCK : 3 * BLOCK] = dot(one, cut(QKV + 32, SO)).astype(LOW)
    out(2)
    halves = 2
    span = tok_count // halves
    swaps = []
    for k in range(halves):
        at = pl.ds(k * span, span)
        self_forward((k * span // 128, (k + 1) * span // 128), qkv, low, lse, row_seg, col_seg)
        if k == 0:
            after_stage(c_mid, 1)
            after_stage(c_mid, 2)
        after = start_ref[at, :] + dot(low[at, :], cut(SO, CQ))
        after_ref[at, :] = after
        two = (normalised(after)[0] * table[1:2] + table[5:6]).astype(LOW)
        two_ref[at, :] = two
        query[at, :] = dot(two, cut(CQ, KV)).astype(LOW)
        swap = remote(query.at[at], other_out.at[at], sw_send.at[1 + k], sw_recv.at[1 + k], me.across_y())
        swap.start()
        swaps.append(swap)
        if k == 0 and gathers:
            line[0].wait_recv()
            along(gz1.at[:, z_far], near)
            line[2].wait_recv()
            along(gz2.at[:, z_far], near)
    for k in range(3, 8):
        out(k)
    after_stage(c_kv, 1)
    after_stage(c_kv, 2)
    if gathers:
        own(ga, ga_out)
        own(gs, gs_out)
    fetch.wait()
    w_key, w_val = cut(KV, KV + 16), cut(KV + 16, EARLY)
    parts = 4
    for k in range(parts):
        span = src_count // parts
        at = pl.ds(k * span, span)
        kv[at, 0:width] = dot(enc[at, :], w_key).astype(LOW)
        kv[at, width : 2 * width] = dot(enc[at, :], w_val).astype(LOW)
    out(8)
    for copy in swaps + [meet]:
        copy.wait()
    for k, copy in enumerate(line):
        if k not in (0, 2):
            copy.wait_recv()
        copy.wait_send()
    end()
    for copy in outs + (owns[-2:] if gathers else []):
        copy.wait()


def first_part(depth, gathers, seg, pad, pair, dec, enc, tiny, raw, late, whole):
    tok_count, width = dec.shape
    src_count = enc.shape[0]
    lead = (depth, 2, 2, 2) if gathers else (BLOCK // 16,)
    results = [
        shape_of((tok_count, width), WIDE),
        shape_of((tok_count, width), LOW),
        shape_of((tok_count, 3 * width), LOW),
        shape_of((tok_count, width), LOW),
        shape_of((width // HD, tok_count), WIDE),
        shape_of((tok_count, width), WIDE),
        shape_of((tok_count, width), LOW),
        shape_of((tok_count, width), LOW),
        shape_of((src_count, 2 * width), LOW),
    ]
    outs = results + [shape_of((tok_count, width), LOW), shape_of((1, tok_count), jnp.int32)]
    if gathers:
        outs = [
            shape_of(lead + (EARLY, BLOCK), LOW),
            shape_of(lead + (16, 128), LOW),
            shape_of((2, depth, PERMUTED, BLOCK), LOW),
            shape_of((2, depth, LATE - PERMUTED, BLOCK), LOW),
        ] + outs
    extra = (*tiny, *raw, *late) if gathers else whole
    res = pl.pallas_call(
        partial(first_kernel, depth, gathers),
        name="first_part",
        out_shape=outs,
        in_specs=[ANY] * (5 + len(extra)),
        out_specs=[ANY] * len(outs),
        scratch_shapes=[pltpu.VMEM(a.shape, a.dtype) for a in results]
        + [
            pltpu.VMEM(enc.shape, LOW),
            pltpu.VMEM(lead + (EARLY, BLOCK), LOW),
            pltpu.VMEM(lead + (16, 128), LOW),
            pltpu.VMEM((1, tok_count), WIDE),
            pltpu.VMEM((1, tok_count), WIDE),
            pltpu.VMEM((tok_count, 128), WIDE),
            pltpu.SemaphoreType.DMA((20,)),
            pltpu.SemaphoreType.DMA((12,)),
            pltpu.SemaphoreType.DMA((6, depth + 3)),
            pltpu.SemaphoreType.DMA((6, depth + 3)),
            pltpu.SemaphoreType.DMA((2 * depth + 3,)),
            pltpu.SemaphoreType.DMA((2 * depth + 3,)),
            pltpu.VMEM((PERMUTED, BLOCK), LOW),
            pltpu.VMEM((LATE - PERMUTED, BLOCK), LOW),
            *[pltpu.VMEM(a.shape, a.dtype) for a in (seg, pad, pair, dec)],
            pltpu.SemaphoreType.DMA((4,)),
        ]
        + ([pltpu.VMEM(a.shape, a.dtype) for a in tiny] + [pltpu.SemaphoreType.DMA((4,))] if gathers else []),
        compiler_params=pltpu.CompilerParams(
            collective_id=0, has_side_effects=True, vmem_limit_bytes=LIMIT
        ),
    )(seg, pad, pair, dec, enc, *extra)
    if gathers:
        whole, line, res = res[:2], res[2:4], res[4:]
    else:
        line = None
    start, one, qkv, low, lse, after, two, query, kv, other_query, other_seg = res
    return whole, line, (start, one, qkv, low, lse, after, two, query, other_query, kv, other_seg)


def segment_ends(lengths, ends):
    total = jnp.int32(0)
    ends[0] = total
    for s in range(2 * SEGS):
        total = total + lengths[0, s]
        ends[s + 1] = total


def block_ranges(seg_s, first_seg, ends, off, src_count, block):
    at = pl.multiple_of(block * 128, 128)
    low = jnp.clip(ends[first_seg + seg_s[0, at]] - off, 0, src_count)
    high = jnp.clip(ends[first_seg + seg_s[0, at + 127] + 1] - off, 0, src_count)
    first = low // TILE
    return first, jnp.where(high > low, (high + TILE - 1) // TILE, first)


def key_bounds(segs, firsts, ends, off):
    rows = []
    for seg, first_seg in zip(segs, firsts):
        low = jnp.zeros(seg.shape, jnp.int32)
        high = jnp.zeros(seg.shape, jnp.int32)
        for s in range(SEGS):
            low = jnp.where(seg == s, ends[first_seg + s] - off, low)
            high = jnp.where(seg == s, ends[first_seg + s + 1] - off, high)
        rows += [low, high]
    return jnp.concatenate(rows + [jnp.zeros((4, rows[0].shape[1]), jnp.int32)], axis=0)


TILE = 256


def side_by_side(x):
    return jnp.concatenate([x, x], axis=1)


def side_by_side_rows(rows, k, at):
    return jnp.concatenate([rows[k : k + 1, at], rows[k + 1 : k + 2, at]], axis=1)


def heads_apart(x):
    n = x.shape[1] // 2
    return jnp.concatenate([x[:HD, :n], x[HD:, n:]], axis=0).T


def cross_forward_kernel(
    lengths, seg_so, seg_sp, seg_vo, seg_vp, q_own, q_other, kv, o_own, o_other, lse_own, lse_other,
    ends, bounds, qs, top_ref, total_ref, acc_ref,
):
    tok_count, width = q_own.shape
    src_count = kv.shape[0]
    pairs = width // 128
    pos = lax.axis_index("src")
    off = pos * src_count
    firsts = (pos * SEGS, (1 - pos) * SEGS)
    segment_ends(lengths, ends)
    bounds[...] = key_bounds((seg_vo[...], seg_vp[...]), firsts, ends, off)
    for side, (q, o, lse_ref) in enumerate(((q_own, o_own, lse_own), (q_other, o_other, lse_other))):

        @pl.loop(0, tok_count // 128)
        def _(block):
            at = pl.ds(pl.multiple_of(block * 128, 128), 128)
            first, last = block_ranges((seg_so, seg_sp)[side], firsts[side], ends, off, src_count, block)
            low, high = bounds[2 * side : 2 * side + 1, at], bounds[2 * side + 1 : 2 * side + 2, at]
            for p in range(pairs):
                qs[p] = both_heads(q[at, p * 128 : (p + 1) * 128] * SCALE)
            top_ref[...] = jnp.full_like(top_ref, FILL)
            total_ref[...] = jnp.zeros_like(total_ref)
            acc_ref[...] = jnp.zeros_like(acc_ref)

            def one(t, carry):
                base = pl.multiple_of(t * TILE, TILE)
                keys = pl.ds(base, TILE)
                index = rows_of((TILE, 128)) + base
                barred = side_by_side(jnp.where((index >= low) & (index < high), 0.0, FILL))
                every = range(pairs)
                scores = [dot_nt(kv[keys, pl.ds(p * 128, 128)], qs[p]) for p in every]
                scores = [scores[p] + barred for p in every]
                olds = [top_ref[p] for p in every]
                tops = [jnp.maximum(olds[p], jnp.max(scores[p], axis=0, keepdims=True)) for p in every]
                exps = [jnp.exp(scores[p] - jnp.maximum(tops[p], 0.1 * FILL)) for p in every]
                fades = [jnp.exp(olds[p] - tops[p]) for p in every]
                sums = [total_ref[p] * fades[p] + jnp.sum(exps[p], axis=0, keepdims=True) for p in every]
                mixed = [dot_tn(kv[keys, pl.ds(width + p * 128, 128)], exps[p].astype(LOW)) for p in every]
                mixed = [acc_ref[p] * fades[p] + mixed[p] for p in every]
                for p in every:
                    top_ref[p] = tops[p]
                    total_ref[p] = sums[p]
                    acc_ref[p] = mixed[p]
                return carry

            lax.fori_loop(first, last, one, 0)
            stats = []
            for p in range(pairs):
                total = total_ref[p]
                safe = jnp.where(total > 0.0, total, 1.0)
                o[at, p * 128 : (p + 1) * 128] = heads_apart(acc_ref[p] * (1.0 / safe)).astype(LOW)
                lse = jnp.where(total > 0.0, top_ref[p] + jnp.log(safe), FILL)
                stats += [lse[:, :128], lse[:, 128:]]
            lse_ref[:, at] = jnp.concatenate(stats, axis=0)


def cross_forward(lengths, seg_own, seg_other, q_own, q_other, kv):
    tok_count, width = q_own.shape
    heads = width // HD
    pairs = width // 128
    out = shape_of((tok_count, width), LOW)
    lse = shape_of((heads, tok_count), WIDE)
    return pl.pallas_call(
        cross_forward_kernel,
        name="cross_forward",
        out_shape=[out, out, lse, lse],
        in_specs=[SMEM] * 3 + [VMEM] * 5,
        out_specs=[VMEM] * 4,
        scratch_shapes=[
            pltpu.SMEM((32,), jnp.int32),
            pltpu.VMEM((8, tok_count), jnp.int32),
            pltpu.VMEM((pairs, 256, 128), LOW),
            pltpu.VMEM((pairs, 1, 256), WIDE),
            pltpu.VMEM((pairs, 1, 256), WIDE),
            pltpu.VMEM((pairs, 128, 256), WIDE),
        ],
        compiler_params=pltpu.CompilerParams(vmem_limit_bytes=LIMIT),
        cost_estimate=pl.CostEstimate(flops=1 << 33, bytes_accessed=8 << 20, transcendentals=0),
    )(lengths, seg_own, seg_other, seg_own, seg_other, q_own, q_other, kv)


def cross_backward_kernel(
    lengths, seg_so, seg_sp, seg_vo, seg_vp, q_in, q_in_2, g_in, g_in_2, st_in, st_in_2, kv_in, pass_0, pass_1,
    dq_out, dq_out_2, dkv_out, given_0, given_1, ends, bounds, acc, qs, gs, dq_acc, kv, dkv, held_0, held_1,
    q_own, q_other, g_own, g_other, st_own, st_other, dq_own, dq_other, sems, io_sems, in_sems,
):
    fetch = [pltpu.make_async_copy(kv_in, kv, io_sems.at[0])]
    given = (q_in, q_in_2, g_in, g_in_2, st_in, st_in_2)
    for k, (src, dst) in enumerate(zip(given, (q_own, q_other, g_own, g_other, st_own, st_other))):
        fetch.append(pltpu.make_async_copy(src, dst, in_sems.at[k]))
    for copy in fetch:
        copy.start()
    ways = ((pass_0, held_0, given_0), (pass_1, held_1, given_1))
    taking = [pltpu.make_async_copy(way[0], way[1], sems.at[0, k]) for k, way in enumerate(ways)]
    giving = [pltpu.make_async_copy(way[1], way[2], sems.at[1, k]) for k, way in enumerate(ways)]
    for copy in taking:
        copy.start()
    tok_count, width = q_own.shape
    src_count = kv.shape[0]
    pairs = width // 128
    pos = lax.axis_index("src")
    off = pos * src_count
    firsts = (pos * SEGS, (1 - pos) * SEGS)
    segment_ends(lengths, ends)
    bounds[...] = key_bounds((seg_vo[...], seg_vp[...]), firsts, ends, off)
    acc[...] = jnp.zeros_like(acc)
    for copy in fetch:
        copy.wait()
    stores = []
    sides = ((q_own, g_own, st_own, dq_own), (q_other, g_other, st_other, dq_other))
    for side, (q, g, st, dq) in enumerate(sides):

        @pl.loop(0, tok_count // 128)
        def _(block):
            at = pl.ds(pl.multiple_of(block * 128, 128), 128)
            first, last = block_ranges((seg_so, seg_sp)[side], firsts[side], ends, off, src_count, block)
            low, high = bounds[2 * side : 2 * side + 1, at], bounds[2 * side + 1 : 2 * side + 2, at]
            for p in range(pairs):
                cols = slice(p * 128, (p + 1) * 128)
                qs[p] = both_heads(q[at, cols] * SCALE)
                gs[p] = both_heads(g[at, cols])
            dq_acc[...] = jnp.zeros_like(dq_acc)
            lses = [side_by_side_rows(st, 2 * p, at) for p in range(pairs)]
            deltas = [side_by_side_rows(st, 8 + 2 * p, at) for p in range(pairs)]

            def one(t, carry):
                base = pl.multiple_of(t * TILE, TILE)
                keys = pl.ds(base, TILE)
                index = rows_of((TILE, 128)) + base
                barred = side_by_side(jnp.where((index >= low) & (index < high), 0.0, FILL))
                every = range(pairs)
                cols = [pl.ds(p * 128, 128) for p in every]
                vals = [pl.ds(width + p * 128, 128) for p in every]
                scores = [dot_nt(kv[keys, cols[p]], qs[p]) for p in every]
                slopes = [dot_nt(kv[keys, vals[p]], gs[p]) for p in every]
                probs = [jnp.exp(scores[p] - lses[p] + barred) for p in every]
                gscores = [(probs[p] * (slopes[p] - deltas[p])).astype(LOW) for p in every]
                grad_k = [acc[keys, cols[p]] + dot(gscores[p], qs[p]) for p in every]
                grad_v = [acc[keys, vals[p]] + dot(probs[p].astype(LOW), gs[p]) for p in every]
                grad_q = [dq_acc[p] + dot_tn(kv[keys, cols[p]], gscores[p]) for p in every]
                for p in every:
                    acc[keys, cols[p]] = grad_k[p]
                    acc[keys, vals[p]] = grad_v[p]
                    dq_acc[p] = grad_q[p]
                return carry

            lax.fori_loop(first, last, one, 0)
            for p in range(pairs):
                dq[at, p * 128 : (p + 1) * 128] = (heads_apart(dq_acc[p]) * SCALE).astype(dq.dtype)

        stores.append(pltpu.make_async_copy(dq, (dq_out, dq_out_2)[side], io_sems.at[5 + side]))
        stores[-1].start()

    for first, second in zip(taking, giving):
        first.wait()
        second.start()

    parts = 4
    span = src_count // parts
    for k in range(parts):
        at = pl.ds(k * span, span)
        dkv[at, :] = acc[at, :].astype(LOW)
        stores.append(pltpu.make_async_copy(dkv.at[at], dkv_out.at[at], io_sems.at[1 + k]))
        stores[-1].start()
    for copy in stores:
        copy.wait()
    for copy in giving:
        copy.wait()


def cross_backward(lengths, seg_own, seg_other, q_own, q_other, g_own, g_other, st_own, st_other, kv, passed):
    tok_count, width = q_own.shape
    src_count = kv.shape[0]
    pairs = width // 128
    return pl.pallas_call(
        cross_backward_kernel,
        name="cross_backward",
        out_shape=[
            shape_of((tok_count, width), WIDE),
            shape_of((tok_count, width), LOW),
            shape_of((src_count, 2 * width), LOW),
        ]
        + [shape_of(a.shape, a.dtype) for a in passed],
        in_specs=[SMEM] * 3 + [VMEM] * 2 + [ANY] * 9,
        out_specs=[ANY] * 5,
        scratch_shapes=[
            pltpu.SMEM((32,), jnp.int32),
            pltpu.VMEM((8, tok_count), jnp.int32),
            pltpu.VMEM((src_count, 2 * width), WIDE),
            pltpu.VMEM((pairs, 256, 128), LOW),
            pltpu.VMEM((pairs, 256, 128), LOW),
            pltpu.VMEM((pairs, 128, 256), WIDE),
            pltpu.VMEM(kv.shape, LOW),
            pltpu.VMEM(kv.shape, LOW),
        ]
        + [pltpu.VMEM(a.shape, a.dtype) for a in (*passed, q_own, q_other, g_own, g_other, st_own, st_other)]
        + [pltpu.VMEM((tok_count, width), WIDE), pltpu.VMEM((tok_count, width), LOW)]
        + [pltpu.SemaphoreType.DMA((2, 2)), pltpu.SemaphoreType.DMA((7,)), pltpu.SemaphoreType.DMA((6,))],
        compiler_params=pltpu.CompilerParams(vmem_limit_bytes=LIMIT),
        cost_estimate=pl.CostEstimate(flops=1 << 34, bytes_accessed=16 << 20, transcendentals=0),
    )(lengths, seg_own, seg_other, seg_own, seg_other, q_own, q_other, g_own, g_other, st_own, st_other, kv, *passed)


def merge_all(parts, count):
    top = parts[0]
    for part in parts[1:]:
        top = jnp.maximum(top, part)
    total = sum(jnp.exp(part - top) for part in parts)
    return jnp.where(rows_of(top.shape) < count, top + jnp.log(total), sum(parts))


def folded(row):
    return jnp.concatenate([row[:, k : k + 128] for k in range(0, row.shape[1], 128)], axis=0)


def unfolded(rows):
    return jnp.concatenate([rows[k : k + 1] for k in range(rows.shape[0])], axis=1)


def middle_kernel(depth, split, *refs):
    (
        seg_in, pad_in, labels_in, counts_in, positions_in, targets_in, lse_in, lse_other, vocab_in, after_in, o_in,
        o_other, gs,
    ) = refs[:13]
    parts = refs[13 : 13 + (3 if split else 1)]
    refs = refs[13 + len(parts) :]
    count = 4 if split else 1
    sums = refs[:count]
    refs = refs[count:]
    (
        block_out, state_out, g_own, g_other, st_own, st_other, small_rows, small_cols, grad_vocab, token_out, loss_out,
    ) = refs[:11]
    numbers = refs[11:18]
    (seg, pad, labels, counts, positions, targets, lse_own) = numbers
    few_sem = refs[18]
    refs = refs[:11] + refs[19:]
    given = (seg_in, pad_in, labels_in, counts_in, positions_in, targets_in, lse_in)
    few = bring(given, numbers, few_sem)
    (
        w_vocab, after_self, o_own, block_ref, state_ref, g_ref, vocab_ref, out_sem,
        wm, eb, eb_got, w_s, got_o, got_lse, cross_o, cross_low, ac, bs, n3, act, slope, gpre, head,
        lt, gt, gt_got, ew, hw, pb, pb_got, rb, got_rq, got_rz, st_c, st_q, st_z, gh, g_ffn, load_sem, send, recv,
    ) = refs[11 : 11 + 41]
    sum_refs = refs[11 + 41 :]
    tok_count, width = after_self.shape
    hidden = act.shape[1]
    masked = positions.shape[1]
    vocab_local = w_vocab.shape[1]
    everyone = depth * 8
    me = Place(depth)
    z, x, c, y = me.z, me.x, me.c, me.y
    greet(me.others() + [me.across_x(), me.across_y(), me.across_both(), me.across_core()])
    used = [0]

    def push(src, dst, peer):
        k = used[0]
        used[0] += 1
        copy = remote(src, dst, send.at[k], recv.at[k], peer)
        copy.start()
        return copy

    pending = []

    def arrive(copies):
        for copy in copies:
            copy.wait_recv()
        pending.extend(copies)

    loads = []

    def load(src, dst):
        copy = pltpu.make_async_copy(src, dst, load_sem.at[len(loads)])
        copy.start()
        loads.append(copy)

    halves = 2
    span = tok_count // halves
    ranges = [pl.ds(k * span, span) for k in range(halves)]

    def swap_outputs():
        copies = [push(lse_other, got_lse, me.across_y())]
        return copies + [push(o_other.at[at], got_o.at[at], me.across_y()) for at in ranges]

    load(gs, w_s)
    load(after_in, after_self)
    load(o_in, o_own)
    load(vocab_in, w_vocab.at[c])
    shared = [push(vocab_in, w_vocab.at[c], me.across_core())]
    if split:
        rest = pl.ds(PERMUTED, LATE - PERMUTED)
        soon = pl.ds(0, PERMUTED)
        late_part = [push(parts[1].at[py], wm.at[:, x, c, py, rest], me.across_x()) for py in range(2)]
        swap = swap_outputs()
        for py in range(2):
            load(parts[0].at[py], wm.at[:, x, c, py, soon])
            load(parts[1].at[py], wm.at[:, x, c, py, rest])
            load(parts[2].at[py], wm.at[:, 1 - x, c, py, soon])
            shared.append(push(parts[0].at[py], wm.at[:, x, c, py, soon], me.across_core()))
            shared.append(push(parts[1].at[py], wm.at[:, x, c, py, rest], me.across_core()))
            shared.append(push(parts[2].at[py], wm.at[:, 1 - x, c, py, soon], me.across_core()))
    else:
        swap = swap_outputs()
        load(parts[0], wm)

    def cut(lo, hi):
        value = wm[:, :, :, :, lo:hi] if split else wm[:, lo:hi]
        return value.reshape((-1, BLOCK))

    def put(lo, value, first=0, last=None, cols=slice(0, BLOCK)):
        groups, rows, wide = value.shape
        last = depth if last is None else last
        if split:
            eb[first:last, :, :, :, lo : lo + rows, cols] = value.reshape((last - first, 2, 2, 2, rows, wide))
        else:
            step = eb.shape[0] // depth
            eb[first * step : last * step, lo : lo + rows, cols] = value

    for copy in few:
        copy.wait()
    segments = seg[...].astype(WIDE)
    keep = 1.0 - pad[...].astype(WIDE)
    lane_row = lanes((1, tok_count))
    inside = lane_row < tok_count - 1

    def following(row):
        return pltpu.roll(jnp.concatenate([row, jnp.zeros((7, tok_count), WIDE)], axis=0), tok_count - 1, 1)[0:1]

    follows = inside & (following(segments) == segments) & (keep > 0.5) & (following(keep) > 0.5)
    valid = jnp.where(follows, 1.0, 0.0)
    rows = [keep, valid, labels[...].astype(WIDE), counts[...].astype(WIDE)]
    columns = transposed_rows(jnp.concatenate(rows + [jnp.zeros((4, tok_count), WIDE)], axis=0))
    col_keep, col_valid = columns[:, 0:1], columns[:, 1:2]
    col_label, col_count = columns[:, 2:3], columns[:, 3:4].astype(jnp.int32)

    picker = (positions[...] == rows_of((tok_count, masked))).astype(LOW)
    kept = dot(jnp.concatenate([keep, jnp.zeros((7, tok_count), WIDE)], axis=0).astype(LOW), picker)
    code = jnp.where(kept[0:1] > 0.5, targets[...] + 1, 0)
    digits = jnp.concatenate([code >> 8, code & 255, jnp.zeros((6, masked), jnp.int32)], axis=0)
    digits = dot_tn(digits.astype(WIDE).astype(LOW), (rows_of((8, 128)) == lanes((8, 128))).astype(LOW)).astype(LOW)
    pb[z, x, y, :, width : width + 128] = digits

    for copy in loads:
        copy.wait()
    arrive(shared)
    table = w_s[...].reshape((-1, 128)).astype(WIDE).T

    outs = []

    def out(src, dst):
        copy = pltpu.make_async_copy(src, dst, out_sem.at[len(outs)])
        copy.start()
        outs.append(copy)

    blocks = hidden // BLOCK
    weight_co = cut(0, 16)
    arrive(swap[:1])
    top = jnp.maximum(lse_own[...], got_lse[...])
    lse = top + jnp.log(jnp.exp(lse_own[...] - top) + jnp.exp(got_lse[...] - top))
    shares = jnp.concatenate([jnp.exp(lse_own[...] - lse), jnp.exp(got_lse[...] - lse)], axis=0)
    shares = transposed_rows(shares)
    low_half = lanes((span, 128)) < HD
    for k, at in enumerate(ranges):
        arrive(swap[1 + k : 2 + k])
        mine = shares[k * span : (k + 1) * span]
        for p in range(width // 128):
            cols = slice(p * 128, (p + 1) * 128)
            share_own = jnp.where(low_half, mine[:, 2 * p : 2 * p + 1], mine[:, 2 * p + 1 : 2 * p + 2])
            share_got = jnp.where(low_half, mine[:, 8 + 2 * p : 9 + 2 * p], mine[:, 9 + 2 * p : 10 + 2 * p])
            mixed = o_own[at, cols].astype(WIDE) * share_own + got_o[at, cols].astype(WIDE) * share_got
            cross_o[at, cols] = mixed
            cross_low[at, cols] = mixed.astype(LOW)
        after_cross = after_self[at, :] + dot(cross_low[at, :], weight_co)
        ac[at, :] = after_cross
        normed = (normalised(after_cross)[0] * table[2:3] + table[6:7]).astype(LOW)
        n3[at, :] = normed
        for j in range(blocks):
            cols = slice(j * BLOCK, (j + 1) * BLOCK)
            pre = dot(normed, cut(16 + 16 * j, 32 + 16 * j))
            square = pre * pre
            bent = jnp.tanh(GELU * pre * (1.0 + CUBIC * square))
            half = 0.5 * (1.0 + bent)
            act[at, cols] = (pre * half).astype(LOW)
            slope[at, cols] = half + 0.5 * pre * (1.0 - bent * bent) * (GELU * (1.0 + 3.0 * CUBIC * square))
        if k == 0 and split:
            arrive(late_part)
            block = wm.at[:, 1 - x, c, :, rest]
            late_part = [push(block, block, me.across_core())]
    if split:
        arrive(late_part)
    flat_fo = cut(80, 144)
    state = ac[...] + dot(act[...], flat_fo)
    bs[...] = state
    head_in = (normalised(state)[0] * table[3:4] + table[7:8]).astype(LOW)
    head[...] = head_in

    picked = dot_tn(picker, head_in).astype(LOW)
    pb[z, x, y, :, 0:width] = picked
    mine = pb.at[z, x, y]
    flight = [push(mine, mine, peer) for peer in me.others()]

    block_ref[...] = bs[...].astype(LOW)
    out(block_ref, block_out)

    classes = BLOCK // 2
    flat_in = cut(144, 160).reshape((-1, 16, BLOCK))
    flat_in = jnp.concatenate([flat_in[:, :, :classes], flat_in[:, :, classes:]], axis=1).reshape((-1, classes))
    w_one, w_two = flat_in[:width], flat_in[width:]
    token_row = rows_of((tok_count, classes))
    ahead = pltpu.roll(dot(head_in, w_two), tok_count - 1, 0)
    logits = dot(head_in, w_one) + jnp.where(token_row == tok_count - 1, 0.0, ahead)
    top = jnp.max(logits, axis=1, keepdims=True)
    exps = jnp.exp(logits - top)
    total = jnp.sum(exps, axis=1, keepdims=True)
    hits = lanes((tok_count, classes)) == col_count
    entropy = top + jnp.log(total) - jnp.sum(jnp.where(hits, logits, 0.0), axis=1, keepdims=True)
    loss_col = col_valid * entropy
    grads = col_valid * (exps * (1.0 / total) - jnp.where(hits, 1.0, 0.0))
    g_insert = grads.astype(LOW)
    before = pltpu.roll(g_insert.astype(WIDE), 1, 0)
    g_before = jnp.where(token_row == 0, 0.0, before).astype(LOW)

    arrive(flight)
    column = pb.at[:, x, y]
    flight = [push(column, column, peer) for peer in (me.across_x(), me.across_y(), me.across_both())]

    flat_s = w_s[...].reshape((-1, 128))
    two = dot(head_in, flat_s)
    l_zero, l_one = two[:, 16:17], two[:, 17:18]
    top = jnp.maximum(l_zero, l_one)
    e_zero, e_one = jnp.exp(l_zero - top), jnp.exp(l_one - top)
    total = e_zero + e_one
    is_one = col_label > 0.5
    loss_col = loss_col + col_keep * (top + jnp.log(total) - jnp.where(is_one, l_one, l_zero))
    d_zero = col_keep * (e_zero / total - jnp.where(is_one, 0.0, 1.0))
    d_one = col_keep * (e_one / total - jnp.where(is_one, 1.0, 0.0))
    lane = lanes((tok_count, 128))
    g_delete = jnp.where(lane == 16, d_zero, jnp.where(lane == 17, d_one, 0.0)).astype(LOW)
    gh[...] = dot_nt(g_delete, flat_s) + dot_nt(g_insert, w_one) + dot_nt(g_before, w_two)
    arrive(flight)
    sibling = [push(pb, pb_got, me.across_core())]
    def rows_from(ref):
        return ref[...].reshape((-1, width + 128))

    gathered = rows_from(pb)
    rows_all = gathered[:, 0:width]
    numbers = gathered[:, width : width + 128].astype(WIDE).T
    code = numbers[0:1] * 256.0 + numbers[1:2]
    weight = jnp.where(code > 0.5, 1.0, 0.0)
    count = rows_all.shape[0]
    target = code.astype(jnp.int32) - 1
    place = rows_of((vocab_local, count))
    lt[...] = dot_nt(w_vocab[...].reshape((-1, width)), rows_all)
    hits = []
    for k in range(2):
        first = lax.axis_index(BOTH) + 2 * (k - c)
        hits.append(place + first * vocab_local == target)
    hits = jnp.concatenate(hits, axis=0)
    logits = lt[...]
    top = jnp.max(logits, axis=0, keepdims=True)
    exps = jnp.exp(logits - top)
    gt[...] = exps.astype(LOW)
    total = jnp.sum(exps, axis=0, keepdims=True)
    chosen = jnp.sum(jnp.where(hits, logits, 0.0), axis=0, keepdims=True)
    loss_here = jnp.sum(loss_col, axis=0, keepdims=True)
    folds = count // 128
    loss_rows = jnp.broadcast_to(loss_here, (st_z.shape[1] - 2 * folds, 128))
    st_q[x, y] = jnp.concatenate([folded(top + jnp.log(total)), folded(chosen), loss_rows], axis=0)
    spot = st_q.at[x, y]
    flight = [push(spot, spot, peer) for peer in (me.across_x(), me.across_y(), me.across_both())]
    small_cols[...] = dot_tn(head_in, g_delete)
    for k, grad in enumerate((g_insert, g_before)):
        pairs = dot_tn(head_in, grad).astype(LOW).reshape((-1, 2, 16, classes))
        for side in range(2):
            cols = slice(side * classes, (side + 1) * classes)
            put(144, pairs[:, side], k * (depth // 2), (k + 1) * (depth // 2), cols)
    arrive(flight)
    st_z[z] = merge_all([st_q[0, 0], st_q[0, 1], st_q[1, 0], st_q[1, 1]], folds)
    flight = [push(st_z.at[z], st_z.at[z], peer) for peer in me.others()]
    flat_vocab = w_vocab[...].reshape((-1, width))
    ew[...] = dot_tn(gt[...], flat_vocab)
    hw[...] = dot_tn(jnp.where(hits, 1.0, 0.0).astype(LOW), flat_vocab).astype(LOW)
    arrive(flight)
    stat = merge_all([st_z[k] for k in range(depth)], folds)
    all_loss = stat[2 * folds : 2 * folds + 1]
    stat = jnp.concatenate([unfolded(stat[0:folds]), unfolded(stat[folds : 2 * folds])], axis=0)
    factors = [weight * jnp.exp(top - stat[0:1]), weight, jnp.zeros((6, count), WIDE)]
    factors = transposed_rows(jnp.concatenate(factors, axis=0))
    mixed = ew[...] * factors[:, 0:1] - hw[...].astype(WIDE) * factors[:, 1:2]
    rb[...] = mixed.astype(LOW).reshape(rb.shape)
    flight = [
        push(rb.at[:, 1 - x, y], got_rq.at[0], me.across_x()),
        push(rb.at[:, x, 1 - y], got_rq.at[1], me.across_y()),
        push(rb.at[:, 1 - x, 1 - y], got_rq.at[2], me.across_both()),
    ]
    gt[...] = (weight * (jnp.exp(lt[...] - stat[0:1]) - jnp.where(hits, 1.0, 0.0))).astype(LOW)
    sibling.append(push(gt.at[pl.ds((1 - c) * vocab_local, vocab_local)], gt_got, me.across_core()))
    tokens = weight * (stat[0:1] - stat[1:2])
    mine = rows_of((masked, count)) + ((z * 2 + x) * 2 + y) * masked == lanes((masked, count))
    own = jnp.sum(jnp.where(mine, tokens, 0.0), axis=1, keepdims=True)
    token_out[...] = jnp.sum(
        jnp.where(rows_of((masked, masked)) == lanes((masked, masked)), own, 0.0), axis=0, keepdims=True
    )
    loss = (all_loss + jnp.sum(tokens, axis=1, keepdims=True)) * (1.0 / (tok_count * everyone))
    st_c[0] = jnp.broadcast_to(loss, (8, 128))
    sibling.append(push(st_c.at[0], st_c.at[1], me.across_core()))
    arrive(flight)
    line = rb[:, x, y].astype(WIDE)
    for k in range(3):
        line = line + got_rq[k].astype(WIDE)
    got_rq[3] = line.astype(LOW)
    flight = [
        push(got_rq.at[3, lax.rem(z + k, depth)], got_rz.at[k - 1], me.along(k)) for k in range(1, depth)
    ]
    arrive(sibling)
    loss_out[...] = st_c[0, 0:1, 0:1] + st_c[1, 0:1, 0:1]
    scale = (tok_count * everyone) ** (-0.5)
    mine = gt[pl.ds(pl.multiple_of(c * vocab_local, vocab_local), vocab_local), :]
    vocab_ref[...] = (dot(mine, rows_all) + dot(gt_got[...], rows_from(pb_got)[:, 0:width])) * scale
    out(vocab_ref, grad_vocab)
    arrive(flight)
    grad_picked = got_rq[3, z].astype(WIDE)
    for k in range(1, depth):
        grad_picked = grad_picked + got_rz[k - 1].astype(WIDE)
    coarse = grad_picked.astype(LOW)
    fine = (grad_picked - coarse.astype(WIDE)).astype(LOW)
    grad_head = gh[...] + dot(picker, coarse) + dot(picker, fine)

    gh[...] = grad_head
    gain_2 = gain_3 = bias_2 = bias_3 = 0.0
    low_half = lanes((span, 128)) < HD
    lane = lanes((span, 128))
    swap, delta_rows = [], []
    for at in ranges:
        grad_block, gain, bias = norm_back(bs[at, :], table[3:4], gh[at, :])
        gain_3, bias_3 = gain_3 + gain, bias_3 + bias
        g_half = grad_block.astype(LOW)
        g_ffn[at, :] = g_half
        slopes = [dot_nt(g_half, flat_fo[j * BLOCK : (j + 1) * BLOCK]) for j in range(blocks)]
        slopes = [(slopes[j] * slope[at, j * BLOCK : (j + 1) * BLOCK]).astype(LOW) for j in range(blocks)]
        upstream = sum(dot_nt(slopes[j], cut(16 + 16 * j, 32 + 16 * j)) for j in range(blocks))
        for j in range(blocks):
            gpre[at, j * BLOCK : (j + 1) * BLOCK] = slopes[j]
        back, gain, bias = norm_back(ac[at, :], table[2:3], upstream)
        gain_2, bias_2 = gain_2 + gain, bias_2 + bias
        grad_state = grad_block + back
        state_ref[at, :] = grad_state
        g_attn = dot_nt(grad_state.astype(LOW), weight_co).astype(LOW)
        g_ref[at, :] = g_attn
        swap.append(push(g_ref.at[at], g_other.at[at], me.across_y()))
        deltas = jnp.zeros((span, 128), WIDE)
        for p in range(width // 128):
            cols = slice(p * 128, (p + 1) * 128)
            product = g_attn[:, cols].astype(WIDE) * cross_o[at, cols]
            first = jnp.sum(jnp.where(low_half, product, 0.0), axis=1, keepdims=True)
            second = jnp.sum(jnp.where(low_half, 0.0, product), axis=1, keepdims=True)
            deltas = jnp.where(lane == 2 * p, first, jnp.where(lane == 2 * p + 1, second, deltas))
        delta_rows.append(deltas.T[0:8])
    st_own[...] = jnp.concatenate([lse, jnp.concatenate(delta_rows, axis=1)], axis=0)
    swap.append(push(st_own, st_other, me.across_y()))
    out(state_ref, state_out)
    out(g_ref, g_own)
    g_cross = state_ref[...].astype(LOW)

    cores = []

    def to_core(lo, hi):
        if split:
            at = pl.ds(lo, hi - lo)
            cores.append(push(eb.at[:, :, 1 - c, :, at], eb_got.at[:, :, :, at], me.across_core()))

    to_core(144, 160)
    for j in range(blocks):
        grad = dot_tn(act[:, j * BLOCK : (j + 1) * BLOCK], g_ffn[...]).astype(LOW)
        put(80, grad.reshape((-1, 64, BLOCK)), j * depth // blocks, (j + 1) * depth // blocks)
    to_core(80, 144)
    for j in range(blocks):
        grad = dot_tn(n3[...], gpre[:, j * BLOCK : (j + 1) * BLOCK]).astype(LOW)
        put(16 + 16 * j, grad.reshape((-1, 16, BLOCK)))
    to_core(16, 80)
    put(0, dot_tn(cross_low[...], g_cross).astype(LOW).reshape((-1, 16, BLOCK)))
    to_core(0, 16)
    small_rows[...] = jnp.concatenate([gain_2, gain_3, bias_2, bias_3, jnp.zeros((4, width), WIDE)], axis=0)
    if split:
        arrive(cores)
        one, two = pl.ds(0, RETURNED), pl.ds(RETURNED, LATE - RETURNED)
        for k, (at, first, spot) in enumerate(((one, 1 - y, 1), (two, 1 - x, 0), (one, y, 1), (two, x, 0))):
            for other in range(2):
                px, py = (other, first) if spot else (first, other)

                @pl.loop(0, depth)
                def _(zz):
                    total = eb[zz, px, c, py, at].astype(WIDE) + eb_got[zz, px, py, at].astype(WIDE)
                    sum_refs[k][other, zz] = total.astype(LOW)

            out(sum_refs[k], sums[k])
    else:
        sums[0][...] = eb[...]
    arrive(swap)
    for copy in pending:
        copy.wait_send()
    for copy in outs:
        copy.wait()


def middle_part(depth, split, seg, pad, labels, counts, positions, targets, w_vocab, after_self, attended, gs, parts):
    tok_count, width = after_self.shape
    hidden = 4 * BLOCK
    vocab_local = w_vocab.shape[0]
    everyone = depth * 8
    masked = positions.shape[1]
    count = masked * everyone // 2
    stat_rows = (2 * (count // 128) + 15) // 8 * 8
    sharded = (depth, 2, 2, 2)
    lead = sharded if split else (BLOCK // 16,)
    sharded = (depth, 2, 2, 2)
    if split:
        outs = [(shape_of((2, depth, n, BLOCK), LOW), ANY) for n in (RETURNED, LATE - RETURNED)] * 2
    else:
        outs = [(shape_of(parts[0].shape, LOW), VMEM)]
    outs += [
        (shape_of((tok_count, width), LOW), ANY),
        (shape_of((tok_count, width), WIDE), ANY),
        (shape_of((tok_count, width), LOW), ANY),
        (shape_of((tok_count, width), LOW), ANY),
        (shape_of((16, tok_count), WIDE), VMEM),
        (shape_of((16, tok_count), WIDE), ANY),
        (shape_of((8, width), WIDE), VMEM),
        (shape_of((width, 128), WIDE), VMEM),
        (shape_of((vocab_local, width), WIDE), ANY),
        (shape_of((1, masked), WIDE), VMEM),
        (shape_of((1, 1), WIDE), VMEM),
    ]
    copies = 32 + 2 * (depth - 1) + 3 + 1 + 1 + 3 + 1 + 3 + (depth - 1)
    return pl.pallas_call(
        partial(middle_kernel, depth, split),
        name="middle_part",
        out_shape=[o for o, _ in outs],
        in_specs=[ANY] * (13 + len(parts)),
        out_specs=[s for _, s in outs],
        scratch_shapes=[
            *[pltpu.VMEM(a.shape, a.dtype) for a in (seg, pad, labels, counts, positions, targets, attended[2])],
            pltpu.SemaphoreType.DMA((7,)),
            pltpu.VMEM((2, vocab_local, width), LOW),
            pltpu.VMEM((tok_count, width), WIDE),
            pltpu.VMEM((tok_count, width), LOW),
            pltpu.VMEM((tok_count, width), LOW),
            pltpu.VMEM((tok_count, width), WIDE),
            pltpu.VMEM((tok_count, width), LOW),
            pltpu.VMEM((vocab_local, width), WIDE),
            pltpu.SemaphoreType.DMA((10,)),
            pltpu.VMEM(lead + (160, BLOCK), LOW),
            pltpu.VMEM(lead + (160, BLOCK), LOW),
            pltpu.VMEM(((depth, 2, 2) if split else (1,)) + (160, BLOCK), LOW),
            pltpu.VMEM(gs.shape, LOW),
            pltpu.VMEM((tok_count, width), LOW),
            pltpu.VMEM((8, tok_count), WIDE),
            pltpu.VMEM((tok_count, width), WIDE),
            pltpu.VMEM((tok_count, width), LOW),
            pltpu.VMEM((tok_count, width), WIDE),
            pltpu.VMEM((tok_count, width), WIDE),
            pltpu.VMEM((tok_count, width), LOW),
            pltpu.VMEM((tok_count, hidden), LOW),
            pltpu.VMEM((tok_count, hidden), WIDE),
            pltpu.VMEM((tok_count, hidden), LOW),
            pltpu.VMEM((tok_count, width), LOW),
            pltpu.VMEM((2 * vocab_local, count), WIDE),
            pltpu.VMEM((2 * vocab_local, count), LOW),
            pltpu.VMEM((vocab_local, count), LOW),
            pltpu.VMEM((count, width), WIDE),
            pltpu.VMEM((count, width), LOW),
            pltpu.VMEM((depth, 2, 2, masked, width + 128), LOW),
            pltpu.VMEM((depth, 2, 2, masked, width + 128), LOW),
            pltpu.VMEM((depth, 2, 2, masked, width), LOW),
            pltpu.VMEM((4, depth, masked, width), LOW),
            pltpu.VMEM((max(depth - 1, 1), masked, width), LOW),
            pltpu.VMEM((2, 8, 128), WIDE),
            pltpu.VMEM((2, 2, stat_rows, 128), WIDE),
            pltpu.VMEM((depth, stat_rows, 128), WIDE),
            pltpu.VMEM((tok_count, width), WIDE),
            pltpu.VMEM((tok_count, width), LOW),
            pltpu.SemaphoreType.DMA((12,)),
            pltpu.SemaphoreType.DMA((copies + depth,)),
            pltpu.SemaphoreType.DMA((copies + depth,)),
        ]
        + ([pltpu.VMEM((2, depth, n, BLOCK), LOW) for n in (RETURNED, LATE - RETURNED)] * 2 if split else []),
        compiler_params=pltpu.CompilerParams(
            collective_id=1, has_side_effects=True, vmem_limit_bytes=LIMIT
        ),
    )(seg, pad, labels, counts, positions, targets, *attended[2:], w_vocab, after_self, *attended[:2], gs, *parts)


def self_backward_start(dk, dv):
    dk[...] = jnp.zeros_like(dk)
    dv[...] = jnp.zeros_like(dv)


def self_backward(blocks, qkv, out, lse_ref, g_ref, dqkv, dk, dv, row_seg, col_seg):
    tok_count, width = out.shape
    first, last = blocks
    pairs = width // 128

    def one(block, carry):
        at = pl.ds(pl.multiple_of(block * 128, 128), 128)
        low = self_window(block, tok_count)
        keys = pl.ds(low, 384)
        barred = self_bar(row_seg, col_seg, block, low)
        shape = (8, 128)
        halves = (rows_of(shape) == lanes(shape) // HD).astype(LOW)
        every = range(pairs)
        cols = [slice(p * 128, (p + 1) * 128) for p in every]
        q = [both_heads(qkv[at, cols[p]] * SCALE) for p in every]
        g = [both_heads(g_ref[at, cols[p]]) for p in every]
        keyed = [qkv[keys, width + p * 128 : width + (p + 1) * 128] for p in every]
        scores = [dot_nt(keyed[p], q[p]) + barred for p in every]
        slopes = [dot_nt(qkv[keys, 2 * width + p * 128 : 2 * width + (p + 1) * 128], g[p]) for p in every]
        products = [g_ref[at, cols[p]].astype(WIDE) * out[at, cols[p]].astype(WIDE) for p in every]
        coarse = [products[p].astype(LOW) for p in every]
        fine = [(products[p] - coarse[p].astype(WIDE)).astype(LOW) for p in every]
        deltas = [dot_nt(halves, coarse[p]) + dot_nt(halves, fine[p]) for p in every]
        deltas = [jnp.concatenate([deltas[p][0:1], deltas[p][1:2]], axis=1) for p in every]
        lses = [side_by_side_rows(lse_ref, 2 * p, at) for p in every]
        probs = [jnp.exp(scores[p] - lses[p]) for p in every]
        gscores = [(probs[p] * (slopes[p] - deltas[p])).astype(LOW) for p in every]
        grad_q = [heads_apart(dot_tn(keyed[p], gscores[p])) * SCALE for p in every]
        grad_k = [dk[keys, cols[p]] + dot(gscores[p], q[p]) for p in every]
        grad_v = [dv[keys, cols[p]] + dot(probs[p].astype(LOW), g[p]) for p in every]
        for p in every:
            dqkv[at, cols[p]] = grad_q[p].astype(LOW)
            dk[keys, cols[p]] = grad_k[p]
            dv[keys, cols[p]] = grad_v[p]
        return carry

    lax.fori_loop(first, last, one, 0)


def self_backward_end(dqkv, dk, dv):
    width = dk.shape[1]
    dqkv[:, width : 2 * width] = dk[...].astype(LOW)
    dqkv[:, 2 * width : 3 * width] = dv[...].astype(LOW)


def reduction(me, chunks, send, recv):
    z, x, c, y = me.z, me.x, me.c, me.y
    depth = me.depth
    count = len(chunks)
    started = [[None] * 3 for _ in chunks]
    used = [0] * count

    def launch(k, stage):
        copies = []

        def push(src, dst, peer):
            slot = used[k]
            used[k] += 1
            copy = remote(src, dst, send.at[k, slot], recv.at[k, slot], peer)
            copy.start()
            copies.append(copy)

        for src, got_c, got_q, got_z, at, put in chunks[k]:
            if stage == 0:
                push(src.at[:, :, 1 - c, :, at], got_c.at[:, :, :, at], me.across_core())
            elif stage == 1:
                push(got_c.at[:, 1 - x, y, at], got_q.at[0, :, at], me.across_x())
                push(got_c.at[:, x, 1 - y, at], got_q.at[1, :, at], me.across_y())
                push(got_c.at[:, 1 - x, 1 - y, at], got_q.at[2, :, at], me.across_both())
            else:
                for j in range(1, depth):
                    push(got_c.at[lax.rem(z + j, depth), x, y, at], got_z.at[j - 1, at], me.along(j))
        started[k][stage] = copies

    def absorb(k, stage):
        for copy in started[k][stage]:
            copy.wait_recv()
        for src, got_c, got_q, got_z, at, put in chunks[k]:
            if stage == 0:

                @pl.loop(0, depth)
                def _(zz):
                    for xx in range(2):
                        for yy in range(2):
                            total = src[zz, xx, c, yy, at].astype(WIDE) + got_c[zz, xx, yy, at].astype(WIDE)
                            got_c[zz, xx, yy, at] = total.astype(LOW)

            elif stage == 1:

                @pl.loop(0, depth)
                def _(zz):
                    total = got_c[zz, x, y, at].astype(WIDE)
                    for k in range(3):
                        total = total + got_q[k, zz, at].astype(WIDE)
                    got_c[zz, x, y, at] = total.astype(LOW)

            else:
                total = got_c[z, x, y, at].astype(WIDE)
                for j in range(1, depth):
                    total = total + got_z[j - 1, at].astype(WIDE)
                put(total)

    def begin(k):
        launch(k, 0)

    def after(k, stage):
        absorb(k, stage)
        if stage < 2:
            launch(k, stage + 1)

    def end():
        for stages in started:
            for copies in stages:
                for copy in copies:
                    copy.wait_send()

    return begin, after, end


def last_kernel(depth, reduces, *refs):
    given, dq_other = refs[:3], refs[3]
    held = refs[4:15]
    given += refs[15:17]
    (ga_in, gs_in) = refs[17:19]
    refs = refs[19:]
    if reduces:
        parts_in, refs = refs[:4], refs[4:]
    input_out, enc_out = refs[:2]
    refs = refs[2:]
    outs = refs[:9] if reduces else refs[:2]
    refs = refs[9:] if reduces else refs[2:]
    (dkv, enc, dq_own, start, one, qkv, low, lse, after, two, gstate) = refs[:11]
    (ga, gs, g_query, g_attn, dqkv, dk, dv, row_seg, row_keep, col_seg, load_sem, dq_got, sw_send, sw_recv) = refs[11:25]
    grad_input, grad_enc, out_sem = refs[25:28]
    (pair, seg, pad, small_rows, small_cols, few_sem) = refs[28:34]
    refs = refs[34:]
    few = bring(given, (pair, seg, pad, small_rows, small_cols), few_sem)
    if reduces:
        parts, part_sem, refs = refs[:4], refs[4], refs[5:]
        fetched = [pltpu.make_async_copy(parts_in[k], parts[k], part_sem.at[k]) for k in range(4)]
        for copy in fetched:
            copy.start()
    refs_held = (dkv, enc, dq_own, start, one, qkv, low, lse, after, two, gstate)
    tok_count, width = dq_own.shape
    src_count = enc.shape[0]
    everyone = depth * 8
    me = Place(depth)
    scale = (tok_count * everyone) ** (-0.5)
    loads = []
    for src, dst in list(zip(held, refs_held)) + [(gs_in, gs), (ga_in, ga)]:
        copy = pltpu.make_async_copy(src, dst, load_sem.at[len(loads)])
        copy.start()
        loads.append(copy)
    if reduces:
        greet(me.others() + [me.across_x(), me.across_y(), me.across_both(), me.across_core()])
    else:
        greet([me.across_y()])
    halves = 2
    half = tok_count // halves
    swaps = []
    for k in range(halves):
        at = pl.ds(k * half, half)
        swaps.append(remote(dq_other.at[at], dq_got.at[at], sw_send.at[k], sw_recv.at[k], me.across_y()))
        swaps[-1].start()

    if reduces:
        (late, late_s, ex, ey, ex_got, ey_got, ez, ez_got, c_a, c_s, q_a, q_s, z_a, z_s, ez_send, ez_recv, send, recv) = refs
        (o_qkv, o_so, o_cq, o_kv, o_co, o_fi, o_fo, o_in, o_s) = outs

        def put_kv(total):
            o_kv[:, 0:BLOCK] = total[0:16] * scale
            o_kv[:, BLOCK : 2 * BLOCK] = total[16:32] * scale

        def put_mid(total):
            o_so[...] = total[0:16] * scale
            o_cq[...] = total[16:32] * scale

        def put_qkv(k, total):
            o_qkv[:, k * BLOCK : (k + 1) * BLOCK] = total * scale

        def put_s(total):
            o_s[...] = total * scale

        def rows(lo, hi, put):
            return (late, c_a, q_a, z_a, pl.ds(lo, hi - lo), put)

        chunks = [
            [rows(KV, EARLY, put_kv)],
            [rows(SO, KV, put_mid)],
            [rows(0, 16, partial(put_qkv, 0))],
            [rows(16, 32, partial(put_qkv, 1))],
            [rows(32, SO, partial(put_qkv, 2))],
            [(late_s, c_s, q_s, z_s, pl.ds(0, 16), put_s)],
        ]

        z, x, y = me.z, me.x, me.y
        for copy in fetched:
            copy.wait()
        for total, own, got in ((ex, parts[0], parts[1]), (ey, parts[2], parts[3])):

            @pl.loop(0, depth)
            def _(zz):
                for k in range(2):
                    total[k, zz] = (own[k, zz].astype(WIDE) + got[k, zz].astype(WIDE)).astype(LOW)

        plane = [
            remote(ex.at[1 - x], ex_got, ez_send.at[0], ez_recv.at[0], me.across_x()),
            remote(ey.at[1 - y], ey_got, ez_send.at[1], ez_recv.at[1], me.across_y()),
        ]
        for copy in plane:
            copy.start()
        along = []

        def onward():
            for copy in plane:
                copy.wait_recv()

            @pl.loop(0, depth)
            def _(zz):
                ez[zz, 0:RETURNED] = (ex[x, zz].astype(WIDE) + ex_got[zz].astype(WIDE)).astype(LOW)
                ez[zz, RETURNED:LATE] = (ey[y, zz].astype(WIDE) + ey_got[zz].astype(WIDE)).astype(LOW)

            for k in range(1, depth):
                to = lax.rem(z + k, depth)
                at = 1 + k
                along.append(remote(ez.at[to], ez_got.at[k - 1], ez_send.at[at], ez_recv.at[at], me.along(k)))
                along[-1].start()

        def settle():
            for copy in plane:
                copy.wait_send()
            for copy in along:
                copy.wait()
            total = ez[me.z].astype(WIDE)
            for k in range(depth - 1):
                total = total + ez_got[k].astype(WIDE)
            total = total * scale
            o_co[...] = total[0:16]
            for k in range(4):
                o_fi[:, k * BLOCK : (k + 1) * BLOCK] = total[16 + 16 * k : 32 + 16 * k]
            o_fo[...] = total[80:144]
            half = BLOCK // 2
            for k in range(2):
                o_in[16 * k : 16 * (k + 1)] = total[144:160, half * k : half * (k + 1)]

        begin, after_stage, end = reduction(me, chunks, send, recv)

        def keep(lo, value):
            late[:, :, :, :, lo : lo + 16] = value.astype(LOW).reshape(late.shape[:4] + (16, BLOCK))

        def keep_small(value):
            late_s[...] = value.astype(LOW).reshape(late_s.shape)
    else:
        def begin(k):
            return None

        def after_stage(k, stage):
            return None

        end = onward = settle = lambda: None
        o_late, o_small = outs

        def keep(lo, value):
            o_late[:, lo : lo + 16] = value.astype(LOW).reshape((-1, 16, BLOCK))

        def keep_small(value):
            o_small[...] = value

    chunk_kv, chunk_mid, chunk_q, chunk_k, chunk_v, chunk_s = range(6)
    for copy in few:
        copy.wait()
    onehot = token_numbers(seg, pad, pair, row_seg, row_keep, col_seg)
    cut = cutter(ga)
    for copy in loads[:2]:
        copy.wait()
    keep(KV, dot_tn(enc[...], dkv[:, 0:width]))
    keep(KV + 16, dot_tn(enc[...], dkv[:, width : 2 * width]))
    begin(chunk_kv)
    for copy in loads[2:]:
        copy.wait()
    table = cutter(gs)(0, gs.shape[-2]).astype(WIDE).T
    self_backward_start(dk, dv)
    gains = biases = 0.0
    for k in range(halves):
        at = pl.ds(k * half, half)
        swaps[k].wait()
        query = (dq_own[at, :] + dq_got[at, :].astype(WIDE)).astype(LOW)
        g_query[at, :] = query
        back, gain_1, bias_1 = norm_back(after[at, :], table[1:2], dot_nt(query, cut(CQ, KV)))
        gains, biases = gains + gain_1, biases + bias_1
        state = gstate[at, :] + back
        gstate[at, :] = state
        g_attn[at, :] = dot_nt(state.astype(LOW), cut(SO, CQ)).astype(LOW)
        if k == 0:
            after_stage(chunk_kv, 0)
        if k == halves - 1:
            keep(CQ, dot_tn(two[...], g_query[...]))
            keep(SO, dot_tn(low[...], gstate[...].astype(LOW)))
            begin(chunk_mid)
        blocks = (k * half // 128, (k + 1) * half // 128)
        self_backward(blocks, qkv, low, lse, g_attn, dqkv, dk, dv, row_seg, col_seg)
        if k == 0:
            onward()
    after_stage(chunk_mid, 0)
    self_backward_end(dqkv, dk, dv)
    for k, chunk in enumerate((chunk_q, chunk_k, chunk_v)):
        keep(QKV + 16 * k, dot_tn(one[...], dqkv[:, k * width : (k + 1) * width]))
        begin(chunk)
    after_stage(chunk_q, 0)
    after_stage(chunk_k, 0)
    after_stage(chunk_v, 0)
    after_stage(chunk_kv, 1)
    upstream = dot_nt(dqkv[:, 0:width], cut(QKV, QKV + 16))
    upstream = upstream + dot_nt(dqkv[:, width : 2 * width], cut(QKV + 16, QKV + 32))
    upstream = upstream + dot_nt(dqkv[:, 2 * width : 3 * width], cut(QKV + 32, SO))
    back, gain_0, bias_0 = norm_back(start[...], table[0:1], upstream)
    grad_start = gstate[...] + back
    grad_input[...] = grad_start.astype(LOW)
    stores = [pltpu.make_async_copy(grad_input, input_out, out_sem.at[4])]
    stores[0].start()
    coarse = grad_start.astype(LOW)
    fine = (grad_start - coarse.astype(WIDE)).astype(LOW)
    g_table = (dot_tn(onehot, coarse) + dot_tn(onehot, fine))[8:16]
    mid = small_rows[...]
    stacked = jnp.concatenate([gain_0, gains, mid[0:2], bias_0, biases, mid[2:4], g_table], axis=0)
    keep_small(transposed_rows(stacked) + small_cols[...])
    begin(chunk_s)
    after_stage(chunk_mid, 1)
    w_key, w_val = cut(KV, KV + 16), cut(KV + 16, EARLY)
    span = src_count // 4

    def source_grads(k):
        at = pl.ds(k * span, span)
        grads = dot_nt(dkv[at, 0:width], w_key) + dot_nt(dkv[at, width : 2 * width], w_val)
        grad_enc[at, :] = grads.astype(LOW)
        stores.append(pltpu.make_async_copy(grad_enc.at[at], enc_out.at[at], out_sem.at[k]))
        stores[-1].start()

    source_grads(0)
    after_stage(chunk_s, 0)
    after_stage(chunk_kv, 2)
    after_stage(chunk_q, 1)
    source_grads(1)
    after_stage(chunk_k, 1)
    source_grads(2)
    after_stage(chunk_v, 1)
    after_stage(chunk_s, 1)
    source_grads(3)
    settle()
    for chunk in (chunk_mid, chunk_q, chunk_k, chunk_v, chunk_s):
        after_stage(chunk, 2)
    end()
    for copy in stores:
        copy.wait()


def last_part(depth, reduces, pair, seg, pad, dq_own, dq_other, dkv, enc, kept, gstate, grads, whole):
    tok_count, width = dq_own.shape
    src_count = enc.shape[0]
    ga, gs = whole
    parts, small_rows, small_cols = grads
    everyone = depth * 8
    rows = BLOCK // everyone
    sharded = (depth, 2, 2, 2)
    held = (dkv, enc, dq_own, *kept, gstate)
    outs = [shape_of((tok_count, width), LOW), shape_of((src_count, width), LOW)]
    scratch = [pltpu.VMEM(a.shape, a.dtype) for a in held]
    scratch += [
        pltpu.VMEM(ga.shape, LOW),
        pltpu.VMEM(gs.shape, LOW),
        pltpu.VMEM((tok_count, width), LOW),
        pltpu.VMEM((tok_count, width), LOW),
        pltpu.VMEM((tok_count, 3 * width), LOW),
        pltpu.VMEM((tok_count, width), WIDE),
        pltpu.VMEM((tok_count, width), WIDE),
        pltpu.VMEM((1, tok_count), WIDE),
        pltpu.VMEM((1, tok_count), WIDE),
        pltpu.VMEM((tok_count, 128), WIDE),
        pltpu.SemaphoreType.DMA((14,)),
        pltpu.VMEM((tok_count, width), LOW),
        pltpu.SemaphoreType.DMA((2,)),
        pltpu.SemaphoreType.DMA((2,)),
        pltpu.VMEM((tok_count, width), LOW),
        pltpu.VMEM((src_count, width), LOW),
        pltpu.SemaphoreType.DMA((5,)),
        *[pltpu.VMEM(a.shape, a.dtype) for a in (pair, seg, pad, small_rows, small_cols)],
        pltpu.SemaphoreType.DMA((5,)),
    ]
    if reduces:
        shapes = [(EARLY, BLOCK), (16, 128)]
        outs += [
            shape_of((rows, 3 * BLOCK), WIDE),
            shape_of((rows, BLOCK), WIDE),
            shape_of((rows, BLOCK), WIDE),
            shape_of((rows, 2 * BLOCK), WIDE),
            shape_of((rows, BLOCK), WIDE),
            shape_of((rows, 4 * BLOCK), WIDE),
            shape_of((4 * rows, BLOCK), WIDE),
            shape_of((2 * rows, BLOCK // 2), WIDE),
            shape_of((rows, 128), WIDE),
        ]
        scratch += [pltpu.VMEM(a.shape, LOW) for a in parts] + [pltpu.SemaphoreType.DMA((4,))]
        scratch += [pltpu.VMEM(sharded + s, LOW) for s in shapes]
        scratch += [pltpu.VMEM(parts[0].shape, LOW), pltpu.VMEM(parts[2].shape, LOW)]
        scratch += [pltpu.VMEM(parts[0].shape[1:], LOW), pltpu.VMEM(parts[2].shape[1:], LOW)]
        scratch += [pltpu.VMEM((depth, LATE, BLOCK), LOW), pltpu.VMEM((depth - 1, LATE, BLOCK), LOW)]
        for lead in ((depth, 2, 2), (3, depth), (depth - 1,)):
            scratch += [pltpu.VMEM(lead + s, LOW) for s in shapes]
        scratch += [pltpu.SemaphoreType.DMA((depth + 2,))] * 2
        slots = 2 * (depth + 3)
        scratch += [pltpu.SemaphoreType.DMA((6, slots)), pltpu.SemaphoreType.DMA((6, slots))]
    else:
        outs += [shape_of((BLOCK // 16, EARLY, BLOCK), LOW), shape_of((BLOCK, 128), WIDE)]
    return pl.pallas_call(
        partial(last_kernel, depth, reduces),
        name="last_part",
        out_shape=outs,
        in_specs=[ANY] * (19 + len(parts)),
        out_specs=[ANY] * 2 + [VMEM] * (len(outs) - 2),
        scratch_shapes=scratch,
        compiler_params=pltpu.CompilerParams(
            collective_id=2, has_side_effects=True, vmem_limit_bytes=LIMIT
        ),
    )(pair, seg, pad, dq_other, *held, small_rows, small_cols, ga, gs, *parts)


def finish_kernel(count, *refs):
    ins, (small_in, loss_in) = refs[:count], refs[count : count + 2]
    outs, tiny_outs = refs[count + 2 : 2 * count + 2], refs[2 * count + 2 : 2 * count + 7]
    refs = refs[2 * count + 7 :]
    held, (small, loss) = refs[:count], refs[count : count + 2]
    tiny, sems = refs[count + 2 : count + 7], refs[count + 7]
    ahead = [pltpu.make_async_copy(small_in, small, sems.at[0, count]), pltpu.make_async_copy(loss_in, loss, sems.at[0, count + 1])]
    first = [pltpu.make_async_copy(ins[k], held[k], sems.at[0, k]) for k in range(count)]
    copies = [pltpu.make_async_copy(held[k], outs[k], sems.at[1, k]) for k in range(count)]
    for copy in ahead + first:
        copy.start()
    for copy in ahead:
        copy.wait()
    values = small[...]
    rows = values.shape[0]
    turned = jnp.concatenate([values, jnp.zeros((128 - rows, 128), WIDE)], axis=0).T
    for ref, lo, hi in zip(tiny[:4], (0, 4, 8, 16), (4, 8, 16, 18)):
        ref[...] = turned[lo:hi, 0:rows]
    tiny[4][...] = loss[...]
    for k in range(5):
        copies.append(pltpu.make_async_copy(tiny[k], tiny_outs[k], sems.at[1, count + k]))
        copies[-1].start()
    for k in range(count):
        first[k].wait()
        copies[k].start()
    for copy in copies:
        copy.wait()


def finish(results, small, loss):
    count = len(results)
    rows = small.shape[0]
    tiny = [shape_of(s, WIDE) for s in ((4, rows), (4, rows), (PAIRS, rows), (2, rows), (1, 1))]
    outs = [shape_of(a.shape, a.dtype) for a in results] + tiny
    held = list(results) + [small, loss] + tiny
    res = pl.pallas_call(
        partial(finish_kernel, count),
        name="finish",
        out_shape=outs,
        in_specs=[ANY] * (count + 2),
        out_specs=[ANY] * len(outs),
        scratch_shapes=[pltpu.VMEM(a.shape, a.dtype) for a in held]
        + [pltpu.SemaphoreType.DMA((2, count + 5))],
        compiler_params=pltpu.CompilerParams(vmem_limit_bytes=LIMIT),
    )(*results, small, loss)
    return res[:count], res[count:]


def late_blocks(cross_out, ffn_in, ffn_out, insert):
    groups = cross_out.shape[0] // 16
    return jnp.concatenate(
        [
            cross_out.reshape(groups, 16, BLOCK),
            ffn_in.reshape(groups, 16, 4, BLOCK).swapaxes(1, 2).reshape(groups, 64, BLOCK),
            ffn_out.reshape(groups, 64, BLOCK),
            insert.reshape(groups, 2, 16, BLOCK // 2).swapaxes(1, 2).reshape(groups, 16, BLOCK),
        ],
        axis=1,
    )


def gather_by_ops(qkv, self_out, cross_q, cross_kv, small):
    wide = jnp.concatenate([qkv, self_out, cross_q, cross_kv], axis=1)
    ga = lax.all_gather(wide, BOTH, axis=0, tiled=True).reshape(-1, 16, 7, BLOCK).swapaxes(1, 2)
    gs = lax.all_gather(small, BOTH, axis=0, tiled=True)
    return ga.reshape(-1, EARLY, BLOCK), gs.reshape(-1, 16, 128)


def partner(array, depth, axis):
    dx, dy = (1, 0) if axis == "x" else (0, 1)
    pairs = []
    for z in range(depth):
        for x in range(2):
            for c in range(2):
                for y in range(2):
                    here = ((z * 2 + x) * 2 + c) * 2 + y
                    there = ((z * 2 + (x ^ dx)) * 2 + c) * 2 + (y ^ dy)
                    pairs.append((here, there))
    return lax.ppermute(array, BOTH, pairs)


def reduce_by_ops(early, small, late, scale):
    groups = late.shape[0]
    gw_f = late[:, 80:144].reshape(groups * 64, BLOCK)
    gw_i = late[:, 144:160].reshape(groups, 16, 2, BLOCK // 2).swapaxes(1, 2).reshape(groups * 32, BLOCK // 2)
    late = late[:, 0:80].reshape(groups, 5, 16, BLOCK).swapaxes(0, 1).reshape(5, BLOCK, BLOCK)
    early = early.reshape(groups, 7, 16, BLOCK).swapaxes(0, 1).reshape(7, BLOCK, BLOCK)
    wide = jnp.concatenate([early, late]).swapaxes(0, 1).reshape(BLOCK, 12 * BLOCK)

    def sums(a):
        return lax.psum_scatter(a.astype(WIDE), BOTH, scatter_dimension=0, tiled=True) * scale

    own = sums(wide)
    edges = (0, 3, 4, 5, 7, 8, 12)
    pieces = [own[:, lo * BLOCK : hi * BLOCK] for lo, hi in zip(edges[:-1], edges[1:])]
    return pieces + [sums(gw_f), sums(gw_i), sums(small)]


def body(
    dec_input, enc_output, segment_ids, padding, pair_ids, src_lengths, delete_labels, insert_counts,
    masked_positions, masked_targets, norm_gain, norm_bias, pair_table, self_qkv, self_out, cross_q, cross_kv,
    cross_out, ffn_in, ffn_out, w_delete, w_insert, w_vocab,
):
    everyone = lax.axis_size(BOTH)
    depth = everyone // 8
    tok_count = dec_input.shape[0]
    aligned = self_qkv.shape[0] == 16
    late = (cross_out, ffn_in, ffn_out, w_insert)
    tiny = (norm_gain, norm_bias, pair_table, w_delete.T)
    raw = (self_qkv, self_out, cross_q, cross_kv)
    whole = gathered = None
    if not aligned:
        gathered = late_blocks(*[lax.all_gather(a, BOTH, axis=0, tiled=True) for a in late])
        small = jnp.concatenate([norm_gain, norm_bias, pair_table, w_delete.T], axis=0).T
        small = jnp.pad(small, ((0, 0), (0, 128 - small.shape[1])))
        whole = gather_by_ops(*raw, small)
    whole, line, firsts = first_part(
        depth, aligned, segment_ids, padding, pair_ids, dec_input, enc_output, tiny, raw, late, whole
    )
    start, one, qkv, low, lse, after, two, query, other_query, kv, other_seg = firsts
    parts = (*line, partner(line[0], depth, "x")) if aligned else (gathered,)
    o_own, o_other, lse_own, lse_other = cross_forward(src_lengths, segment_ids, other_seg, query, other_query, kv)
    mids = middle_part(
        depth, aligned, segment_ids, padding, delete_labels, insert_counts, masked_positions, masked_targets,
        w_vocab, after, (o_own, o_other, lse_own, lse_other), whole[1], parts,
    )
    count = 4 if aligned else 1
    parts, mids = mids[:count], mids[count:]
    block_out, gstate, g_own, g_other, st_own, st_other, small_rows, small_cols, grad_vocab, tokens, loss = mids
    sums = ()
    if aligned:
        sums = (parts[2], partner(parts[0], depth, "y"), parts[3], partner(parts[1], depth, "x"))
    dq_own, dq_other, dkv, block_out, grad_vocab = cross_backward(
        src_lengths, segment_ids, other_seg, query, other_query, g_own, g_other, st_own, st_other, kv,
        (block_out, grad_vocab),
    )
    res = last_part(
        depth, aligned, pair_ids, segment_ids, padding, dq_own, dq_other, dkv, enc_output,
        (start, one, qkv, low, lse, after, two), gstate, (sums, small_rows, small_cols), whole,
    )
    if aligned:
        sums = res[2:]
    else:
        scale = (tok_count * everyone) ** (-0.5)
        sums = reduce_by_ops(res[2], res[3], parts[0], scale)
    results, smalls = finish((res[1], res[0], *sums[:8], tokens), sums[8], loss)
    grad_enc, grad_input, qkv, so, cq, kv, co, fi, fo, insert, tokens = results
    gain, bias, table, delete, loss = smalls
    return (
        block_out, grad_input, grad_enc, gain, bias, table, qkv, so, cq, kv, co, fi, fo, delete.T, insert,
        grad_vocab, loss[0, 0], tokens,
    )


def solution(mesh):
    shared = P(BOTH, None)
    across = P(None, BOTH)
    return jax.shard_map(
        body,
        mesh=mesh,
        in_specs=(shared,) * 5 + (P("batch", None),) + (shared,) * 4 + (across,) * 3 + (shared,) * 10,
        out_specs=(shared,) * 3 + (across,) * 3 + (shared,) * 10 + (P(), shared),
        check_vma=False,
    )
```
